32 devices in a mesh: dp: 8 (over y, x, core), tensor: 4 (over z).
Axes of the slice: x: 2, y: 2, z: 4, core: 2. Of those that a mesh axis runs over, the one named last changes fastest.
Arguments:
- inputs: float32 [8192, 2048], P(('dp', 'tensor')), may hold values from -6 to 6
- lengths: int32 [8], P('dp'), may hold values from 128 to 1024, as said below
- gain_mix: bfloat16 [2048], P(('dp', 'tensor')), may hold values from 0.5 to 1.5
- gain_glu: bfloat16 [2048], P(('dp', 'tensor')), may hold values from 0.5 to 1.5
- lower_bound: bfloat16 [2048], P(('dp', 'tensor')), may hold values from 0 to 0.997
- w_input: bfloat16 [2048, 2048], P(('dp', 'tensor')), may hold values from -0.125 to 0.125
- w_forget: bfloat16 [2048, 2048], P(('dp', 'tensor')), may hold values from -0.125 to 0.125
- w_gate_mix: bfloat16 [2048, 2048], P(('dp', 'tensor')), may hold values from -0.125 to 0.125
- w_out: bfloat16 [2048, 2048], P(('dp', 'tensor')), may hold values from -0.5 to 0.5
- w_gate: bfloat16 [2048, 5632], P('dp', 'tensor'), may hold values from -0.125 to 0.125
- w_up: bfloat16 [2048, 5632], P('dp', 'tensor'), may hold values from -0.125 to 0.125
- w_down: bfloat16 [5632, 2048], P('tensor', 'dp'), may hold values from -0.15625 to 0.15625
- cotangent: float32 [8192, 2048], P(('dp', 'tensor')), may hold values from -6 to 6
Outputs:
- output: float32 [8192, 2048], P(('dp', 'tensor'))
- grad_inputs: float32 [8192, 2048], P(('dp', 'tensor'))
- grad_gain_mix: float32 [2048], P(('dp', 'tensor'))
- grad_gain_glu: float32 [2048], P(('dp', 'tensor'))
- grad_lower_bound: float32 [2048], P(('dp', 'tensor'))
- grad_w_input: float32 [2048, 2048], P(('dp', 'tensor'))
- grad_w_forget: float32 [2048, 2048], P(('dp', 'tensor'))
- grad_w_gate_mix: float32 [2048, 2048], P(('dp', 'tensor'))
- grad_w_out: float32 [2048, 2048], P(('dp', 'tensor'))
- grad_w_gate: float32 [2048, 5632], P('dp', 'tensor')
- grad_w_up: float32 [2048, 5632], P('dp', 'tensor')
- grad_w_down: float32 [5632, 2048], P('tensor', 'dp')
The draws below stay inside these ranges and needn't reach their ends.
Inputs may be any that keep to these rules, and one draw needn't show every extreme that they name: `lengths`: each entry is the live length of one sequence, its live rows first; in every draw one entry equals 1024.
All inputs are finite; a program needn't handle non-finite values.
Results may differ from the reference program's by a relative error of at most 0.0087.
Values may be sent and summed in bfloat16 or wider, within the bound.
A program may use at most 320 MiB of HBM per device.

```python
import jax
import jax.numpy as jnp
from jax import lax

D = 2048
FF = 5632
SEQ_LEN = 1024
MIN_LEN = 128
SEQS = 8
TOKENS = 8192


def draw_lengths(key, part):
    key = jax.random.fold_in(key, 11)
    keys = jax.random.split(key, 3)
    halving = jax.random.randint(keys[0], (SEQS,), 0, 3)
    ceiling = jnp.right_shift(jnp.full((SEQS,), SEQ_LEN, jnp.int32), halving)
    offset = jax.random.randint(keys[1], (SEQS,), 0, 1 << 30) % (ceiling // 4 + 1)
    result = jnp.maximum(ceiling - offset, MIN_LEN)
    chosen = jax.random.randint(keys[2], (), 0, SEQS)
    result = jnp.where(jnp.arange(SEQS) == chosen, SEQ_LEN, result)
    return result.astype(jnp.int32)


def near_one(key, share, widest):
    keys = jax.random.split(key, 3)
    spread_low = jax.random.uniform(keys[0], (D,), jnp.float32, 0.0, 0.9)
    gap = jnp.exp(jax.random.uniform(keys[1], (D,), jnp.float32, jnp.log(0.0045), jnp.log(widest)))
    picked = jax.random.bernoulli(keys[2], share, (D,))
    return jnp.where(picked, 1.0 - gap, spread_low).astype(jnp.float32)


def draw_lower_bound(key, part):
    key = jax.random.fold_in(key, 23)
    return near_one(key, 0.375, 0.02).astype(jnp.bfloat16)


def levels(rng, dims, pieces, low, top_value):
    def one(axis_at, parts):
        steps = jax.random.uniform(jax.random.fold_in(jax.random.fold_in(rng, 6), axis_at), (parts,), jnp.float32, low / len(pieces), top_value / len(pieces))
        return jnp.repeat(jnp.exp(steps), dims[axis_at] // parts).reshape((-1,) + (1,) * (len(dims) - axis_at - 1))

    loudness = one(*pieces[0])
    for cut in pieces[1:]:
        loudness = loudness * one(*cut)
    return loudness


def noise(rng, dims, scale, bound, pieces=(), held_as=jnp.bfloat16):
    entries = scale * jax.random.normal(rng, dims, jnp.float32)
    if pieces:
        entries = entries * levels(rng, dims, pieces, -0.22, 0.18)
    return jnp.clip(entries, -bound, bound).astype(held_as)


def setup_inputs(seed: int = 0) -> dict:
    key_of = jax.random.split(jax.random.key(seed), 14)
    return {
        "inputs": noise(key_of[0], (TOKENS, D), 1.0, 6.0, ((0, 32),), jnp.float32),
        "lengths": draw_lengths(jax.random.fold_in(key_of[13], 71), 0),
        "gain_mix": jnp.clip(1.0 + 0.1 * jax.random.normal(key_of[2], (D,), jnp.float32), 0.5, 1.5).astype(jnp.bfloat16),
        "gain_glu": jnp.clip(1.0 + 0.1 * jax.random.normal(key_of[3], (D,), jnp.float32), 0.5, 1.5).astype(jnp.bfloat16),
        "lower_bound": draw_lower_bound(jax.random.fold_in(key_of[13], 71), 0),
        "w_input": noise(key_of[5], (D, D), D ** -0.5, 0.125, ((0, 32),)),
        "w_forget": noise(key_of[6], (D, D), D ** -0.5, 0.125, ((0, 32),)),
        "w_gate_mix": noise(key_of[7], (D, D), D ** -0.5, 0.125, ((0, 32),)),
        "w_out": noise(key_of[8], (D, D), (D // 16) ** -0.5, 0.5, ((0, 32),)),
        "w_gate": noise(key_of[9], (D, FF), D ** -0.5, 0.125, ((0, 8), (1, 4))),
        "w_up": noise(key_of[10], (D, FF), D ** -0.5, 0.125, ((0, 8), (1, 4))),
        "w_down": noise(key_of[11], (FF, D), (FF // 4) ** -0.5, 0.15625, ((0, 4), (1, 8))),
        "cotangent": noise(key_of[12], (TOKENS, D), 1.0, 6.0, ((0, 32),), jnp.float32),
    }


epsilon = 1e-06
highest = lax.Precision.HIGHEST

@jax.custom_vjp
def low(v):
    return lax.optimization_barrier(v.astype(jnp.bfloat16)).astype(jnp.float32)

@jax.custom_vjp
def low_back(v):
    return v

def low_keep(v):
    return (low(v), None)

def low_pass(kept, grad):
    return (grad,)

def back_keep(v):
    return (v, None)

def back_low(kept, grad):
    return (low(grad),)
low.defvjp(low_keep, low_pass)
low_back.defvjp(back_keep, back_low)

def product(left, right):
    return jnp.dot(left, right, precision=highest)

def silu_of(value):
    return value * jax.nn.sigmoid(value)

def normalize(value):
    return value * lax.rsqrt(lax.optimization_barrier(jnp.mean(value * value, axis=-1, keepdims=True)) + epsilon)

def recurrence(forget, inflow):
    forget_seq = forget.reshape(SEQS, SEQ_LEN, D).swapaxes(0, 1)
    inflow_seq = inflow.reshape(SEQS, SEQ_LEN, D).swapaxes(0, 1)

    def advance(carry, pair):
        carry = pair[0] * carry + pair[1]
        return (carry, carry)
    start = jnp.zeros((SEQS, D), jnp.float32)
    _, states = lax.scan(advance, start, (forget_seq, inflow_seq))
    return states.swapaxes(0, 1).reshape(TOKENS, D)

def layer(inputs, gain_mix, gain_glu, lower_bound, w_input, w_forget, w_gate_mix, w_out, w_gate, w_up, w_down, live_mask):
    normed_one = low(normalize(inputs) * gain_mix)
    input_pre = low_back(product(normed_one, w_input))
    forget_pre = low_back(product(normed_one, w_forget))
    gate_pre = low_back(product(normed_one, w_gate_mix))
    forget = lower_bound + (1.0 - lower_bound) * jax.nn.sigmoid(forget_pre)
    inflow = live_mask * (1.0 - forget) * silu_of(input_pre)
    state = recurrence(forget, inflow)
    mixed_low = low(state * silu_of(gate_pre))
    stream = inputs + low_back(product(mixed_low, w_out))
    normed_two = low(normalize(stream) * gain_glu)
    glu_gate = low_back(product(normed_two, w_gate))
    glu_up = low_back(product(normed_two, w_up))
    hidden = low(silu_of(glu_gate) * glu_up)
    glu_result = low_back(product(hidden, w_down))
    return live_mask * (stream + glu_result)

def reference(inputs, lengths, gain_mix, gain_glu, lower_bound, w_input, w_forget, w_gate_mix, w_out, w_gate, w_up, w_down, cotangent):
    position = jnp.arange(TOKENS, dtype=jnp.int32)
    owner = position // SEQ_LEN
    live_mask = (position - owner * SEQ_LEN < lengths[owner]).astype(jnp.float32)[:, None]
    params = tuple((param.astype(jnp.float32) for param in (gain_mix, gain_glu, lower_bound, w_input, w_forget, w_gate_mix, w_out, w_gate, w_up, w_down)))

    def forward(*values):
        return layer(*values, live_mask)
    output, pullback = jax.vjp(forward, inputs, *params)
    grads = pullback(cotangent)
    return (output, grads[0], grads[1], grads[2], grads[3], grads[4], grads[5], grads[6], grads[7], grads[8], grads[9], grads[10])
```

```python
import functools

import jax
import jax.numpy as jnp
from jax import lax
from jax.experimental import pallas as pl
from jax.experimental.pallas import tpu as pltpu
from jax.sharding import PartitionSpec as P

epsilon = 1e-06
bf16 = jnp.bfloat16
f32 = jnp.float32


def matmul(left, right):
    return jnp.dot(left, right, preferred_element_type=f32)


def matmul_rt(left, right):
    return lax.dot_general(left, right, (((1,), (1,)), ((), ())), preferred_element_type=f32)


def matmul_lt(left, right):
    return lax.dot_general(left, right, (((0,), (0,)), ((), ())), preferred_element_type=f32)


def silu_of(value):
    return value * jax.nn.sigmoid(value)


def silu_slope(value):
    squash = jax.nn.sigmoid(value)
    return squash * (1.0 + value * (1.0 - squash))


def norm_rows(value):
    scale = lax.rsqrt(jnp.mean(value * value, axis=-1, keepdims=True) + epsilon)
    return (scale, value * scale)


def norm_back(grad_norm, unit, scale, gain):
    scaled = grad_norm * gain
    return scale * (scaled - unit * jnp.mean(scaled * unit, axis=-1, keepdims=True))


def swap(value, mask):
    return lax.ppermute(value, "dp", [(i, i ^ mask) for i in range(lax.axis_size("dp"))])


def own_bit(mask):
    return lax.rem(lax.div(lax.axis_index("dp"), mask), 2)


def gather_bits(value, order):
    base = value.shape
    done = []
    for mask in order:
        other = swap(value, mask)
        at = sum(1 for seen in done if seen > mask)
        low = jnp.stack([value, other], axis=at)
        high = jnp.stack([other, value], axis=at)
        value = jnp.where(own_bit(mask) == 0, low, high)
        done.append(mask)
    return value.reshape((1 << len(order),) + base)


def scatter_bits(value, order):
    count = len(order)
    value = value.reshape((2,) * count + value.shape[1:])
    left = sorted(order, reverse=True)
    for mask in order:
        at = left.index(mask)
        left.remove(mask)
        bit = own_bit(mask)
        send = lax.dynamic_index_in_dim(value, 1 - bit, at, keepdims=False)
        keep = lax.dynamic_index_in_dim(value, bit, at, keepdims=False)
        total = keep.astype(f32) + swap(send.astype(bf16), mask).astype(f32)
        value = total.astype(bf16) if left else total
    return value


def orders(masks):
    down = sorted(masks, reverse=True)
    if len(down) < 3:
        return down, down
    return down, [down[1], down[0]] + down[2:]


def gather_rows(value, masks):
    first, second = orders(masks)
    half = value.shape[0] // 2
    return jnp.concatenate(
        [gather_bits(value[:half], first), gather_bits(value[half:], second)], axis=1
    )


def scatter_rows(value, masks):
    first, second = orders(masks)
    half = value.shape[1] // 2
    return jnp.concatenate(
        [
            scatter_bits(value[:, :half], first[::-1]),
            scatter_bits(value[:, half:], second[::-1]),
        ],
        axis=0,
    )


def ring(value):
    parts = lax.axis_size("tensor")
    return lax.ppermute(value, "tensor", [(i, (i + 1) % parts) for i in range(parts)])


def ring_blocks(value):
    blocks = [value]
    for _ in range(lax.axis_size("tensor") - 1):
        blocks.append(ring(blocks[-1]))
    return blocks


def ring_scatter(blocks):
    total = blocks[1 % len(blocks)]
    for k in range(2, len(blocks) + 1):
        moved = ring(total.astype(bf16)).astype(f32)
        total = moved + blocks[k % len(blocks)].astype(f32)
    return total


def forward_kernel(steps, seqs, forget_ref, drive_ref, state_ref, decay_ref):
    width = forget_ref.shape[1]

    def step(at, carry):
        state, decay = carry
        rows = pl.ds(at, seqs, stride=steps)
        forget = forget_ref[rows, :]
        state = forget * state + drive_ref[rows, :]
        decay = decay * forget
        state_ref[rows, :] = state
        decay_ref[rows, :] = decay
        return state, decay

    lax.fori_loop(
        0, steps, step, (jnp.zeros((seqs, width), f32), jnp.ones((seqs, width), f32)), unroll=8
    )


def backward_kernel(steps, seqs, forget_ref, drive_ref, carried_ref, decay_ref):
    width = forget_ref.shape[1]

    def step(k, carry):
        coming, decay = carry
        rows = pl.ds(steps - 1 - k, seqs, stride=steps)
        forget = forget_ref[rows, :]
        carried = drive_ref[rows, :] + coming
        carried_ref[rows, :] = carried
        decay_ref[rows, :] = decay
        return forget * carried, decay * forget

    lax.fori_loop(
        0, steps, step, (jnp.zeros((seqs, width), f32), jnp.ones((seqs, width), f32)), unroll=8
    )


def local_scan(body, seqs, forget, drive):
    rows, width = forget.shape
    lanes = 128 if width % 128 == 0 else width
    spec = pl.BlockSpec((rows, lanes), lambda c: (0, c))
    return pl.pallas_call(
        functools.partial(body, rows // seqs, seqs),
        grid=(width // lanes,),
        in_specs=[spec, spec],
        out_specs=[spec, spec],
        out_shape=[jax.ShapeDtypeStruct((rows, width), f32)] * 2,
        compiler_params=pltpu.CompilerParams(vmem_limit_bytes=32 * 1024 * 1024),
        cost_estimate=pl.CostEstimate(
            flops=4 * rows * width, bytes_accessed=16 * rows * width, transcendentals=0
        ),
    )(forget, drive)


def on_device(
    inputs,
    lengths,
    gain_mix,
    gain_glu,
    lower_bound,
    w_input,
    w_forget,
    w_gate_mix,
    w_out,
    w_gate,
    w_up,
    w_down,
    cotangent,
):
    tensor_parts = lax.axis_size("tensor")
    data_parts = lax.axis_size("dp")
    tensor_index = lax.axis_index("tensor")
    data_index = lax.axis_index("dp")
    rows_here, width = inputs.shape
    group = min(8, data_parts)
    copies = data_parts // group
    group_index = lax.div(data_index, copies)
    copy_index = lax.rem(data_index, copies)
    group_masks = [copies << k for k in range(group.bit_length() - 1)]
    copy_masks = [1 << k for k in range(copies.bit_length() - 1)]
    all_masks = [1 << k for k in range(data_parts.bit_length() - 1)]
    group_lists = [[g * copies + o for g in range(group)] for o in range(copies)]
    channels = width // group
    own_rows = w_input.shape[0]

    high = lax.div(lengths, 32).astype(bf16)
    low = lax.rem(lengths, 32).astype(bf16)
    length_row = jnp.concatenate([high, low, jnp.zeros((own_rows - 2,), bf16)])
    small = jnp.stack([gain_mix, gain_glu, lower_bound, length_row])
    small = lax.all_gather(small, ("dp", "tensor"), axis=0, tiled=False).astype(f32)
    gain_one = small[:, 0].reshape(width)
    gain_two = small[:, 1].reshape(width)
    bound = lax.dynamic_slice_in_dim(small[:, 2].reshape(width), group_index * channels, channels)
    every_length = small[:, 3].reshape(data_parts, tensor_parts, own_rows)[:, 0, :2]
    every_length = (every_length[:, 0] * 32.0 + every_length[:, 1]).astype(jnp.int32)
    group_lengths = lax.dynamic_index_in_dim(
        every_length.reshape(group, copies), copy_index, axis=1, keepdims=False
    )
    position = tensor_index * rows_here + jnp.arange(rows_here, dtype=jnp.int32)
    live_own = (position < lengths[0]).astype(f32)[:, None]
    live = (position[None, :] < group_lengths[:, None]).astype(f32)
    live = live.reshape(group * rows_here, 1)

    def spread(weight):
        return weight.reshape(own_rows, group, channels).transpose(1, 0, 2)

    pieces = jnp.concatenate([spread(w_input), spread(w_forget), spread(w_gate_mix)], axis=2)
    pieces = lax.all_to_all(
        pieces, "dp", 0, 0, axis_index_groups=group_lists if copies > 1 else None, tiled=True
    )
    out_piece = w_out
    if copies > 1:
        pieces = gather_bits(pieces, copy_masks[::-1]).transpose(1, 0, 2, 3)
        out_piece = gather_bits(out_piece, copy_masks[::-1])
    pieces = pieces.reshape(group * copies, own_rows, 3 * channels)
    out_piece = out_piece.reshape(copies, own_rows, width)
    mixer_w = lax.all_gather(pieces, "tensor", axis=1, tiled=False)
    mixer_w = mixer_w.reshape(width, 3 * channels)
    out_w = lax.all_gather(out_piece, "tensor", axis=1, tiled=False).reshape(channels, width)

    first, second = orders(all_masks)
    half = w_gate.shape[0] // 2
    down_t = w_down.T
    hidden_here = w_gate.shape[1]
    gate_w = gather_bits(w_gate, first).reshape(width, hidden_here)
    up_w = gather_bits(w_up, second).reshape(width, hidden_here)
    down_w = jnp.concatenate(
        [gather_bits(down_t[:half], first), gather_bits(down_t[half:], second)], axis=1
    ).reshape(width, hidden_here)

    masked_grad = live_own * cotangent
    masked_blocks = ring_blocks(masked_grad.astype(bf16))

    scale_one, unit_one = norm_rows(inputs)
    normed_one = gather_rows((unit_one * gain_one).astype(bf16), group_masks)
    normed_one = normed_one.reshape(group * rows_here, width)
    pre = matmul(normed_one, mixer_w)
    input_pre = pre[:, :channels]
    forget_sig = jax.nn.sigmoid(pre[:, channels : 2 * channels])
    gate_pre = pre[:, 2 * channels :]
    forget = bound + (1.0 - bound) * forget_sig
    input_act = silu_of(input_pre)
    gate_act = silu_of(gate_pre)
    inflow = live * (1.0 - forget) * input_act
    part_state, part_decay = local_scan(forward_kernel, group, forget, inflow)
    shaped = (group, rows_here, channels)
    part_state = part_state.reshape(shaped)
    part_decay = part_decay.reshape(shaped)
    ends = jnp.stack([part_state[:, -1], part_decay[:, -1]])
    all_ends = lax.all_gather(ends, "tensor", axis=0, tiled=False)
    coming = jnp.zeros((group, channels), f32)
    entering = coming
    for k in range(tensor_parts - 1):
        coming = all_ends[k, 1] * coming + all_ends[k, 0]
        entering = jnp.where(tensor_index == k + 1, coming, entering)
    state = part_state + part_decay * entering[:, None, :]
    prior_state = jnp.concatenate([entering[:, None, :], state[:, :-1]], axis=1)
    state = state.reshape(group * rows_here, channels)
    prior_state = prior_state.reshape(group * rows_here, channels)
    mixed_low = (state * gate_act).astype(bf16)
    mixed = matmul(mixed_low, out_w).astype(bf16).reshape(group, rows_here, width)
    stream = inputs + scatter_rows(mixed, group_masks)

    scale_two, unit_two = norm_rows(stream)
    normed_blocks = ring_blocks((unit_two * gain_two).astype(bf16))
    hidden_blocks, gate_low, up_low, back_parts, out_parts = [], [], [], [], []
    for normed, masked in zip(normed_blocks, masked_blocks):
        glu_gate = matmul(normed, gate_w)
        glu_up = matmul(normed, up_w)
        hidden = (silu_of(glu_gate) * glu_up).astype(bf16)
        grad_hidden = matmul(masked, down_w)
        grad_gate = (grad_hidden * glu_up * silu_slope(glu_gate)).astype(bf16)
        grad_up = (grad_hidden * silu_of(glu_gate)).astype(bf16)
        back_parts.append((matmul_rt(grad_gate, gate_w) + matmul_rt(grad_up, up_w)).astype(bf16))
        out_parts.append(matmul_rt(hidden, down_w).astype(bf16))
        hidden_blocks.append(hidden)
        gate_low.append(grad_gate)
        up_low.append(grad_up)
    grad_norm_two = ring_scatter(back_parts)
    output = live_own * (stream + ring_scatter(out_parts))

    all_normed = jnp.concatenate(normed_blocks)
    all_masked = jnp.concatenate(masked_blocks)
    by_owner = (data_parts, width // data_parts, hidden_here)
    grad_gate_w = matmul_lt(all_normed, jnp.concatenate(gate_low)).astype(bf16).reshape(by_owner)
    grad_up_w = matmul_lt(all_normed, jnp.concatenate(up_low)).astype(bf16).reshape(by_owner)
    grad_down_t = (
        matmul_lt(all_masked, jnp.concatenate(hidden_blocks)).astype(bf16).reshape(by_owner)
    )
    grad_gate_mine = scatter_bits(grad_gate_w, first[::-1])
    grad_up_mine = scatter_bits(grad_up_w, second[::-1])
    grad_down_mine = scatter_rows(grad_down_t, all_masks).T

    gain_two_part = jnp.sum(grad_norm_two * unit_two, axis=0)
    grad_stream = masked_grad + norm_back(grad_norm_two, unit_two, scale_two, gain_two)
    stream_low = gather_rows(grad_stream.astype(bf16), group_masks)
    stream_low = stream_low.reshape(group * rows_here, width)

    grad_out_w = matmul_lt(mixed_low, stream_low).astype(bf16)
    grad_mixed = matmul_rt(stream_low, out_w)
    grad_gate_pre = (grad_mixed * state * silu_slope(gate_pre)).astype(bf16)
    grad_state = grad_mixed * gate_act
    part_carried, part_after = local_scan(backward_kernel, group, forget, grad_state)
    part_carried = part_carried.reshape(shaped)
    part_after = part_after.reshape(shaped)
    first_forget = forget.reshape(shaped)[:, 0]
    begins = jnp.stack([first_forget * part_carried[:, 0], first_forget * part_after[:, 0]])
    all_begins = lax.all_gather(begins, "tensor", axis=0, tiled=False)
    coming = jnp.zeros((group, channels), f32)
    entering = coming
    for k in range(tensor_parts - 1, 0, -1):
        coming = all_begins[k, 1] * coming + all_begins[k, 0]
        entering = jnp.where(tensor_index == k - 1, coming, entering)
    carried = (part_carried + part_after * entering[:, None, :]).reshape(
        group * rows_here, channels
    )
    grad_forget = carried * prior_state - carried * live * input_act
    grad_input_pre = (carried * live * (1.0 - forget) * silu_slope(input_pre)).astype(bf16)
    grad_bound = jnp.sum(grad_forget * (1.0 - forget_sig), axis=0)
    grad_forget_pre = (grad_forget * (1.0 - bound) * forget_sig * (1.0 - forget_sig)).astype(bf16)
    grad_pre = jnp.concatenate([grad_input_pre, grad_forget_pre, grad_gate_pre], axis=1)
    grad_normed = matmul_rt(grad_pre, mixer_w).astype(bf16).reshape(group, rows_here, width)
    grad_norm_one = scatter_rows(grad_normed, group_masks)
    gain_one_part = jnp.sum(grad_norm_one * unit_one, axis=0)
    grad_inputs = grad_stream + norm_back(grad_norm_one, unit_one, scale_one, gain_one)

    grad_mixer = matmul_lt(normed_one, grad_pre).astype(bf16)
    grad_mixer = grad_mixer.reshape(data_parts, tensor_parts, own_rows, 3 * channels)
    grad_mixer = grad_mixer.transpose(1, 0, 2, 3)
    grad_mixer = lax.psum_scatter(grad_mixer, "tensor", scatter_dimension=0, tiled=False)
    grad_out = grad_out_w.reshape(copies, tensor_parts, own_rows, width).transpose(1, 0, 2, 3)
    grad_out = lax.psum_scatter(grad_out, "tensor", scatter_dimension=0, tiled=False)
    if copies > 1:
        grad_mixer = grad_mixer.reshape(group, copies, own_rows, 3 * channels)
        grad_mixer = scatter_bits(grad_mixer.transpose(1, 0, 2, 3), copy_masks).astype(bf16)
        grad_out = scatter_bits(grad_out, copy_masks)
    grad_mixer = grad_mixer.reshape(group, own_rows, 3 * channels)
    grad_mixer = lax.all_to_all(
        grad_mixer, "dp", 0, 0, axis_index_groups=group_lists if copies > 1 else None, tiled=True
    )
    grad_mixer = grad_mixer.reshape(group, own_rows, 3, channels).transpose(2, 1, 0, 3)
    grad_mixer = grad_mixer.reshape(3, own_rows, width).astype(f32)
    grad_out = grad_out.reshape(own_rows, width).astype(f32)

    bound_part = lax.dynamic_update_slice_in_dim(
        jnp.zeros((width,), f32), grad_bound, group_index * channels, 0
    )
    sums = jnp.stack([gain_one_part, gain_two_part, bound_part])
    sums = sums.reshape(3, data_parts * tensor_parts, own_rows).transpose(1, 0, 2)
    sums = lax.psum_scatter(sums, ("dp", "tensor"), scatter_dimension=0, tiled=False)
    return (
        output,
        grad_inputs,
        sums[0],
        sums[1],
        sums[2],
        grad_mixer[0],
        grad_mixer[1],
        grad_mixer[2],
        grad_out,
        grad_gate_mine,
        grad_up_mine,
        grad_down_mine,
    )


def solution(mesh):
    both = ("dp", "tensor")
    placed = (
        P(both, None),
        P("dp"),
        P(both),
        P(both),
        P(both),
        P(both, None),
        P(both, None),
        P(both, None),
        P(both, None),
        P("dp", "tensor"),
        P("dp", "tensor"),
        P("tensor", "dp"),
        P(both, None),
    )
    return jax.shard_map(
        on_device,
        mesh=mesh,
        in_specs=placed,
        out_specs=(
            P(both, None),
            P(both, None),
            P(both),
            P(both),
            P(both),
            P(both, None),
            P(both, None),
            P(both, None),
            P(both, None),
            P("dp", "tensor"),
            P("dp", "tensor"),
            P("tensor", "dp"),
        ),
        check_vma=False,
    )
```

```python
import functools

import jax
import jax.numpy as jnp
from jax import lax
from jax.experimental import pallas as pl
from jax.experimental.pallas import tpu as pltpu
from jax.sharding import PartitionSpec as P

epsilon = 1e-06
bf16 = jnp.bfloat16
f32 = jnp.float32


def matmul(left, right):
    return jnp.dot(left, right, preferred_element_type=f32)


def matmul_rt(left, right):
    return lax.dot_general(left, right, (((1,), (1,)), ((), ())), preferred_element_type=f32)


def matmul_lt(left, right):
    return lax.dot_general(left, right, (((0,), (0,)), ((), ())), preferred_element_type=f32)


def silu_of(value):
    return value * jax.nn.sigmoid(value)


def silu_slope(value):
    squash = jax.nn.sigmoid(value)
    return squash * (1.0 + value * (1.0 - squash))


def norm_rows(value):
    scale = lax.rsqrt(jnp.mean(value * value, axis=-1, keepdims=True) + epsilon)
    return (scale, value * scale)


def norm_back(grad_norm, unit, scale, gain):
    scaled = grad_norm * gain
    return scale * (scaled - unit * jnp.mean(scaled * unit, axis=-1, keepdims=True))


def untouched_kernel(*refs):
    pass


def after(value, *others):
    somewhere = pl.BlockSpec(memory_space=pl.ANY)
    return pl.pallas_call(
        untouched_kernel,
        out_shape=jax.ShapeDtypeStruct(value.shape, value.dtype),
        in_specs=[somewhere] * (1 + len(others)),
        out_specs=somewhere,
        input_output_aliases={0: 0},
        cost_estimate=pl.CostEstimate(flops=0, bytes_accessed=0, transcendentals=0),
    )(value, *others)


def swap(value, mask):
    return lax.ppermute(value, "dp", [(i, i ^ mask) for i in range(lax.axis_size("dp"))])


def own_bit(mask):
    return lax.rem(lax.div(lax.axis_index("dp"), mask), 2)


def gather_bits(value, order):
    base = value.shape
    done = []
    for mask in order:
        other = swap(value, mask)
        at = sum(1 for seen in done if seen > mask)
        low = jnp.stack([value, other], axis=at)
        high = jnp.stack([other, value], axis=at)
        value = jnp.where(own_bit(mask) == 0, low, high)
        done.append(mask)
    return value.reshape((1 << len(order),) + base)


def scatter_bits(value, order, sent=bf16, hold=(None, None)):
    count = len(order)
    value = value.reshape((2,) * count + value.shape[1:])
    left = sorted(order, reverse=True)
    for mask in order:
        at = left.index(mask)
        left.remove(mask)
        bit = own_bit(mask)
        send = lax.dynamic_index_in_dim(value, 1 - bit, at, keepdims=False).astype(sent)
        keep = lax.dynamic_index_in_dim(value, bit, at, keepdims=False)
        if hold[0] == count - len(left) - 1:
            send = after(send, hold[1])
        total = keep.astype(f32) + swap(send, mask).astype(f32)
        value = total.astype(sent) if left else total
    return value


def orders(masks):
    down = sorted(masks, reverse=True)
    if len(down) < 3:
        return down, down
    return down, [down[1], down[0]] + down[2:]


def gather_halves(value, masks):
    first, second = orders(masks)
    half = value.shape[-1] // 2
    return gather_bits(value[..., :half], first), gather_bits(value[..., half:], second)


def scatter_halves(left, right, masks):
    first, second = orders(masks)
    return jnp.concatenate(
        [scatter_bits(left, first[::-1]), scatter_bits(right, second[::-1])], axis=-1
    )


def ring(value):
    parts = lax.axis_size("tensor")
    return lax.ppermute(value, "tensor", [(i, (i + 1) % parts) for i in range(parts)])


def ring_blocks(value):
    blocks = [value]
    for _ in range(lax.axis_size("tensor") - 1):
        blocks.append(ring(blocks[-1]))
    return blocks


def ring_scatter(blocks):
    total = blocks[1 % len(blocks)]
    totals = [total]
    for k in range(2, len(blocks) + 1):
        moved = ring(total).astype(f32)
        total = moved + blocks[k % len(blocks)].astype(f32)
        if k < len(blocks):
            total = total.astype(bf16)
            totals.append(total)
    return total, totals


def shifted_blocks(value):
    parts = lax.axis_size("tensor")
    blocks = [value]
    for k in range(1, parts):
        blocks.append(lax.ppermute(value, "tensor", [(i, (i + k) % parts) for i in range(parts)]))
    return blocks


def scatter_straight(value):
    here = lax.axis_index("tensor")
    parts = lax.axis_size("tensor")
    total = lax.dynamic_index_in_dim(value, here, 0, keepdims=False)
    for k in range(1, parts):
        send = lax.dynamic_index_in_dim(value, lax.rem(here + k, parts), 0, keepdims=False)
        total += lax.ppermute(send, "tensor", [(i, (i + k) % parts) for i in range(parts)])
    return total


def in_order(blocks):
    here = lax.axis_index("tensor")
    parts = len(blocks)
    stacked = jnp.stack(blocks[::-1] + blocks[::-1])
    return lax.dynamic_slice_in_dim(stacked, parts - 1 - here, parts, 0)


def partner(mask):
    me = lax.axis_index("dp")
    return me + mask * (1 - 2 * lax.rem(lax.div(me, mask), 2))


def greet(masks, ring_too=False):
    barrier = pltpu.get_barrier_semaphore()
    others = [{"dp": partner(mask)} for mask in masks]
    if ring_too:
        others += [{"tensor": beside(1)}, {"tensor": beside(-1)}]
    for other in others:
        pl.semaphore_signal(
            barrier, inc=1, device_id=other, device_id_type=pl.DeviceIdType.MESH
        )
    pl.semaphore_wait(barrier, len(others))


def beside(step):
    parts = lax.axis_size("tensor")
    return lax.rem(lax.axis_index("tensor") + step + parts, parts)


def slot_of(copies, masks):
    me = lax.axis_index("dp")
    for mask in masks:
        me = me + mask * (1 - 2 * lax.rem(lax.div(me, mask), 2))
    return lax.div(me, copies)


def to_right(source, target, send_sem, recv_sem):
    return pltpu.make_async_remote_copy(
        src_ref=source,
        dst_ref=target,
        send_sem=send_sem,
        recv_sem=recv_sem,
        device_id={"tensor": beside(1)},
        device_id_type=pl.DeviceIdType.MESH,
    )


def plane_gather_kernel(
    copies, value_ref, all_ref, own_sem, send_sem, recv_sem, weight_ref=None, weights_ref=None,
    ring_send=None, ring_recv=None,
):
    near, one, two = copies, 2 * copies, 4 * copies
    half = value_ref.shape[0] // 2
    top, low = pl.ds(0, half), pl.ds(half, half)
    mine = slot_of(copies, ())
    at_one, at_two = slot_of(copies, (one,)), slot_of(copies, (two,))
    at_both = slot_of(copies, (one, two))
    greet((near, one, two), weight_ref is not None)
    local = pltpu.make_async_copy(value_ref, all_ref.at[mine], own_sem.at[0])
    local.start()
    copies_out = []
    ring_steps = []
    if weight_ref is not None:
        own = beside(0)
        keep = pltpu.make_async_copy(weight_ref, weights_ref.at[own], own_sem.at[1])
        keep.start()
        for k in range(lax.axis_size("tensor") - 1):
            source = weight_ref if k == 0 else weights_ref.at[beside(-k)]
            ring_steps.append(
                to_right(source, weights_ref.at[beside(-k)], ring_send.at[k], ring_recv.at[k])
            )
        ring_steps[0].start()

    def send(source, slot, rows, mask):
        index = len(copies_out)
        copy = pltpu.make_async_remote_copy(
            src_ref=source,
            dst_ref=all_ref.at[slot, rows],
            send_sem=send_sem.at[index],
            recv_sem=recv_sem.at[index],
            device_id={"dp": partner(mask)},
            device_id_type=pl.DeviceIdType.MESH,
        )
        copy.start()
        copies_out.append(copy)
        return copy

    def forward(slot, rows, mask):
        return send(all_ref.at[slot, rows], slot, rows, mask)

    two_top = send(value_ref.at[top], mine, top, two)
    one_low = send(value_ref.at[low], mine, low, one)
    two_low = send(value_ref.at[low], mine, low, two)
    one_top = send(value_ref.at[top], mine, top, one)
    last = [send(value_ref.at[top], mine, top, near), send(value_ref.at[low], mine, low, near)]
    two_top.wait_recv()
    over_one = forward(at_two, top, one)
    last.append(forward(at_two, top, near))
    one_low.wait_recv()
    over_two = forward(at_one, low, two)
    last.append(forward(at_one, low, near))
    two_low.wait_recv()
    last.append(forward(at_two, low, near))
    one_top.wait_recv()
    last.append(forward(at_one, top, near))
    over_one.wait_recv()
    last.append(forward(at_both, top, near))
    over_two.wait_recv()
    last.append(forward(at_both, low, near))
    for k, step in enumerate(ring_steps):
        step.wait_recv()
        if k + 1 < len(ring_steps):
            ring_steps[k + 1].start()
    for copy in last:
        copy.wait_recv()
    for copy in copies_out + ring_steps:
        copy.wait_send()
    local.wait()
    if weight_ref is not None:
        keep.wait()


def gather_late_kernel(copies, late, weighty, value_ref, *refs):
    if weighty:
        weight_ref, all_ref, weights_ref = refs[0], refs[1 + late], refs[2 + late]
        own_sem, send_sem, recv_sem, ring_send, ring_recv = refs[3 + late :]
        plane_gather_kernel(
            copies, value_ref, all_ref, own_sem, send_sem, recv_sem, weight_ref, weights_ref,
            ring_send, ring_recv,
        )
    else:
        plane_gather_kernel(copies, value_ref, *refs[late:])


def plane_gather(value, copies, collective, weight=None, before=()):
    rows, width = value.shape
    parts = lax.axis_size("tensor")
    somewhere = pl.BlockSpec(memory_space=pl.ANY)
    shapes = [jax.ShapeDtypeStruct((8, rows, width), value.dtype)]
    operands = [value]
    scratch = [
        pltpu.SemaphoreType.DMA((2,)),
        pltpu.SemaphoreType.DMA((14,)),
        pltpu.SemaphoreType.DMA((14,)),
    ]
    if weight is not None:
        shapes.append(jax.ShapeDtypeStruct((parts,) + weight.shape, weight.dtype))
        operands.append(weight)
        scratch += [pltpu.SemaphoreType.DMA((parts - 1,))] * 2
    operands += before
    return pl.pallas_call(
        functools.partial(gather_late_kernel, copies, len(before), weight is not None),
        out_shape=shapes,
        in_specs=[somewhere] * len(operands),
        out_specs=[somewhere] * len(shapes),
        scratch_shapes=scratch,
        compiler_params=pltpu.CompilerParams(collective_id=collective, has_side_effects=True),
        cost_estimate=pl.CostEstimate(
            flops=0, bytes_accessed=320 * rows * width, transcendentals=0
        ),
    )(*operands)


def plane_scatter_kernel(
    copies, transposed, left_ref, right_ref, sum_ref, near_ref, one_ref, two_ref, part_ref,
    send_sem, recv_sem, block_ref=None, blocks_ref=None, ring_send=None, ring_recv=None,
    total_ref=None, shares=None, ring_buf=None, load_sem=None,
):
    near, one, two = copies, 2 * copies, 4 * copies
    rows, width = sum_ref.shape
    half = rows // 2
    top, low = pl.ds(0, half), pl.ds(half, half)
    tile = min(512, width)
    greet((near, one, two), ring_send is not None)
    ring_steps = []
    parts = lax.axis_size("tensor")
    if shares is not None:
        loads = [
            pltpu.make_async_copy(block_ref.at[beside(-k)], shares.at[k], load_sem.at[k])
            for k in range(parts)
        ]
        for load in loads:
            load.start()
        for load in loads:
            load.wait()
        sum_steps = [
            to_right(shares.at[k + 1], ring_buf.at[k], ring_send.at[k], ring_recv.at[k])
            for k in range(parts - 1)
        ]
        sum_steps[0].start()
    elif block_ref is not None:
        for k in range(blocks_ref.shape[0]):
            source = block_ref if k == 0 else blocks_ref.at[k - 1]
            ring_steps.append(
                to_right(source, blocks_ref.at[k], ring_send.at[k], ring_recv.at[k])
            )
        ring_steps[0].start()
    flips = [(), (one,), (two,), (one, two)]
    copies_out = []

    def send(source, target, mask):
        index = len(copies_out)
        copy = pltpu.make_async_remote_copy(
            src_ref=source,
            dst_ref=target,
            send_sem=send_sem.at[index],
            recv_sem=recv_sem.at[index],
            device_id={"dp": partner(mask)},
            device_id_type=pl.DeviceIdType.MESH,
        )
        copy.start()
        copies_out.append(copy)
        return copy

    def each_tile(body):
        @pl.loop(0, width // tile)
        def _(k):
            body(pl.ds(pl.multiple_of(k * tile, tile), tile))

    def product(slot, columns):
        left = left_ref[slot]
        if transposed:
            return matmul_rt(left, right_ref[columns, :])
        return matmul(left, right_ref[:, columns])

    arriving = {}
    for k in (3, 1, 2, 0):
        slot = slot_of(copies, flips[k] + (near,))

        def theirs(columns, k=k, slot=slot):
            part_ref[k, :, columns] = product(slot, columns).astype(bf16)

        each_tile(theirs)
        arriving[k] = send(part_ref.at[k], near_ref.at[k], near)

    def added(k):
        slot = slot_of(copies, flips[k])
        arriving[k].wait_recv()

        def mine(columns):
            total = product(slot, columns) + near_ref[k, :, columns].astype(f32)
            if k == 0:
                sum_ref[:, columns] = total
            else:
                near_ref[k, :, columns] = total.astype(bf16)

        each_tile(mine)

    added(3)
    one_first = send(near_ref.at[3, top], one_ref.at[0], one)
    two_first = send(near_ref.at[3, low], two_ref.at[0], two)
    added(1)
    one_second = send(near_ref.at[1, top], one_ref.at[1], one)
    added(2)
    two_second = send(near_ref.at[2, low], two_ref.at[1], two)
    added(0)

    one_first.wait_recv()

    def pass_top(columns):
        total = near_ref[2, top, columns].astype(f32) + one_ref[0, :, columns].astype(f32)
        near_ref[2, top, columns] = total.astype(bf16)

    each_tile(pass_top)
    two_last = send(near_ref.at[2, top], two_ref.at[2], two)
    two_first.wait_recv()

    def pass_low(columns):
        total = near_ref[1, low, columns].astype(f32) + two_ref[0, :, columns].astype(f32)
        near_ref[1, low, columns] = total.astype(bf16)

    each_tile(pass_low)
    one_last = send(near_ref.at[1, low], one_ref.at[2], one)

    def finish(rows_at, first, at_first, second, at_second):
        def body(columns):
            sum_ref[rows_at, columns] += (
                first[at_first, :, columns].astype(f32) + second[at_second, :, columns].astype(f32)
            )

        each_tile(body)

    def sum_step(k):
        sum_steps[k].wait_recv()
        many = shares.shape[1] // 4

        @pl.loop(0, 4)
        def _(n):
            some = pl.ds(pl.multiple_of(n * many, many), many)
            at = (k + 2) % parts
            total = shares[at, some, :].astype(f32) + ring_buf[k, some, :].astype(f32)
            if at:
                shares[at, some, :] = total.astype(bf16)
            else:
                total_ref[some, :] = total

        if k + 1 < parts - 1:
            sum_steps[k + 1].start()

    if shares is not None:
        sum_step(0)
    for k, step in enumerate(ring_steps):
        step.wait_recv()
        if k + 1 < len(ring_steps):
            ring_steps[k + 1].start()
    one_second.wait_recv()
    two_last.wait_recv()
    finish(top, one_ref, 1, two_ref, 2)
    two_second.wait_recv()
    one_last.wait_recv()
    finish(low, two_ref, 1, one_ref, 2)
    if shares is not None:
        for k in range(1, parts - 1):
            sum_step(k)
        ring_steps = sum_steps
    for copy in copies_out + ring_steps:
        copy.wait_send()


def scatter_late_kernel(copies, transposed, late, left_ref, right_ref, block_ref, *refs):
    sum_ref, blocks_ref = refs[late : late + 2]
    refs = refs[late + 2 :]
    if len(refs) == 8:
        plane_scatter_kernel(
            copies, transposed, left_ref, right_ref, sum_ref, *refs[:6], block_ref, blocks_ref,
            *refs[6:],
        )
    else:
        plane_scatter_kernel(
            copies, transposed, left_ref, right_ref, sum_ref, *refs[:6], block_ref, None,
            *refs[6:8], blocks_ref, *refs[8:],
        )


def plane_scatter(left, right, copies, transposed, collective, block=None, sums=None, before=()):
    group, rows, depth = left.shape
    width = right.shape[0] if transposed else right.shape[1]
    half = rows // 2
    vmem = pl.BlockSpec(memory_space=pltpu.VMEM)
    somewhere = pl.BlockSpec(memory_space=pl.ANY)
    scratch = [
        pltpu.VMEM((4, rows, width), bf16),
        pltpu.VMEM((3, half, width), bf16),
        pltpu.VMEM((3, half, width), bf16),
        pltpu.VMEM((4, rows, width), bf16),
        pltpu.SemaphoreType.DMA((10,)),
        pltpu.SemaphoreType.DMA((10,)),
    ]
    shapes = [jax.ShapeDtypeStruct((rows, width), f32)]
    out_specs = [vmem]
    parts = lax.axis_size("tensor")
    if block is not None:
        operands = [left, right, block]
        steps = parts - 2
        shapes.append(jax.ShapeDtypeStruct((steps,) + block.shape, block.dtype))
        out_specs.append(somewhere)
        scratch += [pltpu.SemaphoreType.DMA((steps,))] * 2
    else:
        operands = [left, right, sums]
        shapes.append(jax.ShapeDtypeStruct(sums.shape[1:], f32))
        out_specs.append(vmem)
        scratch += [pltpu.SemaphoreType.DMA((parts - 1,))] * 2
        scratch += [
            pltpu.VMEM(sums.shape, bf16),
            pltpu.VMEM((parts - 1,) + sums.shape[1:], bf16),
            pltpu.SemaphoreType.DMA((parts,)),
        ]
    operands += before
    return pl.pallas_call(
        functools.partial(
            scatter_late_kernel, copies, transposed, len(before)
        ),
        out_shape=shapes,
        in_specs=[vmem, vmem] + [somewhere] * (len(operands) - 2),
        out_specs=out_specs,
        scratch_shapes=scratch,
        compiler_params=pltpu.CompilerParams(
            collective_id=collective, has_side_effects=True, vmem_limit_bytes=48 * 1024 * 1024
        ),
        cost_estimate=pl.CostEstimate(
            flops=2 * group * rows * depth * width,
            bytes_accessed=400 * rows * width,
            transcendentals=0,
        ),
    )(*operands)


def column_tiles(width, most=512):
    return [(at, min(most, width - at)) for at in range(0, width, most)]


def swiglu_kernel(
    copies,
    normed_ref, own_ref, first_ref, others_ref, gate_hbm, up_hbm, down_hbm,
    rows_out, norm_sum, gate_sum, up_sum, down_sum,
    normed, masked, gate_w, up_w, down_w, hidden, gate_low, up_low, back, rows, ring_buf,
    one_buf, two_buf, in_sem, out_sem, send_sem, recv_sem, sum_send, sum_recv, near_send,
    near_recv, one_send, one_recv, two_send, two_recv, ready_sem,
):
    parts = lax.axis_size("tensor")
    near, one, two = copies, 2 * copies, 4 * copies
    greet((near, one, two), True)
    own = pltpu.make_async_copy(normed_ref, normed.at[0], in_sem.at[0])
    own.start()
    loads = [
        pltpu.make_async_copy(gate_hbm, gate_w, in_sem.at[1]),
        pltpu.make_async_copy(up_hbm, up_w, in_sem.at[2]),
        pltpu.make_async_copy(own_ref, masked.at[0], in_sem.at[3]),
        pltpu.make_async_copy(down_hbm, down_w, in_sem.at[4]),
        pltpu.make_async_copy(first_ref, masked.at[1], in_sem.at[5]),
        pltpu.make_async_copy(others_ref, masked.at[pl.ds(2, parts - 2)], in_sem.at[6]),
    ]
    own.wait()
    for load in loads:
        load.start()
    width = normed.shape[2]
    tile = min(512, width)

    def hop(k):
        return to_right(normed.at[k], normed.at[k + 1], send_sem.at[k], recv_sem.at[k])

    def sum_hop(k):
        return to_right(back.at[k + 1], ring_buf.at[k], sum_send.at[k], sum_recv.at[k])

    hop(0).start()
    for load in loads:
        load.wait()

    def store(k):
        home = lax.rem(lax.axis_index("tensor") + parts - k, parts)
        slot = lax.rem(k, 2)
        return pltpu.make_async_copy(rows.at[slot], rows_out.at[home], out_sem.at[slot])

    def block(k, nothing):
        @pl.when(k > 0)
        def _():
            hop(k - 1).wait_recv()

        @pl.when(jnp.logical_and(k > 0, k < parts - 1))
        def _():
            hop(k).start()

        @pl.when(k == parts - 1)
        def _():
            sum_hop(0).start()

        for at, size in column_tiles(hidden.shape[2]):
            columns = pl.ds(at, size)
            glu_gate = matmul(normed[k], gate_w[:, columns])
            glu_up = matmul(normed[k], up_w[:, columns])
            grad_hidden = matmul(masked[k], down_w[:, columns])
            squash = jax.nn.sigmoid(glu_gate)
            act = glu_gate * squash
            slope = squash * (1.0 + glu_gate * (1.0 - squash))
            hidden[k, :, columns] = (act * glu_up).astype(bf16)
            gate_low[k, :, columns] = (grad_hidden * glu_up * slope).astype(bf16)
            up_low[k, :, columns] = (grad_hidden * act).astype(bf16)

        @pl.when(k > 1)
        def _():
            store(k - 2).wait()

        slot = lax.rem(k, 2)

        @pl.loop(0, width // tile)
        def _(n):
            some = pl.ds(pl.multiple_of(n * tile, tile), tile)
            back[k, :, some] = (
                matmul_rt(gate_low[k], gate_w[some, :]) + matmul_rt(up_low[k], up_w[some, :])
            ).astype(bf16)
            rows[slot, :, some] = matmul_rt(hidden[k], down_w[some, :]).astype(bf16)

        store(k).start()
        return nothing

    lax.fori_loop(0, parts, block, 0)

    pl.semaphore_signal(
        ready_sem,
        inc=1,
        device_id={"dp": partner(near)},
        device_id_type=pl.DeviceIdType.MESH,
    )
    share = width // 8
    half = share // 2
    hidden_width = hidden.shape[2]
    tall = parts * normed.shape[1]
    kinds = (
        (normed, gate_low, gate_w, gate_sum),
        (normed, up_low, up_w, up_sum),
        (masked, hidden, down_w, down_sum),
    )

    def product(kind, slot):
        left, right, _, _ = kinds[kind]
        some = pl.ds(pl.multiple_of(slot * share, share), share)
        return matmul_lt(
            left[:, :, some].reshape(tall, share), right[...].reshape(tall, hidden_width)
        )

    def part_at(k):
        return pl.ds(pl.multiple_of(k * share, share), share)

    def near_at(k):
        return pl.ds(pl.multiple_of((4 + k) * share, share), share)

    def halves(k):
        at = (4 + k) * share
        return (
            pl.ds(pl.multiple_of(at, half), half),
            pl.ds(pl.multiple_of(at + half, half), half),
        )

    def across(source, target, send, recv, mask):
        return pltpu.make_async_remote_copy(
            src_ref=source,
            dst_ref=target,
            send_sem=send,
            recv_sem=recv,
            device_id={"dp": partner(mask)},
            device_id_type=pl.DeviceIdType.MESH,
        )

    def near_copy(kind, k):
        room = kinds[kind][2]
        return across(
            room.at[part_at(k)], room.at[near_at(k)], near_send.at[kind, k],
            near_recv.at[kind, k], near,
        )

    def one_copy(kind, n):
        room = kinds[kind][2]
        rows_at = (halves(3)[0], halves(1)[0], halves(1)[1])[n]
        return across(
            room.at[rows_at], one_buf.at[kind, n], one_send.at[kind, n], one_recv.at[kind, n], one
        )

    def two_copy(kind, n):
        room = kinds[kind][2]
        rows_at = (halves(3)[1], halves(2)[1], halves(2)[0])[n]
        return across(
            room.at[rows_at], two_buf.at[kind, n], two_send.at[kind, n], two_recv.at[kind, n], two
        )

    def flipped(k, near_too):
        me = lax.axis_index("dp")

        def turn(mask, on):
            return on * mask * (1 - 2 * lax.rem(lax.div(me, mask), 2))

        there = me + turn(one, lax.rem(k, 2)) + turn(two, lax.div(k, 2)) + turn(near, near_too)
        return lax.div(there, copies)

    def in_turn(i):
        return 3 - 2 * i + 3 * lax.div(i, 2)

    def sum_step(k):
        sum_hop(k).wait_recv()
        if k + 1 < parts - 1:

            @pl.loop(0, width // tile)
            def _(n):
                some = pl.ds(pl.multiple_of(n * tile, tile), tile)
                total = back[k + 2, :, some].astype(f32) + ring_buf[k, :, some].astype(f32)
                back[k + 2, :, some] = total.astype(bf16)

            sum_hop(k + 1).start()
        else:

            @pl.loop(0, width // tile)
            def _(n):
                some = pl.ds(pl.multiple_of(n * tile, tile), tile)
                norm_sum[:, some] = back[0, :, some].astype(f32) + ring_buf[k, :, some].astype(f32)

    pl.semaphore_wait(ready_sem, 1)

    def theirs(i, nothing):
        k = in_turn(i)
        slot = flipped(k, 1)
        for kind in range(3):
            kinds[kind][2][part_at(k), :] = product(kind, slot).astype(bf16)
            near_copy(kind, k).start()
        return nothing

    lax.fori_loop(0, 4, theirs, 0)
    sum_step(0)

    def mine(i, nothing):
        k = in_turn(i)
        slot = flipped(k, 0)
        for kind in range(3):
            near_copy(kind, k).wait_recv()
            room = kinds[kind][2]
            total = product(kind, slot) + room[near_at(k), :].astype(f32)
            room[near_at(k), :] = total.astype(bf16)

            @pl.when(k == 3)
            def _():
                one_copy(kind, 0).start()
                two_copy(kind, 0).start()

            @pl.when(k == 1)
            def _():
                one_copy(kind, 1).start()

            @pl.when(k == 2)
            def _():
                two_copy(kind, 1).start()

        return nothing

    lax.fori_loop(0, 3, mine, 0)
    for k in range(1, parts - 2):
        sum_step(k)
    for kind in range(3):
        near_copy(kind, 0).wait_recv()
        room, total_ref = kinds[kind][2:]
        total_ref[...] = product(kind, flipped(0, 0)) + room[near_at(0), :].astype(f32)
    for kind in range(3):
        room = kinds[kind][2]
        one_copy(kind, 0).wait_recv()
        at = halves(2)[0]
        room[at, :] = (room[at, :].astype(f32) + one_buf[kind, 0].astype(f32)).astype(bf16)
        two_copy(kind, 2).start()
        two_copy(kind, 0).wait_recv()
        at = halves(1)[1]
        room[at, :] = (room[at, :].astype(f32) + two_buf[kind, 0].astype(f32)).astype(bf16)
        one_copy(kind, 2).start()
    sum_step(parts - 2)
    for kind in range(3):
        total_ref = kinds[kind][3]
        one_copy(kind, 1).wait_recv()
        two_copy(kind, 2).wait_recv()
        total_ref[:half, :] += one_buf[kind, 1].astype(f32) + two_buf[kind, 2].astype(f32)
        two_copy(kind, 1).wait_recv()
        one_copy(kind, 2).wait_recv()
        total_ref[half:, :] += two_buf[kind, 1].astype(f32) + one_buf[kind, 2].astype(f32)
    for kind in range(3):
        for k in range(4):
            near_copy(kind, k).wait_send()
        for n in range(3):
            one_copy(kind, n).wait_send()
            two_copy(kind, n).wait_send()
    for k in range(parts - 1):
        hop(k).wait_send()
        sum_hop(k).wait_send()
    for k in (parts - 2, parts - 1):
        store(k).wait()


def swiglu(normed, own, first, others, gate_w, up_w, down_w, copies, collective):
    parts = lax.axis_size("tensor")
    rows, width = normed.shape
    hidden = gate_w.shape[1]
    share = width // 8
    somewhere = pl.BlockSpec(memory_space=pl.ANY)
    vmem = pl.BlockSpec(memory_space=pltpu.VMEM)
    wide, narrow = (parts, rows, width), (parts, rows, hidden)
    return pl.pallas_call(
        functools.partial(swiglu_kernel, copies),
        out_shape=[jax.ShapeDtypeStruct(wide, bf16), jax.ShapeDtypeStruct((rows, width), f32)]
        + [jax.ShapeDtypeStruct((share, hidden), f32)] * 3,
        in_specs=[somewhere] * 7,
        out_specs=[somewhere] + [vmem] * 4,
        scratch_shapes=[pltpu.VMEM(wide, bf16)] * 2
        + [pltpu.VMEM((width, hidden), bf16)] * 3
        + [pltpu.VMEM(narrow, bf16)] * 3
        + [
            pltpu.VMEM(wide, bf16),
            pltpu.VMEM((2, rows, width), bf16),
            pltpu.VMEM((parts - 1, rows, width), bf16),
        ]
        + [pltpu.VMEM((3, 3, share // 2, hidden), bf16)] * 2
        + [pltpu.SemaphoreType.DMA((7,)), pltpu.SemaphoreType.DMA((2,))]
        + [pltpu.SemaphoreType.DMA((parts - 1,))] * 4
        + [pltpu.SemaphoreType.DMA((3, 4))] * 2
        + [pltpu.SemaphoreType.DMA((3, 3))] * 4
        + [pltpu.SemaphoreType.REGULAR],
        compiler_params=pltpu.CompilerParams(
            collective_id=collective, has_side_effects=True, vmem_limit_bytes=60 * 1024 * 1024
        ),
        cost_estimate=pl.CostEstimate(
            flops=18 * parts * rows * width * hidden,
            bytes_accessed=1100 * rows * width,
            transcendentals=parts * rows * hidden,
        ),
    )(normed, own, first, others, gate_w, up_w, down_w)


def forward_kernel(steps, seqs, forget_ref, drive_ref, state_ref, decay_ref):
    width = forget_ref.shape[1]

    def step(at, carry):
        state, decay = carry
        rows = pl.ds(at, seqs, stride=steps)
        forget = forget_ref[rows, :]
        state = forget * state + drive_ref[rows, :]
        decay = decay * forget
        state_ref[rows, :] = state
        decay_ref[rows, :] = decay
        return state, decay

    lax.fori_loop(
        0, steps, step, (jnp.zeros((seqs, width), f32), jnp.ones((seqs, width), f32)), unroll=8
    )


def backward_kernel(steps, seqs, forget_ref, drive_ref, carried_ref, decay_ref):
    width = forget_ref.shape[1]

    def step(k, carry):
        coming, decay = carry
        rows = pl.ds(steps - 1 - k, seqs, stride=steps)
        forget = forget_ref[rows, :]
        carried = drive_ref[rows, :] + coming
        carried_ref[rows, :] = carried
        decay_ref[rows, :] = decay
        return forget * carried, decay * forget

    lax.fori_loop(
        0, steps, step, (jnp.zeros((seqs, width), f32), jnp.ones((seqs, width), f32)), unroll=8
    )


def local_scan(body, seqs, forget, drive):
    rows, width = forget.shape
    lanes = 128 if width % 128 == 0 else width
    spec = pl.BlockSpec((rows, lanes), lambda c: (0, c))
    return pl.pallas_call(
        functools.partial(body, rows // seqs, seqs),
        grid=(width // lanes,),
        in_specs=[spec, spec],
        out_specs=[spec, spec],
        out_shape=[jax.ShapeDtypeStruct((rows, width), f32)] * 2,
        compiler_params=pltpu.CompilerParams(vmem_limit_bytes=32 * 1024 * 1024),
        cost_estimate=pl.CostEstimate(
            flops=4 * rows * width, bytes_accessed=16 * rows * width, transcendentals=0
        ),
    )(forget, drive)


def on_device(
    inputs,
    lengths,
    gain_mix,
    gain_glu,
    lower_bound,
    w_input,
    w_forget,
    w_gate_mix,
    w_out,
    w_gate,
    w_up,
    w_down,
    cotangent,
):
    tensor_parts = lax.axis_size("tensor")
    data_parts = lax.axis_size("dp")
    tensor_index = lax.axis_index("tensor")
    data_index = lax.axis_index("dp")
    rows_here, width = inputs.shape
    group = min(8, data_parts)
    copies = data_parts // group
    group_index = lax.div(data_index, copies)
    copy_index = lax.rem(data_index, copies)
    group_masks = [copies << k for k in range(group.bit_length() - 1)]
    copy_masks = [1 << k for k in range(copies.bit_length() - 1)]
    all_masks = [1 << k for k in range(data_parts.bit_length() - 1)]
    group_lists = [[g * copies + o for g in range(group)] for o in range(copies)]
    channels = width // group
    own_rows = w_input.shape[0]

    high = lax.div(lengths, 32).astype(bf16)
    low = lax.rem(lengths, 32).astype(bf16)
    length_row = jnp.concatenate([high, low, jnp.zeros((own_rows - 2,), bf16)])
    small = jnp.stack([gain_mix, gain_glu, lower_bound, length_row])
    small = in_order(shifted_blocks(small))
    small = gather_bits(small, sorted(all_masks, reverse=True)).astype(f32)
    small = small.reshape((data_parts * tensor_parts,) + small.shape[2:])
    gain_one = small[:, 0].reshape(width)
    gain_two = small[:, 1].reshape(width)
    bound = lax.dynamic_slice_in_dim(small[:, 2].reshape(width), group_index * channels, channels)
    every_length = small[:, 3].reshape(data_parts, tensor_parts, own_rows)[:, 0, :2]
    every_length = (every_length[:, 0] * 32.0 + every_length[:, 1]).astype(jnp.int32)
    group_lengths = lax.dynamic_index_in_dim(
        every_length.reshape(group, copies), copy_index, axis=1, keepdims=False
    )
    position = tensor_index * rows_here + jnp.arange(rows_here, dtype=jnp.int32)
    live_own = (position < lengths[0]).astype(f32)[:, None]
    live = (position[None, :] < group_lengths[:, None]).astype(f32)
    live = live.reshape(group * rows_here, 1)

    def spread(weight):
        return weight.reshape(own_rows, group, channels).transpose(1, 0, 2)

    pieces = jnp.concatenate([spread(w_input), spread(w_forget), spread(w_gate_mix)], axis=2)
    pieces = lax.all_to_all(
        pieces, "dp", 0, 0, axis_index_groups=group_lists if copies > 1 else None, tiled=True
    )
    pieces = jnp.concatenate([pieces, spread(w_out)], axis=2)
    if copies > 1:
        pieces = gather_bits(pieces, copy_masks[::-1])
    pieces = pieces.reshape(copies, group, own_rows, 4 * channels)
    masked_grad = live_own * cotangent
    masked_own = masked_grad.astype(bf16)
    masked_first = ring(masked_own)

    scale_one, unit_one = norm_rows(inputs)
    normed_one, pieces = plane_gather(
        (unit_one * gain_one).astype(bf16),
        copies,
        1,
        pieces.reshape(copies * group * own_rows, 4 * channels),
        [masked_first],
    )
    rows_all = group * rows_here
    normed_one = normed_one.reshape(rows_all, width)
    pieces = pieces.reshape(tensor_parts, copies, group, own_rows, 4 * channels)
    mixer_w = pieces[..., : 3 * channels].transpose(2, 1, 0, 3, 4).reshape(width, 3 * channels)
    out_w = pieces[..., 3 * channels :].transpose(1, 0, 3, 2, 4).reshape(channels, width)

    first, second = orders(all_masks)
    hidden_here = w_gate.shape[1]
    gate_w, up_w, down_w = (
        lax.all_gather(weight, "dp", axis=0, tiled=True) for weight in (w_gate, w_up, w_down.T)
    )

    pre = matmul(normed_one, mixer_w)
    input_pre = pre[:, :channels]
    forget_sig = jax.nn.sigmoid(pre[:, channels : 2 * channels])
    gate_pre = pre[:, 2 * channels :]
    forget = bound + (1.0 - bound) * forget_sig
    input_act = silu_of(input_pre)
    gate_act = silu_of(gate_pre)
    inflow = live * (1.0 - forget) * input_act
    part_state, part_decay = local_scan(forward_kernel, group, forget, inflow)
    shaped = (group, rows_here, channels)
    part_state = part_state.reshape(shaped)
    part_decay = part_decay.reshape(shaped)
    ends = jnp.stack([part_state[:, -1], part_decay[:, -1]])
    all_ends = in_order(shifted_blocks(ends))
    coming = jnp.zeros((group, channels), f32)
    entering = coming
    for k in range(tensor_parts - 1):
        coming = all_ends[k, 1] * coming + all_ends[k, 0]
        entering = jnp.where(tensor_index == k + 1, coming, entering)
    state = part_state + part_decay * entering[:, None, :]
    prior_state = jnp.concatenate([entering[:, None, :], state[:, :-1]], axis=1)
    state = state.reshape(group * rows_here, channels)
    prior_state = prior_state.reshape(group * rows_here, channels)
    mixed_low = (state * gate_act).astype(bf16)
    mixed = mixed_low.reshape(shaped)
    mixed_sum, masked_others = plane_scatter(mixed, out_w, copies, False, 2, masked_first)
    stream = inputs + mixed_sum

    scale_two, unit_two = norm_rows(stream)
    normed_two = (unit_two * gain_two).astype(bf16)
    out_rows, grad_norm_two, *weight_sums = swiglu(
        normed_two, masked_own, masked_first, masked_others, gate_w, up_w, down_w, copies, 4
    )
    if copies > 1:
        weight_sums = [
            scatter_bits(total.reshape(copies, width // data_parts, hidden_here), copy_masks, f32)
            for total in weight_sums
        ]
    grad_gate_mine, grad_up_mine, grad_down_mine = weight_sums
    grad_down_mine = grad_down_mine.T

    out_rows = out_rows.reshape(tensor_parts * rows_here, width)
    out_sum = lax.psum_scatter(out_rows, "tensor", scatter_dimension=0, tiled=True)

    gain_two_part = jnp.sum(grad_norm_two * unit_two, axis=0)
    grad_stream = masked_grad + norm_back(grad_norm_two, unit_two, scale_two, gain_two)
    (stream_low,) = plane_gather(grad_stream.astype(bf16), copies, 5)
    stream_low = stream_low.reshape(rows_all, width)

    grad_out_w = matmul_lt(mixed_low, stream_low).astype(bf16)
    grad_mixed = matmul_rt(stream_low, out_w)
    grad_gate_pre = (grad_mixed * state * silu_slope(gate_pre)).astype(bf16)
    grad_state = grad_mixed * gate_act
    part_carried, part_after = local_scan(backward_kernel, group, forget, grad_state)
    part_carried = part_carried.reshape(shaped)
    part_after = part_after.reshape(shaped)
    first_forget = forget.reshape(shaped)[:, 0]
    begins = jnp.stack([first_forget * part_carried[:, 0], first_forget * part_after[:, 0]])
    all_begins = in_order(shifted_blocks(begins))
    coming = jnp.zeros((group, channels), f32)
    entering = coming
    for k in range(tensor_parts - 1, 0, -1):
        coming = all_begins[k, 1] * coming + all_begins[k, 0]
        entering = jnp.where(tensor_index == k - 1, coming, entering)
    carried = (part_carried + part_after * entering[:, None, :]).reshape(
        group * rows_here, channels
    )
    grad_forget = carried * prior_state - carried * live * input_act
    grad_input_pre = (carried * live * (1.0 - forget) * silu_slope(input_pre)).astype(bf16)
    grad_bound = jnp.sum(grad_forget * (1.0 - forget_sig), axis=0)
    grad_forget_pre = (grad_forget * (1.0 - bound) * forget_sig * (1.0 - forget_sig)).astype(bf16)
    grad_pre = jnp.concatenate([grad_input_pre, grad_forget_pre, grad_gate_pre], axis=1)
    grad_parts = grad_pre.reshape(group, rows_here, 3 * channels)
    grad_mixer = matmul_lt(normed_one, grad_pre).astype(bf16)
    mixer_sums = jnp.concatenate(
        [
            grad_mixer.reshape(group, copies, tensor_parts, own_rows, 3 * channels).transpose(
                2, 1, 0, 3, 4
            ),
            grad_out_w.reshape(copies, tensor_parts, own_rows, group, channels).transpose(
                1, 0, 3, 2, 4
            ),
        ],
        axis=-1,
    ).reshape(tensor_parts, copies * group * own_rows, 4 * channels)
    grad_norm_one, mixer_sums = plane_scatter(
        grad_parts, mixer_w, copies, True, 3, sums=mixer_sums, before=[out_sum]
    )
    output = live_own * (stream + after(out_sum, grad_norm_one).astype(f32))
    gain_one_part = jnp.sum(grad_norm_one * unit_one, axis=0)
    grad_inputs = grad_stream + norm_back(grad_norm_one, unit_one, scale_one, gain_one)

    mixer_sums = mixer_sums.reshape(copies, group, own_rows, 4 * channels)
    if copies > 1:
        mixer_sums = scatter_bits(mixer_sums, copy_masks, f32)
    mixer_sums = mixer_sums.reshape(group, own_rows, 4 * channels)
    grad_out = mixer_sums[..., 3 * channels :].transpose(1, 0, 2).reshape(own_rows, width)
    grad_mixer = lax.all_to_all(
        mixer_sums[..., : 3 * channels].astype(bf16),
        "dp",
        0,
        0,
        axis_index_groups=group_lists if copies > 1 else None,
        tiled=True,
    )
    grad_mixer = grad_mixer.reshape(group, own_rows, 3, channels).transpose(2, 1, 0, 3)
    grad_mixer = grad_mixer.reshape(3, own_rows, width).astype(f32)

    bound_part = lax.dynamic_update_slice_in_dim(
        jnp.zeros((width,), f32), grad_bound, group_index * channels, 0
    )
    sums = jnp.stack([gain_one_part, gain_two_part, bound_part])
    sums = sums.reshape(3, data_parts, tensor_parts, own_rows).transpose(1, 2, 0, 3)
    sums = scatter_straight(scatter_bits(sums, sorted(all_masks), f32))
    return (
        output,
        grad_inputs,
        sums[0],
        sums[1],
        sums[2],
        grad_mixer[0],
        grad_mixer[1],
        grad_mixer[2],
        grad_out,
        grad_gate_mine,
        grad_up_mine,
        grad_down_mine,
    )


def solution(mesh):
    both = ("dp", "tensor")
    placed = (
        P(both, None),
        P("dp"),
        P(both),
        P(both),
        P(both),
        P(both, None),
        P(both, None),
        P(both, None),
        P(both, None),
        P("dp", "tensor"),
        P("dp", "tensor"),
        P("tensor", "dp"),
        P(both, None),
    )
    return jax.shard_map(
        on_device,
        mesh=mesh,
        in_specs=placed,
        out_specs=(
            P(both, None),
            P(both, None),
            P(both),
            P(both),
            P(both),
            P(both, None),
            P(both, None),
            P(both, None),
            P(both, None),
            P("dp", "tensor"),
            P("dp", "tensor"),
            P("tensor", "dp"),
        ),
        check_vma=False,
    )
```

```python
import functools

import jax
import jax.numpy as jnp
from jax import lax
from jax.experimental import pallas as pl
from jax.experimental.pallas import tpu as pltpu
from jax.sharding import PartitionSpec as P

epsilon = 1e-06
bf16 = jnp.bfloat16
f32 = jnp.float32


def matmul(left, right):
    return jnp.dot(left, right, preferred_element_type=f32)


def matmul_rt(left, right):
    return lax.dot_general(left, right, (((1,), (1,)), ((), ())), preferred_element_type=f32)


def matmul_lt(left, right):
    return lax.dot_general(left, right, (((0,), (0,)), ((), ())), preferred_element_type=f32)


def silu_of(value):
    return value * jax.nn.sigmoid(value)


def silu_slope(value):
    squash = jax.nn.sigmoid(value)
    return squash * (1.0 + value * (1.0 - squash))


def norm_rows(value):
    scale = lax.rsqrt(jnp.mean(value * value, axis=-1, keepdims=True) + epsilon)
    return (scale, value * scale)


def norm_back(grad_norm, unit, scale, gain):
    scaled = grad_norm * gain
    return scale * (scaled - unit * jnp.mean(scaled * unit, axis=-1, keepdims=True))


def untouched_kernel(*refs):
    pass


def after(value, *others):
    somewhere = pl.BlockSpec(memory_space=pl.ANY)
    return pl.pallas_call(
        untouched_kernel,
        out_shape=jax.ShapeDtypeStruct(value.shape, value.dtype),
        in_specs=[somewhere] * (1 + len(others)),
        out_specs=somewhere,
        input_output_aliases={0: 0},
        cost_estimate=pl.CostEstimate(flops=0, bytes_accessed=0, transcendentals=0),
    )(value, *others)


def swap(value, mask):
    return lax.ppermute(value, "dp", [(i, i ^ mask) for i in range(lax.axis_size("dp"))])


def own_bit(mask):
    return lax.rem(lax.div(lax.axis_index("dp"), mask), 2)


def gather_bits(value, order):
    base = value.shape
    done = []
    for mask in order:
        other = swap(value, mask)
        at = sum(1 for seen in done if seen > mask)
        low = jnp.stack([value, other], axis=at)
        high = jnp.stack([other, value], axis=at)
        value = jnp.where(own_bit(mask) == 0, low, high)
        done.append(mask)
    return value.reshape((1 << len(order),) + base)


def scatter_bits(value, order, sent=bf16, hold=(None, None)):
    count = len(order)
    value = value.reshape((2,) * count + value.shape[1:])
    left = sorted(order, reverse=True)
    for mask in order:
        at = left.index(mask)
        left.remove(mask)
        bit = own_bit(mask)
        send = lax.dynamic_index_in_dim(value, 1 - bit, at, keepdims=False).astype(sent)
        keep = lax.dynamic_index_in_dim(value, bit, at, keepdims=False)
        if hold[0] == count - len(left) - 1:
            send = after(send, hold[1])
        total = keep.astype(f32) + swap(send, mask).astype(f32)
        value = total.astype(sent) if left else total
    return value


def orders(masks):
    down = sorted(masks, reverse=True)
    if len(down) < 3:
        return down, down
    return down, [down[1], down[0]] + down[2:]


def gather_halves(value, masks):
    first, second = orders(masks)
    half = value.shape[-1] // 2
    return gather_bits(value[..., :half], first), gather_bits(value[..., half:], second)


def scatter_halves(left, right, masks):
    first, second = orders(masks)
    return jnp.concatenate(
        [scatter_bits(left, first[::-1]), scatter_bits(right, second[::-1])], axis=-1
    )


def ring(value):
    parts = lax.axis_size("tensor")
    return lax.ppermute(value, "tensor", [(i, (i + 1) % parts) for i in range(parts)])


def ring_blocks(value):
    blocks = [value]
    for _ in range(lax.axis_size("tensor") - 1):
        blocks.append(ring(blocks[-1]))
    return blocks


def ring_scatter(blocks):
    total = blocks[1 % len(blocks)]
    totals = [total]
    for k in range(2, len(blocks) + 1):
        moved = ring(total).astype(f32)
        total = moved + blocks[k % len(blocks)].astype(f32)
        if k < len(blocks):
            total = total.astype(bf16)
            totals.append(total)
    return total, totals


def shifted_blocks(value):
    parts = lax.axis_size("tensor")
    blocks = [value]
    for k in range(1, parts):
        blocks.append(lax.ppermute(value, "tensor", [(i, (i + k) % parts) for i in range(parts)]))
    return blocks


def scatter_straight(value):
    here = lax.axis_index("tensor")
    parts = lax.axis_size("tensor")
    total = lax.dynamic_index_in_dim(value, here, 0, keepdims=False)
    for k in range(1, parts):
        send = lax.dynamic_index_in_dim(value, lax.rem(here + k, parts), 0, keepdims=False)
        total += lax.ppermute(send, "tensor", [(i, (i + k) % parts) for i in range(parts)])
    return total


def in_order(blocks):
    here = lax.axis_index("tensor")
    parts = len(blocks)
    stacked = jnp.stack(blocks[::-1] + blocks[::-1])
    return lax.dynamic_slice_in_dim(stacked, parts - 1 - here, parts, 0)


def partner(mask):
    me = lax.axis_index("dp")
    return me + mask * (1 - 2 * lax.rem(lax.div(me, mask), 2))


def greet(masks, ring_too=False):
    barrier = pltpu.get_barrier_semaphore()
    others = [{"dp": partner(mask)} for mask in masks]
    if ring_too:
        others += [{"tensor": beside(1)}, {"tensor": beside(-1)}]
    for other in others:
        pl.semaphore_signal(
            barrier, inc=1, device_id=other, device_id_type=pl.DeviceIdType.MESH
        )
    pl.semaphore_wait(barrier, len(others))


def beside(step):
    parts = lax.axis_size("tensor")
    return lax.rem(lax.axis_index("tensor") + step + parts, parts)


def slot_of(copies, masks):
    me = lax.axis_index("dp")
    for mask in masks:
        me = me + mask * (1 - 2 * lax.rem(lax.div(me, mask), 2))
    return lax.div(me, copies)


def to_right(source, target, send_sem, recv_sem):
    return pltpu.make_async_remote_copy(
        src_ref=source,
        dst_ref=target,
        send_sem=send_sem,
        recv_sem=recv_sem,
        device_id={"tensor": beside(1)},
        device_id_type=pl.DeviceIdType.MESH,
    )


def plane_gather_steps(copies, value_ref, all_ref, own_sem, send_sem, recv_sem):
    near, one, two = copies, 2 * copies, 4 * copies
    half = value_ref.shape[0] // 2
    top, low = pl.ds(0, half), pl.ds(half, half)
    mine = slot_of(copies, ())
    at_one, at_two = slot_of(copies, (one,)), slot_of(copies, (two,))
    at_both = slot_of(copies, (one, two))
    local = pltpu.make_async_copy(value_ref, all_ref.at[mine], own_sem)
    sent = []
    last = []

    def send(source, slot, rows, mask):
        index = len(sent)
        copy = pltpu.make_async_remote_copy(
            src_ref=source,
            dst_ref=all_ref.at[slot, rows],
            send_sem=send_sem.at[index],
            recv_sem=recv_sem.at[index],
            device_id={"dp": partner(mask)},
            device_id_type=pl.DeviceIdType.MESH,
        )
        copy.start()
        sent.append(copy)
        if mask == near:
            last.append(copy)
        return copy

    def forward(slot, rows, mask):
        return send(all_ref.at[slot, rows], slot, rows, mask)

    first = []
    second = []

    def begin():
        local.start()
        first.append(send(value_ref.at[top], mine, top, two))
        first.append(send(value_ref.at[low], mine, low, one))
        first.append(send(value_ref.at[low], mine, low, two))
        first.append(send(value_ref.at[top], mine, top, one))
        send(value_ref.at[top], mine, top, near)
        send(value_ref.at[low], mine, low, near)

    def pass_first():
        first[0].wait_recv()
        second.append(forward(at_two, top, one))
        forward(at_two, top, near)
        first[1].wait_recv()
        second.append(forward(at_one, low, two))
        forward(at_one, low, near)

    def pass_second():
        first[2].wait_recv()
        forward(at_two, low, near)
        first[3].wait_recv()
        forward(at_one, top, near)

    def pass_last():
        second[0].wait_recv()
        forward(at_both, top, near)
        second[1].wait_recv()
        forward(at_both, low, near)

    def arrive(some=slice(None)):
        for copy in last[some]:
            copy.wait_recv()
        if some == slice(None):
            local.wait()

    def finish():
        for copy in sent:
            copy.wait_send()

    return begin, pass_first, pass_second, pass_last, arrive, finish


def plane_gather_kernel(copies, value_ref, all_ref, own_sem, send_sem, recv_sem):
    greet((copies, 2 * copies, 4 * copies))
    for step in plane_gather_steps(
        copies, value_ref, all_ref, own_sem.at[0], send_sem, recv_sem
    ):
        step()


def plane_gather(value, copies, collective):
    rows, width = value.shape
    somewhere = pl.BlockSpec(memory_space=pl.ANY)
    return pl.pallas_call(
        functools.partial(plane_gather_kernel, copies),
        out_shape=jax.ShapeDtypeStruct((8, rows, width), value.dtype),
        in_specs=[somewhere],
        out_specs=somewhere,
        scratch_shapes=[
            pltpu.SemaphoreType.DMA((1,)),
            pltpu.SemaphoreType.DMA((14,)),
            pltpu.SemaphoreType.DMA((14,)),
        ],
        compiler_params=pltpu.CompilerParams(collective_id=collective, has_side_effects=True),
        cost_estimate=pl.CostEstimate(
            flops=0, bytes_accessed=320 * rows * width, transcendentals=0
        ),
    )(value)


def plane_scatter_kernel(
    copies, transposed, left_ref, right_ref, sum_ref, near_ref, one_ref, two_ref, part_ref,
    send_sem, recv_sem, block_ref=None, blocks_ref=None, ring_send=None, ring_recv=None,
    total_ref=None, shares=None, ring_buf=None, load_sem=None, greeted=False, product=None,
    between=lambda point: None,
):
    near, one, two = copies, 2 * copies, 4 * copies
    rows, width = sum_ref.shape
    half = rows // 2
    top, low = pl.ds(0, half), pl.ds(half, half)
    tile = min(512, width)
    if not greeted:
        greet((near, one, two), ring_send is not None)
    ring_steps = []
    parts = lax.axis_size("tensor")
    if shares is not None:
        loads = [
            pltpu.make_async_copy(block_ref.at[beside(-k)], shares.at[k], load_sem.at[k])
            for k in range(parts)
        ]
        for load in loads:
            load.start()
        for load in loads:
            load.wait()
        sum_steps = [
            to_right(shares.at[k + 1], ring_buf.at[k], ring_send.at[k], ring_recv.at[k])
            for k in range(parts - 1)
        ]
        sum_steps[0].start()
    elif block_ref is not None:
        for k in range(blocks_ref.shape[0]):
            source = block_ref if k == 0 else blocks_ref.at[k - 1]
            ring_steps.append(
                to_right(source, blocks_ref.at[k], ring_send.at[k], ring_recv.at[k])
            )
        ring_steps[0].start()
    flips = [(), (one,), (two,), (one, two)]
    copies_out = []

    def send(source, target, mask):
        index = len(copies_out)
        copy = pltpu.make_async_remote_copy(
            src_ref=source,
            dst_ref=target,
            send_sem=send_sem.at[index],
            recv_sem=recv_sem.at[index],
            device_id={"dp": partner(mask)},
            device_id_type=pl.DeviceIdType.MESH,
        )
        copy.start()
        copies_out.append(copy)
        return copy

    def each_tile(body):
        @pl.loop(0, width // tile)
        def _(k):
            body(pl.ds(pl.multiple_of(k * tile, tile), tile))

    def block_product(slot, columns):
        left = left_ref[slot]
        if transposed:
            return matmul_rt(left, right_ref[columns, :])
        return matmul(left, right_ref[:, columns])

    product = product or block_product

    arriving = {}
    for k in (3, 1, 2, 0):
        slot = slot_of(copies, flips[k] + (near,))

        def theirs(columns, k=k, slot=slot):
            part_ref[k, :, columns] = product(slot, columns).astype(bf16)

        each_tile(theirs)
        arriving[k] = send(part_ref.at[k], near_ref.at[k], near)

    between("sent")

    def added(k):
        slot = slot_of(copies, flips[k])
        arriving[k].wait_recv()

        def mine(columns):
            total = product(slot, columns) + near_ref[k, :, columns].astype(f32)
            if k == 0:
                sum_ref[:, columns] = total
            else:
                near_ref[k, :, columns] = total.astype(bf16)

        each_tile(mine)

    added(3)
    one_first = send(near_ref.at[3, top], one_ref.at[0], one)
    two_first = send(near_ref.at[3, low], two_ref.at[0], two)
    added(1)
    one_second = send(near_ref.at[1, top], one_ref.at[1], one)
    added(2)
    two_second = send(near_ref.at[2, low], two_ref.at[1], two)
    added(0)
    between("added")

    one_first.wait_recv()

    def pass_top(columns):
        total = near_ref[2, top, columns].astype(f32) + one_ref[0, :, columns].astype(f32)
        near_ref[2, top, columns] = total.astype(bf16)

    each_tile(pass_top)
    two_last = send(near_ref.at[2, top], two_ref.at[2], two)
    between("top")
    two_first.wait_recv()

    def pass_low(columns):
        total = near_ref[1, low, columns].astype(f32) + two_ref[0, :, columns].astype(f32)
        near_ref[1, low, columns] = total.astype(bf16)

    each_tile(pass_low)
    one_last = send(near_ref.at[1, low], one_ref.at[2], one)
    between("low")

    def finish(rows_at, first, at_first, second, at_second):
        def body(columns):
            sum_ref[rows_at, columns] += (
                first[at_first, :, columns].astype(f32) + second[at_second, :, columns].astype(f32)
            )

        each_tile(body)

    def sum_step(k):
        sum_steps[k].wait_recv()
        many = shares.shape[1] // 4

        @pl.loop(0, 4)
        def _(n):
            some = pl.ds(pl.multiple_of(n * many, many), many)
            at = (k + 2) % parts
            total = shares[at, some, :].astype(f32) + ring_buf[k, some, :].astype(f32)
            if at:
                shares[at, some, :] = total.astype(bf16)
            else:
                total_ref[some, :] = total

        if k + 1 < parts - 1:
            sum_steps[k + 1].start()

    if shares is not None:
        sum_step(0)
    for k, step in enumerate(ring_steps):
        step.wait_recv()
        if k + 1 < len(ring_steps):
            ring_steps[k + 1].start()
    one_second.wait_recv()
    two_last.wait_recv()
    finish(top, one_ref, 1, two_ref, 2)
    two_second.wait_recv()
    one_last.wait_recv()
    finish(low, two_ref, 1, one_ref, 2)
    between("whole")
    if shares is not None:
        for k in range(1, parts - 1):
            sum_step(k)
        ring_steps = sum_steps
    for copy in copies_out + ring_steps:
        copy.wait_send()


def scatter_late_kernel(copies, transposed, late, left_ref, right_ref, block_ref, *refs):
    sum_ref, blocks_ref = refs[late : late + 2]
    refs = refs[late + 2 :]
    if len(refs) == 8:
        plane_scatter_kernel(
            copies, transposed, left_ref, right_ref, sum_ref, *refs[:6], block_ref, blocks_ref,
            *refs[6:],
        )
    else:
        plane_scatter_kernel(
            copies, transposed, left_ref, right_ref, sum_ref, *refs[:6], block_ref, None,
            *refs[6:8], blocks_ref, *refs[8:],
        )


def plane_scatter(left, right, copies, transposed, collective, block=None, sums=None, before=()):
    group, rows, depth = left.shape
    width = right.shape[0] if transposed else right.shape[1]
    half = rows // 2
    vmem = pl.BlockSpec(memory_space=pltpu.VMEM)
    somewhere = pl.BlockSpec(memory_space=pl.ANY)
    scratch = [
        pltpu.VMEM((4, rows, width), bf16),
        pltpu.VMEM((3, half, width), bf16),
        pltpu.VMEM((3, half, width), bf16),
        pltpu.VMEM((4, rows, width), bf16),
        pltpu.SemaphoreType.DMA((10,)),
        pltpu.SemaphoreType.DMA((10,)),
    ]
    shapes = [jax.ShapeDtypeStruct((rows, width), f32)]
    out_specs = [vmem]
    parts = lax.axis_size("tensor")
    if block is not None:
        operands = [left, right, block]
        steps = parts - 2
        shapes.append(jax.ShapeDtypeStruct((steps,) + block.shape, block.dtype))
        out_specs.append(somewhere)
        scratch += [pltpu.SemaphoreType.DMA((steps,))] * 2
    else:
        operands = [left, right, sums]
        shapes.append(jax.ShapeDtypeStruct(sums.shape[1:], f32))
        out_specs.append(vmem)
        scratch += [pltpu.SemaphoreType.DMA((parts - 1,))] * 2
        scratch += [
            pltpu.VMEM(sums.shape, bf16),
            pltpu.VMEM((parts - 1,) + sums.shape[1:], bf16),
            pltpu.SemaphoreType.DMA((parts,)),
        ]
    operands += before
    return pl.pallas_call(
        functools.partial(
            scatter_late_kernel, copies, transposed, len(before)
        ),
        out_shape=shapes,
        in_specs=[vmem, vmem] + [somewhere] * (len(operands) - 2),
        out_specs=out_specs,
        scratch_shapes=scratch,
        compiler_params=pltpu.CompilerParams(
            collective_id=collective, has_side_effects=True, vmem_limit_bytes=48 * 1024 * 1024
        ),
        cost_estimate=pl.CostEstimate(
            flops=2 * group * rows * depth * width,
            bytes_accessed=400 * rows * width,
            transcendentals=0,
        ),
    )(*operands)


def column_tiles(width, most=512):
    return [(at, min(most, width - at)) for at in range(0, width, most)]


def swiglu_kernel(
    copies,
    normed_ref, own_ref, first_ref, others_ref, gate_hbm, up_hbm, down_hbm,
    rows_out, norm_sum, gate_sum, up_sum, down_sum,
    normed, masked, gate_w, up_w, down_w, hidden, gate_low, up_low, back, rows, ring_buf,
    one_buf, two_buf, in_sem, out_sem, send_sem, recv_sem, sum_send, sum_recv, near_send,
    near_recv, one_send, one_recv, two_send, two_recv, ready_sem,
):
    parts = lax.axis_size("tensor")
    near, one, two = copies, 2 * copies, 4 * copies
    greet((near, one, two), True)
    own = pltpu.make_async_copy(normed_ref, normed.at[0], in_sem.at[0])
    own.start()
    loads = [
        pltpu.make_async_copy(gate_hbm, gate_w, in_sem.at[1]),
        pltpu.make_async_copy(up_hbm, up_w, in_sem.at[2]),
        pltpu.make_async_copy(own_ref, masked.at[0], in_sem.at[3]),
        pltpu.make_async_copy(down_hbm, down_w, in_sem.at[4]),
        pltpu.make_async_copy(first_ref, masked.at[1], in_sem.at[5]),
        pltpu.make_async_copy(others_ref, masked.at[pl.ds(2, parts - 2)], in_sem.at[6]),
    ]
    own.wait()
    for load in loads:
        load.start()
    width = normed.shape[2]
    tile = min(512, width)

    def hop(k):
        return to_right(normed.at[k], normed.at[k + 1], send_sem.at[k], recv_sem.at[k])

    def sum_hop(k):
        return to_right(back.at[k + 1], ring_buf.at[k], sum_send.at[k], sum_recv.at[k])

    hop(0).start()
    for load in loads:
        load.wait()

    def store(k):
        home = lax.rem(lax.axis_index("tensor") + parts - k, parts)
        slot = lax.rem(k, 2)
        return pltpu.make_async_copy(rows.at[slot], rows_out.at[home], out_sem.at[slot])

    def block(k, nothing):
        @pl.when(k > 0)
        def _():
            hop(k - 1).wait_recv()

        @pl.when(jnp.logical_and(k > 0, k < parts - 1))
        def _():
            hop(k).start()

        @pl.when(k == parts - 1)
        def _():
            sum_hop(0).start()

        for at, size in column_tiles(hidden.shape[2]):
            columns = pl.ds(at, size)
            glu_gate = matmul(normed[k], gate_w[:, columns])
            glu_up = matmul(normed[k], up_w[:, columns])
            grad_hidden = matmul(masked[k], down_w[:, columns])
            squash = jax.nn.sigmoid(glu_gate)
            act = glu_gate * squash
            slope = squash * (1.0 + glu_gate * (1.0 - squash))
            hidden[k, :, columns] = (act * glu_up).astype(bf16)
            gate_low[k, :, columns] = (grad_hidden * glu_up * slope).astype(bf16)
            up_low[k, :, columns] = (grad_hidden * act).astype(bf16)

        @pl.when(k > 1)
        def _():
            store(k - 2).wait()

        slot = lax.rem(k, 2)

        @pl.loop(0, width // tile)
        def _(n):
            some = pl.ds(pl.multiple_of(n * tile, tile), tile)
            back[k, :, some] = (
                matmul_rt(gate_low[k], gate_w[some, :]) + matmul_rt(up_low[k], up_w[some, :])
            ).astype(bf16)
            rows[slot, :, some] = matmul_rt(hidden[k], down_w[some, :]).astype(bf16)

        store(k).start()
        return nothing

    lax.fori_loop(0, parts, block, 0)

    pl.semaphore_signal(
        ready_sem,
        inc=1,
        device_id={"dp": partner(near)},
        device_id_type=pl.DeviceIdType.MESH,
    )
    share = width // 8
    half = share // 2
    hidden_width = hidden.shape[2]
    tall = parts * normed.shape[1]
    kinds = (
        (normed, gate_low, gate_w, gate_sum),
        (normed, up_low, up_w, up_sum),
        (masked, hidden, down_w, down_sum),
    )

    def product(kind, slot):
        left, right, _, _ = kinds[kind]
        some = pl.ds(pl.multiple_of(slot * share, share), share)
        return matmul_lt(
            left[:, :, some].reshape(tall, share), right[...].reshape(tall, hidden_width)
        )

    def part_at(k):
        return pl.ds(pl.multiple_of(k * share, share), share)

    def near_at(k):
        return pl.ds(pl.multiple_of((4 + k) * share, share), share)

    def halves(k):
        at = (4 + k) * share
        return (
            pl.ds(pl.multiple_of(at, half), half),
            pl.ds(pl.multiple_of(at + half, half), half),
        )

    def across(source, target, send, recv, mask):
        return pltpu.make_async_remote_copy(
            src_ref=source,
            dst_ref=target,
            send_sem=send,
            recv_sem=recv,
            device_id={"dp": partner(mask)},
            device_id_type=pl.DeviceIdType.MESH,
        )

    def near_copy(kind, k):
        room = kinds[kind][2]
        return across(
            room.at[part_at(k)], room.at[near_at(k)], near_send.at[kind, k],
            near_recv.at[kind, k], near,
        )

    def one_copy(kind, n):
        room = kinds[kind][2]
        rows_at = (halves(3)[0], halves(1)[0], halves(1)[1])[n]
        return across(
            room.at[rows_at], one_buf.at[kind, n], one_send.at[kind, n], one_recv.at[kind, n], one
        )

    def two_copy(kind, n):
        room = kinds[kind][2]
        rows_at = (halves(3)[1], halves(2)[1], halves(2)[0])[n]
        return across(
            room.at[rows_at], two_buf.at[kind, n], two_send.at[kind, n], two_recv.at[kind, n], two
        )

    def flipped(k, near_too):
        me = lax.axis_index("dp")

        def turn(mask, on):
            return on * mask * (1 - 2 * lax.rem(lax.div(me, mask), 2))

        there = me + turn(one, lax.rem(k, 2)) + turn(two, lax.div(k, 2)) + turn(near, near_too)
        return lax.div(there, copies)

    def in_turn(i):
        return 3 - 2 * i + 3 * lax.div(i, 2)

    def sum_step(k):
        sum_hop(k).wait_recv()
        if k + 1 < parts - 1:

            @pl.loop(0, width // tile)
            def _(n):
                some = pl.ds(pl.multiple_of(n * tile, tile), tile)
                total = back[k + 2, :, some].astype(f32) + ring_buf[k, :, some].astype(f32)
                back[k + 2, :, some] = total.astype(bf16)

            sum_hop(k + 1).start()
        else:

            @pl.loop(0, width // tile)
            def _(n):
                some = pl.ds(pl.multiple_of(n * tile, tile), tile)
                norm_sum[:, some] = back[0, :, some].astype(f32) + ring_buf[k, :, some].astype(f32)

    pl.semaphore_wait(ready_sem, 1)

    def theirs(i, nothing):
        k = in_turn(i)
        slot = flipped(k, 1)
        for kind in range(3):
            kinds[kind][2][part_at(k), :] = product(kind, slot).astype(bf16)
            near_copy(kind, k).start()
        return nothing

    lax.fori_loop(0, 4, theirs, 0)
    sum_step(0)

    def mine(i, nothing):
        k = in_turn(i)
        slot = flipped(k, 0)
        for kind in range(3):
            near_copy(kind, k).wait_recv()
            room = kinds[kind][2]
            total = product(kind, slot) + room[near_at(k), :].astype(f32)
            room[near_at(k), :] = total.astype(bf16)

            @pl.when(k == 3)
            def _():
                one_copy(kind, 0).start()
                two_copy(kind, 0).start()

            @pl.when(k == 1)
            def _():
                one_copy(kind, 1).start()

            @pl.when(k == 2)
            def _():
                two_copy(kind, 1).start()

        return nothing

    lax.fori_loop(0, 3, mine, 0)
    for k in range(1, parts - 2):
        sum_step(k)
    for kind in range(3):
        near_copy(kind, 0).wait_recv()
        room, total_ref = kinds[kind][2:]
        total_ref[...] = product(kind, flipped(0, 0)) + room[near_at(0), :].astype(f32)
    for kind in range(3):
        room = kinds[kind][2]
        one_copy(kind, 0).wait_recv()
        at = halves(2)[0]
        room[at, :] = (room[at, :].astype(f32) + one_buf[kind, 0].astype(f32)).astype(bf16)
        two_copy(kind, 2).start()
        two_copy(kind, 0).wait_recv()
        at = halves(1)[1]
        room[at, :] = (room[at, :].astype(f32) + two_buf[kind, 0].astype(f32)).astype(bf16)
        one_copy(kind, 2).start()
    sum_step(parts - 2)
    for kind in range(3):
        total_ref = kinds[kind][3]
        one_copy(kind, 1).wait_recv()
        two_copy(kind, 2).wait_recv()
        total_ref[:half, :] += one_buf[kind, 1].astype(f32) + two_buf[kind, 2].astype(f32)
        two_copy(kind, 1).wait_recv()
        one_copy(kind, 2).wait_recv()
        total_ref[half:, :] += two_buf[kind, 1].astype(f32) + one_buf[kind, 2].astype(f32)
    for kind in range(3):
        for k in range(4):
            near_copy(kind, k).wait_send()
        for n in range(3):
            one_copy(kind, n).wait_send()
            two_copy(kind, n).wait_send()
    for k in range(parts - 1):
        hop(k).wait_send()
        sum_hop(k).wait_send()
    for k in (parts - 2, parts - 1):
        store(k).wait()


def swiglu(normed, own, first, others, gate_w, up_w, down_w, copies, collective):
    parts = lax.axis_size("tensor")
    rows, width = normed.shape
    hidden = gate_w.shape[1]
    share = width // 8
    somewhere = pl.BlockSpec(memory_space=pl.ANY)
    vmem = pl.BlockSpec(memory_space=pltpu.VMEM)
    wide, narrow = (parts, rows, width), (parts, rows, hidden)
    return pl.pallas_call(
        functools.partial(swiglu_kernel, copies),
        out_shape=[jax.ShapeDtypeStruct(wide, bf16), jax.ShapeDtypeStruct((rows, width), f32)]
        + [jax.ShapeDtypeStruct((share, hidden), f32)] * 3,
        in_specs=[somewhere] * 7,
        out_specs=[somewhere] + [vmem] * 4,
        scratch_shapes=[pltpu.VMEM(wide, bf16)] * 2
        + [pltpu.VMEM((width, hidden), bf16)] * 3
        + [pltpu.VMEM(narrow, bf16)] * 3
        + [
            pltpu.VMEM(wide, bf16),
            pltpu.VMEM((2, rows, width), bf16),
            pltpu.VMEM((parts - 1, rows, width), bf16),
        ]
        + [pltpu.VMEM((3, 3, share // 2, hidden), bf16)] * 2
        + [pltpu.SemaphoreType.DMA((7,)), pltpu.SemaphoreType.DMA((2,))]
        + [pltpu.SemaphoreType.DMA((parts - 1,))] * 4
        + [pltpu.SemaphoreType.DMA((3, 4))] * 2
        + [pltpu.SemaphoreType.DMA((3, 3))] * 4
        + [pltpu.SemaphoreType.REGULAR],
        compiler_params=pltpu.CompilerParams(
            collective_id=collective, has_side_effects=True, vmem_limit_bytes=60 * 1024 * 1024
        ),
        cost_estimate=pl.CostEstimate(
            flops=18 * parts * rows * width * hidden,
            bytes_accessed=1100 * rows * width,
            transcendentals=parts * rows * hidden,
        ),
    )(normed, own, first, others, gate_w, up_w, down_w)


def greet_all(copies, masks):
    barrier = pltpu.get_barrier_semaphore()
    others = [{"dp": group_member(copies, k)} for k in range(1, 8)]
    others += [{"tensor": beside(k)} for k in range(1, lax.axis_size("tensor"))]
    others += [{"dp": partner(mask)} for mask in masks]
    for other in others:
        pl.semaphore_signal(
            barrier, inc=1, device_id=other, device_id_type=pl.DeviceIdType.MESH
        )
    pl.semaphore_wait(barrier, len(others))


def group_member(copies, step):
    me = lax.axis_index("dp")
    return lax.rem(lax.div(me, copies) + step, 8) * copies + lax.rem(me, copies)


def mixer_forward_kernel(
    copies,
    own_ref, input_hbm, forget_hbm, gate_hbm, out_hbm, masked_hbm, bound_ref, live_ref,
    normed_out, weights_out, project_out, pre_out, squash_out, state_out, entering_out, mixed_out,
    masked_out, sum_ref,
    normed, weights, project, pre, squashed, forget, state, decay, ends, entering, mixed,
    near_buf, one_buf, two_buf, part_buf,
    own_sem, gather_send, gather_recv, spread_send, spread_recv, spread_own, ring_send, ring_recv,
    carry_send, carry_recv, scatter_send, scatter_recv, masked_send, masked_recv, out_sem,
):
    parts = lax.axis_size("tensor")
    here = lax.axis_index("tensor")
    seqs, rows, width = normed.shape
    strips, _, lanes = forget.shape
    channels = strips * lanes
    mine = slot_of(copies, ())
    greet_all(copies, ())

    def own_rows_of(index):
        return pl.ds(pl.multiple_of(index * copies, copies), copies)

    def columns_of(index):
        return pl.ds(pl.multiple_of(index * channels, channels), channels)

    spread = []
    for kind, source in enumerate((input_hbm, forget_hbm, gate_hbm)):
        target = weights.at[kind, own_rows_of(mine), here]
        kept = pltpu.make_async_copy(
            source.at[:, :, columns_of(mine)], target, spread_own.at[kind]
        )
        sent = []
        for k in range(1, 8):
            there = group_member(copies, k)
            sent.append(
                pltpu.make_async_remote_copy(
                    src_ref=source.at[:, :, columns_of(lax.div(there, copies))],
                    dst_ref=target,
                    send_sem=spread_send.at[kind, k - 1],
                    recv_sem=spread_recv.at[kind, k - 1],
                    device_id={"dp": there},
                    device_id_type=pl.DeviceIdType.MESH,
                )
            )
        spread.append((kept, sent))

    def ring_copy(kind, k):
        at = beside(-k)
        target = project.at[:, at] if kind == 3 else weights.at[kind, :, at]
        source = out_hbm if kind == 3 and k == 0 else target
        return to_right(source, target, ring_send.at[kind, k], ring_recv.at[kind, k])

    def spread_arrive(kind):
        kept, sent = spread[kind]
        kept.wait()
        for copy in sent:
            copy.wait_recv()

    out_kept = pltpu.make_async_copy(out_hbm, project.at[:, here], spread_own.at[3])
    out_kept.start()
    for kept, sent in spread:
        kept.start()
        for copy in sent:
            copy.start()
    ring_copy(3, 0).start()
    begin, pass_first, pass_second, pass_last, arrive, finish = plane_gather_steps(
        copies, own_ref, normed, own_sem, gather_send, gather_recv
    )
    begin()
    spread_arrive(0)
    ring_copy(0, 0).start()
    spread_arrive(1)
    ring_copy(3, 0).wait_recv()
    ring_copy(1, 0).start()
    spread_arrive(2)
    pass_first()
    for k in range(parts - 2):
        ring_copy(0, k).wait_recv()
        ring_copy(0, k + 1).start()
        if k == 0:
            pass_second()
        ring_copy(1, k).wait_recv()
        ring_copy(1, k + 1).start()
    ring_copy(0, parts - 2).wait_recv()
    ring_copy(2, 0).start()
    pass_last()
    ring_copy(1, parts - 2).wait_recv()
    ring_copy(3, 1).start()
    arrive()

    many = 2

    def project_rows(kind, at):
        left = normed[pl.ds(at * many, many)].reshape(many * rows, width)
        return matmul(left, weights[kind].reshape(width, channels))

    def rows_at(at):
        return pl.ds(pl.multiple_of(at * many * rows, many * rows), many * rows)

    def strip_of(value, n):
        return value[:, n * lanes : (n + 1) * lanes]

    @pl.loop(0, seqs // many)
    def _(at):
        some = rows_at(at)
        value = project_rows(0, at)
        pre[0, some, :] = value
        inflow = live_ref[some, :] * silu_of(value)
        for n in range(strips):
            state[n, some, :] = strip_of(inflow, n)

    ring_copy(2, 0).wait_recv()
    ring_copy(2, 1).start()

    @pl.loop(0, seqs // many)
    def _(at):
        some = rows_at(at)
        squash = jax.nn.sigmoid(project_rows(1, at))
        bound = bound_ref[...]
        value = bound + (1.0 - bound) * squash
        for n in range(strips):
            squashed[n, some, :] = strip_of(squash, n)
            forget[n, some, :] = strip_of(value, n)
            state[n, some, :] = (1.0 - strip_of(value, n)) * state[n, some, :]

    ring_copy(3, 1).wait_recv()
    ring_copy(3, 2).start()

    def step(at, carry):
        some = pl.ds(at, seqs, stride=rows)
        following = []
        for n, (total, product) in enumerate(carry):
            keep = forget[n, some, :]
            total = keep * total + state[n, some, :]
            product = product * keep
            state[n, some, :] = total
            decay[n, some, :] = product
            following.append((total, product))
        return tuple(following)

    start = (jnp.zeros((seqs, lanes), f32), jnp.ones((seqs, lanes), f32))
    carry = lax.fori_loop(0, rows, step, (start,) * strips, unroll=8)
    for n, (total, product) in enumerate(carry):
        ends[here, 0, :, n * lanes : (n + 1) * lanes] = total
        ends[here, 1, :, n * lanes : (n + 1) * lanes] = product
    carries = []
    for k in range(1, parts):
        copy = pltpu.make_async_remote_copy(
            src_ref=ends.at[here],
            dst_ref=ends.at[here],
            send_sem=carry_send.at[k - 1],
            recv_sem=carry_recv.at[k - 1],
            device_id={"tensor": beside(k)},
            device_id_type=pl.DeviceIdType.MESH,
        )
        copy.start()
        carries.append(copy)
    ring_copy(2, 1).wait_recv()
    ring_copy(2, 2).start()
    for copy in carries:
        copy.wait_recv()
    coming = jnp.zeros((seqs, channels), f32)
    entered = coming
    for k in range(parts - 1):
        coming = ends[k, 1] * coming + ends[k, 0]
        entered = jnp.where(here == k + 1, coming, entered)
    for n in range(seqs):
        entering[n] = entered[n : n + 1]
    ring_copy(3, 2).wait_recv()
    ring_copy(2, 2).wait_recv()

    @pl.loop(0, seqs // many)
    def _(at):
        some = rows_at(at)
        value = project_rows(2, at)
        pre[1, some, :] = value
        act = silu_of(value)
        for n in range(many):
            slot = at * many + n
            one = pl.ds(pl.multiple_of(slot * rows, rows), rows)
            for strip in range(strips):
                columns = slice(strip * lanes, (strip + 1) * lanes)
                whole = state[strip, one, :] + (
                    decay[strip, one, :] * entering[slot, :, columns]
                )
                state[strip, one, :] = whole
                mixed[slot, :, columns] = (
                    whole * act[n * rows : (n + 1) * rows, columns]
                ).astype(bf16)

    out_kept.wait()
    stores = [
        pltpu.make_async_copy(source, target, out_sem.at[n])
        for n, (source, target) in enumerate(
            (
                (normed, normed_out),
                (weights, weights_out),
                (project, project_out),
                (pre, pre_out),
                (squashed, squash_out),
                (state, state_out),
                (entering, entering_out),
                (mixed, mixed_out),
            )
        )
    ]
    for store in stores:
        store.start()

    def out_product(slot, columns):
        right = project[:, :, :, columns]
        return matmul(mixed[slot], right.reshape(channels, right.shape[-1]))

    plane_scatter_kernel(
        copies, False, None, None, sum_ref, near_buf, one_buf, two_buf, part_buf, scatter_send,
        scatter_recv, masked_hbm, masked_out, masked_send, masked_recv, greeted=True,
        product=out_product,
    )
    finish()
    for kept, sent in spread:
        for copy in sent:
            copy.wait_send()
    for kind in range(4):
        for k in range(parts - 1):
            ring_copy(kind, k).wait_send()
    for copy in carries:
        copy.wait_send()
    for store in stores:
        store.wait()


def mixer_forward(
    normed, w_input, w_forget, w_gate, w_out, masked, bound, live, copies, collective
):
    parts = lax.axis_size("tensor")
    rows, width = normed.shape
    channels = width // 8
    own_rows = w_input.shape[1]
    somewhere = pl.BlockSpec(memory_space=pl.ANY)
    vmem = pl.BlockSpec(memory_space=pltpu.VMEM)
    wide = (8, rows, width)
    weights = (3, 8 * copies, parts, own_rows, channels)
    project = (copies, parts, own_rows, width)
    flat = (8 * rows, channels)
    lanes = min(128, channels)
    strips = (channels // lanes, 8 * rows, lanes)
    shaped = (8, rows, channels)
    half = rows // 2
    dma = pltpu.SemaphoreType.DMA
    return pl.pallas_call(
        functools.partial(mixer_forward_kernel, copies),
        out_shape=[
            jax.ShapeDtypeStruct(wide, bf16),
            jax.ShapeDtypeStruct(weights, bf16),
            jax.ShapeDtypeStruct(project, bf16),
            jax.ShapeDtypeStruct((2,) + flat, f32),
            jax.ShapeDtypeStruct(strips, f32),
            jax.ShapeDtypeStruct(strips, f32),
            jax.ShapeDtypeStruct((8, 1, channels), f32),
            jax.ShapeDtypeStruct(shaped, bf16),
            jax.ShapeDtypeStruct((parts - 2, rows, width), bf16),
            jax.ShapeDtypeStruct((rows, width), f32),
        ],
        in_specs=[somewhere] * 6 + [vmem] * 2,
        out_specs=[somewhere] * 9 + [vmem],
        scratch_shapes=[
            pltpu.VMEM(wide, bf16),
            pltpu.VMEM(weights, bf16),
            pltpu.VMEM(project, bf16),
            pltpu.VMEM((2,) + flat, f32),
            pltpu.VMEM(strips, f32),
            pltpu.VMEM(strips, f32),
            pltpu.VMEM(strips, f32),
            pltpu.VMEM(strips, f32),
            pltpu.VMEM((parts, 2, 8, channels), f32),
            pltpu.VMEM((8, 1, channels), f32),
            pltpu.VMEM(shaped, bf16),
            pltpu.VMEM((4, rows, width), bf16),
            pltpu.VMEM((3, half, width), bf16),
            pltpu.VMEM((3, half, width), bf16),
            pltpu.VMEM((4, rows, width), bf16),
            dma,
            dma((14,)),
            dma((14,)),
            dma((3, 7)),
            dma((3, 7)),
            dma((4,)),
            dma((4, parts - 1)),
            dma((4, parts - 1)),
            dma((parts - 1,)),
            dma((parts - 1,)),
            dma((10,)),
            dma((10,)),
            dma((parts - 2,)),
            dma((parts - 2,)),
            dma((8,)),
        ],
        compiler_params=pltpu.CompilerParams(
            collective_id=collective, has_side_effects=True, vmem_limit_bytes=56 * 1024 * 1024
        ),
        cost_estimate=pl.CostEstimate(
            flops=8 * rows * width * width,
            bytes_accessed=900 * rows * width,
            transcendentals=0,
        ),
    )(normed, w_input, w_forget, w_gate, w_out, masked, bound, live)


def mixer_backward_kernel(
    copies, masks,
    own_ref, normed_hbm, weights_hbm, project_hbm, pre_hbm, squash_hbm, state_hbm, mixed_hbm,
    unit_hbm, stream_hbm, entering_ref, bound_ref, live_ref, gain_ref, scale_ref, gain_two_ref,
    result_ref, weight_sums, project_sum, small_sums,
    rows_buf, weights, project, pre, squashed, state, mixed, unit, stream, drive, decay, ends,
    entered, grad_pre, grad_w, grad_project, ring_w, ring_project, bound_sum, whole_w, spread_w,
    small_recv, small_ring, near_buf, one_buf, two_buf, part_buf,
    load_sem, gather_send, gather_recv, carry_send, carry_recv, ring_send, ring_recv,
    scatter_send, scatter_recv, spread_send, spread_recv, spread_own, small_send, small_got,
):
    parts = lax.axis_size("tensor")
    here = lax.axis_index("tensor")
    seqs, rows, width = rows_buf.shape
    strips, _, lanes = drive.shape
    channels = strips * lanes
    own_rows = weights.shape[3]
    near, one, two = copies, 2 * copies, 4 * copies
    mine = slot_of(copies, ())
    greet_all(copies, masks)
    begin, pass_first, pass_second, pass_last, arrive, finish = plane_gather_steps(
        copies, own_ref, rows_buf, load_sem.at[0], gather_send, gather_recv
    )
    begin()
    loads = [
        pltpu.make_async_copy(source, target, load_sem.at[n + 1])
        for n, (source, target) in enumerate(
            (
                (project_hbm, project),
                (pre_hbm, pre),
                (state_hbm, state),
                (mixed_hbm, mixed),
                (squash_hbm, squashed),
                (weights_hbm, weights),
                (unit_hbm, unit),
                (stream_hbm, stream),
            )
        )
    ]
    for load in loads:
        load.start()
    for load in loads[:3]:
        load.wait()

    def slot_rows(slot):
        return pl.ds(pl.multiple_of(slot * rows, rows), rows)

    def take(slot):
        some = slot_rows(slot)
        grad_mixed = matmul_rt(rows_buf[slot], project[...].reshape(channels, width))
        gate = pre[1, some, :]
        squash = jax.nn.sigmoid(gate)
        act = gate * squash
        slope = squash * (1.0 + gate * (1.0 - squash))
        for n in range(strips):
            columns = slice(n * lanes, (n + 1) * lanes)
            part = grad_mixed[:, columns]
            drive[n, some, :] = part * act[:, columns]
            at = 2 * channels + n * lanes
            grad_pre[slot, :, at : at + lanes] = (
                part * state[n, some, :] * slope[:, columns]
            ).astype(bf16)

    pass_first()
    pass_second()
    arrive(slice(0, 6))
    pltpu.make_async_copy(own_ref, rows_buf.at[mine], load_sem.at[0]).wait()
    for flips in ((), (near,), (one,), (two,), (near, one), (near, two)):
        take(slot_of(copies, flips))
    pass_last()
    take(slot_of(copies, (one, two)))
    arrive(slice(6, 8))
    take(slot_of(copies, (near, one, two)))

    tile = min(512, width)
    loads[3].wait()

    @pl.loop(0, width // tile)
    def _(k):
        columns = pl.ds(pl.multiple_of(k * tile, tile), tile)
        value = matmul_lt(
            mixed[...].reshape(seqs * rows, channels),
            rows_buf[:, :, columns].reshape(seqs * rows, tile),
        )
        grad_project[:, :, :, columns] = value.astype(bf16).reshape(
            copies, parts, own_rows, tile
        )

    def ring_copy(kind, k):
        at = beside(-(k + 1))
        if kind == 3:
            source, target = grad_project.at[:, at], ring_project.at[k]
        else:
            source, target = grad_w.at[kind, :, at], ring_w.at[kind, k]
        return to_right(source, target, ring_send.at[kind, k], ring_recv.at[kind, k])

    def advance(kind, k):
        ring_copy(kind, k).wait_recv()
        at = beside(-(k + 2))
        if kind == 3:
            total = grad_project[:, at].astype(f32) + ring_project[k].astype(f32)
        else:
            total = grad_w[kind, :, at].astype(f32) + ring_w[kind, k].astype(f32)
        if k + 1 < parts - 1:
            if kind == 3:
                grad_project[:, at] = total.astype(bf16)
            else:
                grad_w[kind, :, at] = total.astype(bf16)
            ring_copy(kind, k + 1).start()
        elif kind == 3:
            project_sum[...] = total
        else:
            whole_w[kind] = total.astype(bf16)
            for copy in spread_copies(kind):
                copy.start()

    def spread_copies(kind, own=True):
        found = []
        for k in range(1, 8):
            there = group_member(copies, k)
            source = pl.ds(pl.multiple_of(lax.div(there, copies) * copies, copies), copies)
            found.append(
                pltpu.make_async_remote_copy(
                    src_ref=whole_w.at[kind, source],
                    dst_ref=spread_w.at[kind, mine],
                    send_sem=spread_send.at[kind, k - 1],
                    recv_sem=spread_recv.at[kind, k - 1],
                    device_id={"dp": there},
                    device_id_type=pl.DeviceIdType.MESH,
                )
            )
        if own:
            source = pl.ds(pl.multiple_of(mine * copies, copies), copies)
            found.append(
                pltpu.make_async_copy(
                    whole_w.at[kind, source], spread_w.at[kind, mine], spread_own.at[kind]
                )
            )
        return found

    ring_copy(3, 0).start()
    finish()
    normed_load = pltpu.make_async_copy(normed_hbm, rows_buf, load_sem.at[0])
    normed_load.start()
    loads[4].wait()

    def step(k, carry):
        some = pl.ds(rows - 1 - k, seqs, stride=rows)
        following = []
        for n, (coming, product) in enumerate(carry):
            bound = bound_ref[:, n * lanes : (n + 1) * lanes]
            keep = bound + (1.0 - bound) * squashed[n, some, :]
            carried = drive[n, some, :] + coming
            drive[n, some, :] = carried
            decay[n, some, :] = product
            following.append((keep * carried, product * keep))
        return tuple(following)

    start = (jnp.zeros((seqs, lanes), f32), jnp.ones((seqs, lanes), f32))
    carry = lax.fori_loop(0, rows, step, (start,) * strips, unroll=8)
    for n, (coming, product) in enumerate(carry):
        ends[here, 0, :, n * lanes : (n + 1) * lanes] = coming
        ends[here, 1, :, n * lanes : (n + 1) * lanes] = product
    carries = []
    for k in range(1, parts):
        copy = pltpu.make_async_remote_copy(
            src_ref=ends.at[here],
            dst_ref=ends.at[here],
            send_sem=carry_send.at[k - 1],
            recv_sem=carry_recv.at[k - 1],
            device_id={"tensor": beside(k)},
            device_id_type=pl.DeviceIdType.MESH,
        )
        copy.start()
        carries.append(copy)
    normed_load.wait()

    def weight_grad(kind):
        @pl.loop(0, width // tile)
        def _(k):
            columns = pl.ds(pl.multiple_of(k * tile, tile), tile)
            value = matmul_lt(
                grad_pre[:, :, kind * channels : (kind + 1) * channels].reshape(
                    seqs * rows, channels
                ),
                rows_buf[:, :, columns].reshape(seqs * rows, tile),
            )
            count = tile // (parts * own_rows)
            grad_w[kind, pl.ds(k * count, count)] = value.T.astype(bf16).reshape(
                count, parts, own_rows, channels
            )

        ring_copy(kind, 0).start()

    advance(3, 0)
    weight_grad(2)
    for copy in carries:
        copy.wait_recv()
    coming = jnp.zeros((seqs, channels), f32)
    arrived = coming
    for k in range(parts - 1, 0, -1):
        coming = ends[k, 1] * coming + ends[k, 0]
        arrived = jnp.where(here == k - 1, coming, arrived)
    for n in range(seqs):
        entered[n] = arrived[n : n + 1]
    bound_sum[...] = jnp.zeros_like(bound_sum)
    first_row = lax.broadcasted_iota(jnp.int32, (rows, lanes), 0) == 0

    @pl.loop(0, seqs)
    def _(slot):
        some = slot_rows(slot)
        alive = live_ref[some, :]
        for n in range(strips):
            columns = slice(n * lanes, (n + 1) * lanes)
            bound = bound_ref[:, columns]
            squash = squashed[n, some, :]
            keep = bound + (1.0 - bound) * squash
            carried = drive[n, some, :] + decay[n, some, :] * entered[slot, :, columns]
            prior = jnp.where(
                first_row, entering_ref[slot, :, columns], pltpu.roll(state[n, some, :], 1, 0)
            )
            value = pre[0, some, columns]
            gate = jax.nn.sigmoid(value)
            slope = gate * (1.0 + value * (1.0 - gate))
            grad_forget = carried * prior - carried * alive * value * gate
            at = n * lanes
            grad_pre[slot, :, at : at + lanes] = (
                carried * alive * (1.0 - keep) * slope
            ).astype(bf16)
            at = channels + n * lanes
            grad_pre[slot, :, at : at + lanes] = (
                grad_forget * (1.0 - bound) * squash * (1.0 - squash)
            ).astype(bf16)
            bound_sum[:, columns] += jnp.sum(
                grad_forget * (1.0 - squash), axis=0, keepdims=True
            )

    advance(3, 1)
    weight_grad(0)
    advance(2, 0)
    weight_grad(1)
    loads[5].wait()

    def normed_product(slot, columns):
        at = lax.div(columns.start, parts * own_rows)
        count = tile // (parts * own_rows)
        total = None
        for kind in range(3):
            part = matmul_rt(
                grad_pre[slot, :, kind * channels : (kind + 1) * channels],
                weights[kind, pl.ds(at, count)].reshape(tile, channels),
            )
            total = part if total is None else total + part
        return total

    def between(point):
        if point == "sent":
            advance(3, 2)
            advance(2, 1)
        elif point == "added":
            advance(0, 0)
            advance(2, 2)
        elif point == "top":
            advance(1, 0)
        elif point == "low":
            advance(0, 1)
            advance(1, 1)

    plane_scatter_kernel(
        copies, True, None, None, result_ref, near_buf, one_buf, two_buf, part_buf, scatter_send,
        scatter_recv, greeted=True, product=normed_product, between=between,
    )

    for load in loads[6:]:
        load.wait()
    small_sums[...] = jnp.zeros_like(small_sums)
    small_sums[1:2, :] = gain_two_ref[...]
    small_sums[2:3, pl.ds(pl.multiple_of(mine * channels, channels), channels)] = bound_sum[...]
    some_rows = min(64, rows)

    @pl.loop(0, rows // some_rows)
    def _(k):
        some = pl.ds(pl.multiple_of(k * some_rows, some_rows), some_rows)
        grad_norm = result_ref[some, :]
        units = unit[some, :]
        small_sums[0:1, :] += jnp.sum(grad_norm * units, axis=0, keepdims=True)
        scaled = grad_norm * gain_ref[...]
        mean = jnp.mean(scaled * units, axis=-1, keepdims=True)
        result_ref[some, :] = stream[some, :] + scale_ref[some, :] * (scaled - units * mean)

    def small_copy(n):
        return pltpu.make_async_remote_copy(
            src_ref=small_sums,
            dst_ref=small_recv.at[n],
            send_sem=small_send.at[n],
            recv_sem=small_got.at[n],
            device_id={"dp": partner(masks[n])},
            device_id_type=pl.DeviceIdType.MESH,
        )

    def small_step(n):
        small_copy(n).wait()
        small_sums[...] += small_recv[n]

    small_copy(0).start()
    advance(0, 2)
    advance(1, 2)
    for n in range(len(masks)):
        small_step(n)
        if n + 1 < len(masks):
            small_copy(n + 1).start()
    ring_small = []
    for k in range(1, parts):
        copy = pltpu.make_async_remote_copy(
            src_ref=small_sums,
            dst_ref=small_ring.at[k - 1],
            send_sem=small_send.at[len(masks) + k - 1],
            recv_sem=small_got.at[len(masks) + k - 1],
            device_id={"tensor": beside(k)},
            device_id_type=pl.DeviceIdType.MESH,
        )
        copy.start()
        ring_small.append(copy)
    for kind in (2, 0, 1):
        spread = spread_copies(kind)
        for copy in spread[:-1]:
            copy.wait_recv()
        spread[-1].wait()
        for slot in range(8):
            weight_sums[kind, :, :, slot * channels : (slot + 1) * channels] = spread_w[
                kind, slot
            ].astype(f32)
    for copy in ring_small:
        copy.wait()
    for k in range(parts - 1):
        small_sums[...] += small_ring[k]
    for kind in range(4):
        for k in range(parts - 1):
            ring_copy(kind, k).wait_send()
    for kind in range(3):
        for copy in spread_copies(kind, False):
            copy.wait_send()
    for copy in carries:
        copy.wait_send()


def mixer_backward(
    own, normed, weights, project, pre, squashed, state, mixed, unit, stream, entering, bound,
    live, gain, scale, gain_two, copies, masks, collective,
):
    parts = lax.axis_size("tensor")
    _, rows, width = normed.shape
    channels = width // 8
    own_rows = project.shape[2]
    somewhere = pl.BlockSpec(memory_space=pl.ANY)
    vmem = pl.BlockSpec(memory_space=pltpu.VMEM)
    half = rows // 2
    dma = pltpu.SemaphoreType.DMA
    blocks = (8 * copies, own_rows, channels)
    small = pltpu.VMEM((len(masks), 8, width), f32)
    return pl.pallas_call(
        functools.partial(mixer_backward_kernel, copies, masks),
        out_shape=[
            jax.ShapeDtypeStruct((rows, width), f32),
            jax.ShapeDtypeStruct((3, copies, own_rows, width), f32),
            jax.ShapeDtypeStruct((copies, own_rows, width), f32),
            jax.ShapeDtypeStruct((8, width), f32),
        ],
        in_specs=[somewhere] * 10 + [vmem] * 6,
        out_specs=[vmem] * 4,
        scratch_shapes=[
            pltpu.VMEM(normed.shape, bf16),
            pltpu.VMEM(weights.shape, bf16),
            pltpu.VMEM(project.shape, bf16),
            pltpu.VMEM(pre.shape, f32),
            pltpu.VMEM(squashed.shape, f32),
            pltpu.VMEM(state.shape, f32),
            pltpu.VMEM(mixed.shape, bf16),
            pltpu.VMEM((rows, width), f32),
            pltpu.VMEM((rows, width), f32),
            pltpu.VMEM(state.shape, f32),
            pltpu.VMEM(state.shape, f32),
            pltpu.VMEM((parts, 2, 8, channels), f32),
            pltpu.VMEM((8, 1, channels), f32),
            pltpu.VMEM((8, rows, 3 * channels), bf16),
            pltpu.VMEM(weights.shape, bf16),
            pltpu.VMEM(project.shape, bf16),
            pltpu.VMEM((3, parts - 1) + blocks, bf16),
            pltpu.VMEM((parts - 1, copies, own_rows, width), bf16),
            pltpu.VMEM((1, channels), f32),
            pltpu.VMEM((3,) + blocks, bf16),
            pltpu.VMEM((3, 8, copies, own_rows, channels), bf16),
            small,
            pltpu.VMEM((parts - 1, 8, width), f32),
            pltpu.VMEM((4, rows, width), bf16),
            pltpu.VMEM((3, half, width), bf16),
            pltpu.VMEM((3, half, width), bf16),
            pltpu.VMEM((4, rows, width), bf16),
            dma((9,)),
            dma((14,)),
            dma((14,)),
            dma((parts - 1,)),
            dma((parts - 1,)),
            dma((4, parts - 1)),
            dma((4, parts - 1)),
            dma((10,)),
            dma((10,)),
            dma((3, 7)),
            dma((3, 7)),
            dma((3,)),
            dma((len(masks) + parts - 1,)),
            dma((len(masks) + parts - 1,)),
        ],
        compiler_params=pltpu.CompilerParams(
            collective_id=collective, has_side_effects=True, vmem_limit_bytes=62 * 1024 * 1024
        ),
        cost_estimate=pl.CostEstimate(
            flops=16 * rows * width * width,
            bytes_accessed=900 * rows * width,
            transcendentals=0,
        ),
    )(
        own, normed, weights, project, pre, squashed, state, mixed, unit, stream, entering, bound,
        live, gain, scale, gain_two,
    )


def on_device(
    inputs,
    lengths,
    gain_mix,
    gain_glu,
    lower_bound,
    w_input,
    w_forget,
    w_gate_mix,
    w_out,
    w_gate,
    w_up,
    w_down,
    cotangent,
):
    tensor_parts = lax.axis_size("tensor")
    data_parts = lax.axis_size("dp")
    tensor_index = lax.axis_index("tensor")
    data_index = lax.axis_index("dp")
    rows_here, width = inputs.shape
    group = min(8, data_parts)
    copies = data_parts // group
    group_index = lax.div(data_index, copies)
    copy_index = lax.rem(data_index, copies)
    group_masks = [copies << k for k in range(group.bit_length() - 1)]
    copy_masks = [1 << k for k in range(copies.bit_length() - 1)]
    all_masks = [1 << k for k in range(data_parts.bit_length() - 1)]
    group_lists = [[g * copies + o for g in range(group)] for o in range(copies)]
    channels = width // group
    own_rows = w_input.shape[0]

    high = lax.div(lengths, 32).astype(bf16)
    low = lax.rem(lengths, 32).astype(bf16)
    length_row = jnp.concatenate([high, low, jnp.zeros((own_rows - 2,), bf16)])
    small = jnp.stack([gain_mix, gain_glu, lower_bound, length_row])
    small = in_order(shifted_blocks(small))
    small = gather_bits(small, sorted(all_masks, reverse=True)).astype(f32)
    small = small.reshape((data_parts * tensor_parts,) + small.shape[2:])
    gain_one = small[:, 0].reshape(width)
    gain_two = small[:, 1].reshape(width)
    bound = lax.dynamic_slice_in_dim(small[:, 2].reshape(width), group_index * channels, channels)
    every_length = small[:, 3].reshape(data_parts, tensor_parts, own_rows)[:, 0, :2]
    every_length = (every_length[:, 0] * 32.0 + every_length[:, 1]).astype(jnp.int32)
    group_lengths = lax.dynamic_index_in_dim(
        every_length.reshape(group, copies), copy_index, axis=1, keepdims=False
    )
    position = tensor_index * rows_here + jnp.arange(rows_here, dtype=jnp.int32)
    live_own = (position < lengths[0]).astype(f32)[:, None]
    live = (position[None, :] < group_lengths[:, None]).astype(f32)
    live = live.reshape(group * rows_here, 1)

    mixer_weights = [w_input, w_forget, w_gate_mix, w_out]
    if copies > 1:
        mixer_weights = [gather_bits(weight, copy_masks[::-1]) for weight in mixer_weights]
    mixer_weights = [weight.reshape(copies, own_rows, width) for weight in mixer_weights]

    masked_grad = live_own * cotangent
    masked_own = masked_grad.astype(bf16)
    masked_first = ring(masked_own)

    scale_one, unit_one = norm_rows(inputs)
    rows_all = group * rows_here
    *mixer_kept, mixed, masked_others, mixed_sum = (
        mixer_forward(
            (unit_one * gain_one).astype(bf16),
            *mixer_weights,
            masked_first,
            bound[None, :],
            live,
            copies,
            1,
        )
    )
    stream = inputs + mixed_sum

    first, second = orders(all_masks)
    hidden_here = w_gate.shape[1]
    gate_w, up_w, down_w = (
        lax.all_gather(weight, "dp", axis=0, tiled=True) for weight in (w_gate, w_up, w_down.T)
    )

    scale_two, unit_two = norm_rows(stream)
    normed_two = (unit_two * gain_two).astype(bf16)
    out_rows, grad_norm_two, *weight_sums = swiglu(
        normed_two, masked_own, masked_first, masked_others, gate_w, up_w, down_w, copies, 4
    )
    if copies > 1:
        weight_sums = [
            scatter_bits(total.reshape(copies, width // data_parts, hidden_here), copy_masks, f32)
            for total in weight_sums
        ]
    grad_gate_mine, grad_up_mine, grad_down_mine = weight_sums
    grad_down_mine = grad_down_mine.T

    out_rows = out_rows.reshape(tensor_parts * rows_here, width)
    out_sum = lax.psum_scatter(out_rows, "tensor", scatter_dimension=0, tiled=True)

    gain_two_part = jnp.sum(grad_norm_two * unit_two, axis=0)
    grad_stream = masked_grad + norm_back(grad_norm_two, unit_two, scale_two, gain_two)

    normed_one, mixer_w, out_w, pre, squashed, state, entering = mixer_kept
    grad_inputs, mixer_sums, out_w_sum, small_sums = mixer_backward(
        grad_stream.astype(bf16),
        normed_one,
        mixer_w,
        out_w,
        pre,
        squashed,
        state,
        mixed,
        unit_one,
        grad_stream,
        entering,
        bound[None, :],
        live,
        gain_one[None, :],
        scale_one,
        gain_two_part[None, :],
        copies,
        all_masks,
        3,
    )
    output = live_own * (stream + after(out_sum, small_sums).astype(f32))
    grad_weights = [mixer_sums[0], mixer_sums[1], mixer_sums[2], out_w_sum]
    if copies > 1:
        grad_weights = [scatter_bits(total, copy_masks, f32) for total in grad_weights]
    grad_weights = [total.reshape(own_rows, width) for total in grad_weights]
    place = (data_index * tensor_parts + tensor_index) * own_rows
    small_own = lax.dynamic_slice(small_sums, (0, place), (3, own_rows))
    return (
        output,
        grad_inputs,
        small_own[0],
        small_own[1],
        small_own[2],
        *grad_weights,
        grad_gate_mine,
        grad_up_mine,
        grad_down_mine,
    )


def solution(mesh):
    both = ("dp", "tensor")
    placed = (
        P(both, None),
        P("dp"),
        P(both),
        P(both),
        P(both),
        P(both, None),
        P(both, None),
        P(both, None),
        P(both, None),
        P("dp", "tensor"),
        P("dp", "tensor"),
        P("tensor", "dp"),
        P(both, None),
    )
    return jax.shard_map(
        on_device,
        mesh=mesh,
        in_specs=placed,
        out_specs=(
            P(both, None),
            P(both, None),
            P(both),
            P(both),
            P(both),
            P(both, None),
            P(both, None),
            P(both, None),
            P(both, None),
            P("dp", "tensor"),
            P("dp", "tensor"),
            P("tensor", "dp"),
        ),
        check_vma=False,
    )
```

```python
import functools

import jax
import jax.numpy as jnp
from jax import lax
from jax.experimental import pallas as pl
from jax.experimental.pallas import tpu as pltpu
from jax.sharding import PartitionSpec as P

epsilon = 1e-06
bf16 = jnp.bfloat16
f32 = jnp.float32


def matmul(left, right):
    return jnp.dot(left, right, preferred_element_type=f32)


def matmul_rt(left, right):
    return lax.dot_general(left, right, (((1,), (1,)), ((), ())), preferred_element_type=f32)


def matmul_lt(left, right):
    return lax.dot_general(left, right, (((0,), (0,)), ((), ())), preferred_element_type=f32)


def silu_of(value):
    return value * jax.nn.sigmoid(value)


def silu_slope(value):
    squash = jax.nn.sigmoid(value)
    return squash * (1.0 + value * (1.0 - squash))


def norm_rows(value):
    scale = lax.rsqrt(jnp.mean(value * value, axis=-1, keepdims=True) + epsilon)
    return (scale, value * scale)


def norm_back(grad_norm, unit, scale, gain):
    scaled = grad_norm * gain
    return scale * (scaled - unit * jnp.mean(scaled * unit, axis=-1, keepdims=True))


def untouched_kernel(*refs):
    pass


def after(value, *others):
    somewhere = pl.BlockSpec(memory_space=pl.ANY)
    return pl.pallas_call(
        untouched_kernel,
        out_shape=jax.ShapeDtypeStruct(value.shape, value.dtype),
        in_specs=[somewhere] * (1 + len(others)),
        out_specs=somewhere,
        input_output_aliases={0: 0},
        cost_estimate=pl.CostEstimate(flops=0, bytes_accessed=0, transcendentals=0),
    )(value, *others)


def swap(value, mask):
    return lax.ppermute(value, "dp", [(i, i ^ mask) for i in range(lax.axis_size("dp"))])


def own_bit(mask):
    return lax.rem(lax.div(lax.axis_index("dp"), mask), 2)


def gather_bits(value, order):
    base = value.shape
    done = []
    for mask in order:
        other = swap(value, mask)
        at = sum(1 for seen in done if seen > mask)
        low = jnp.stack([value, other], axis=at)
        high = jnp.stack([other, value], axis=at)
        value = jnp.where(own_bit(mask) == 0, low, high)
        done.append(mask)
    return value.reshape((1 << len(order),) + base)


def scatter_bits(value, order, sent=bf16, hold=(None, None)):
    count = len(order)
    value = value.reshape((2,) * count + value.shape[1:])
    left = sorted(order, reverse=True)
    for mask in order:
        at = left.index(mask)
        left.remove(mask)
        bit = own_bit(mask)
        send = lax.dynamic_index_in_dim(value, 1 - bit, at, keepdims=False).astype(sent)
        keep = lax.dynamic_index_in_dim(value, bit, at, keepdims=False)
        if hold[0] == count - len(left) - 1:
            send = after(send, hold[1])
        total = keep.astype(f32) + swap(send, mask).astype(f32)
        value = total.astype(sent) if left else total
    return value


def orders(masks):
    down = sorted(masks, reverse=True)
    if len(down) < 3:
        return down, down
    return down, [down[1], down[0]] + down[2:]


def gather_halves(value, masks):
    first, second = orders(masks)
    half = value.shape[-1] // 2
    return gather_bits(value[..., :half], first), gather_bits(value[..., half:], second)


def scatter_halves(left, right, masks):
    first, second = orders(masks)
    return jnp.concatenate(
        [scatter_bits(left, first[::-1]), scatter_bits(right, second[::-1])], axis=-1
    )


def ring(value):
    parts = lax.axis_size("tensor")
    return lax.ppermute(value, "tensor", [(i, (i + 1) % parts) for i in range(parts)])


def ring_blocks(value):
    blocks = [value]
    for _ in range(lax.axis_size("tensor") - 1):
        blocks.append(ring(blocks[-1]))
    return blocks


def ring_scatter(blocks):
    total = blocks[1 % len(blocks)]
    totals = [total]
    for k in range(2, len(blocks) + 1):
        moved = ring(total).astype(f32)
        total = moved + blocks[k % len(blocks)].astype(f32)
        if k < len(blocks):
            total = total.astype(bf16)
            totals.append(total)
    return total, totals


def shifted_blocks(value):
    parts = lax.axis_size("tensor")
    blocks = [value]
    for k in range(1, parts):
        blocks.append(lax.ppermute(value, "tensor", [(i, (i + k) % parts) for i in range(parts)]))
    return blocks


def scatter_straight(value):
    here = lax.axis_index("tensor")
    parts = lax.axis_size("tensor")
    total = lax.dynamic_index_in_dim(value, here, 0, keepdims=False)
    for k in range(1, parts):
        send = lax.dynamic_index_in_dim(value, lax.rem(here + k, parts), 0, keepdims=False)
        total += lax.ppermute(send, "tensor", [(i, (i + k) % parts) for i in range(parts)])
    return total


def in_order(blocks):
    here = lax.axis_index("tensor")
    parts = len(blocks)
    stacked = jnp.stack(blocks[::-1] + blocks[::-1])
    return lax.dynamic_slice_in_dim(stacked, parts - 1 - here, parts, 0)


def partner(mask):
    me = lax.axis_index("dp")
    return me + mask * (1 - 2 * lax.rem(lax.div(me, mask), 2))


def greet(masks, ring_too=False):
    barrier = pltpu.get_barrier_semaphore()
    others = [{"dp": partner(mask)} for mask in masks]
    if ring_too:
        others += [{"tensor": beside(1)}, {"tensor": beside(-1)}]
    for other in others:
        pl.semaphore_signal(
            barrier, inc=1, device_id=other, device_id_type=pl.DeviceIdType.MESH
        )
    pl.semaphore_wait(barrier, len(others))


def beside(step):
    parts = lax.axis_size("tensor")
    return lax.rem(lax.axis_index("tensor") + step + parts, parts)


def slot_of(copies, masks):
    me = lax.axis_index("dp")
    for mask in masks:
        me = me + mask * (1 - 2 * lax.rem(lax.div(me, mask), 2))
    return lax.div(me, copies)


def to_right(source, target, send_sem, recv_sem):
    return pltpu.make_async_remote_copy(
        src_ref=source,
        dst_ref=target,
        send_sem=send_sem,
        recv_sem=recv_sem,
        device_id={"tensor": beside(1)},
        device_id_type=pl.DeviceIdType.MESH,
    )


def along(step, source, target, send_sem, recv_sem):
    return pltpu.make_async_remote_copy(
        src_ref=source,
        dst_ref=target,
        send_sem=send_sem,
        recv_sem=recv_sem,
        device_id={"tensor": beside(step)},
        device_id_type=pl.DeviceIdType.MESH,
    )


def plane_gather_steps(copies, value_ref, all_ref, own_sem, send_sem, recv_sem):
    near, one, two = copies, 2 * copies, 4 * copies
    half = value_ref.shape[0] // 2
    top, low = pl.ds(0, half), pl.ds(half, half)
    mine = slot_of(copies, ())
    at_one, at_two = slot_of(copies, (one,)), slot_of(copies, (two,))
    at_both = slot_of(copies, (one, two))
    local = pltpu.make_async_copy(value_ref, all_ref.at[mine], own_sem)
    sent = []
    last = []

    def send(source, slot, rows, mask):
        index = len(sent)
        copy = pltpu.make_async_remote_copy(
            src_ref=source,
            dst_ref=all_ref.at[slot, rows],
            send_sem=send_sem.at[index],
            recv_sem=recv_sem.at[index],
            device_id={"dp": partner(mask)},
            device_id_type=pl.DeviceIdType.MESH,
        )
        copy.start()
        sent.append(copy)
        if mask == near:
            last.append(copy)
        return copy

    def forward(slot, rows, mask):
        return send(all_ref.at[slot, rows], slot, rows, mask)

    first = []
    second = []

    def begin():
        local.start()
        first.append(send(value_ref.at[top], mine, top, two))
        first.append(send(value_ref.at[low], mine, low, one))
        first.append(send(value_ref.at[low], mine, low, two))
        first.append(send(value_ref.at[top], mine, top, one))
        send(value_ref.at[top], mine, top, near)
        send(value_ref.at[low], mine, low, near)

    def pass_first():
        first[0].wait_recv()
        second.append(forward(at_two, top, one))
        forward(at_two, top, near)
        first[1].wait_recv()
        second.append(forward(at_one, low, two))
        forward(at_one, low, near)

    def pass_second():
        first[2].wait_recv()
        forward(at_two, low, near)
        first[3].wait_recv()
        forward(at_one, top, near)

    def pass_last():
        second[0].wait_recv()
        forward(at_both, top, near)
        second[1].wait_recv()
        forward(at_both, low, near)

    def arrive(some=slice(None)):
        for copy in last[some]:
            copy.wait_recv()
        if some == slice(None):
            local.wait()

    def finish():
        for copy in sent:
            copy.wait_send()

    return begin, pass_first, pass_second, pass_last, arrive, finish


def plane_scatter_steps(
    copies, sum_ref, near_ref, one_ref, two_ref, part_ref,
    send_sem, recv_sem, product, between,
):
    near, one, two = copies, 2 * copies, 4 * copies
    rows, width = sum_ref.shape
    half = rows // 2
    top, low = pl.ds(0, half), pl.ds(half, half)
    tile = min(512, width)
    flips = [(), (one,), (two,), (one, two)]
    copies_out = []

    def send(source, target, mask):
        index = len(copies_out)
        copy = pltpu.make_async_remote_copy(
            src_ref=source,
            dst_ref=target,
            send_sem=send_sem.at[index],
            recv_sem=recv_sem.at[index],
            device_id={"dp": partner(mask)},
            device_id_type=pl.DeviceIdType.MESH,
        )
        copy.start()
        copies_out.append(copy)
        return copy

    def each_tile(body):
        @pl.loop(0, width // tile)
        def _(k):
            body(pl.ds(pl.multiple_of(k * tile, tile), tile))

    arriving = {}
    for k in (3, 1, 2, 0):
        slot = slot_of(copies, flips[k] + (near,))

        def theirs(columns, k=k, slot=slot):
            part_ref[k, :, columns] = product(slot, columns).astype(bf16)

        each_tile(theirs)
        arriving[k] = send(part_ref.at[k], near_ref.at[k], near)

    between("sent")

    def added(k):
        slot = slot_of(copies, flips[k])
        arriving[k].wait_recv()

        def mine(columns):
            total = product(slot, columns) + near_ref[k, :, columns].astype(f32)
            if k == 0:
                sum_ref[:, columns] = total
            else:
                near_ref[k, :, columns] = total.astype(bf16)

        each_tile(mine)

    added(3)
    one_first = send(near_ref.at[3, top], one_ref.at[0], one)
    two_first = send(near_ref.at[3, low], two_ref.at[0], two)
    added(1)
    one_second = send(near_ref.at[1, top], one_ref.at[1], one)
    added(2)
    two_second = send(near_ref.at[2, low], two_ref.at[1], two)
    added(0)
    between("added")

    one_first.wait_recv()

    def pass_top(columns):
        total = near_ref[2, top, columns].astype(f32) + one_ref[0, :, columns].astype(f32)
        near_ref[2, top, columns] = total.astype(bf16)

    each_tile(pass_top)
    two_last = send(near_ref.at[2, top], two_ref.at[2], two)
    between("top")
    two_first.wait_recv()

    def pass_low(columns):
        total = near_ref[1, low, columns].astype(f32) + two_ref[0, :, columns].astype(f32)
        near_ref[1, low, columns] = total.astype(bf16)

    each_tile(pass_low)
    one_last = send(near_ref.at[1, low], one_ref.at[2], one)
    between("low")

    def finish(rows_at, first, at_first, second, at_second):
        def body(columns):
            sum_ref[rows_at, columns] += (
                first[at_first, :, columns].astype(f32) + second[at_second, :, columns].astype(f32)
            )

        each_tile(body)

    one_second.wait_recv()
    two_last.wait_recv()
    finish(top, one_ref, 1, two_ref, 2)
    two_second.wait_recv()
    one_last.wait_recv()
    finish(low, two_ref, 1, one_ref, 2)
    for copy in copies_out:
        copy.wait_send()


def column_tiles(width, most=512):
    return [(at, min(most, width - at)) for at in range(0, width, most)]


def swiglu_kernel(
    copies,
    normed_ref, own_ref, first_ref, others_ref, gate_hbm, up_hbm, down_ref,
    rows_out, moved_out, norm_sum, gate_sum, up_sum, down_sum,
    normed, masked, gate_w, up_w, down_w, hidden, gate_low, up_low, back, rows, ring_buf,
    one_buf, two_buf, lead, lead_near, in_sem, out_sem, gather_send, gather_recv, send_sem,
    recv_sem, sum_send, sum_recv, near_send, near_recv, one_send, one_recv, two_send, two_recv,
    ready_sem, moved_send, moved_recv,
):
    parts = lax.axis_size("tensor")
    near, one, two = copies, 2 * copies, 4 * copies
    greet((near, one, two), True)
    own = pltpu.make_async_copy(normed_ref, normed.at[0], in_sem.at[0])
    own.start()
    gather = plane_gather_steps(
        copies, down_ref, down_w, in_sem.at[4], gather_send, gather_recv
    )
    gather[0]()
    loads = [
        pltpu.make_async_copy(gate_hbm, gate_w, in_sem.at[1]),
        pltpu.make_async_copy(up_hbm, up_w, in_sem.at[2]),
        pltpu.make_async_copy(own_ref, masked.at[0], in_sem.at[3]),
        pltpu.make_async_copy(first_ref, masked.at[1], in_sem.at[5]),
        pltpu.make_async_copy(others_ref, masked.at[pl.ds(2, parts - 2)], in_sem.at[6]),
    ]
    own.wait()
    for load in loads:
        load.start()
    _, block_rows, width = normed.shape
    hidden_width = hidden.shape[2]
    share = width // 8
    half = share // 2
    many = 2
    tile = many * share
    both = [pl.ds(n * (block_rows // 2), block_rows // 2) for n in range(2)]

    def hop(k, n):
        return to_right(
            normed.at[k, both[n]], normed.at[k + 1, both[n]], send_sem.at[k, n], recv_sem.at[k, n]
        )

    def sum_hop(k, n):
        return to_right(
            back.at[k + 1, both[n]], ring_buf.at[k, both[n]], sum_send.at[k, n], sum_recv.at[k, n]
        )

    for n in range(2):
        hop(0, n).start()
    for load in loads:
        load.wait()
    gather[1]()
    gather[2]()
    for n in range(2):
        hop(0, n).wait_recv()
        hop(1, n).start()
    gather[3]()
    gather[4]()

    def store(k):
        home = lax.rem(lax.axis_index("tensor") + parts - k, parts)
        slot = lax.rem(k, 2)
        return pltpu.make_async_copy(rows.at[slot], rows_out.at[home], out_sem.at[slot])

    def front(k):
        for at, size in column_tiles(hidden_width):
            columns = pl.ds(at, size)

            def weight(ref):
                return ref[:, :, columns].reshape(width, size)

            glu_gate = matmul(normed[k], weight(gate_w))
            glu_up = matmul(normed[k], weight(up_w))
            grad_hidden = matmul(masked[k], weight(down_w))
            squash = jax.nn.sigmoid(glu_gate)
            act = glu_gate * squash
            slope = squash * (1.0 + glu_gate * (1.0 - squash))
            hidden[k, :, columns] = (act * glu_up).astype(bf16)
            gate_low[k, :, columns] = (grad_hidden * glu_up * slope).astype(bf16)
            up_low[k, :, columns] = (grad_hidden * act).astype(bf16)

    def rear(k):
        slot = lax.rem(k, 2)

        @pl.loop(0, 8 // many)
        def _(n):
            some = pl.ds(pl.multiple_of(n * tile, tile), tile)

            def weight(ref):
                return ref[pl.ds(n * many, many)].reshape(tile, hidden_width)

            back[k, :, some] = (
                matmul_rt(gate_low[k], weight(gate_w)) + matmul_rt(up_low[k], weight(up_w))
            ).astype(bf16)
            rows[slot, :, some] = matmul_rt(hidden[k], weight(down_w)).astype(bf16)

        store(k).start()

    def block(k, nothing):
        for n in range(2):

            @pl.when(jnp.logical_and(k > 0, k < parts - 2))
            def _():
                hop(k, n).wait_recv()
                hop(k + 1, n).start()

            @pl.when(k == parts - 1)
            def _():
                hop(parts - 2, n).wait_recv()
                sum_hop(0, n).start()

        front(k)

        @pl.when(k > 1)
        def _():
            store(k - 2).wait()

        @pl.when(k < parts - 1)
        def _():
            rear(k)

        return nothing

    lax.fori_loop(0, parts, block, 0)

    tall = parts * block_rows
    kinds = (
        (normed, gate_low, gate_w, gate_sum),
        (normed, up_low, up_w, up_sum),
        (masked, hidden, down_w, down_sum),
    )

    def product(kind, slot, store):
        left, right, _, _ = kinds[kind]
        some = pl.ds(pl.multiple_of(slot * share, share), share)
        for at, size in column_tiles(hidden_width):
            columns = pl.ds(at, size)
            store(
                columns,
                matmul_lt(
                    left[:, :, some].reshape(tall, share), right[:, :, columns].reshape(tall, size)
                ),
            )

    def across(source, target, send, recv, mask):
        return pltpu.make_async_remote_copy(
            src_ref=source,
            dst_ref=target,
            send_sem=send,
            recv_sem=recv,
            device_id={"dp": partner(mask)},
            device_id_type=pl.DeviceIdType.MESH,
        )

    top, low = pl.ds(0, half), pl.ds(half, half)

    def near_copy(kind, k):
        room = kinds[kind][2]
        return across(
            room.at[k], room.at[4 + k], near_send.at[kind, k], near_recv.at[kind, k], near
        )

    def lead_copy(kind):
        return across(
            lead.at[kind], lead_near.at[kind], near_send.at[kind, 3], near_recv.at[kind, 3], near
        )

    def one_copy(kind, n):
        room = kinds[kind][2]
        source = (lead_near.at[kind, top], room.at[5, top], room.at[5, low])[n]
        return across(
            source, one_buf.at[kind, n], one_send.at[kind, n], one_recv.at[kind, n], one
        )

    def two_copy(kind, n):
        room = kinds[kind][2]
        source = (lead_near.at[kind, low], room.at[6, low], room.at[6, top])[n]
        return across(
            source, two_buf.at[kind, n], two_send.at[kind, n], two_recv.at[kind, n], two
        )

    def flipped(k, near_too):
        me = lax.axis_index("dp")

        def turn(mask, on):
            return on * mask * (1 - 2 * lax.rem(lax.div(me, mask), 2))

        there = me + turn(one, lax.rem(k, 2)) + turn(two, lax.div(k, 2)) + turn(near, near_too)
        return lax.div(there, copies)

    def sum_step(k):
        for n in range(2):
            sum_hop(k, n).wait_recv()

            @pl.loop(0, 8 // many)
            def _(at):
                some = pl.ds(pl.multiple_of(at * tile, tile), tile)
                moved = ring_buf[k, both[n], some].astype(f32)
                if k + 1 < parts - 1:
                    total = back[k + 2, both[n], some].astype(f32) + moved
                    back[k + 2, both[n], some] = total.astype(bf16)
                else:
                    norm_sum[both[n], some] = back[0, both[n], some].astype(f32) + moved

            if k + 1 < parts - 1:
                sum_hop(k + 1, n).start()

    def keep(ref, at):
        def store(columns, value):
            ref[at, :, columns] = value.astype(bf16)

        return store

    def add(ref, at):
        def store(columns, value):
            ref[at, :, columns] = (value + ref[at, :, columns].astype(f32)).astype(bf16)

        return store

    def add_wide(total_ref, ref, at):
        def store(columns, value):
            total_ref[:, columns] = value + ref[at, :, columns].astype(f32)

        return store

    for kind in range(3):
        product(kind, flipped(3, 1), keep(lead, kind))
        lead_copy(kind).start()
    for kind in range(3):
        lead_copy(kind).wait_recv()
        product(kind, flipped(3, 0), add(lead_near, kind))
        one_copy(kind, 0).start()
        two_copy(kind, 0).start()
    rear(parts - 1)

    gather[5]()
    pl.semaphore_signal(
        ready_sem,
        inc=1,
        device_id={"dp": partner(near)},
        device_id_type=pl.DeviceIdType.MESH,
    )
    pl.semaphore_wait(ready_sem, 1)

    def theirs(k):
        for kind in range(3):
            product(kind, flipped(k, 1), keep(kinds[kind][2], k))
            near_copy(kind, k).start()

    def mine(k):
        for kind in range(3):
            near_copy(kind, k).wait_recv()
            product(kind, flipped(k, 0), add(kinds[kind][2], 4 + k))
            if k == 1:
                one_copy(kind, 1).start()
            else:
                two_copy(kind, 1).start()

    sum_step(0)
    theirs(1)
    theirs(2)
    mine(1)
    mine(2)
    theirs(0)
    for kind in range(3):
        one_copy(kind, 0).wait_recv()
        room = kinds[kind][2]
        room[6, top] = (room[6, top].astype(f32) + one_buf[kind, 0].astype(f32)).astype(bf16)
        two_copy(kind, 2).start()
        two_copy(kind, 0).wait_recv()
        room[5, low] = (room[5, low].astype(f32) + two_buf[kind, 0].astype(f32)).astype(bf16)
        one_copy(kind, 2).start()
    for k in range(1, parts - 2):
        sum_step(k)
    for kind in range(3):
        near_copy(kind, 0).wait_recv()
        room, total_ref = kinds[kind][2:]
        product(kind, flipped(0, 0), add_wide(total_ref, room, 4))
    sum_step(parts - 2)
    for k in (parts - 2, parts - 1):
        store(k).wait()
    here = lax.axis_index("tensor")
    at_start, at_end = here == 0, here == parts - 1
    moved_up = along(1, rows_out.at[parts - 1], moved_out, moved_send, moved_recv)
    moved_down = along(-1, rows_out.at[0], moved_out, moved_send, moved_recv)

    @pl.when(at_start)
    def _():
        moved_up.start()

    @pl.when(at_end)
    def _():
        moved_down.start()

    for kind in range(3):
        total_ref = kinds[kind][3]
        one_copy(kind, 1).wait_recv()
        two_copy(kind, 2).wait_recv()
        total_ref[:half, :] += one_buf[kind, 1].astype(f32) + two_buf[kind, 2].astype(f32)
        two_copy(kind, 1).wait_recv()
        one_copy(kind, 2).wait_recv()
        total_ref[half:, :] += two_buf[kind, 1].astype(f32) + one_buf[kind, 2].astype(f32)
    for kind in range(3):
        lead_copy(kind).wait_send()
        for k in range(3):
            near_copy(kind, k).wait_send()
        for n in range(3):
            one_copy(kind, n).wait_send()
            two_copy(kind, n).wait_send()
    for k in range(parts - 1):
        for n in range(2):
            hop(k, n).wait_send()
            sum_hop(k, n).wait_send()

    @pl.when(at_start)
    def _():
        moved_up.wait_send()

    @pl.when(at_end)
    def _():
        moved_down.wait_send()

    @pl.when(jnp.logical_not(jnp.logical_or(at_start, at_end)))
    def _():
        moved_up.wait_recv()


def swiglu(normed, own, first, others, gate_w, up_w, down_w, copies, collective):
    parts = lax.axis_size("tensor")
    rows, width = normed.shape
    hidden = gate_w.shape[2]
    share = width // 8
    somewhere = pl.BlockSpec(memory_space=pl.ANY)
    vmem = pl.BlockSpec(memory_space=pltpu.VMEM)
    wide, narrow = (parts, rows, width), (parts, rows, hidden)
    return pl.pallas_call(
        functools.partial(swiglu_kernel, copies),
        out_shape=[
            jax.ShapeDtypeStruct(wide, bf16),
            jax.ShapeDtypeStruct((rows, width), bf16),
            jax.ShapeDtypeStruct((rows, width), f32),
        ]
        + [jax.ShapeDtypeStruct((share, hidden), f32)] * 3,
        in_specs=[somewhere] * 7,
        out_specs=[somewhere] * 2 + [vmem] * 4,
        scratch_shapes=[pltpu.VMEM(wide, bf16)] * 2
        + [pltpu.VMEM((8, share, hidden), bf16)] * 3
        + [pltpu.VMEM(narrow, bf16)] * 3
        + [
            pltpu.VMEM(wide, bf16),
            pltpu.VMEM((2, rows, width), bf16),
            pltpu.VMEM((parts - 1, rows, width), bf16),
        ]
        + [pltpu.VMEM((3, 3, share // 2, hidden), bf16)] * 2
        + [pltpu.VMEM((3, share, hidden), bf16)] * 2
        + [pltpu.SemaphoreType.DMA((7,)), pltpu.SemaphoreType.DMA((2,))]
        + [pltpu.SemaphoreType.DMA((14,))] * 2
        + [pltpu.SemaphoreType.DMA((parts - 1, 2))] * 4
        + [pltpu.SemaphoreType.DMA((3, 4))] * 2
        + [pltpu.SemaphoreType.DMA((3, 3))] * 4
        + [pltpu.SemaphoreType.REGULAR]
        + [pltpu.SemaphoreType.DMA] * 2,
        compiler_params=pltpu.CompilerParams(
            collective_id=collective, has_side_effects=True, vmem_limit_bytes=62 * 1024 * 1024
        ),
        cost_estimate=pl.CostEstimate(
            flops=18 * parts * rows * width * hidden,
            bytes_accessed=1100 * rows * width,
            transcendentals=parts * rows * hidden,
        ),
    )(normed, own, first, others, gate_w, up_w, down_w)


def greet_all(copies, masks):
    barrier = pltpu.get_barrier_semaphore()
    others = [{"dp": group_member(copies, k)} for k in range(1, 8)]
    others += [{"tensor": beside(k)} for k in range(1, lax.axis_size("tensor"))]
    others += [{"dp": partner(mask)} for mask in masks]
    for other in others:
        pl.semaphore_signal(
            barrier, inc=1, device_id=other, device_id_type=pl.DeviceIdType.MESH
        )
    pl.semaphore_wait(barrier, len(others))


def group_member(copies, step):
    me = lax.axis_index("dp")
    return lax.rem(lax.div(me, copies) + step, 8) * copies + lax.rem(me, copies)


def mixer_forward_kernel(
    copies,
    own_ref, input_hbm, forget_hbm, gate_hbm, out_hbm, masked_hbm, bound_ref, live_ref,
    normed_out, weights_out, project_out, pre_out, squash_out, state_out, entering_out, mixed_out,
    masked_out, sum_ref,
    normed, weights, project, pre, squashed, forget, state, decay, ends, entering, mixed,
    near_buf, one_buf, two_buf, part_buf,
    own_sem, gather_send, gather_recv, spread_send, spread_recv, spread_own, ring_send, ring_recv,
    carry_send, carry_recv, scatter_send, scatter_recv, masked_send, masked_recv, out_sem,
):
    parts = lax.axis_size("tensor")
    here = lax.axis_index("tensor")
    seqs, rows, width = normed.shape
    strips, _, lanes = forget.shape
    channels = strips * lanes
    mine = slot_of(copies, ())
    greet_all(copies, ())

    def own_rows_of(index):
        return pl.ds(pl.multiple_of(index * copies, copies), copies)

    def columns_of(index):
        return pl.ds(pl.multiple_of(index * channels, channels), channels)

    spread = []
    for kind, source in enumerate((input_hbm, forget_hbm, gate_hbm)):
        target = weights.at[kind, own_rows_of(mine), here]
        kept = pltpu.make_async_copy(
            source.at[:, :, columns_of(mine)], target, spread_own.at[kind]
        )
        sent = []
        for k in range(1, 8):
            there = group_member(copies, k)
            sent.append(
                pltpu.make_async_remote_copy(
                    src_ref=source.at[:, :, columns_of(lax.div(there, copies))],
                    dst_ref=target,
                    send_sem=spread_send.at[kind, k - 1],
                    recv_sem=spread_recv.at[kind, k - 1],
                    device_id={"dp": there},
                    device_id_type=pl.DeviceIdType.MESH,
                )
            )
        spread.append((kept, sent))

    def ring_copy(kind, k):
        at = beside(-k)
        target = project.at[:, at] if kind == 3 else weights.at[kind, :, at]
        source = out_hbm if kind == 3 and k == 0 else target
        return to_right(source, target, ring_send.at[kind, k], ring_recv.at[kind, k])

    def spread_arrive(kind):
        kept, sent = spread[kind]
        kept.wait()
        for copy in sent:
            copy.wait_recv()

    out_kept = pltpu.make_async_copy(out_hbm, project.at[:, here], spread_own.at[3])
    out_kept.start()
    for kept, sent in spread:
        kept.start()
        for copy in sent:
            copy.start()
    ring_copy(3, 0).start()
    begin, pass_first, pass_second, pass_last, arrive, finish = plane_gather_steps(
        copies, own_ref, normed, own_sem, gather_send, gather_recv
    )
    begin()
    spread_arrive(0)
    ring_copy(0, 0).start()
    spread_arrive(1)
    ring_copy(3, 0).wait_recv()
    ring_copy(1, 0).start()
    spread_arrive(2)
    pass_first()
    for k in range(parts - 2):
        ring_copy(0, k).wait_recv()
        ring_copy(0, k + 1).start()
        if k == 0:
            pass_second()
        ring_copy(1, k).wait_recv()
        ring_copy(1, k + 1).start()
    ring_copy(0, parts - 2).wait_recv()
    ring_copy(2, 0).start()
    pass_last()
    ring_copy(1, parts - 2).wait_recv()
    ring_copy(3, 1).start()
    arrive()

    many = 2

    def project_rows(kind, at):
        left = normed[pl.ds(at * many, many)].reshape(many * rows, width)
        return matmul(left, weights[kind].reshape(width, channels))

    def rows_at(at):
        return pl.ds(pl.multiple_of(at * many * rows, many * rows), many * rows)

    def strip_of(value, n):
        return value[:, n * lanes : (n + 1) * lanes]

    @pl.loop(0, seqs // many)
    def _(at):
        some = rows_at(at)
        value = project_rows(0, at)
        pre[0, some, :] = value
        inflow = live_ref[some, :] * silu_of(value)
        for n in range(strips):
            state[n, some, :] = strip_of(inflow, n)

    ring_copy(2, 0).wait_recv()
    ring_copy(2, 1).start()

    @pl.loop(0, seqs // many)
    def _(at):
        some = rows_at(at)
        squash = jax.nn.sigmoid(project_rows(1, at))
        bound = bound_ref[...]
        value = bound + (1.0 - bound) * squash
        for n in range(strips):
            squashed[n, some, :] = strip_of(squash, n)
            forget[n, some, :] = strip_of(value, n)
            state[n, some, :] = (1.0 - strip_of(value, n)) * state[n, some, :]

    ring_copy(3, 1).wait_recv()
    ring_copy(3, 2).start()

    def step(at, carry):
        some = pl.ds(at, seqs, stride=rows)
        following = []
        for n, (total, product) in enumerate(carry):
            keep = forget[n, some, :]
            total = keep * total + state[n, some, :]
            product = product * keep
            state[n, some, :] = total
            decay[n, some, :] = product
            following.append((total, product))
        return tuple(following)

    start = (jnp.zeros((seqs, lanes), f32), jnp.ones((seqs, lanes), f32))
    carry = lax.fori_loop(0, rows, step, (start,) * strips, unroll=8)
    for n, (total, product) in enumerate(carry):
        ends[here, 0, :, n * lanes : (n + 1) * lanes] = total
        ends[here, 1, :, n * lanes : (n + 1) * lanes] = product
    carries = []
    for k in range(1, parts):
        copy = pltpu.make_async_remote_copy(
            src_ref=ends.at[here],
            dst_ref=ends.at[here],
            send_sem=carry_send.at[k - 1],
            recv_sem=carry_recv.at[k - 1],
            device_id={"tensor": beside(k)},
            device_id_type=pl.DeviceIdType.MESH,
        )
        copy.start()
        carries.append(copy)
    ring_copy(2, 1).wait_recv()
    ring_copy(2, 2).start()

    def masked_copy(k):
        source = masked_hbm if k == 0 else masked_out.at[k - 1]
        return to_right(source, masked_out.at[k], masked_send.at[k], masked_recv.at[k])

    for copy in carries:
        copy.wait_recv()
    coming = jnp.zeros((seqs, channels), f32)
    entered = coming
    for k in range(parts - 1):
        coming = ends[k, 1] * coming + ends[k, 0]
        entered = jnp.where(here == k + 1, coming, entered)
    for n in range(seqs):
        entering[n] = entered[n : n + 1]
    ring_copy(3, 2).wait_recv()
    ring_copy(2, 2).wait_recv()

    @pl.loop(0, seqs // many)
    def _(at):
        some = rows_at(at)
        value = project_rows(2, at)
        pre[1, some, :] = value
        act = silu_of(value)
        for n in range(many):
            slot = at * many + n
            one = pl.ds(pl.multiple_of(slot * rows, rows), rows)
            for strip in range(strips):
                columns = slice(strip * lanes, (strip + 1) * lanes)
                whole = state[strip, one, :] + (
                    decay[strip, one, :] * entering[slot, :, columns]
                )
                state[strip, one, :] = whole
                mixed[slot, :, columns] = (
                    whole * act[n * rows : (n + 1) * rows, columns]
                ).astype(bf16)

    out_kept.wait()
    stores = [
        pltpu.make_async_copy(source, target, out_sem.at[n])
        for n, (source, target) in enumerate(
            (
                (normed, normed_out),
                (weights, weights_out),
                (project, project_out),
                (pre, pre_out),
                (squashed, squash_out),
                (state, state_out),
                (entering, entering_out),
                (mixed, mixed_out),
            )
        )
    ]
    for store in stores:
        store.start()

    def out_product(slot, columns):
        right = project[:, :, :, columns]
        return matmul(mixed[slot], right.reshape(channels, right.shape[-1]))

    masked_copy(0).start()

    def between(point):
        if point == "low":
            for k in range(parts - 3):
                masked_copy(k).wait_recv()
                masked_copy(k + 1).start()

    plane_scatter_steps(
        copies, sum_ref, near_buf, one_buf, two_buf, part_buf, scatter_send, scatter_recv,
        out_product, between,
    )
    masked_copy(parts - 3).wait_recv()
    for k in range(parts - 2):
        masked_copy(k).wait_send()
    finish()
    for kept, sent in spread:
        for copy in sent:
            copy.wait_send()
    for kind in range(4):
        for k in range(parts - 1):
            ring_copy(kind, k).wait_send()
    for copy in carries:
        copy.wait_send()
    for store in stores:
        store.wait()


def mixer_forward(
    normed, w_input, w_forget, w_gate, w_out, masked, bound, live, copies, collective
):
    parts = lax.axis_size("tensor")
    rows, width = normed.shape
    channels = width // 8
    own_rows = w_input.shape[1]
    somewhere = pl.BlockSpec(memory_space=pl.ANY)
    vmem = pl.BlockSpec(memory_space=pltpu.VMEM)
    wide = (8, rows, width)
    weights = (3, 8 * copies, parts, own_rows, channels)
    project = (copies, parts, own_rows, width)
    flat = (8 * rows, channels)
    lanes = min(128, channels)
    strips = (channels // lanes, 8 * rows, lanes)
    shaped = (8, rows, channels)
    half = rows // 2
    dma = pltpu.SemaphoreType.DMA
    return pl.pallas_call(
        functools.partial(mixer_forward_kernel, copies),
        out_shape=[
            jax.ShapeDtypeStruct(wide, bf16),
            jax.ShapeDtypeStruct(weights, bf16),
            jax.ShapeDtypeStruct(project, bf16),
            jax.ShapeDtypeStruct((2,) + flat, f32),
            jax.ShapeDtypeStruct(strips, f32),
            jax.ShapeDtypeStruct(strips, f32),
            jax.ShapeDtypeStruct((8, 1, channels), f32),
            jax.ShapeDtypeStruct(shaped, bf16),
            jax.ShapeDtypeStruct((parts - 2, rows, width), bf16),
            jax.ShapeDtypeStruct((rows, width), f32),
        ],
        in_specs=[somewhere] * 6 + [vmem] * 2,
        out_specs=[somewhere] * 9 + [vmem],
        scratch_shapes=[
            pltpu.VMEM(wide, bf16),
            pltpu.VMEM(weights, bf16),
            pltpu.VMEM(project, bf16),
            pltpu.VMEM((2,) + flat, f32),
            pltpu.VMEM(strips, f32),
            pltpu.VMEM(strips, f32),
            pltpu.VMEM(strips, f32),
            pltpu.VMEM(strips, f32),
            pltpu.VMEM((parts, 2, 8, channels), f32),
            pltpu.VMEM((8, 1, channels), f32),
            pltpu.VMEM(shaped, bf16),
            pltpu.VMEM((4, rows, width), bf16),
            pltpu.VMEM((3, half, width), bf16),
            pltpu.VMEM((3, half, width), bf16),
            pltpu.VMEM((4, rows, width), bf16),
            dma,
            dma((14,)),
            dma((14,)),
            dma((3, 7)),
            dma((3, 7)),
            dma((4,)),
            dma((4, parts - 1)),
            dma((4, parts - 1)),
            dma((parts - 1,)),
            dma((parts - 1,)),
            dma((10,)),
            dma((10,)),
            dma((parts - 2,)),
            dma((parts - 2,)),
            dma((8,)),
        ],
        compiler_params=pltpu.CompilerParams(
            collective_id=collective, has_side_effects=True, vmem_limit_bytes=56 * 1024 * 1024
        ),
        cost_estimate=pl.CostEstimate(
            flops=8 * rows * width * width,
            bytes_accessed=900 * rows * width,
            transcendentals=0,
        ),
    )(normed, w_input, w_forget, w_gate, w_out, masked, bound, live)


def mixer_backward_kernel(
    copies, masks,
    own_ref, normed_hbm, weights_hbm, project_hbm, pre_hbm, squash_hbm, state_hbm, mixed_hbm,
    unit_hbm, stream_hbm, entering_ref, bound_ref, live_ref, gain_ref, scale_ref, gain_two_ref,
    rows_hbm, moved_hbm,
    result_ref, weight_sums, project_sum, small_sums, moved_out,
    rows_buf, weights, project, pre, squashed, state, mixed, unit, stream, drive, decay, ends,
    entered, grad_pre, grad_w, grad_project, line_w, line_project, bound_sum, whole_w, spread_w,
    small_recv, small_ring, near_buf, one_buf, two_buf, part_buf,
    load_sem, gather_send, gather_recv, carry_send, carry_recv, up_send, down_send, line_recv,
    scatter_send, scatter_recv, spread_send, spread_recv, spread_own, small_send, small_got,
    moved_sem, moved_send, moved_recv,
):
    parts = lax.axis_size("tensor")
    here = lax.axis_index("tensor")
    seqs, rows, width = rows_buf.shape
    strips, _, lanes = drive.shape
    channels = strips * lanes
    own_rows = weights.shape[3]
    near, one, two = copies, 2 * copies, 4 * copies
    mine = slot_of(copies, ())
    greet_all(copies, masks)
    begin, pass_first, pass_second, pass_last, arrive, finish = plane_gather_steps(
        copies, own_ref, rows_buf, load_sem.at[0], gather_send, gather_recv
    )
    begin()

    at_start, at_end = here == 0, here == parts - 1
    inside = jnp.logical_not(jnp.logical_or(at_start, at_end))
    low_half = here == 1

    def fetch(block, came, first, second):
        loads = (
            pltpu.make_async_copy(rows_hbm.at[block], part_buf.at[first], moved_sem.at[0]),
            pltpu.make_async_copy(came, part_buf.at[second], moved_sem.at[1]),
        )
        for load in loads:
            load.start()
        for load in loads:
            load.wait()
        part_buf[first] = (
            part_buf[first].astype(f32) + part_buf[second].astype(f32)
        ).astype(bf16)

    def moved_copy(n, step, source):
        return along(step, source, moved_out.at[n], moved_send.at[n], moved_recv.at[n])

    def moved_second():
        @pl.when(at_start)
        def _():
            moved_copy(0, 1, rows_hbm.at[2]).start()

        @pl.when(at_end)
        def _():
            moved_copy(1, -1, rows_hbm.at[1]).start()

        @pl.when(inside)
        def _():
            fetch(3 - 3 * (here - 1), moved_hbm, 0, 1)

        @pl.when(low_half)
        def _():
            moved_copy(0, 1, part_buf.at[0]).start()

        @pl.when(here == 2)
        def _():
            moved_copy(1, -1, part_buf.at[0]).start()

    def moved_last():
        @pl.when(at_start)
        def _():
            moved_copy(0, 1, rows_hbm.at[2]).wait_send()
            moved_copy(2, 1, rows_hbm.at[1]).start()

        @pl.when(at_end)
        def _():
            moved_copy(1, -1, rows_hbm.at[1]).wait_send()
            moved_copy(3, -1, rows_hbm.at[2]).start()

        @pl.when(inside)
        def _():
            moved_copy(0, 1, part_buf.at[0]).wait_recv()
            fetch(here + 1, moved_out.at[0], 1, 2)
            moved_copy(2, 1, part_buf.at[1]).start()

        @pl.when(low_half)
        def _():
            moved_copy(0, 1, part_buf.at[0]).wait_send()

        @pl.when(here == 2)
        def _():
            moved_copy(1, -1, part_buf.at[0]).wait_send()

        @pl.when(inside)
        def _():
            moved_copy(1, -1, part_buf.at[0]).wait_recv()
            fetch(here - 1, moved_out.at[1], 2, 3)
            moved_copy(3, -1, part_buf.at[2]).start()

    def moved_end():
        @pl.when(here < parts - 1)
        def _():
            moved_copy(2, 1, part_buf.at[1]).wait_send()
            moved_copy(3, -1, part_buf.at[2]).wait_recv()

        @pl.when(here > 0)
        def _():
            moved_copy(3, -1, part_buf.at[2]).wait_send()
            moved_copy(2, 1, part_buf.at[1]).wait_recv()

    loads = [
        pltpu.make_async_copy(source, target, load_sem.at[n + 1])
        for n, (source, target) in enumerate(
            (
                (project_hbm, project),
                (pre_hbm, pre),
                (state_hbm, state),
                (mixed_hbm, mixed),
                (squash_hbm, squashed),
                (weights_hbm, weights),
                (unit_hbm, unit),
                (stream_hbm, stream),
            )
        )
    ]
    for load in loads:
        load.start()
    moved_second()
    for load in loads[:3]:
        load.wait()

    def slot_rows(slot):
        return pl.ds(pl.multiple_of(slot * rows, rows), rows)

    def take(slot):
        some = slot_rows(slot)
        grad_mixed = matmul_rt(rows_buf[slot], project[...].reshape(channels, width))
        gate = pre[1, some, :]
        squash = jax.nn.sigmoid(gate)
        act = gate * squash
        slope = squash * (1.0 + gate * (1.0 - squash))
        for n in range(strips):
            columns = slice(n * lanes, (n + 1) * lanes)
            part = grad_mixed[:, columns]
            drive[n, some, :] = part * act[:, columns]
            at = 2 * channels + n * lanes
            grad_pre[slot, :, at : at + lanes] = (
                part * state[n, some, :] * slope[:, columns]
            ).astype(bf16)

    pass_first()
    pass_second()
    arrive(slice(0, 6))
    pltpu.make_async_copy(own_ref, rows_buf.at[mine], load_sem.at[0]).wait()
    for flips in ((), (near,), (one,), (two,), (near, one), (near, two)):
        take(slot_of(copies, flips))
    moved_last()
    pass_last()
    take(slot_of(copies, (one, two)))
    arrive(slice(6, 8))
    take(slot_of(copies, (near, one, two)))

    tile = min(512, width)
    loads[3].wait()

    @pl.loop(0, width // tile)
    def _(k):
        columns = pl.ds(pl.multiple_of(k * tile, tile), tile)
        value = matmul_lt(
            mixed[...].reshape(seqs * rows, channels),
            rows_buf[:, :, columns].reshape(seqs * rows, tile),
        )
        grad_project[:, :, :, columns] = value.astype(bf16).reshape(
            copies, parts, own_rows, tile
        )

    def part_of(kind, block):
        return grad_project.at[:, block] if kind == 3 else grad_w.at[kind, :, block]

    def room_of(kind, index):
        return line_project.at[index] if kind == 3 else line_w.at[kind, index]

    def line_up(kind, k):
        block = parts - 1 - k + here
        return along(
            1, part_of(kind, block), room_of(kind, block), up_send.at[kind, k],
            line_recv.at[kind, block],
        )

    def line_down(kind, k):
        block = k - parts + 1 + here
        index = parts if k == parts - 2 else block
        return along(
            -1, part_of(kind, block), room_of(kind, index), down_send.at[kind, k],
            line_recv.at[kind, index],
        )

    def came(kind, index):
        return along(1, part_of(kind, 0), room_of(kind, index), up_send.at[kind, 0],
                     line_recv.at[kind, index])

    def add_came(kind, block):
        came(kind, block).wait_recv()
        if kind == 3:
            total = grad_project[:, block].astype(f32) + line_project[block].astype(f32)
            grad_project[:, block] = total.astype(bf16)
        else:
            total = grad_w[kind, :, block].astype(f32) + line_w[kind, block].astype(f32)
            grad_w[kind, :, block] = total.astype(bf16)

    def goes_up(k):
        return jnp.logical_and(here <= k, here < parts - 1)

    def goes_down(k):
        return jnp.logical_and(parts - 1 - here <= k, here > 0)

    def line_step(kind, k):
        @pl.when(jnp.logical_and(goes_up(k), here > 0))
        def _():
            add_came(kind, parts - 1 - k + here)

        @pl.when(goes_up(k))
        def _():
            line_up(kind, k).start()

        @pl.when(jnp.logical_and(goes_down(k), here < parts - 1))
        def _():
            add_came(kind, k - parts + 1 + here)

        @pl.when(goes_down(k))
        def _():
            line_down(kind, k).start()

    def advance(kind, k):
        if k + 1 < parts - 1:
            line_step(kind, k + 1)
            return

        @pl.when(here > 0)
        def _():
            came(kind, here).wait_recv()

        @pl.when(here < parts - 1)
        def _():
            came(kind, parts).wait_recv()

        if kind == 3:
            project_sum[...] = (
                grad_project[:, here].astype(f32)
                + line_project[here].astype(f32)
                + line_project[parts].astype(f32)
            )
        else:
            total = (
                grad_w[kind, :, here].astype(f32)
                + line_w[kind, here].astype(f32)
                + line_w[kind, parts].astype(f32)
            )
            whole_w[kind] = total.astype(bf16)
            for copy in spread_copies(kind):
                copy.start()

    @pl.when(at_start)
    def _():
        line_w[:, 0] = jnp.zeros_like(line_w[:, 0])
        line_project[0] = jnp.zeros_like(line_project[0])

    @pl.when(at_end)
    def _():
        line_w[:, parts] = jnp.zeros_like(line_w[:, parts])
        line_project[parts] = jnp.zeros_like(line_project[parts])

    def spread_copies(kind, own=True):
        found = []
        for k in range(1, 8):
            there = group_member(copies, k)
            source = pl.ds(pl.multiple_of(lax.div(there, copies) * copies, copies), copies)
            found.append(
                pltpu.make_async_remote_copy(
                    src_ref=whole_w.at[kind, source],
                    dst_ref=spread_w.at[kind, mine],
                    send_sem=spread_send.at[kind, k - 1],
                    recv_sem=spread_recv.at[kind, k - 1],
                    device_id={"dp": there},
                    device_id_type=pl.DeviceIdType.MESH,
                )
            )
        if own:
            source = pl.ds(pl.multiple_of(mine * copies, copies), copies)
            found.append(
                pltpu.make_async_copy(
                    whole_w.at[kind, source], spread_w.at[kind, mine], spread_own.at[kind]
                )
            )
        return found

    line_step(3, 0)
    finish()
    normed_load = pltpu.make_async_copy(normed_hbm, rows_buf, load_sem.at[0])
    normed_load.start()
    loads[4].wait()

    def step(k, carry):
        some = pl.ds(rows - 1 - k, seqs, stride=rows)
        following = []
        for n, (coming, product) in enumerate(carry):
            bound = bound_ref[:, n * lanes : (n + 1) * lanes]
            keep = bound + (1.0 - bound) * squashed[n, some, :]
            carried = drive[n, some, :] + coming
            drive[n, some, :] = carried
            decay[n, some, :] = product
            following.append((keep * carried, product * keep))
        return tuple(following)

    start = (jnp.zeros((seqs, lanes), f32), jnp.ones((seqs, lanes), f32))
    carry = lax.fori_loop(0, rows, step, (start,) * strips, unroll=8)
    for n, (coming, product) in enumerate(carry):
        ends[here, 0, :, n * lanes : (n + 1) * lanes] = coming
        ends[here, 1, :, n * lanes : (n + 1) * lanes] = product
    carries = []
    for k in range(1, parts):
        copy = pltpu.make_async_remote_copy(
            src_ref=ends.at[here],
            dst_ref=ends.at[here],
            send_sem=carry_send.at[k - 1],
            recv_sem=carry_recv.at[k - 1],
            device_id={"tensor": beside(k)},
            device_id_type=pl.DeviceIdType.MESH,
        )
        copy.start()
        carries.append(copy)
    normed_load.wait()

    def weight_grad(kind):
        @pl.loop(0, width // tile)
        def _(k):
            columns = pl.ds(pl.multiple_of(k * tile, tile), tile)
            value = matmul_lt(
                grad_pre[:, :, kind * channels : (kind + 1) * channels].reshape(
                    seqs * rows, channels
                ),
                rows_buf[:, :, columns].reshape(seqs * rows, tile),
            )
            count = tile // (parts * own_rows)
            grad_w[kind, pl.ds(k * count, count)] = value.T.astype(bf16).reshape(
                count, parts, own_rows, channels
            )

        line_step(kind, 0)

    advance(3, 0)
    weight_grad(2)
    for copy in carries:
        copy.wait_recv()
    coming = jnp.zeros((seqs, channels), f32)
    arrived = coming
    for k in range(parts - 1, 0, -1):
        coming = ends[k, 1] * coming + ends[k, 0]
        arrived = jnp.where(here == k - 1, coming, arrived)
    for n in range(seqs):
        entered[n] = arrived[n : n + 1]
    bound_sum[...] = jnp.zeros_like(bound_sum)
    first_row = lax.broadcasted_iota(jnp.int32, (rows, lanes), 0) == 0

    @pl.loop(0, seqs)
    def _(slot):
        some = slot_rows(slot)
        alive = live_ref[some, :]
        for n in range(strips):
            columns = slice(n * lanes, (n + 1) * lanes)
            bound = bound_ref[:, columns]
            squash = squashed[n, some, :]
            keep = bound + (1.0 - bound) * squash
            carried = drive[n, some, :] + decay[n, some, :] * entered[slot, :, columns]
            prior = jnp.where(
                first_row, entering_ref[slot, :, columns], pltpu.roll(state[n, some, :], 1, 0)
            )
            value = pre[0, some, columns]
            gate = jax.nn.sigmoid(value)
            slope = gate * (1.0 + value * (1.0 - gate))
            grad_forget = carried * prior - carried * alive * value * gate
            at = n * lanes
            grad_pre[slot, :, at : at + lanes] = (
                carried * alive * (1.0 - keep) * slope
            ).astype(bf16)
            at = channels + n * lanes
            grad_pre[slot, :, at : at + lanes] = (
                grad_forget * (1.0 - bound) * squash * (1.0 - squash)
            ).astype(bf16)
            bound_sum[:, columns] += jnp.sum(
                grad_forget * (1.0 - squash), axis=0, keepdims=True
            )

    advance(3, 1)
    weight_grad(0)
    advance(2, 0)
    weight_grad(1)
    loads[5].wait()
    moved_end()

    def normed_product(slot, columns):
        at = lax.div(columns.start, parts * own_rows)
        count = tile // (parts * own_rows)
        total = None
        for kind in range(3):
            part = matmul_rt(
                grad_pre[slot, :, kind * channels : (kind + 1) * channels],
                weights[kind, pl.ds(at, count)].reshape(tile, channels),
            )
            total = part if total is None else total + part
        return total

    def between(point):
        if point == "sent":
            advance(3, 2)
        elif point == "added":
            advance(2, 1)
            advance(0, 0)
        elif point == "top":
            advance(1, 0)
            advance(2, 2)
        elif point == "low":
            advance(0, 1)
            advance(1, 1)

    plane_scatter_steps(
        copies, result_ref, near_buf, one_buf, two_buf, part_buf, scatter_send, scatter_recv,
        normed_product, between,
    )

    for load in loads[6:]:
        load.wait()
    small_sums[...] = jnp.zeros_like(small_sums)
    small_sums[1:2, :] = gain_two_ref[...]
    small_sums[2:3, pl.ds(pl.multiple_of(mine * channels, channels), channels)] = bound_sum[...]
    some_rows = min(64, rows)

    @pl.loop(0, rows // some_rows)
    def _(k):
        some = pl.ds(pl.multiple_of(k * some_rows, some_rows), some_rows)
        grad_norm = result_ref[some, :]
        units = unit[some, :]
        small_sums[0:1, :] += jnp.sum(grad_norm * units, axis=0, keepdims=True)
        scaled = grad_norm * gain_ref[...]
        mean = jnp.mean(scaled * units, axis=-1, keepdims=True)
        result_ref[some, :] = stream[some, :] + scale_ref[some, :] * (scaled - units * mean)

    def small_copy(n):
        return pltpu.make_async_remote_copy(
            src_ref=small_sums,
            dst_ref=small_recv.at[n],
            send_sem=small_send.at[n],
            recv_sem=small_got.at[n],
            device_id={"dp": partner(masks[n])},
            device_id_type=pl.DeviceIdType.MESH,
        )

    def small_step(n):
        small_copy(n).wait()
        small_sums[...] += small_recv[n]

    small_copy(0).start()
    advance(0, 2)
    advance(1, 2)
    for n in range(len(masks)):
        small_step(n)
        if n + 1 < len(masks):
            small_copy(n + 1).start()
    ring_small = []
    for k in range(1, parts):
        copy = pltpu.make_async_remote_copy(
            src_ref=small_sums,
            dst_ref=small_ring.at[k - 1],
            send_sem=small_send.at[len(masks) + k - 1],
            recv_sem=small_got.at[len(masks) + k - 1],
            device_id={"tensor": beside(k)},
            device_id_type=pl.DeviceIdType.MESH,
        )
        copy.start()
        ring_small.append(copy)
    for kind in (2, 0, 1):
        spread = spread_copies(kind)
        for copy in spread[:-1]:
            copy.wait_recv()
        spread[-1].wait()
        for slot in range(8):
            weight_sums[kind, :, :, slot * channels : (slot + 1) * channels] = spread_w[
                kind, slot
            ].astype(f32)
    for copy in ring_small:
        copy.wait()
    for k in range(parts - 1):
        small_sums[...] += small_ring[k]
    for kind in range(4):
        for k in range(parts - 1):

            @pl.when(goes_up(k))
            def _():
                line_up(kind, k).wait_send()

            @pl.when(goes_down(k))
            def _():
                line_down(kind, k).wait_send()

    for kind in range(3):
        for copy in spread_copies(kind, False):
            copy.wait_send()
    for copy in carries:
        copy.wait_send()


def mixer_backward(
    own, normed, weights, project, pre, squashed, state, mixed, unit, stream, entering, bound,
    live, gain, scale, gain_two, out_rows, out_moved, copies, masks, collective,
):
    parts = lax.axis_size("tensor")
    _, rows, width = normed.shape
    channels = width // 8
    own_rows = project.shape[2]
    somewhere = pl.BlockSpec(memory_space=pl.ANY)
    vmem = pl.BlockSpec(memory_space=pltpu.VMEM)
    half = rows // 2
    dma = pltpu.SemaphoreType.DMA
    blocks = (8 * copies, own_rows, channels)
    small = pltpu.VMEM((len(masks), 8, width), f32)
    return pl.pallas_call(
        functools.partial(mixer_backward_kernel, copies, masks),
        out_shape=[
            jax.ShapeDtypeStruct((rows, width), f32),
            jax.ShapeDtypeStruct((3, copies, own_rows, width), f32),
            jax.ShapeDtypeStruct((copies, own_rows, width), f32),
            jax.ShapeDtypeStruct((8, width), f32),
            jax.ShapeDtypeStruct((4, rows, width), bf16),
        ],
        in_specs=[somewhere] * 10 + [vmem] * 6 + [somewhere] * 2,
        out_specs=[vmem] * 4 + [somewhere],
        scratch_shapes=[
            pltpu.VMEM(normed.shape, bf16),
            pltpu.VMEM(weights.shape, bf16),
            pltpu.VMEM(project.shape, bf16),
            pltpu.VMEM(pre.shape, f32),
            pltpu.VMEM(squashed.shape, f32),
            pltpu.VMEM(state.shape, f32),
            pltpu.VMEM(mixed.shape, bf16),
            pltpu.VMEM((rows, width), f32),
            pltpu.VMEM((rows, width), f32),
            pltpu.VMEM(state.shape, f32),
            pltpu.VMEM(state.shape, f32),
            pltpu.VMEM((parts, 2, 8, channels), f32),
            pltpu.VMEM((8, 1, channels), f32),
            pltpu.VMEM((8, rows, 3 * channels), bf16),
            pltpu.VMEM(weights.shape, bf16),
            pltpu.VMEM(project.shape, bf16),
            pltpu.VMEM((3, parts + 1) + blocks, bf16),
            pltpu.VMEM((parts + 1, copies, own_rows, width), bf16),
            pltpu.VMEM((1, channels), f32),
            pltpu.VMEM((3,) + blocks, bf16),
            pltpu.VMEM((3, 8, copies, own_rows, channels), bf16),
            small,
            pltpu.VMEM((parts - 1, 8, width), f32),
            pltpu.VMEM((4, rows, width), bf16),
            pltpu.VMEM((3, half, width), bf16),
            pltpu.VMEM((3, half, width), bf16),
            pltpu.VMEM((4, rows, width), bf16),
            dma((9,)),
            dma((14,)),
            dma((14,)),
            dma((parts - 1,)),
            dma((parts - 1,)),
            dma((4, parts - 1)),
            dma((4, parts - 1)),
            dma((4, parts + 1)),
            dma((10,)),
            dma((10,)),
            dma((3, 7)),
            dma((3, 7)),
            dma((3,)),
            dma((len(masks) + parts - 1,)),
            dma((len(masks) + parts - 1,)),
            dma((2,)),
            dma((4,)),
            dma((4,)),
        ],
        compiler_params=pltpu.CompilerParams(
            collective_id=collective, has_side_effects=True, vmem_limit_bytes=62 * 1024 * 1024
        ),
        cost_estimate=pl.CostEstimate(
            flops=16 * rows * width * width,
            bytes_accessed=900 * rows * width,
            transcendentals=0,
        ),
    )(
        own, normed, weights, project, pre, squashed, state, mixed, unit, stream, entering, bound,
        live, gain, scale, gain_two, out_rows, out_moved,
    )


def on_device(
    inputs,
    lengths,
    gain_mix,
    gain_glu,
    lower_bound,
    w_input,
    w_forget,
    w_gate_mix,
    w_out,
    w_gate,
    w_up,
    w_down,
    cotangent,
):
    tensor_parts = lax.axis_size("tensor")
    data_parts = lax.axis_size("dp")
    tensor_index = lax.axis_index("tensor")
    data_index = lax.axis_index("dp")
    rows_here, width = inputs.shape
    group = min(8, data_parts)
    copies = data_parts // group
    group_index = lax.div(data_index, copies)
    copy_index = lax.rem(data_index, copies)
    group_masks = [copies << k for k in range(group.bit_length() - 1)]
    copy_masks = [1 << k for k in range(copies.bit_length() - 1)]
    all_masks = [1 << k for k in range(data_parts.bit_length() - 1)]
    group_lists = [[g * copies + o for g in range(group)] for o in range(copies)]
    channels = width // group
    own_rows = w_input.shape[0]

    high = lax.div(lengths, 32).astype(bf16)
    low = lax.rem(lengths, 32).astype(bf16)
    length_row = jnp.concatenate([high, low, jnp.zeros((own_rows - 2,), bf16)])
    small = jnp.stack([gain_mix, gain_glu, lower_bound, length_row])
    small = in_order(shifted_blocks(small))
    small = gather_bits(small, sorted(all_masks, reverse=True)).astype(f32)
    small = small.reshape((data_parts * tensor_parts,) + small.shape[2:])
    gain_one = small[:, 0].reshape(width)
    gain_two = small[:, 1].reshape(width)
    bound = lax.dynamic_slice_in_dim(small[:, 2].reshape(width), group_index * channels, channels)
    every_length = small[:, 3].reshape(data_parts, tensor_parts, own_rows)[:, 0, :2]
    every_length = (every_length[:, 0] * 32.0 + every_length[:, 1]).astype(jnp.int32)
    group_lengths = lax.dynamic_index_in_dim(
        every_length.reshape(group, copies), copy_index, axis=1, keepdims=False
    )
    position = tensor_index * rows_here + jnp.arange(rows_here, dtype=jnp.int32)
    live_own = (position < lengths[0]).astype(f32)[:, None]
    live = (position[None, :] < group_lengths[:, None]).astype(f32)
    live = live.reshape(group * rows_here, 1)

    mixer_weights = [w_input, w_forget, w_gate_mix, w_out]
    if copies > 1:
        mixer_weights = [gather_bits(weight, copy_masks[::-1]) for weight in mixer_weights]
    mixer_weights = [weight.reshape(copies, own_rows, width) for weight in mixer_weights]

    masked_grad = live_own * cotangent
    masked_own = masked_grad.astype(bf16)
    masked_first = ring(masked_own)

    scale_one, unit_one = norm_rows(inputs)
    rows_all = group * rows_here
    *mixer_kept, mixed, masked_others, mixed_sum = (
        mixer_forward(
            (unit_one * gain_one).astype(bf16),
            *mixer_weights,
            masked_first,
            bound[None, :],
            live,
            copies,
            1,
        )
    )
    stream = inputs + mixed_sum

    hidden_here = w_gate.shape[1]
    gate_w, up_w = (
        lax.all_gather(weight, "dp", axis=0, tiled=True).reshape(group, channels, hidden_here)
        for weight in (w_gate, w_up)
    )
    down_part = w_down.T
    if copies > 1:
        down_part = gather_bits(down_part, copy_masks[::-1]).reshape(channels, hidden_here)

    scale_two, unit_two = norm_rows(stream)
    normed_two = (unit_two * gain_two).astype(bf16)
    out_rows, out_moved, grad_norm_two, *weight_sums = swiglu(
        normed_two, masked_own, masked_first, masked_others, gate_w, up_w, down_part, copies, 4
    )
    if copies > 1:
        weight_sums = [
            scatter_bits(total.reshape(copies, width // data_parts, hidden_here), copy_masks, f32)
            for total in weight_sums
        ]
    grad_gate_mine, grad_up_mine, grad_down_mine = weight_sums
    grad_down_mine = grad_down_mine.T

    gain_two_part = jnp.sum(grad_norm_two * unit_two, axis=0)
    grad_stream = masked_grad + norm_back(grad_norm_two, unit_two, scale_two, gain_two)

    normed_one, mixer_w, out_w, pre, squashed, state, entering = mixer_kept
    grad_inputs, mixer_sums, out_w_sum, small_sums, out_others = mixer_backward(
        grad_stream.astype(bf16),
        normed_one,
        mixer_w,
        out_w,
        pre,
        squashed,
        state,
        mixed,
        unit_one,
        grad_stream,
        entering,
        bound[None, :],
        live,
        gain_one[None, :],
        scale_one,
        gain_two_part[None, :],
        out_rows,
        out_moved,
        copies,
        all_masks,
        3,
    )
    out_sum = lax.dynamic_index_in_dim(out_rows, tensor_index, 0, keepdims=False).astype(f32)
    out_sum += jnp.where(tensor_index > 0, out_others[2].astype(f32), 0.0)
    out_sum += jnp.where(tensor_index < tensor_parts - 1, out_others[3].astype(f32), 0.0)
    output = live_own * (stream + out_sum)
    grad_weights = [mixer_sums[0], mixer_sums[1], mixer_sums[2], out_w_sum]
    if copies > 1:
        grad_weights = [scatter_bits(total, copy_masks, f32) for total in grad_weights]
    grad_weights = [total.reshape(own_rows, width) for total in grad_weights]
    place = (data_index * tensor_parts + tensor_index) * own_rows
    small_own = lax.dynamic_slice(small_sums, (0, place), (3, own_rows))
    return (
        output,
        grad_inputs,
        small_own[0],
        small_own[1],
        small_own[2],
        *grad_weights,
        grad_gate_mine,
        grad_up_mine,
        grad_down_mine,
    )


def solution(mesh):
    both = ("dp", "tensor")
    placed = (
        P(both, None),
        P("dp"),
        P(both),
        P(both),
        P(both),
        P(both, None),
        P(both, None),
        P(both, None),
        P(both, None),
        P("dp", "tensor"),
        P("dp", "tensor"),
        P("tensor", "dp"),
        P(both, None),
    )
    return jax.shard_map(
        on_device,
        mesh=mesh,
        in_specs=placed,
        out_specs=(
            P(both, None),
            P(both, None),
            P(both),
            P(both),
            P(both),
            P(both, None),
            P(both, None),
            P(both, None),
            P(both, None),
            P("dp", "tensor"),
            P("dp", "tensor"),
            P("tensor", "dp"),
        ),
        check_vma=False,
    )
```

```python
import functools

import jax
import jax.numpy as jnp
from jax import lax
from jax.experimental import pallas as pl
from jax.experimental.pallas import tpu as pltpu
from jax.sharding import PartitionSpec as P

epsilon = 1e-06
bf16 = jnp.bfloat16
f32 = jnp.float32


def matmul(left, right):
    return jnp.dot(left, right, preferred_element_type=f32)


def matmul_rt(left, right):
    return lax.dot_general(left, right, (((1,), (1,)), ((), ())), preferred_element_type=f32)


def matmul_lt(left, right):
    return lax.dot_general(left, right, (((0,), (0,)), ((), ())), preferred_element_type=f32)


def silu_of(value):
    return value * jax.nn.sigmoid(value)


def silu_slope(value):
    squash = jax.nn.sigmoid(value)
    return squash * (1.0 + value * (1.0 - squash))


def norm_rows(value):
    scale = lax.rsqrt(jnp.mean(value * value, axis=-1, keepdims=True) + epsilon)
    return (scale, value * scale)


def norm_back(grad_norm, unit, scale, gain):
    scaled = grad_norm * gain
    return scale * (scaled - unit * jnp.mean(scaled * unit, axis=-1, keepdims=True))


def untouched_kernel(*refs):
    pass


def after(value, *others):
    somewhere = pl.BlockSpec(memory_space=pl.ANY)
    return pl.pallas_call(
        untouched_kernel,
        out_shape=jax.ShapeDtypeStruct(value.shape, value.dtype),
        in_specs=[somewhere] * (1 + len(others)),
        out_specs=somewhere,
        input_output_aliases={0: 0},
        cost_estimate=pl.CostEstimate(flops=0, bytes_accessed=0, transcendentals=0),
    )(value, *others)


def swap(value, mask):
    return lax.ppermute(value, "dp", [(i, i ^ mask) for i in range(lax.axis_size("dp"))])


def own_bit(mask):
    return lax.rem(lax.div(lax.axis_index("dp"), mask), 2)


def gather_bits(value, order):
    base = value.shape
    done = []
    for mask in order:
        other = swap(value, mask)
        at = sum(1 for seen in done if seen > mask)
        low = jnp.stack([value, other], axis=at)
        high = jnp.stack([other, value], axis=at)
        value = jnp.where(own_bit(mask) == 0, low, high)
        done.append(mask)
    return value.reshape((1 << len(order),) + base)


def scatter_bits(value, order, sent=bf16, hold=(None, None)):
    count = len(order)
    value = value.reshape((2,) * count + value.shape[1:])
    left = sorted(order, reverse=True)
    for mask in order:
        at = left.index(mask)
        left.remove(mask)
        bit = own_bit(mask)
        send = lax.dynamic_index_in_dim(value, 1 - bit, at, keepdims=False).astype(sent)
        keep = lax.dynamic_index_in_dim(value, bit, at, keepdims=False)
        if hold[0] == count - len(left) - 1:
            send = after(send, hold[1])
        total = keep.astype(f32) + swap(send, mask).astype(f32)
        value = total.astype(sent) if left else total
    return value


def orders(masks):
    down = sorted(masks, reverse=True)
    if len(down) < 3:
        return down, down
    return down, [down[1], down[0]] + down[2:]


def gather_halves(value, masks):
    first, second = orders(masks)
    half = value.shape[-1] // 2
    return gather_bits(value[..., :half], first), gather_bits(value[..., half:], second)


def scatter_halves(left, right, masks):
    first, second = orders(masks)
    return jnp.concatenate(
        [scatter_bits(left, first[::-1]), scatter_bits(right, second[::-1])], axis=-1
    )


def ring(value):
    parts = lax.axis_size("tensor")
    return lax.ppermute(value, "tensor", [(i, (i + 1) % parts) for i in range(parts)])


def ring_blocks(value):
    blocks = [value]
    for _ in range(lax.axis_size("tensor") - 1):
        blocks.append(ring(blocks[-1]))
    return blocks


def ring_scatter(blocks):
    total = blocks[1 % len(blocks)]
    totals = [total]
    for k in range(2, len(blocks) + 1):
        moved = ring(total).astype(f32)
        total = moved + blocks[k % len(blocks)].astype(f32)
        if k < len(blocks):
            total = total.astype(bf16)
            totals.append(total)
    return total, totals


def shifted_blocks(value):
    parts = lax.axis_size("tensor")
    blocks = [value]
    for k in range(1, parts):
        blocks.append(lax.ppermute(value, "tensor", [(i, (i + k) % parts) for i in range(parts)]))
    return blocks


def scatter_straight(value):
    here = lax.axis_index("tensor")
    parts = lax.axis_size("tensor")
    total = lax.dynamic_index_in_dim(value, here, 0, keepdims=False)
    for k in range(1, parts):
        send = lax.dynamic_index_in_dim(value, lax.rem(here + k, parts), 0, keepdims=False)
        total += lax.ppermute(send, "tensor", [(i, (i + k) % parts) for i in range(parts)])
    return total


def in_order(blocks):
    here = lax.axis_index("tensor")
    parts = len(blocks)
    stacked = jnp.stack(blocks[::-1] + blocks[::-1])
    return lax.dynamic_slice_in_dim(stacked, parts - 1 - here, parts, 0)


def partner(mask):
    me = lax.axis_index("dp")
    return me + mask * (1 - 2 * lax.rem(lax.div(me, mask), 2))


def greet(masks, ring_too=False):
    barrier = pltpu.get_barrier_semaphore()
    others = [{"dp": partner(mask)} for mask in masks]
    if ring_too:
        others += [{"tensor": beside(1)}, {"tensor": beside(-1)}]
    for other in others:
        pl.semaphore_signal(
            barrier, inc=1, device_id=other, device_id_type=pl.DeviceIdType.MESH
        )
    pl.semaphore_wait(barrier, len(others))


def beside(step):
    parts = lax.axis_size("tensor")
    return lax.rem(lax.axis_index("tensor") + step + parts, parts)


def slot_of(copies, masks):
    me = lax.axis_index("dp")
    for mask in masks:
        me = me + mask * (1 - 2 * lax.rem(lax.div(me, mask), 2))
    return lax.div(me, copies)


def to_right(source, target, send_sem, recv_sem):
    return pltpu.make_async_remote_copy(
        src_ref=source,
        dst_ref=target,
        send_sem=send_sem,
        recv_sem=recv_sem,
        device_id={"tensor": beside(1)},
        device_id_type=pl.DeviceIdType.MESH,
    )


def along(step, source, target, send_sem, recv_sem):
    return pltpu.make_async_remote_copy(
        src_ref=source,
        dst_ref=target,
        send_sem=send_sem,
        recv_sem=recv_sem,
        device_id={"tensor": beside(step)},
        device_id_type=pl.DeviceIdType.MESH,
    )


def plane_gather_steps(copies, value_ref, all_ref, own_sem, send_sem, recv_sem):
    near, one, two = copies, 2 * copies, 4 * copies
    half = value_ref.shape[0] // 2
    top, low = pl.ds(0, half), pl.ds(half, half)
    mine = slot_of(copies, ())
    at_one, at_two = slot_of(copies, (one,)), slot_of(copies, (two,))
    at_both = slot_of(copies, (one, two))
    local = pltpu.make_async_copy(value_ref, all_ref.at[mine], own_sem)
    sent = []
    last = []

    def send(source, slot, rows, mask):
        index = len(sent)
        copy = pltpu.make_async_remote_copy(
            src_ref=source,
            dst_ref=all_ref.at[slot, rows],
            send_sem=send_sem.at[index],
            recv_sem=recv_sem.at[index],
            device_id={"dp": partner(mask)},
            device_id_type=pl.DeviceIdType.MESH,
        )
        copy.start()
        sent.append(copy)
        if mask == near:
            last.append(copy)
        return copy

    def forward(slot, rows, mask):
        return send(all_ref.at[slot, rows], slot, rows, mask)

    first = []
    second = []

    def begin():
        local.start()
        first.append(send(value_ref.at[top], mine, top, two))
        first.append(send(value_ref.at[low], mine, low, one))
        first.append(send(value_ref.at[low], mine, low, two))
        first.append(send(value_ref.at[top], mine, top, one))
        send(value_ref.at[top], mine, top, near)
        send(value_ref.at[low], mine, low, near)

    def pass_first():
        first[0].wait_recv()
        second.append(forward(at_two, top, one))
        forward(at_two, top, near)
        first[1].wait_recv()
        second.append(forward(at_one, low, two))
        forward(at_one, low, near)

    def pass_second():
        first[2].wait_recv()
        forward(at_two, low, near)
        first[3].wait_recv()
        forward(at_one, top, near)

    def pass_last():
        second[0].wait_recv()
        forward(at_both, top, near)
        second[1].wait_recv()
        forward(at_both, low, near)

    def arrive(some=slice(None)):
        for copy in last[some]:
            copy.wait_recv()
        if some == slice(None):
            local.wait()

    def finish():
        for copy in sent:
            copy.wait_send()

    return begin, pass_first, pass_second, pass_last, arrive, finish


def plane_scatter_steps(
    copies, sum_ref, near_ref, one_ref, two_ref, part_ref,
    send_sem, recv_sem, product, between,
):
    near, one, two = copies, 2 * copies, 4 * copies
    rows, width = sum_ref.shape
    half = rows // 2
    top, low = pl.ds(0, half), pl.ds(half, half)
    tile = min(512, width)
    flips = [(), (one,), (two,), (one, two)]
    copies_out = []

    def send(source, target, mask):
        index = len(copies_out)
        copy = pltpu.make_async_remote_copy(
            src_ref=source,
            dst_ref=target,
            send_sem=send_sem.at[index],
            recv_sem=recv_sem.at[index],
            device_id={"dp": partner(mask)},
            device_id_type=pl.DeviceIdType.MESH,
        )
        copy.start()
        copies_out.append(copy)
        return copy

    def each_tile(body):
        @pl.loop(0, width // tile)
        def _(k):
            body(pl.ds(pl.multiple_of(k * tile, tile), tile))

    arriving = {}
    for k in (3, 1, 2, 0):
        slot = slot_of(copies, flips[k] + (near,))

        def theirs(columns, k=k, slot=slot):
            part_ref[k, :, columns] = product(slot, columns).astype(bf16)

        each_tile(theirs)
        arriving[k] = send(part_ref.at[k], near_ref.at[k], near)

    between("sent")

    def added(k):
        slot = slot_of(copies, flips[k])
        arriving[k].wait_recv()

        def mine(columns):
            total = product(slot, columns) + near_ref[k, :, columns].astype(f32)
            if k == 0:
                sum_ref[:, columns] = total
            else:
                near_ref[k, :, columns] = total.astype(bf16)

        each_tile(mine)

    added(3)
    one_first = send(near_ref.at[3, top], one_ref.at[0], one)
    two_first = send(near_ref.at[3, low], two_ref.at[0], two)
    added(1)
    one_second = send(near_ref.at[1, top], one_ref.at[1], one)
    added(2)
    two_second = send(near_ref.at[2, low], two_ref.at[1], two)
    added(0)
    between("added")

    one_first.wait_recv()

    def pass_top(columns):
        total = near_ref[2, top, columns].astype(f32) + one_ref[0, :, columns].astype(f32)
        near_ref[2, top, columns] = total.astype(bf16)

    each_tile(pass_top)
    two_last = send(near_ref.at[2, top], two_ref.at[2], two)
    between("top")
    two_first.wait_recv()

    def pass_low(columns):
        total = near_ref[1, low, columns].astype(f32) + two_ref[0, :, columns].astype(f32)
        near_ref[1, low, columns] = total.astype(bf16)

    each_tile(pass_low)
    one_last = send(near_ref.at[1, low], one_ref.at[2], one)
    between("low")

    def finish(rows_at, first, at_first, second, at_second):
        def body(columns):
            sum_ref[rows_at, columns] += (
                first[at_first, :, columns].astype(f32) + second[at_second, :, columns].astype(f32)
            )

        each_tile(body)

    one_second.wait_recv()
    two_last.wait_recv()
    finish(top, one_ref, 1, two_ref, 2)
    two_second.wait_recv()
    one_last.wait_recv()
    finish(low, two_ref, 1, one_ref, 2)
    for copy in copies_out:
        copy.wait_send()


def column_tiles(width, most=512):
    return [(at, min(most, width - at)) for at in range(0, width, most)]


def swiglu_kernel(
    copies,
    normed_ref, own_ref, below_ref, above_ref, others_ref, gate_hbm, up_hbm, down_ref,
    rows_out, moved_out, norm_sum, gate_sum, up_sum, down_sum,
    normed, masked, gate_w, up_w, down_w, hidden, gate_low, up_low, back, rows, ring_buf,
    one_buf, two_buf, lead, lead_near, in_sem, out_sem, gather_send, gather_recv, send_sem,
    recv_sem, sum_send, sum_recv, near_send, near_recv, one_send, one_recv, two_send, two_recv,
    ready_sem, moved_send, moved_recv,
):
    parts = lax.axis_size("tensor")
    near, one, two = copies, 2 * copies, 4 * copies
    greet((near, one, two), True)
    own = pltpu.make_async_copy(normed_ref, normed.at[0], in_sem.at[0])
    own.start()
    gather = plane_gather_steps(
        copies, down_ref, down_w, in_sem.at[4], gather_send, gather_recv
    )
    gather[0]()
    loads = [
        pltpu.make_async_copy(gate_hbm, gate_w, in_sem.at[1]),
        pltpu.make_async_copy(up_hbm, up_w, in_sem.at[2]),
        pltpu.make_async_copy(own_ref, masked.at[0], in_sem.at[3]),
    ]
    own.wait()
    for load in loads:
        load.start()
    here = lax.axis_index("tensor")
    at_start, at_end = here == 0, here == parts - 1

    def load_masked(k, source):
        return pltpu.make_async_copy(source, masked.at[k], in_sem.at[4 + k])

    for k in range(1, parts):
        far = load_masked(k, others_ref.at[beside(-k)])
        if 1 < k < parts - 1:
            far.start()
        else:
            next_to, ref = (at_start, below_ref) if k == 1 else (at_end, above_ref)

            @pl.when(next_to)
            def _():
                far.start()

            @pl.when(jnp.logical_not(next_to))
            def _():
                load_masked(k, ref).start()

        loads.append(far)
    _, block_rows, width = normed.shape
    hidden_width = hidden.shape[2]
    share = width // 8
    half = share // 2
    many = 2
    tile = many * share
    both = [pl.ds(n * (block_rows // 2), block_rows // 2) for n in range(2)]

    def hop(k, n):
        return to_right(
            normed.at[k, both[n]], normed.at[k + 1, both[n]], send_sem.at[k, n], recv_sem.at[k, n]
        )

    def sum_hop(k, n):
        return to_right(
            back.at[k + 1, both[n]], ring_buf.at[k, both[n]], sum_send.at[k, n], sum_recv.at[k, n]
        )

    for n in range(2):
        hop(0, n).start()
    for load in loads:
        load.wait()
    gather[1]()
    gather[2]()
    for n in range(2):
        hop(0, n).wait_recv()
        hop(1, n).start()
    gather[3]()
    gather[4]()

    def store(k):
        home = lax.rem(lax.axis_index("tensor") + parts - k, parts)
        slot = lax.rem(k, 2)
        return pltpu.make_async_copy(rows.at[slot], rows_out.at[home], out_sem.at[slot])

    def front(k):
        for at, size in column_tiles(hidden_width):
            columns = pl.ds(at, size)

            def weight(ref):
                return ref[:, :, columns].reshape(width, size)

            glu_gate = matmul(normed[k], weight(gate_w))
            glu_up = matmul(normed[k], weight(up_w))
            grad_hidden = matmul(masked[k], weight(down_w))
            squash = jax.nn.sigmoid(glu_gate)
            act = glu_gate * squash
            slope = squash * (1.0 + glu_gate * (1.0 - squash))
            hidden[k, :, columns] = (act * glu_up).astype(bf16)
            gate_low[k, :, columns] = (grad_hidden * glu_up * slope).astype(bf16)
            up_low[k, :, columns] = (grad_hidden * act).astype(bf16)

    def rear(k):
        slot = lax.rem(k, 2)

        @pl.loop(0, 8 // many)
        def _(n):
            some = pl.ds(pl.multiple_of(n * tile, tile), tile)

            def weight(ref):
                return ref[pl.ds(n * many, many)].reshape(tile, hidden_width)

            back[k, :, some] = (
                matmul_rt(gate_low[k], weight(gate_w)) + matmul_rt(up_low[k], weight(up_w))
            ).astype(bf16)
            rows[slot, :, some] = matmul_rt(hidden[k], weight(down_w)).astype(bf16)

        store(k).start()

    def block(k, nothing):
        for n in range(2):

            @pl.when(jnp.logical_and(k > 0, k < parts - 2))
            def _():
                hop(k, n).wait_recv()
                hop(k + 1, n).start()

            @pl.when(k == parts - 1)
            def _():
                hop(parts - 2, n).wait_recv()
                sum_hop(0, n).start()

        front(k)

        @pl.when(k > 1)
        def _():
            store(k - 2).wait()

        @pl.when(k < parts - 1)
        def _():
            rear(k)

        return nothing

    lax.fori_loop(0, parts, block, 0)

    tall = parts * block_rows
    kinds = (
        (normed, gate_low, gate_w, gate_sum),
        (normed, up_low, up_w, up_sum),
        (masked, hidden, down_w, down_sum),
    )

    def product(kind, slot, store):
        left, right, _, _ = kinds[kind]
        some = pl.ds(pl.multiple_of(slot * share, share), share)
        for at, size in column_tiles(hidden_width):
            columns = pl.ds(at, size)
            store(
                columns,
                matmul_lt(
                    left[:, :, some].reshape(tall, share), right[:, :, columns].reshape(tall, size)
                ),
            )

    def across(source, target, send, recv, mask):
        return pltpu.make_async_remote_copy(
            src_ref=source,
            dst_ref=target,
            send_sem=send,
            recv_sem=recv,
            device_id={"dp": partner(mask)},
            device_id_type=pl.DeviceIdType.MESH,
        )

    top, low = pl.ds(0, half), pl.ds(half, half)

    def near_copy(kind, k):
        room = kinds[kind][2]
        return across(
            room.at[k], room.at[4 + k], near_send.at[kind, k], near_recv.at[kind, k], near
        )

    def lead_copy(kind):
        return across(
            lead.at[kind], lead_near.at[kind], near_send.at[kind, 3], near_recv.at[kind, 3], near
        )

    def one_copy(kind, n):
        room = kinds[kind][2]
        source = (lead_near.at[kind, top], room.at[5, top], room.at[5, low])[n]
        return across(
            source, one_buf.at[kind, n], one_send.at[kind, n], one_recv.at[kind, n], one
        )

    def two_copy(kind, n):
        room = kinds[kind][2]
        source = (lead_near.at[kind, low], room.at[6, low], room.at[6, top])[n]
        return across(
            source, two_buf.at[kind, n], two_send.at[kind, n], two_recv.at[kind, n], two
        )

    def flipped(k, near_too):
        me = lax.axis_index("dp")

        def turn(mask, on):
            return on * mask * (1 - 2 * lax.rem(lax.div(me, mask), 2))

        there = me + turn(one, lax.rem(k, 2)) + turn(two, lax.div(k, 2)) + turn(near, near_too)
        return lax.div(there, copies)

    def sum_step(k):
        for n in range(2):
            sum_hop(k, n).wait_recv()

            @pl.loop(0, 8 // many)
            def _(at):
                some = pl.ds(pl.multiple_of(at * tile, tile), tile)
                moved = ring_buf[k, both[n], some].astype(f32)
                if k + 1 < parts - 1:
                    total = back[k + 2, both[n], some].astype(f32) + moved
                    back[k + 2, both[n], some] = total.astype(bf16)
                else:
                    norm_sum[both[n], some] = back[0, both[n], some].astype(f32) + moved

            if k + 1 < parts - 1:
                sum_hop(k + 1, n).start()

    def keep(ref, at):
        def store(columns, value):
            ref[at, :, columns] = value.astype(bf16)

        return store

    def add(ref, at):
        def store(columns, value):
            ref[at, :, columns] = (value + ref[at, :, columns].astype(f32)).astype(bf16)

        return store

    def add_wide(total_ref, ref, at):
        def store(columns, value):
            total_ref[:, columns] = value + ref[at, :, columns].astype(f32)

        return store

    for kind in range(3):
        product(kind, flipped(3, 1), keep(lead, kind))
        lead_copy(kind).start()
    for kind in range(3):
        lead_copy(kind).wait_recv()
        product(kind, flipped(3, 0), add(lead_near, kind))
        one_copy(kind, 0).start()
        two_copy(kind, 0).start()
    rear(parts - 1)

    gather[5]()
    pl.semaphore_signal(
        ready_sem,
        inc=1,
        device_id={"dp": partner(near)},
        device_id_type=pl.DeviceIdType.MESH,
    )
    pl.semaphore_wait(ready_sem, 1)

    def theirs(k):
        for kind in range(3):
            product(kind, flipped(k, 1), keep(kinds[kind][2], k))
            near_copy(kind, k).start()

    def mine(k):
        for kind in range(3):
            near_copy(kind, k).wait_recv()
            product(kind, flipped(k, 0), add(kinds[kind][2], 4 + k))
            if k == 1:
                one_copy(kind, 1).start()
            else:
                two_copy(kind, 1).start()

    sum_step(0)
    theirs(1)
    theirs(2)
    mine(1)
    mine(2)
    theirs(0)
    for kind in range(3):
        one_copy(kind, 0).wait_recv()
        room = kinds[kind][2]
        room[6, top] = (room[6, top].astype(f32) + one_buf[kind, 0].astype(f32)).astype(bf16)
        two_copy(kind, 2).start()
        two_copy(kind, 0).wait_recv()
        room[5, low] = (room[5, low].astype(f32) + two_buf[kind, 0].astype(f32)).astype(bf16)
        one_copy(kind, 2).start()
    for k in range(1, parts - 2):
        sum_step(k)
    for kind in range(3):
        near_copy(kind, 0).wait_recv()
        room, total_ref = kinds[kind][2:]
        product(kind, flipped(0, 0), add_wide(total_ref, room, 4))
    sum_step(parts - 2)
    for k in (parts - 2, parts - 1):
        store(k).wait()
    moved_up = along(1, rows_out.at[parts - 1], moved_out, moved_send, moved_recv)
    moved_down = along(-1, rows_out.at[0], moved_out, moved_send, moved_recv)

    @pl.when(at_start)
    def _():
        moved_up.start()

    @pl.when(at_end)
    def _():
        moved_down.start()

    for kind in range(3):
        total_ref = kinds[kind][3]
        one_copy(kind, 1).wait_recv()
        two_copy(kind, 2).wait_recv()
        total_ref[:half, :] += one_buf[kind, 1].astype(f32) + two_buf[kind, 2].astype(f32)
        two_copy(kind, 1).wait_recv()
        one_copy(kind, 2).wait_recv()
        total_ref[half:, :] += two_buf[kind, 1].astype(f32) + one_buf[kind, 2].astype(f32)
    for kind in range(3):
        lead_copy(kind).wait_send()
        for k in range(3):
            near_copy(kind, k).wait_send()
        for n in range(3):
            one_copy(kind, n).wait_send()
            two_copy(kind, n).wait_send()
    for k in range(parts - 1):
        for n in range(2):
            hop(k, n).wait_send()
            sum_hop(k, n).wait_send()

    @pl.when(at_start)
    def _():
        moved_up.wait_send()

    @pl.when(at_end)
    def _():
        moved_down.wait_send()

    @pl.when(jnp.logical_not(jnp.logical_or(at_start, at_end)))
    def _():
        moved_up.wait_recv()


def swiglu(normed, own, below, above, others, gate_w, up_w, down_w, copies, collective):
    parts = lax.axis_size("tensor")
    rows, width = normed.shape
    hidden = gate_w.shape[2]
    share = width // 8
    somewhere = pl.BlockSpec(memory_space=pl.ANY)
    vmem = pl.BlockSpec(memory_space=pltpu.VMEM)
    wide, narrow = (parts, rows, width), (parts, rows, hidden)
    return pl.pallas_call(
        functools.partial(swiglu_kernel, copies),
        out_shape=[
            jax.ShapeDtypeStruct(wide, bf16),
            jax.ShapeDtypeStruct((rows, width), bf16),
            jax.ShapeDtypeStruct((rows, width), f32),
        ]
        + [jax.ShapeDtypeStruct((share, hidden), f32)] * 3,
        in_specs=[somewhere] * 8,
        out_specs=[somewhere] * 2 + [vmem] * 4,
        scratch_shapes=[pltpu.VMEM(wide, bf16)] * 2
        + [pltpu.VMEM((8, share, hidden), bf16)] * 3
        + [pltpu.VMEM(narrow, bf16)] * 3
        + [
            pltpu.VMEM(wide, bf16),
            pltpu.VMEM((2, rows, width), bf16),
            pltpu.VMEM((parts - 1, rows, width), bf16),
        ]
        + [pltpu.VMEM((3, 3, share // 2, hidden), bf16)] * 2
        + [pltpu.VMEM((3, share, hidden), bf16)] * 2
        + [pltpu.SemaphoreType.DMA((8,)), pltpu.SemaphoreType.DMA((2,))]
        + [pltpu.SemaphoreType.DMA((14,))] * 2
        + [pltpu.SemaphoreType.DMA((parts - 1, 2))] * 4
        + [pltpu.SemaphoreType.DMA((3, 4))] * 2
        + [pltpu.SemaphoreType.DMA((3, 3))] * 4
        + [pltpu.SemaphoreType.REGULAR]
        + [pltpu.SemaphoreType.DMA] * 2,
        compiler_params=pltpu.CompilerParams(
            collective_id=collective, has_side_effects=True, vmem_limit_bytes=62 * 1024 * 1024
        ),
        cost_estimate=pl.CostEstimate(
            flops=18 * parts * rows * width * hidden,
            bytes_accessed=1100 * rows * width,
            transcendentals=parts * rows * hidden,
        ),
    )(normed, own, below, above, others, gate_w, up_w, down_w)


def greet_all(copies, masks):
    barrier = pltpu.get_barrier_semaphore()
    others = [{"dp": group_member(copies, k)} for k in range(1, 8)]
    others += [{"tensor": beside(k)} for k in range(1, lax.axis_size("tensor"))]
    others += [{"dp": partner(mask)} for mask in masks]
    for other in others:
        pl.semaphore_signal(
            barrier, inc=1, device_id=other, device_id_type=pl.DeviceIdType.MESH
        )
    pl.semaphore_wait(barrier, len(others))


def group_member(copies, step):
    me = lax.axis_index("dp")
    return lax.rem(lax.div(me, copies) + step, 8) * copies + lax.rem(me, copies)


def mixer_forward_kernel(
    copies,
    own_ref, input_hbm, forget_hbm, gate_hbm, out_hbm, below_hbm, above_hbm, bound_ref, live_ref,
    normed_out, weights_out, project_out, pre_out, squash_out, state_out, entering_out, mixed_out,
    masked_out, sum_ref,
    normed, weights, project, pre, squashed, forget, state, decay, ends, entering, mixed,
    near_buf, one_buf, two_buf, part_buf,
    own_sem, gather_send, gather_recv, spread_send, spread_recv, spread_own, up_send, down_send, line_recv,
    carry_send, carry_recv, scatter_send, scatter_recv, masked_up, masked_down, masked_recv, out_sem,
):
    parts = lax.axis_size("tensor")
    here = lax.axis_index("tensor")
    seqs, rows, width = normed.shape
    strips, _, lanes = forget.shape
    channels = strips * lanes
    mine = slot_of(copies, ())
    greet_all(copies, ())

    def own_rows_of(index):
        return pl.ds(pl.multiple_of(index * copies, copies), copies)

    def columns_of(index):
        return pl.ds(pl.multiple_of(index * channels, channels), channels)

    spread = []
    for kind, source in enumerate((input_hbm, forget_hbm, gate_hbm)):
        target = weights.at[kind, own_rows_of(mine), here]
        kept = pltpu.make_async_copy(
            source.at[:, :, columns_of(mine)], target, spread_own.at[kind]
        )
        sent = []
        for k in range(1, 8):
            there = group_member(copies, k)
            sent.append(
                pltpu.make_async_remote_copy(
                    src_ref=source.at[:, :, columns_of(lax.div(there, copies))],
                    dst_ref=target,
                    send_sem=spread_send.at[kind, k - 1],
                    recv_sem=spread_recv.at[kind, k - 1],
                    device_id={"dp": there},
                    device_id_type=pl.DeviceIdType.MESH,
                )
            )
        spread.append((kept, sent))

    def block_of(kind, block):
        return project.at[:, block] if kind == 3 else weights.at[kind, :, block]

    def line_copy(kind, k, step):
        block = here - step * k
        target = block_of(kind, block)
        source = out_hbm if kind == 3 and k == 0 else target
        sems = up_send if step == 1 else down_send
        return along(step, source, target, sems.at[kind, k], line_recv.at[kind, block])

    def goes(k, step):
        if step == 1:
            return jnp.logical_and(here >= k, here < parts - 1)
        return jnp.logical_and(here + k < parts, here > 0)

    def comes(k, step):
        return here >= k if step == 1 else here + k < parts

    def line_step(kind, k):
        for step in (1, -1):
            if k > 0:

                @pl.when(comes(k, step))
                def _():
                    line_copy(kind, k, step).wait_recv()

            if k < parts - 1:

                @pl.when(goes(k, step))
                def _():
                    line_copy(kind, k, step).start()

    def spread_arrive(kind):
        kept, sent = spread[kind]
        kept.wait()
        for copy in sent:
            copy.wait_recv()

    out_kept = pltpu.make_async_copy(out_hbm, project.at[:, here], spread_own.at[3])
    out_kept.start()
    for kept, sent in spread:
        kept.start()
        for copy in sent:
            copy.start()
    line_step(3, 0)
    begin, pass_first, pass_second, pass_last, arrive, finish = plane_gather_steps(
        copies, own_ref, normed, own_sem, gather_send, gather_recv
    )
    begin()
    spread_arrive(0)
    line_step(0, 0)
    spread_arrive(1)
    line_step(1, 0)
    spread_arrive(2)
    pass_first()
    line_step(0, 1)
    pass_second()
    line_step(1, 1)
    line_step(0, 2)
    line_step(1, 2)
    line_step(0, 3)
    line_step(2, 0)
    pass_last()
    line_step(1, 3)
    line_step(3, 1)
    arrive()

    many = 2

    def project_rows(kind, at):
        left = normed[pl.ds(at * many, many)].reshape(many * rows, width)
        return matmul(left, weights[kind].reshape(width, channels))

    def rows_at(at):
        return pl.ds(pl.multiple_of(at * many * rows, many * rows), many * rows)

    def strip_of(value, n):
        return value[:, n * lanes : (n + 1) * lanes]

    @pl.loop(0, seqs // many)
    def _(at):
        some = rows_at(at)
        value = project_rows(0, at)
        pre[0, some, :] = value
        inflow = live_ref[some, :] * silu_of(value)
        for n in range(strips):
            state[n, some, :] = strip_of(inflow, n)

    line_step(2, 1)

    @pl.loop(0, seqs // many)
    def _(at):
        some = rows_at(at)
        squash = jax.nn.sigmoid(project_rows(1, at))
        bound = bound_ref[...]
        value = bound + (1.0 - bound) * squash
        for n in range(strips):
            squashed[n, some, :] = strip_of(squash, n)
            forget[n, some, :] = strip_of(value, n)
            state[n, some, :] = (1.0 - strip_of(value, n)) * state[n, some, :]

    line_step(3, 2)

    def step(at, carry):
        some = pl.ds(at, seqs, stride=rows)
        following = []
        for n, (total, product) in enumerate(carry):
            keep = forget[n, some, :]
            total = keep * total + state[n, some, :]
            product = product * keep
            state[n, some, :] = total
            decay[n, some, :] = product
            following.append((total, product))
        return tuple(following)

    start = (jnp.zeros((seqs, lanes), f32), jnp.ones((seqs, lanes), f32))
    carry = lax.fori_loop(0, rows, step, (start,) * strips, unroll=8)
    for n, (total, product) in enumerate(carry):
        ends[here, 0, :, n * lanes : (n + 1) * lanes] = total
        ends[here, 1, :, n * lanes : (n + 1) * lanes] = product
    carries = []
    for k in range(1, parts):
        copy = pltpu.make_async_remote_copy(
            src_ref=ends.at[here],
            dst_ref=ends.at[here],
            send_sem=carry_send.at[k - 1],
            recv_sem=carry_recv.at[k - 1],
            device_id={"tensor": beside(k)},
            device_id_type=pl.DeviceIdType.MESH,
        )
        copy.start()
        carries.append(copy)
    line_step(2, 2)

    def masked_copy(k, step):
        block = here - step * k
        if k > 1:
            source = masked_out.at[block]
        else:
            source = below_hbm if step == 1 else above_hbm
        sems = masked_up if step == 1 else masked_down
        return along(step, source, masked_out.at[block], sems.at[k], masked_recv.at[block])

    def masked_step(k):
        for step in (1, -1):
            if k > 1:

                @pl.when(comes(k, step))
                def _():
                    masked_copy(k, step).wait_recv()

            if k < parts - 1:

                @pl.when(goes(k, step))
                def _():
                    masked_copy(k, step).start()

    for copy in carries:
        copy.wait_recv()
    coming = jnp.zeros((seqs, channels), f32)
    entered = coming
    for k in range(parts - 1):
        coming = ends[k, 1] * coming + ends[k, 0]
        entered = jnp.where(here == k + 1, coming, entered)
    for n in range(seqs):
        entering[n] = entered[n : n + 1]
    line_step(3, 3)
    line_step(2, 3)

    @pl.loop(0, seqs // many)
    def _(at):
        some = rows_at(at)
        value = project_rows(2, at)
        pre[1, some, :] = value
        act = silu_of(value)
        for n in range(many):
            slot = at * many + n
            one = pl.ds(pl.multiple_of(slot * rows, rows), rows)
            for strip in range(strips):
                columns = slice(strip * lanes, (strip + 1) * lanes)
                whole = state[strip, one, :] + (
                    decay[strip, one, :] * entering[slot, :, columns]
                )
                state[strip, one, :] = whole
                mixed[slot, :, columns] = (
                    whole * act[n * rows : (n + 1) * rows, columns]
                ).astype(bf16)

    out_kept.wait()
    stores = [
        pltpu.make_async_copy(source, target, out_sem.at[n])
        for n, (source, target) in enumerate(
            (
                (normed, normed_out),
                (weights, weights_out),
                (project, project_out),
                (pre, pre_out),
                (squashed, squash_out),
                (state, state_out),
                (entering, entering_out),
                (mixed, mixed_out),
            )
        )
    ]
    for store in stores:
        store.start()

    def out_product(slot, columns):
        right = project[:, :, :, columns]
        return matmul(mixed[slot], right.reshape(channels, right.shape[-1]))

    masked_step(1)

    def between(point):
        if point == "low":
            masked_step(2)

    plane_scatter_steps(
        copies, sum_ref, near_buf, one_buf, two_buf, part_buf, scatter_send, scatter_recv,
        out_product, between,
    )
    masked_step(3)
    for k in (1, 2):
        for step in (1, -1):

            @pl.when(goes(k, step))
            def _():
                masked_copy(k, step).wait_send()

    finish()
    for kept, sent in spread:
        for copy in sent:
            copy.wait_send()
    for kind in range(4):
        for k in range(parts - 1):
            for step in (1, -1):

                @pl.when(goes(k, step))
                def _():
                    line_copy(kind, k, step).wait_send()

    for copy in carries:
        copy.wait_send()
    for store in stores:
        store.wait()


def mixer_forward(
    normed, w_input, w_forget, w_gate, w_out, below, above, bound, live, copies, collective
):
    parts = lax.axis_size("tensor")
    rows, width = normed.shape
    channels = width // 8
    own_rows = w_input.shape[1]
    somewhere = pl.BlockSpec(memory_space=pl.ANY)
    vmem = pl.BlockSpec(memory_space=pltpu.VMEM)
    wide = (8, rows, width)
    weights = (3, 8 * copies, parts, own_rows, channels)
    project = (copies, parts, own_rows, width)
    flat = (8 * rows, channels)
    lanes = min(128, channels)
    strips = (channels // lanes, 8 * rows, lanes)
    shaped = (8, rows, channels)
    half = rows // 2
    dma = pltpu.SemaphoreType.DMA
    return pl.pallas_call(
        functools.partial(mixer_forward_kernel, copies),
        out_shape=[
            jax.ShapeDtypeStruct(wide, bf16),
            jax.ShapeDtypeStruct(weights, bf16),
            jax.ShapeDtypeStruct(project, bf16),
            jax.ShapeDtypeStruct((2,) + flat, f32),
            jax.ShapeDtypeStruct(strips, f32),
            jax.ShapeDtypeStruct(strips, f32),
            jax.ShapeDtypeStruct((8, 1, channels), f32),
            jax.ShapeDtypeStruct(shaped, bf16),
            jax.ShapeDtypeStruct((parts, rows, width), bf16),
            jax.ShapeDtypeStruct((rows, width), f32),
        ],
        in_specs=[somewhere] * 7 + [vmem] * 2,
        out_specs=[somewhere] * 9 + [vmem],
        scratch_shapes=[
            pltpu.VMEM(wide, bf16),
            pltpu.VMEM(weights, bf16),
            pltpu.VMEM(project, bf16),
            pltpu.VMEM((2,) + flat, f32),
            pltpu.VMEM(strips, f32),
            pltpu.VMEM(strips, f32),
            pltpu.VMEM(strips, f32),
            pltpu.VMEM(strips, f32),
            pltpu.VMEM((parts, 2, 8, channels), f32),
            pltpu.VMEM((8, 1, channels), f32),
            pltpu.VMEM(shaped, bf16),
            pltpu.VMEM((4, rows, width), bf16),
            pltpu.VMEM((3, half, width), bf16),
            pltpu.VMEM((3, half, width), bf16),
            pltpu.VMEM((4, rows, width), bf16),
            dma,
            dma((14,)),
            dma((14,)),
            dma((3, 7)),
            dma((3, 7)),
            dma((4,)),
            dma((4, parts - 1)),
            dma((4, parts - 1)),
            dma((4, parts)),
            dma((parts - 1,)),
            dma((parts - 1,)),
            dma((10,)),
            dma((10,)),
            dma((parts - 1,)),
            dma((parts - 1,)),
            dma((parts,)),
            dma((8,)),
        ],
        compiler_params=pltpu.CompilerParams(
            collective_id=collective, has_side_effects=True, vmem_limit_bytes=56 * 1024 * 1024
        ),
        cost_estimate=pl.CostEstimate(
            flops=8 * rows * width * width,
            bytes_accessed=900 * rows * width,
            transcendentals=0,
        ),
    )(normed, w_input, w_forget, w_gate, w_out, below, above, bound, live)


def mixer_backward_kernel(
    copies, masks,
    own_ref, normed_hbm, weights_hbm, project_hbm, pre_hbm, squash_hbm, state_hbm, mixed_hbm,
    unit_hbm, stream_hbm, entering_ref, bound_ref, live_ref, gain_ref, scale_ref, gain_two_ref,
    rows_hbm, moved_hbm,
    result_ref, input_sum, forget_sum, gate_sum, project_sum, small_sums, moved_out,
    rows_buf, weights, project, pre, squashed, state, mixed, unit, stream, drive, decay, ends,
    entered, grad_pre, grad_w, grad_project, line_w, line_project, bound_sum, whole_w, spread_w,
    small_recv, small_ring, near_buf, one_buf, two_buf, part_buf,
    load_sem, gather_send, gather_recv, carry_send, carry_recv, up_send, down_send, line_recv,
    scatter_send, scatter_recv, spread_send, spread_recv, spread_own, small_send, small_got,
    moved_sem, moved_send, moved_recv,
):
    parts = lax.axis_size("tensor")
    here = lax.axis_index("tensor")
    seqs, rows, width = rows_buf.shape
    strips, _, lanes = drive.shape
    channels = strips * lanes
    own_rows = weights.shape[3]
    weight_sums = (input_sum, forget_sum, gate_sum)
    near, one, two = copies, 2 * copies, 4 * copies
    mine = slot_of(copies, ())
    greet_all(copies, masks)
    begin, pass_first, pass_second, pass_last, arrive, finish = plane_gather_steps(
        copies, own_ref, rows_buf, load_sem.at[0], gather_send, gather_recv
    )
    begin()

    at_start, at_end = here == 0, here == parts - 1
    inside = jnp.logical_not(jnp.logical_or(at_start, at_end))
    low_half = here == 1

    def fetch(block, came, first, second):
        loads = (
            pltpu.make_async_copy(rows_hbm.at[block], part_buf.at[first], moved_sem.at[0]),
            pltpu.make_async_copy(came, part_buf.at[second], moved_sem.at[1]),
        )
        for load in loads:
            load.start()
        for load in loads:
            load.wait()
        part_buf[first] = (
            part_buf[first].astype(f32) + part_buf[second].astype(f32)
        ).astype(bf16)

    def moved_copy(n, step, source):
        return along(step, source, moved_out.at[n], moved_send.at[n], moved_recv.at[n])

    def moved_second():
        @pl.when(at_start)
        def _():
            moved_copy(0, 1, rows_hbm.at[2]).start()

        @pl.when(at_end)
        def _():
            moved_copy(1, -1, rows_hbm.at[1]).start()

        @pl.when(inside)
        def _():
            fetch(3 - 3 * (here - 1), moved_hbm, 0, 1)

        @pl.when(low_half)
        def _():
            moved_copy(0, 1, part_buf.at[0]).start()

        @pl.when(here == 2)
        def _():
            moved_copy(1, -1, part_buf.at[0]).start()

    def moved_last():
        @pl.when(at_start)
        def _():
            moved_copy(0, 1, rows_hbm.at[2]).wait_send()
            moved_copy(2, 1, rows_hbm.at[1]).start()

        @pl.when(at_end)
        def _():
            moved_copy(1, -1, rows_hbm.at[1]).wait_send()
            moved_copy(3, -1, rows_hbm.at[2]).start()

        @pl.when(inside)
        def _():
            moved_copy(0, 1, part_buf.at[0]).wait_recv()
            fetch(here + 1, moved_out.at[0], 1, 2)
            moved_copy(2, 1, part_buf.at[1]).start()

        @pl.when(low_half)
        def _():
            moved_copy(0, 1, part_buf.at[0]).wait_send()

        @pl.when(here == 2)
        def _():
            moved_copy(1, -1, part_buf.at[0]).wait_send()

        @pl.when(inside)
        def _():
            moved_copy(1, -1, part_buf.at[0]).wait_recv()
            fetch(here - 1, moved_out.at[1], 2, 3)
            moved_copy(3, -1, part_buf.at[2]).start()

    def moved_end():
        @pl.when(here < parts - 1)
        def _():
            moved_copy(2, 1, part_buf.at[1]).wait_send()
            moved_copy(3, -1, part_buf.at[2]).wait_recv()

        @pl.when(here > 0)
        def _():
            moved_copy(3, -1, part_buf.at[2]).wait_send()
            moved_copy(2, 1, part_buf.at[1]).wait_recv()

    loads = [
        pltpu.make_async_copy(source, target, load_sem.at[n + 1])
        for n, (source, target) in enumerate(
            (
                (project_hbm, project),
                (pre_hbm, pre),
                (state_hbm, state),
                (mixed_hbm, mixed),
                (squash_hbm, squashed),
                (weights_hbm, weights),
                (unit_hbm, unit),
                (stream_hbm, stream),
            )
        )
    ]
    for load in loads:
        load.start()
    moved_second()
    for load in loads[:3]:
        load.wait()

    def slot_rows(slot):
        return pl.ds(pl.multiple_of(slot * rows, rows), rows)

    def take(slot):
        some = slot_rows(slot)
        grad_mixed = matmul_rt(rows_buf[slot], project[...].reshape(channels, width))
        gate = pre[1, some, :]
        squash = jax.nn.sigmoid(gate)
        act = gate * squash
        slope = squash * (1.0 + gate * (1.0 - squash))
        for n in range(strips):
            columns = slice(n * lanes, (n + 1) * lanes)
            part = grad_mixed[:, columns]
            drive[n, some, :] = part * act[:, columns]
            at = 2 * channels + n * lanes
            grad_pre[slot, :, at : at + lanes] = (
                part * state[n, some, :] * slope[:, columns]
            ).astype(bf16)

    pass_first()
    pass_second()
    arrive(slice(0, 6))
    pltpu.make_async_copy(own_ref, rows_buf.at[mine], load_sem.at[0]).wait()
    for flips in ((), (near,), (one,), (two,), (near, one), (near, two)):
        take(slot_of(copies, flips))
    moved_last()
    pass_last()
    take(slot_of(copies, (one, two)))
    arrive(slice(6, 8))
    take(slot_of(copies, (near, one, two)))

    tile = min(512, width)
    loads[3].wait()

    @pl.loop(0, width // tile)
    def _(k):
        columns = pl.ds(pl.multiple_of(k * tile, tile), tile)
        value = matmul_lt(
            mixed[...].reshape(seqs * rows, channels),
            rows_buf[:, :, columns].reshape(seqs * rows, tile),
        )
        grad_project[:, :, :, columns] = value.astype(bf16).reshape(
            copies, parts, own_rows, tile
        )

    def part_of(kind, block):
        return grad_project.at[:, block] if kind == 3 else grad_w.at[kind, :, block]

    def room_of(kind, index):
        return line_project.at[index] if kind == 3 else line_w.at[kind, index]

    def line_up(kind, k):
        block = parts - 1 - k + here
        return along(
            1, part_of(kind, block), room_of(kind, block), up_send.at[kind, k],
            line_recv.at[kind, block],
        )

    def line_down(kind, k):
        block = k - parts + 1 + here
        index = parts if k == parts - 2 else block
        return along(
            -1, part_of(kind, block), room_of(kind, index), down_send.at[kind, k],
            line_recv.at[kind, index],
        )

    def came(kind, index):
        return along(1, part_of(kind, 0), room_of(kind, index), up_send.at[kind, 0],
                     line_recv.at[kind, index])

    def add_came(kind, block):
        came(kind, block).wait_recv()
        if kind == 3:
            total = grad_project[:, block].astype(f32) + line_project[block].astype(f32)
            grad_project[:, block] = total.astype(bf16)
        else:
            total = grad_w[kind, :, block].astype(f32) + line_w[kind, block].astype(f32)
            grad_w[kind, :, block] = total.astype(bf16)

    def goes_up(k):
        return jnp.logical_and(here <= k, here < parts - 1)

    def goes_down(k):
        return jnp.logical_and(parts - 1 - here <= k, here > 0)

    def line_step(kind, k):
        @pl.when(jnp.logical_and(goes_up(k), here > 0))
        def _():
            add_came(kind, parts - 1 - k + here)

        @pl.when(goes_up(k))
        def _():
            line_up(kind, k).start()

        @pl.when(jnp.logical_and(goes_down(k), here < parts - 1))
        def _():
            add_came(kind, k - parts + 1 + here)

        @pl.when(goes_down(k))
        def _():
            line_down(kind, k).start()

    def advance(kind, k):
        if k + 1 < parts - 1:
            line_step(kind, k + 1)
            return

        @pl.when(here > 0)
        def _():
            came(kind, here).wait_recv()

        @pl.when(here < parts - 1)
        def _():
            came(kind, parts).wait_recv()

        if kind == 3:
            project_sum[...] = (
                grad_project[:, here].astype(f32)
                + line_project[here].astype(f32)
                + line_project[parts].astype(f32)
            )
        else:
            total = (
                grad_w[kind, :, here].astype(f32)
                + line_w[kind, here].astype(f32)
                + line_w[kind, parts].astype(f32)
            )
            whole_w[kind] = total.astype(bf16)
            for copy in spread_copies(kind):
                copy.start()

    @pl.when(at_start)
    def _():
        line_w[:, 0] = jnp.zeros_like(line_w[:, 0])
        line_project[0] = jnp.zeros_like(line_project[0])

    @pl.when(at_end)
    def _():
        line_w[:, parts] = jnp.zeros_like(line_w[:, parts])
        line_project[parts] = jnp.zeros_like(line_project[parts])

    def spread_copies(kind, own=True):
        found = []
        for k in range(1, 8):
            there = group_member(copies, k)
            source = pl.ds(pl.multiple_of(lax.div(there, copies) * copies, copies), copies)
            found.append(
                pltpu.make_async_remote_copy(
                    src_ref=whole_w.at[kind, source],
                    dst_ref=spread_w.at[kind, mine],
                    send_sem=spread_send.at[kind, k - 1],
                    recv_sem=spread_recv.at[kind, k - 1],
                    device_id={"dp": there},
                    device_id_type=pl.DeviceIdType.MESH,
                )
            )
        if own:
            source = pl.ds(pl.multiple_of(mine * copies, copies), copies)
            found.append(
                pltpu.make_async_copy(
                    whole_w.at[kind, source], spread_w.at[kind, mine], spread_own.at[kind]
                )
            )
        return found

    line_step(3, 0)
    finish()
    normed_load = pltpu.make_async_copy(normed_hbm, rows_buf, load_sem.at[0])
    normed_load.start()
    loads[4].wait()

    def step(k, carry):
        some = pl.ds(rows - 1 - k, seqs, stride=rows)
        following = []
        for n, (coming, product) in enumerate(carry):
            bound = bound_ref[:, n * lanes : (n + 1) * lanes]
            keep = bound + (1.0 - bound) * squashed[n, some, :]
            carried = drive[n, some, :] + coming
            drive[n, some, :] = carried
            decay[n, some, :] = product
            following.append((keep * carried, product * keep))
        return tuple(following)

    start = (jnp.zeros((seqs, lanes), f32), jnp.ones((seqs, lanes), f32))
    carry = lax.fori_loop(0, rows, step, (start,) * strips, unroll=8)
    for n, (coming, product) in enumerate(carry):
        ends[here, 0, :, n * lanes : (n + 1) * lanes] = coming
        ends[here, 1, :, n * lanes : (n + 1) * lanes] = product
    carries = []
    for k in range(1, parts):
        copy = pltpu.make_async_remote_copy(
            src_ref=ends.at[here],
            dst_ref=ends.at[here],
            send_sem=carry_send.at[k - 1],
            recv_sem=carry_recv.at[k - 1],
            device_id={"tensor": beside(k)},
            device_id_type=pl.DeviceIdType.MESH,
        )
        copy.start()
        carries.append(copy)
    normed_load.wait()

    def weight_grad(kind):
        @pl.loop(0, width // tile)
        def _(k):
            columns = pl.ds(pl.multiple_of(k * tile, tile), tile)
            value = matmul_lt(
                grad_pre[:, :, kind * channels : (kind + 1) * channels].reshape(
                    seqs * rows, channels
                ),
                rows_buf[:, :, columns].reshape(seqs * rows, tile),
            )
            count = tile // (parts * own_rows)
            grad_w[kind, pl.ds(k * count, count)] = value.T.astype(bf16).reshape(
                count, parts, own_rows, channels
            )

        line_step(kind, 0)

    advance(3, 0)
    weight_grad(2)
    for copy in carries:
        copy.wait_recv()
    coming = jnp.zeros((seqs, channels), f32)
    arrived = coming
    for k in range(parts - 1, 0, -1):
        coming = ends[k, 1] * coming + ends[k, 0]
        arrived = jnp.where(here == k - 1, coming, arrived)
    for n in range(seqs):
        entered[n] = arrived[n : n + 1]
    bound_sum[...] = jnp.zeros_like(bound_sum)
    first_row = lax.broadcasted_iota(jnp.int32, (rows, lanes), 0) == 0

    @pl.loop(0, seqs)
    def _(slot):
        some = slot_rows(slot)
        alive = live_ref[some, :]
        for n in range(strips):
            columns = slice(n * lanes, (n + 1) * lanes)
            bound = bound_ref[:, columns]
            squash = squashed[n, some, :]
            keep = bound + (1.0 - bound) * squash
            carried = drive[n, some, :] + decay[n, some, :] * entered[slot, :, columns]
            prior = jnp.where(
                first_row, entering_ref[slot, :, columns], pltpu.roll(state[n, some, :], 1, 0)
            )
            value = pre[0, some, columns]
            gate = jax.nn.sigmoid(value)
            slope = gate * (1.0 + value * (1.0 - gate))
            grad_forget = carried * prior - carried * alive * value * gate
            at = n * lanes
            grad_pre[slot, :, at : at + lanes] = (
                carried * alive * (1.0 - keep) * slope
            ).astype(bf16)
            at = channels + n * lanes
            grad_pre[slot, :, at : at + lanes] = (
                grad_forget * (1.0 - bound) * squash * (1.0 - squash)
            ).astype(bf16)
            bound_sum[:, columns] += jnp.sum(
                grad_forget * (1.0 - squash), axis=0, keepdims=True
            )

    advance(3, 1)
    weight_grad(0)
    advance(2, 0)
    weight_grad(1)
    loads[5].wait()
    moved_end()

    def normed_product(slot, columns):
        at = lax.div(columns.start, parts * own_rows)
        count = tile // (parts * own_rows)
        total = None
        for kind in range(3):
            part = matmul_rt(
                grad_pre[slot, :, kind * channels : (kind + 1) * channels],
                weights[kind, pl.ds(at, count)].reshape(tile, channels),
            )
            total = part if total is None else total + part
        return total

    def between(point):
        if point == "sent":
            advance(3, 2)
        elif point == "added":
            advance(2, 1)
            advance(0, 0)
        elif point == "top":
            advance(1, 0)
            advance(2, 2)
        elif point == "low":
            advance(0, 1)
            advance(1, 1)

    plane_scatter_steps(
        copies, result_ref, near_buf, one_buf, two_buf, part_buf, scatter_send, scatter_recv,
        normed_product, between,
    )

    for load in loads[6:]:
        load.wait()
    small_sums[...] = jnp.zeros_like(small_sums)
    small_sums[1:2, :] = gain_two_ref[...]
    small_sums[2:3, pl.ds(pl.multiple_of(mine * channels, channels), channels)] = bound_sum[...]
    some_rows = min(64, rows)

    @pl.loop(0, rows // some_rows)
    def _(k):
        some = pl.ds(pl.multiple_of(k * some_rows, some_rows), some_rows)
        grad_norm = result_ref[some, :]
        units = unit[some, :]
        small_sums[0:1, :] += jnp.sum(grad_norm * units, axis=0, keepdims=True)
        scaled = grad_norm * gain_ref[...]
        mean = jnp.mean(scaled * units, axis=-1, keepdims=True)
        result_ref[some, :] = stream[some, :] + scale_ref[some, :] * (scaled - units * mean)

    def small_copy(n):
        return pltpu.make_async_remote_copy(
            src_ref=small_sums,
            dst_ref=small_recv.at[n],
            send_sem=small_send.at[n],
            recv_sem=small_got.at[n],
            device_id={"dp": partner(masks[n])},
            device_id_type=pl.DeviceIdType.MESH,
        )

    def small_step(n):
        small_copy(n).wait()
        small_sums[...] += small_recv[n]

    small_copy(0).start()
    advance(0, 2)
    advance(1, 2)
    for n in range(len(masks)):
        small_step(n)
        if n + 1 < len(masks):
            small_copy(n + 1).start()
    ring_small = []
    for k in range(1, parts):
        copy = pltpu.make_async_remote_copy(
            src_ref=small_sums,
            dst_ref=small_ring.at[k - 1],
            send_sem=small_send.at[len(masks) + k - 1],
            recv_sem=small_got.at[len(masks) + k - 1],
            device_id={"tensor": beside(k)},
            device_id_type=pl.DeviceIdType.MESH,
        )
        copy.start()
        ring_small.append(copy)
    for kind in (2, 0, 1):
        spread = spread_copies(kind)
        for copy in spread[:-1]:
            copy.wait_recv()
        spread[-1].wait()
        for slot in range(8):
            weight_sums[kind][:, :, slot * channels : (slot + 1) * channels] = spread_w[
                kind, slot
            ].astype(f32)
    for copy in ring_small:
        copy.wait()
    for k in range(parts - 1):
        small_sums[...] += small_ring[k]
    for kind in range(4):
        for k in range(parts - 1):

            @pl.when(goes_up(k))
            def _():
                line_up(kind, k).wait_send()

            @pl.when(goes_down(k))
            def _():
                line_down(kind, k).wait_send()

    for kind in range(3):
        for copy in spread_copies(kind, False):
            copy.wait_send()
    for copy in carries:
        copy.wait_send()


def mixer_backward(
    own, normed, weights, project, pre, squashed, state, mixed, unit, stream, entering, bound,
    live, gain, scale, gain_two, out_rows, out_moved, copies, masks, collective,
):
    parts = lax.axis_size("tensor")
    _, rows, width = normed.shape
    channels = width // 8
    own_rows = project.shape[2]
    somewhere = pl.BlockSpec(memory_space=pl.ANY)
    vmem = pl.BlockSpec(memory_space=pltpu.VMEM)
    half = rows // 2
    dma = pltpu.SemaphoreType.DMA
    blocks = (8 * copies, own_rows, channels)
    small = pltpu.VMEM((len(masks), 8, width), f32)
    return pl.pallas_call(
        functools.partial(mixer_backward_kernel, copies, masks),
        out_shape=[
            jax.ShapeDtypeStruct((rows, width), f32),
        ]
        + [jax.ShapeDtypeStruct((copies, own_rows, width), f32)] * 4
        + [
            jax.ShapeDtypeStruct((8, width), f32),
            jax.ShapeDtypeStruct((4, rows, width), bf16),
        ],
        in_specs=[somewhere] * 10 + [vmem] * 6 + [somewhere] * 2,
        out_specs=[vmem] * 6 + [somewhere],
        scratch_shapes=[
            pltpu.VMEM(normed.shape, bf16),
            pltpu.VMEM(weights.shape, bf16),
            pltpu.VMEM(project.shape, bf16),
            pltpu.VMEM(pre.shape, f32),
            pltpu.VMEM(squashed.shape, f32),
            pltpu.VMEM(state.shape, f32),
            pltpu.VMEM(mixed.shape, bf16),
            pltpu.VMEM((rows, width), f32),
            pltpu.VMEM((rows, width), f32),
            pltpu.VMEM(state.shape, f32),
            pltpu.VMEM(state.shape, f32),
            pltpu.VMEM((parts, 2, 8, channels), f32),
            pltpu.VMEM((8, 1, channels), f32),
            pltpu.VMEM((8, rows, 3 * channels), bf16),
            pltpu.VMEM(weights.shape, bf16),
            pltpu.VMEM(project.shape, bf16),
            pltpu.VMEM((3, parts + 1) + blocks, bf16),
            pltpu.VMEM((parts + 1, copies, own_rows, width), bf16),
            pltpu.VMEM((1, channels), f32),
            pltpu.VMEM((3,) + blocks, bf16),
            pltpu.VMEM((3, 8, copies, own_rows, channels), bf16),
            small,
            pltpu.VMEM((parts - 1, 8, width), f32),
            pltpu.VMEM((4, rows, width), bf16),
            pltpu.VMEM((3, half, width), bf16),
            pltpu.VMEM((3, half, width), bf16),
            pltpu.VMEM((4, rows, width), bf16),
            dma((9,)),
            dma((14,)),
            dma((14,)),
            dma((parts - 1,)),
            dma((parts - 1,)),
            dma((4, parts - 1)),
            dma((4, parts - 1)),
            dma((4, parts + 1)),
            dma((10,)),
            dma((10,)),
            dma((3, 7)),
            dma((3, 7)),
            dma((3,)),
            dma((len(masks) + parts - 1,)),
            dma((len(masks) + parts - 1,)),
            dma((2,)),
            dma((4,)),
            dma((4,)),
        ],
        compiler_params=pltpu.CompilerParams(
            collective_id=collective, has_side_effects=True, vmem_limit_bytes=62 * 1024 * 1024
        ),
        cost_estimate=pl.CostEstimate(
            flops=16 * rows * width * width,
            bytes_accessed=900 * rows * width,
            transcendentals=0,
        ),
    )(
        own, normed, weights, project, pre, squashed, state, mixed, unit, stream, entering, bound,
        live, gain, scale, gain_two, out_rows, out_moved,
    )


def on_device(
    inputs,
    lengths,
    gain_mix,
    gain_glu,
    lower_bound,
    w_input,
    w_forget,
    w_gate_mix,
    w_out,
    w_gate,
    w_up,
    w_down,
    cotangent,
):
    tensor_parts = lax.axis_size("tensor")
    data_parts = lax.axis_size("dp")
    tensor_index = lax.axis_index("tensor")
    data_index = lax.axis_index("dp")
    rows_here, width = inputs.shape
    group = min(8, data_parts)
    copies = data_parts // group
    group_index = lax.div(data_index, copies)
    copy_index = lax.rem(data_index, copies)
    group_masks = [copies << k for k in range(group.bit_length() - 1)]
    copy_masks = [1 << k for k in range(copies.bit_length() - 1)]
    all_masks = [1 << k for k in range(data_parts.bit_length() - 1)]
    group_lists = [[g * copies + o for g in range(group)] for o in range(copies)]
    channels = width // group
    own_rows = w_input.shape[0]

    high = lax.div(lengths, 32).astype(bf16)
    low = lax.rem(lengths, 32).astype(bf16)
    length_row = jnp.concatenate([high, low, jnp.zeros((own_rows - 2,), bf16)])
    small = jnp.stack([gain_mix, gain_glu, lower_bound, length_row])
    small = in_order(shifted_blocks(small))
    small = gather_bits(small, sorted(all_masks, reverse=True)).astype(f32)
    small = small.reshape((data_parts * tensor_parts,) + small.shape[2:])
    gain_one = small[:, 0].reshape(width)
    gain_two = small[:, 1].reshape(width)
    bound = lax.dynamic_slice_in_dim(small[:, 2].reshape(width), group_index * channels, channels)
    every_length = small[:, 3].reshape(data_parts, tensor_parts, own_rows)[:, 0, :2]
    every_length = (every_length[:, 0] * 32.0 + every_length[:, 1]).astype(jnp.int32)
    group_lengths = lax.dynamic_index_in_dim(
        every_length.reshape(group, copies), copy_index, axis=1, keepdims=False
    )
    position = tensor_index * rows_here + jnp.arange(rows_here, dtype=jnp.int32)
    live_own = (position < lengths[0]).astype(f32)[:, None]
    live = (position[None, :] < group_lengths[:, None]).astype(f32)
    live = live.reshape(group * rows_here, 1)

    mixer_weights = [w_input, w_forget, w_gate_mix, w_out]
    if copies > 1:
        mixer_weights = [gather_bits(weight, copy_masks[::-1]) for weight in mixer_weights]
    mixer_weights = [weight.reshape(copies, own_rows, width) for weight in mixer_weights]

    masked_grad = live_own * cotangent
    masked_own = masked_grad.astype(bf16)
    masked_below, masked_above = (
        lax.ppermute(
            masked_own,
            "tensor",
            [(i, i + step) for i in range(tensor_parts) if 0 <= i + step < tensor_parts],
        )
        for step in (1, -1)
    )

    scale_one, unit_one = norm_rows(inputs)
    rows_all = group * rows_here
    *mixer_kept, mixed, masked_others, mixed_sum = (
        mixer_forward(
            (unit_one * gain_one).astype(bf16),
            *mixer_weights,
            masked_below,
            masked_above,
            bound[None, :],
            live,
            copies,
            1,
        )
    )
    stream = inputs + mixed_sum

    hidden_here = w_gate.shape[1]
    gate_w, up_w = (
        lax.all_gather(weight, "dp", axis=0, tiled=True).reshape(group, channels, hidden_here)
        for weight in (w_gate, w_up)
    )
    down_part = w_down.T
    if copies > 1:
        down_part = gather_bits(down_part, copy_masks[::-1]).reshape(channels, hidden_here)

    scale_two, unit_two = norm_rows(stream)
    normed_two = (unit_two * gain_two).astype(bf16)
    out_rows, out_moved, grad_norm_two, *weight_sums = swiglu(
        normed_two,
        masked_own,
        masked_below,
        masked_above,
        masked_others,
        gate_w,
        up_w,
        down_part,
        copies,
        4,
    )
    if copies > 1:
        weight_sums = [
            scatter_bits(total.reshape(copies, width // data_parts, hidden_here), copy_masks, f32)
            for total in weight_sums
        ]
    grad_gate_mine, grad_up_mine, grad_down_mine = weight_sums
    grad_down_mine = grad_down_mine.T

    gain_two_part = jnp.sum(grad_norm_two * unit_two, axis=0)
    grad_stream = masked_grad + norm_back(grad_norm_two, unit_two, scale_two, gain_two)

    normed_one, mixer_w, out_w, pre, squashed, state, entering = mixer_kept
    grad_inputs, *grad_weights, small_sums, out_others = mixer_backward(
        grad_stream.astype(bf16),
        normed_one,
        mixer_w,
        out_w,
        pre,
        squashed,
        state,
        mixed,
        unit_one,
        grad_stream,
        entering,
        bound[None, :],
        live,
        gain_one[None, :],
        scale_one,
        gain_two_part[None, :],
        out_rows,
        out_moved,
        copies,
        all_masks,
        3,
    )
    out_sum = lax.dynamic_index_in_dim(out_rows, tensor_index, 0, keepdims=False).astype(f32)
    out_sum += jnp.where(tensor_index > 0, out_others[2].astype(f32), 0.0)
    out_sum += jnp.where(tensor_index < tensor_parts - 1, out_others[3].astype(f32), 0.0)
    output = live_own * (stream + out_sum)
    if copies > 1:
        grad_weights = [scatter_bits(total, copy_masks, f32) for total in grad_weights]
    grad_weights = [total.reshape(own_rows, width) for total in grad_weights]
    place = (data_index * tensor_parts + tensor_index) * own_rows
    small_own = lax.dynamic_slice(small_sums, (0, place), (3, own_rows))
    return (
        output,
        grad_inputs,
        small_own[0],
        small_own[1],
        small_own[2],
        *grad_weights,
        grad_gate_mine,
        grad_up_mine,
        grad_down_mine,
    )


def solution(mesh):
    both = ("dp", "tensor")
    placed = (
        P(both, None),
        P("dp"),
        P(both),
        P(both),
        P(both),
        P(both, None),
        P(both, None),
        P(both, None),
        P(both, None),
        P("dp", "tensor"),
        P("dp", "tensor"),
        P("tensor", "dp"),
        P(both, None),
    )
    return jax.shard_map(
        on_device,
        mesh=mesh,
        in_specs=placed,
        out_specs=(
            P(both, None),
            P(both, None),
            P(both),
            P(both),
            P(both),
            P(both, None),
            P(both, None),
            P(both, None),
            P(both, None),
            P("dp", "tensor"),
            P("dp", "tensor"),
            P("tensor", "dp"),
        ),
        check_vma=False,
    )
```

```python
import functools

import jax
import jax.numpy as jnp
from jax import lax
from jax.experimental import pallas as pl
from jax.experimental.pallas import tpu as pltpu
from jax.sharding import PartitionSpec as P

epsilon = 1e-06
bf16 = jnp.bfloat16
f32 = jnp.float32


def matmul(left, right):
    return jnp.dot(left, right, preferred_element_type=f32)


def matmul_rt(left, right):
    return lax.dot_general(left, right, (((1,), (1,)), ((), ())), preferred_element_type=f32)


def matmul_lt(left, right):
    return lax.dot_general(left, right, (((0,), (0,)), ((), ())), preferred_element_type=f32)


def silu_of(value):
    return value * jax.nn.sigmoid(value)


def silu_slope(value):
    squash = jax.nn.sigmoid(value)
    return squash * (1.0 + value * (1.0 - squash))


def norm_rows(value):
    scale = lax.rsqrt(jnp.mean(value * value, axis=-1, keepdims=True) + epsilon)
    return (scale, value * scale)


def norm_back(grad_norm, unit, scale, gain):
    scaled = grad_norm * gain
    return scale * (scaled - unit * jnp.mean(scaled * unit, axis=-1, keepdims=True))


def untouched_kernel(*refs):
    pass


def after(value, *others):
    somewhere = pl.BlockSpec(memory_space=pl.ANY)
    return pl.pallas_call(
        untouched_kernel,
        out_shape=jax.ShapeDtypeStruct(value.shape, value.dtype),
        in_specs=[somewhere] * (1 + len(others)),
        out_specs=somewhere,
        input_output_aliases={0: 0},
        cost_estimate=pl.CostEstimate(flops=0, bytes_accessed=0, transcendentals=0),
    )(value, *others)


def swap(value, mask):
    return lax.ppermute(value, "dp", [(i, i ^ mask) for i in range(lax.axis_size("dp"))])


def own_bit(mask):
    return lax.rem(lax.div(lax.axis_index("dp"), mask), 2)


def gather_bits(value, order):
    base = value.shape
    done = []
    for mask in order:
        other = swap(value, mask)
        at = sum(1 for seen in done if seen > mask)
        low = jnp.stack([value, other], axis=at)
        high = jnp.stack([other, value], axis=at)
        value = jnp.where(own_bit(mask) == 0, low, high)
        done.append(mask)
    return value.reshape((1 << len(order),) + base)


def scatter_bits(value, order, sent=bf16, hold=(None, None)):
    count = len(order)
    value = value.reshape((2,) * count + value.shape[1:])
    left = sorted(order, reverse=True)
    for mask in order:
        at = left.index(mask)
        left.remove(mask)
        bit = own_bit(mask)
        send = lax.dynamic_index_in_dim(value, 1 - bit, at, keepdims=False).astype(sent)
        keep = lax.dynamic_index_in_dim(value, bit, at, keepdims=False)
        if hold[0] == count - len(left) - 1:
            send = after(send, hold[1])
        total = keep.astype(f32) + swap(send, mask).astype(f32)
        value = total.astype(sent) if left else total
    return value


def orders(masks):
    down = sorted(masks, reverse=True)
    if len(down) < 3:
        return down, down
    return down, [down[1], down[0]] + down[2:]


def gather_halves(value, masks):
    first, second = orders(masks)
    half = value.shape[-1] // 2
    return gather_bits(value[..., :half], first), gather_bits(value[..., half:], second)


def scatter_halves(left, right, masks):
    first, second = orders(masks)
    return jnp.concatenate(
        [scatter_bits(left, first[::-1]), scatter_bits(right, second[::-1])], axis=-1
    )


def ring(value):
    parts = lax.axis_size("tensor")
    return lax.ppermute(value, "tensor", [(i, (i + 1) % parts) for i in range(parts)])


def ring_blocks(value):
    blocks = [value]
    for _ in range(lax.axis_size("tensor") - 1):
        blocks.append(ring(blocks[-1]))
    return blocks


def ring_scatter(blocks):
    total = blocks[1 % len(blocks)]
    totals = [total]
    for k in range(2, len(blocks) + 1):
        moved = ring(total).astype(f32)
        total = moved + blocks[k % len(blocks)].astype(f32)
        if k < len(blocks):
            total = total.astype(bf16)
            totals.append(total)
    return total, totals


def shifted_blocks(value):
    parts = lax.axis_size("tensor")
    blocks = [value]
    for k in range(1, parts):
        blocks.append(lax.ppermute(value, "tensor", [(i, (i + k) % parts) for i in range(parts)]))
    return blocks


def scatter_straight(value):
    here = lax.axis_index("tensor")
    parts = lax.axis_size("tensor")
    total = lax.dynamic_index_in_dim(value, here, 0, keepdims=False)
    for k in range(1, parts):
        send = lax.dynamic_index_in_dim(value, lax.rem(here + k, parts), 0, keepdims=False)
        total += lax.ppermute(send, "tensor", [(i, (i + k) % parts) for i in range(parts)])
    return total


def in_order(blocks):
    here = lax.axis_index("tensor")
    parts = len(blocks)
    stacked = jnp.stack(blocks[::-1] + blocks[::-1])
    return lax.dynamic_slice_in_dim(stacked, parts - 1 - here, parts, 0)


def partner(mask):
    me = lax.axis_index("dp")
    return me + mask * (1 - 2 * lax.rem(lax.div(me, mask), 2))


def greet(masks, ring_too=False):
    barrier = pltpu.get_barrier_semaphore()
    others = [{"dp": partner(mask)} for mask in masks]
    if ring_too:
        others += [{"tensor": beside(1)}, {"tensor": beside(-1)}]
    for other in others:
        pl.semaphore_signal(
            barrier, inc=1, device_id=other, device_id_type=pl.DeviceIdType.MESH
        )
    pl.semaphore_wait(barrier, len(others))


def beside(step):
    parts = lax.axis_size("tensor")
    return lax.rem(lax.axis_index("tensor") + step + parts, parts)


def slot_of(copies, masks):
    me = lax.axis_index("dp")
    for mask in masks:
        me = me + mask * (1 - 2 * lax.rem(lax.div(me, mask), 2))
    return lax.div(me, copies)


def to_right(source, target, send_sem, recv_sem):
    return pltpu.make_async_remote_copy(
        src_ref=source,
        dst_ref=target,
        send_sem=send_sem,
        recv_sem=recv_sem,
        device_id={"tensor": beside(1)},
        device_id_type=pl.DeviceIdType.MESH,
    )


def along(step, source, target, send_sem, recv_sem):
    return pltpu.make_async_remote_copy(
        src_ref=source,
        dst_ref=target,
        send_sem=send_sem,
        recv_sem=recv_sem,
        device_id={"tensor": beside(step)},
        device_id_type=pl.DeviceIdType.MESH,
    )


def plane_gather_steps(copies, value_ref, all_ref, own_sem, send_sem, recv_sem):
    near, one, two = copies, 2 * copies, 4 * copies
    half = value_ref.shape[0] // 2
    top, low = pl.ds(0, half), pl.ds(half, half)
    mine = slot_of(copies, ())
    at_one, at_two = slot_of(copies, (one,)), slot_of(copies, (two,))
    at_both = slot_of(copies, (one, two))
    local = None
    if own_sem is not None:
        local = pltpu.make_async_copy(value_ref, all_ref.at[mine], own_sem)
    sent = []
    last = []

    def send(source, slot, rows, mask):
        index = len(sent)
        copy = pltpu.make_async_remote_copy(
            src_ref=source,
            dst_ref=all_ref.at[slot, rows],
            send_sem=send_sem.at[index],
            recv_sem=recv_sem.at[index],
            device_id={"dp": partner(mask)},
            device_id_type=pl.DeviceIdType.MESH,
        )
        copy.start()
        sent.append(copy)
        if mask == near:
            last.append(copy)
        return copy

    def forward(slot, rows, mask):
        return send(all_ref.at[slot, rows], slot, rows, mask)

    first = []
    second = []

    def begin():
        if local is not None:
            local.start()
        first.append(send(value_ref.at[top], mine, top, two))
        first.append(send(value_ref.at[low], mine, low, one))
        first.append(send(value_ref.at[low], mine, low, two))
        first.append(send(value_ref.at[top], mine, top, one))
        send(value_ref.at[top], mine, top, near)
        send(value_ref.at[low], mine, low, near)

    def pass_first():
        first[0].wait_recv()
        second.append(forward(at_two, top, one))
        forward(at_two, top, near)
        first[1].wait_recv()
        second.append(forward(at_one, low, two))
        forward(at_one, low, near)

    def pass_second():
        first[2].wait_recv()
        forward(at_two, low, near)
        first[3].wait_recv()
        forward(at_one, top, near)

    def pass_last():
        second[0].wait_recv()
        forward(at_both, top, near)
        second[1].wait_recv()
        forward(at_both, low, near)

    def arrive(some=slice(None)):
        for copy in last[some]:
            copy.wait_recv()
        if some == slice(None) and local is not None:
            local.wait()

    def finish():
        for copy in sent:
            copy.wait_send()

    return begin, pass_first, pass_second, pass_last, arrive, finish


def plane_scatter_steps(
    copies, sum_ref, near_ref, one_ref, two_ref, part_ref,
    send_sem, recv_sem, product, between,
):
    near, one, two = copies, 2 * copies, 4 * copies
    rows, width = sum_ref.shape
    half = rows // 2
    top, low = pl.ds(0, half), pl.ds(half, half)
    tile = min(512, width)
    flips = [(), (one,), (two,), (one, two)]
    copies_out = []

    def send(source, target, mask):
        index = len(copies_out)
        copy = pltpu.make_async_remote_copy(
            src_ref=source,
            dst_ref=target,
            send_sem=send_sem.at[index],
            recv_sem=recv_sem.at[index],
            device_id={"dp": partner(mask)},
            device_id_type=pl.DeviceIdType.MESH,
        )
        copy.start()
        copies_out.append(copy)
        return copy

    def each_tile(body):
        @pl.loop(0, width // tile)
        def _(k):
            body(pl.ds(pl.multiple_of(k * tile, tile), tile))

    arriving = {}
    for k in (3, 1, 2, 0):
        slot = slot_of(copies, flips[k] + (near,))

        def theirs(columns, k=k, slot=slot):
            part_ref[k, :, columns] = product(slot, columns).astype(bf16)

        each_tile(theirs)
        arriving[k] = send(part_ref.at[k], near_ref.at[k], near)

    between("sent")

    def added(k):
        slot = slot_of(copies, flips[k])
        arriving[k].wait_recv()

        def mine(columns):
            total = product(slot, columns) + near_ref[k, :, columns].astype(f32)
            if k == 0:
                sum_ref[:, columns] = total
            else:
                near_ref[k, :, columns] = total.astype(bf16)

        each_tile(mine)

    added(3)
    one_first = send(near_ref.at[3, top], one_ref.at[0], one)
    two_first = send(near_ref.at[3, low], two_ref.at[0], two)
    added(1)
    one_second = send(near_ref.at[1, top], one_ref.at[1], one)
    added(2)
    two_second = send(near_ref.at[2, low], two_ref.at[1], two)
    added(0)
    between("added")

    one_first.wait_recv()

    def pass_top(columns):
        total = near_ref[2, top, columns].astype(f32) + one_ref[0, :, columns].astype(f32)
        near_ref[2, top, columns] = total.astype(bf16)

    each_tile(pass_top)
    two_last = send(near_ref.at[2, top], two_ref.at[2], two)
    between("top")
    two_first.wait_recv()

    def pass_low(columns):
        total = near_ref[1, low, columns].astype(f32) + two_ref[0, :, columns].astype(f32)
        near_ref[1, low, columns] = total.astype(bf16)

    each_tile(pass_low)
    one_last = send(near_ref.at[1, low], one_ref.at[2], one)
    between("low")

    def finish(rows_at, first, at_first, second, at_second):
        def body(columns):
            sum_ref[rows_at, columns] += (
                first[at_first, :, columns].astype(f32) + second[at_second, :, columns].astype(f32)
            )

        each_tile(body)

    one_second.wait_recv()
    two_last.wait_recv()
    finish(top, one_ref, 1, two_ref, 2)
    two_second.wait_recv()
    one_last.wait_recv()
    finish(low, two_ref, 1, one_ref, 2)
    for copy in copies_out:
        copy.wait_send()


def column_tiles(width, most=512):
    return [(at, min(most, width - at)) for at in range(0, width, most)]


def swiglu_kernel(
    copies,
    normed_ref, own_ref, below_ref, above_ref, others_ref, gate_hbm, up_hbm, down_ref,
    rows_out, moved_out, norm_sum, gate_sum, up_sum, down_sum,
    normed, masked, gate_w, up_w, down_w, hidden, gate_low, up_low, back, rows, ring_buf,
    one_buf, two_buf, lead, lead_near, in_sem, out_sem, gather_send, gather_recv, send_sem,
    recv_sem, sum_send, sum_recv, near_send, near_recv, one_send, one_recv, two_send, two_recv,
    ready_sem, moved_send, moved_recv,
):
    parts = lax.axis_size("tensor")
    near, one, two = copies, 2 * copies, 4 * copies
    greet((near, one, two), True)
    own = pltpu.make_async_copy(normed_ref, normed.at[0], in_sem.at[0])
    own.start()
    gather = plane_gather_steps(
        copies, down_ref, down_w, in_sem.at[4], gather_send, gather_recv
    )
    gather[0]()
    loads = [
        pltpu.make_async_copy(gate_hbm, gate_w, in_sem.at[1]),
        pltpu.make_async_copy(up_hbm, up_w, in_sem.at[2]),
        pltpu.make_async_copy(own_ref, masked.at[0], in_sem.at[3]),
    ]
    own.wait()
    for load in loads:
        load.start()
    here = lax.axis_index("tensor")
    at_start, at_end = here == 0, here == parts - 1

    def load_masked(k, source):
        return pltpu.make_async_copy(source, masked.at[k], in_sem.at[4 + k])

    for k in range(1, parts):
        far = load_masked(k, others_ref.at[beside(-k)])
        if 1 < k < parts - 1:
            far.start()
        else:
            next_to, ref = (at_start, below_ref) if k == 1 else (at_end, above_ref)

            @pl.when(next_to)
            def _():
                far.start()

            @pl.when(jnp.logical_not(next_to))
            def _():
                load_masked(k, ref).start()

        loads.append(far)
    _, block_rows, width = normed.shape
    hidden_width = hidden.shape[2]
    share = width // 8
    half = share // 2
    many = 2
    tile = many * share
    both = [pl.ds(n * (block_rows // 2), block_rows // 2) for n in range(2)]

    def hop(k, n):
        return to_right(
            normed.at[k, both[n]], normed.at[k + 1, both[n]], send_sem.at[k, n], recv_sem.at[k, n]
        )

    def sum_hop(k, n):
        return to_right(
            back.at[k + 1, both[n]], ring_buf.at[k, both[n]], sum_send.at[k, n], sum_recv.at[k, n]
        )

    for n in range(2):
        hop(0, n).start()
    for load in loads:
        load.wait()
    gather[1]()
    gather[2]()
    for n in range(2):
        hop(0, n).wait_recv()
        hop(1, n).start()
    gather[3]()
    gather[4]()

    def store(k):
        home = lax.rem(lax.axis_index("tensor") + parts - k, parts)
        slot = lax.rem(k, 2)
        return pltpu.make_async_copy(rows.at[slot], rows_out.at[home], out_sem.at[slot])

    def front(k):
        for at, size in column_tiles(hidden_width):
            columns = pl.ds(at, size)

            def weight(ref):
                return ref[:, :, columns].reshape(width, size)

            glu_gate = matmul(normed[k], weight(gate_w))
            glu_up = matmul(normed[k], weight(up_w))
            grad_hidden = matmul(masked[k], weight(down_w))
            squash = jax.nn.sigmoid(glu_gate)
            act = glu_gate * squash
            slope = squash * (1.0 + glu_gate * (1.0 - squash))
            hidden[k, :, columns] = (act * glu_up).astype(bf16)
            gate_low[k, :, columns] = (grad_hidden * glu_up * slope).astype(bf16)
            up_low[k, :, columns] = (grad_hidden * act).astype(bf16)

    def rear(k):
        slot = lax.rem(k, 2)

        @pl.loop(0, 8 // many)
        def _(n):
            some = pl.ds(pl.multiple_of(n * tile, tile), tile)

            def weight(ref):
                return ref[pl.ds(n * many, many)].reshape(tile, hidden_width)

            back[k, :, some] = (
                matmul_rt(gate_low[k], weight(gate_w)) + matmul_rt(up_low[k], weight(up_w))
            ).astype(bf16)
            rows[slot, :, some] = matmul_rt(hidden[k], weight(down_w)).astype(bf16)

        store(k).start()

    def block(k, nothing):
        for n in range(2):

            @pl.when(jnp.logical_and(k > 0, k < parts - 2))
            def _():
                hop(k, n).wait_recv()
                hop(k + 1, n).start()

            @pl.when(k == parts - 1)
            def _():
                hop(parts - 2, n).wait_recv()
                sum_hop(0, n).start()

        front(k)

        @pl.when(k > 1)
        def _():
            store(k - 2).wait()

        @pl.when(k < parts - 1)
        def _():
            rear(k)

        return nothing

    lax.fori_loop(0, parts, block, 0)

    tall = parts * block_rows
    kinds = (
        (normed, gate_low, gate_w, gate_sum),
        (normed, up_low, up_w, up_sum),
        (masked, hidden, down_w, down_sum),
    )

    def product(kind, slot, store):
        left, right, _, _ = kinds[kind]
        some = pl.ds(pl.multiple_of(slot * share, share), share)
        for at, size in column_tiles(hidden_width):
            columns = pl.ds(at, size)
            store(
                columns,
                matmul_lt(
                    left[:, :, some].reshape(tall, share), right[:, :, columns].reshape(tall, size)
                ),
            )

    def across(source, target, send, recv, mask):
        return pltpu.make_async_remote_copy(
            src_ref=source,
            dst_ref=target,
            send_sem=send,
            recv_sem=recv,
            device_id={"dp": partner(mask)},
            device_id_type=pl.DeviceIdType.MESH,
        )

    top, low = pl.ds(0, half), pl.ds(half, half)

    def near_copy(kind, k):
        room = kinds[kind][2]
        return across(
            room.at[k], room.at[4 + k], near_send.at[kind, k], near_recv.at[kind, k], near
        )

    def lead_copy(kind):
        return across(
            lead.at[kind], lead_near.at[kind], near_send.at[kind, 3], near_recv.at[kind, 3], near
        )

    def one_copy(kind, n):
        room = kinds[kind][2]
        source = (lead_near.at[kind, top], room.at[5, top], room.at[5, low])[n]
        return across(
            source, one_buf.at[kind, n], one_send.at[kind, n], one_recv.at[kind, n], one
        )

    def two_copy(kind, n):
        room = kinds[kind][2]
        source = (lead_near.at[kind, low], room.at[6, low], room.at[6, top])[n]
        return across(
            source, two_buf.at[kind, n], two_send.at[kind, n], two_recv.at[kind, n], two
        )

    def flipped(k, near_too):
        me = lax.axis_index("dp")

        def turn(mask, on):
            return on * mask * (1 - 2 * lax.rem(lax.div(me, mask), 2))

        there = me + turn(one, lax.rem(k, 2)) + turn(two, lax.div(k, 2)) + turn(near, near_too)
        return lax.div(there, copies)

    def sum_step(k):
        for n in range(2):
            sum_hop(k, n).wait_recv()

            @pl.loop(0, 8 // many)
            def _(at):
                some = pl.ds(pl.multiple_of(at * tile, tile), tile)
                moved = ring_buf[k, both[n], some].astype(f32)
                if k + 1 < parts - 1:
                    total = back[k + 2, both[n], some].astype(f32) + moved
                    back[k + 2, both[n], some] = total.astype(bf16)
                else:
                    norm_sum[both[n], some] = back[0, both[n], some].astype(f32) + moved

            if k + 1 < parts - 1:
                sum_hop(k + 1, n).start()

    def keep(ref, at):
        def store(columns, value):
            ref[at, :, columns] = value.astype(bf16)

        return store

    def add(ref, at):
        def store(columns, value):
            ref[at, :, columns] = (value + ref[at, :, columns].astype(f32)).astype(bf16)

        return store

    def add_wide(total_ref, ref, at):
        def store(columns, value):
            total_ref[:, columns] = value + ref[at, :, columns].astype(f32)

        return store

    for kind in range(3):
        product(kind, flipped(3, 1), keep(lead, kind))
        lead_copy(kind).start()
    for kind in range(3):
        lead_copy(kind).wait_recv()
        product(kind, flipped(3, 0), add(lead_near, kind))
        one_copy(kind, 0).start()
        two_copy(kind, 0).start()
    rear(parts - 1)

    gather[5]()
    pl.semaphore_signal(
        ready_sem,
        inc=1,
        device_id={"dp": partner(near)},
        device_id_type=pl.DeviceIdType.MESH,
    )
    pl.semaphore_wait(ready_sem, 1)

    def theirs(k):
        for kind in range(3):
            product(kind, flipped(k, 1), keep(kinds[kind][2], k))
            near_copy(kind, k).start()

    def mine(k):
        for kind in range(3):
            near_copy(kind, k).wait_recv()
            product(kind, flipped(k, 0), add(kinds[kind][2], 4 + k))
            if k == 1:
                one_copy(kind, 1).start()
            else:
                two_copy(kind, 1).start()

    sum_step(0)
    theirs(1)
    theirs(2)
    mine(1)
    mine(2)
    theirs(0)
    for kind in range(3):
        one_copy(kind, 0).wait_recv()
        room = kinds[kind][2]
        room[6, top] = (room[6, top].astype(f32) + one_buf[kind, 0].astype(f32)).astype(bf16)
        two_copy(kind, 2).start()
        two_copy(kind, 0).wait_recv()
        room[5, low] = (room[5, low].astype(f32) + two_buf[kind, 0].astype(f32)).astype(bf16)
        one_copy(kind, 2).start()
    for k in range(1, parts - 2):
        sum_step(k)
    for kind in range(3):
        near_copy(kind, 0).wait_recv()
        room, total_ref = kinds[kind][2:]
        product(kind, flipped(0, 0), add_wide(total_ref, room, 4))
    sum_step(parts - 2)
    for k in (parts - 2, parts - 1):
        store(k).wait()
    moved_up = along(1, rows_out.at[parts - 1], moved_out, moved_send, moved_recv)
    moved_down = along(-1, rows_out.at[0], moved_out, moved_send, moved_recv)

    @pl.when(at_start)
    def _():
        moved_up.start()

    @pl.when(at_end)
    def _():
        moved_down.start()

    for kind in range(3):
        total_ref = kinds[kind][3]
        one_copy(kind, 1).wait_recv()
        two_copy(kind, 2).wait_recv()
        total_ref[:half, :] += one_buf[kind, 1].astype(f32) + two_buf[kind, 2].astype(f32)
        two_copy(kind, 1).wait_recv()
        one_copy(kind, 2).wait_recv()
        total_ref[half:, :] += two_buf[kind, 1].astype(f32) + one_buf[kind, 2].astype(f32)
    for kind in range(3):
        lead_copy(kind).wait_send()
        for k in range(3):
            near_copy(kind, k).wait_send()
        for n in range(3):
            one_copy(kind, n).wait_send()
            two_copy(kind, n).wait_send()
    for k in range(parts - 1):
        for n in range(2):
            hop(k, n).wait_send()
            sum_hop(k, n).wait_send()

    @pl.when(at_start)
    def _():
        moved_up.wait_send()

    @pl.when(at_end)
    def _():
        moved_down.wait_send()

    @pl.when(jnp.logical_not(jnp.logical_or(at_start, at_end)))
    def _():
        moved_up.wait_recv()


def swiglu(normed, own, below, above, others, gate_w, up_w, down_w, copies, collective):
    parts = lax.axis_size("tensor")
    rows, width = normed.shape
    hidden = gate_w.shape[2]
    share = width // 8
    somewhere = pl.BlockSpec(memory_space=pl.ANY)
    vmem = pl.BlockSpec(memory_space=pltpu.VMEM)
    wide, narrow = (parts, rows, width), (parts, rows, hidden)
    return pl.pallas_call(
        functools.partial(swiglu_kernel, copies),
        out_shape=[
            jax.ShapeDtypeStruct(wide, bf16),
            jax.ShapeDtypeStruct((rows, width), bf16),
            jax.ShapeDtypeStruct((rows, width), f32),
        ]
        + [jax.ShapeDtypeStruct((share, hidden), f32)] * 3,
        in_specs=[somewhere] * 8,
        out_specs=[somewhere] * 2 + [vmem] * 4,
        scratch_shapes=[pltpu.VMEM(wide, bf16)] * 2
        + [pltpu.VMEM((8, share, hidden), bf16)] * 3
        + [pltpu.VMEM(narrow, bf16)] * 3
        + [
            pltpu.VMEM(wide, bf16),
            pltpu.VMEM((2, rows, width), bf16),
            pltpu.VMEM((parts - 1, rows, width), bf16),
        ]
        + [pltpu.VMEM((3, 3, share // 2, hidden), bf16)] * 2
        + [pltpu.VMEM((3, share, hidden), bf16)] * 2
        + [pltpu.SemaphoreType.DMA((8,)), pltpu.SemaphoreType.DMA((2,))]
        + [pltpu.SemaphoreType.DMA((14,))] * 2
        + [pltpu.SemaphoreType.DMA((parts - 1, 2))] * 4
        + [pltpu.SemaphoreType.DMA((3, 4))] * 2
        + [pltpu.SemaphoreType.DMA((3, 3))] * 4
        + [pltpu.SemaphoreType.REGULAR]
        + [pltpu.SemaphoreType.DMA] * 2,
        compiler_params=pltpu.CompilerParams(
            collective_id=collective, has_side_effects=True, vmem_limit_bytes=62 * 1024 * 1024
        ),
        cost_estimate=pl.CostEstimate(
            flops=18 * parts * rows * width * hidden,
            bytes_accessed=1100 * rows * width,
            transcendentals=parts * rows * hidden,
        ),
    )(normed, own, below, above, others, gate_w, up_w, down_w)


def greet_all(copies, masks):
    barrier = pltpu.get_barrier_semaphore()
    others = [{"dp": group_member(copies, k)} for k in range(1, 8)]
    others += [{"tensor": beside(k)} for k in range(1, lax.axis_size("tensor"))]
    others += [{"dp": partner(mask)} for mask in masks]
    for other in others:
        pl.semaphore_signal(
            barrier, inc=1, device_id=other, device_id_type=pl.DeviceIdType.MESH
        )
    pl.semaphore_wait(barrier, len(others))


def group_member(copies, step):
    me = lax.axis_index("dp")
    return lax.rem(lax.div(me, copies) + step, 8) * copies + lax.rem(me, copies)


def mixer_forward_kernel(
    copies,
    own_ref, input_hbm, forget_hbm, gate_hbm, out_hbm, below_hbm, above_hbm, inputs_hbm, bound_ref,
    live_ref, gain_ref,
    normed_out, weights_out, project_out, pre_out, squash_out, state_out, entering_out, mixed_out,
    masked_out, stream_ref, following_ref,
    normed, weights, project, pre, squashed, forget, state, decay, ends, entering, mixed,
    near_buf, one_buf, two_buf, part_buf, inputs,
    own_sem, gather_send, gather_recv, spread_send, spread_recv, spread_own, up_send, down_send, line_recv,
    carry_send, carry_recv, scatter_send, scatter_recv, masked_up, masked_down, masked_recv, out_sem, inputs_sem,
):
    parts = lax.axis_size("tensor")
    here = lax.axis_index("tensor")
    seqs, rows, width = normed.shape
    strips, _, lanes = forget.shape
    channels = strips * lanes
    mine = slot_of(copies, ())
    greet_all(copies, ())

    def own_rows_of(index):
        return pl.ds(pl.multiple_of(index * copies, copies), copies)

    def columns_of(index):
        return pl.ds(pl.multiple_of(index * channels, channels), channels)

    spread = []
    for kind, source in enumerate((input_hbm, forget_hbm, gate_hbm)):
        target = weights.at[kind, own_rows_of(mine), here]
        kept = pltpu.make_async_copy(
            source.at[:, :, columns_of(mine)], target, spread_own.at[kind]
        )
        sent = []
        for k in range(1, 8):
            there = group_member(copies, k)
            sent.append(
                pltpu.make_async_remote_copy(
                    src_ref=source.at[:, :, columns_of(lax.div(there, copies))],
                    dst_ref=target,
                    send_sem=spread_send.at[kind, k - 1],
                    recv_sem=spread_recv.at[kind, k - 1],
                    device_id={"dp": there},
                    device_id_type=pl.DeviceIdType.MESH,
                )
            )
        spread.append((kept, sent))

    def block_of(kind, block):
        return project.at[:, block] if kind == 3 else weights.at[kind, :, block]

    def line_copy(kind, k, step):
        block = here - step * k
        target = block_of(kind, block)
        source = out_hbm if kind == 3 and k == 0 else target
        sems = up_send if step == 1 else down_send
        return along(step, source, target, sems.at[kind, k], line_recv.at[kind, block])

    def goes(k, step):
        if step == 1:
            return jnp.logical_and(here >= k, here < parts - 1)
        return jnp.logical_and(here + k < parts, here > 0)

    def comes(k, step):
        return here >= k if step == 1 else here + k < parts

    def line_step(kind, k):
        for step in (1, -1):
            if k > 0:

                @pl.when(comes(k, step))
                def _():
                    line_copy(kind, k, step).wait_recv()

            if k < parts - 1:

                @pl.when(goes(k, step))
                def _():
                    line_copy(kind, k, step).start()

    def spread_arrive(kind):
        kept, sent = spread[kind]
        kept.wait()
        for copy in sent:
            copy.wait_recv()

    inputs_load = pltpu.make_async_copy(inputs_hbm, inputs, inputs_sem)
    inputs_load.start()
    out_kept = pltpu.make_async_copy(out_hbm, project.at[:, here], spread_own.at[3])
    out_kept.start()
    for kept, sent in spread:
        kept.start()
        for copy in sent:
            copy.start()
    line_step(3, 0)
    begin, pass_first, pass_second, pass_last, arrive, finish = plane_gather_steps(
        copies, own_ref, normed, own_sem, gather_send, gather_recv
    )
    begin()
    spread_arrive(0)
    line_step(0, 0)
    spread_arrive(1)
    line_step(1, 0)
    spread_arrive(2)
    pass_first()
    line_step(0, 1)
    pass_second()
    line_step(1, 1)
    line_step(0, 2)
    line_step(1, 2)
    line_step(0, 3)
    line_step(2, 0)
    pass_last()
    line_step(1, 3)
    line_step(3, 1)
    arrive()

    many = 2

    def project_rows(kind, at):
        left = normed[pl.ds(at * many, many)].reshape(many * rows, width)
        return matmul(left, weights[kind].reshape(width, channels))

    def rows_at(at):
        return pl.ds(pl.multiple_of(at * many * rows, many * rows), many * rows)

    def strip_of(value, n):
        return value[:, n * lanes : (n + 1) * lanes]

    @pl.loop(0, seqs // many)
    def _(at):
        some = rows_at(at)
        value = project_rows(0, at)
        pre[0, some, :] = value
        inflow = live_ref[some, :] * silu_of(value)
        for n in range(strips):
            state[n, some, :] = strip_of(inflow, n)

    line_step(2, 1)

    @pl.loop(0, seqs // many)
    def _(at):
        some = rows_at(at)
        squash = jax.nn.sigmoid(project_rows(1, at))
        bound = bound_ref[...]
        value = bound + (1.0 - bound) * squash
        for n in range(strips):
            squashed[n, some, :] = strip_of(squash, n)
            forget[n, some, :] = strip_of(value, n)
            state[n, some, :] = (1.0 - strip_of(value, n)) * state[n, some, :]

    line_step(3, 2)

    def step(at, carry):
        some = pl.ds(at, seqs, stride=rows)
        following = []
        for n, (total, product) in enumerate(carry):
            keep = forget[n, some, :]
            total = keep * total + state[n, some, :]
            product = product * keep
            state[n, some, :] = total
            decay[n, some, :] = product
            following.append((total, product))
        return tuple(following)

    start = (jnp.zeros((seqs, lanes), f32), jnp.ones((seqs, lanes), f32))
    carry = lax.fori_loop(0, rows, step, (start,) * strips, unroll=8)
    for n, (total, product) in enumerate(carry):
        ends[here, 0, :, n * lanes : (n + 1) * lanes] = total
        ends[here, 1, :, n * lanes : (n + 1) * lanes] = product
    carries = []
    for k in range(1, parts):
        copy = pltpu.make_async_remote_copy(
            src_ref=ends.at[here],
            dst_ref=ends.at[here],
            send_sem=carry_send.at[k - 1],
            recv_sem=carry_recv.at[k - 1],
            device_id={"tensor": beside(k)},
            device_id_type=pl.DeviceIdType.MESH,
        )
        copy.start()
        carries.append(copy)
    line_step(2, 2)

    def masked_copy(k, step):
        block = here - step * k
        if k > 1:
            source = masked_out.at[block]
        else:
            source = below_hbm if step == 1 else above_hbm
        sems = masked_up if step == 1 else masked_down
        return along(step, source, masked_out.at[block], sems.at[k], masked_recv.at[block])

    def masked_step(k):
        for step in (1, -1):
            if k > 1:

                @pl.when(comes(k, step))
                def _():
                    masked_copy(k, step).wait_recv()

            if k < parts - 1:

                @pl.when(goes(k, step))
                def _():
                    masked_copy(k, step).start()

    for copy in carries:
        copy.wait_recv()
    coming = jnp.zeros((seqs, channels), f32)
    entered = coming
    for k in range(parts - 1):
        coming = ends[k, 1] * coming + ends[k, 0]
        entered = jnp.where(here == k + 1, coming, entered)
    for n in range(seqs):
        entering[n] = entered[n : n + 1]
    line_step(3, 3)
    line_step(2, 3)

    @pl.loop(0, seqs // many)
    def _(at):
        some = rows_at(at)
        value = project_rows(2, at)
        pre[1, some, :] = value
        act = silu_of(value)
        for n in range(many):
            slot = at * many + n
            one = pl.ds(pl.multiple_of(slot * rows, rows), rows)
            for strip in range(strips):
                columns = slice(strip * lanes, (strip + 1) * lanes)
                whole = state[strip, one, :] + (
                    decay[strip, one, :] * entering[slot, :, columns]
                )
                state[strip, one, :] = whole
                mixed[slot, :, columns] = (
                    whole * act[n * rows : (n + 1) * rows, columns]
                ).astype(bf16)

    out_kept.wait()
    stores = [
        pltpu.make_async_copy(source, target, out_sem.at[n])
        for n, (source, target) in enumerate(
            (
                (normed, normed_out),
                (weights, weights_out),
                (project, project_out),
                (pre, pre_out),
                (squashed, squash_out),
                (state, state_out),
                (entering, entering_out),
                (mixed, mixed_out),
            )
        )
    ]
    for store in stores:
        store.start()

    def out_product(slot, columns):
        right = project[:, :, :, columns]
        return matmul(mixed[slot], right.reshape(channels, right.shape[-1]))

    masked_step(1)

    def between(point):
        if point == "low":
            masked_step(2)

    plane_scatter_steps(
        copies, stream_ref, near_buf, one_buf, two_buf, part_buf, scatter_send, scatter_recv,
        out_product, between,
    )

    inputs_load.wait()
    some_rows = min(64, rows)

    @pl.loop(0, rows // some_rows)
    def _(k):
        some = pl.ds(pl.multiple_of(k * some_rows, some_rows), some_rows)
        stream = inputs[some, :] + stream_ref[some, :]
        stream_ref[some, :] = stream
        following_ref[some, :] = (norm_rows(stream)[1] * gain_ref[...]).astype(bf16)

    masked_step(3)
    for k in (1, 2):
        for step in (1, -1):

            @pl.when(goes(k, step))
            def _():
                masked_copy(k, step).wait_send()

    finish()
    for kept, sent in spread:
        for copy in sent:
            copy.wait_send()
    for kind in range(4):
        for k in range(parts - 1):
            for step in (1, -1):

                @pl.when(goes(k, step))
                def _():
                    line_copy(kind, k, step).wait_send()

    for copy in carries:
        copy.wait_send()
    for store in stores:
        store.wait()


def mixer_forward(
    normed, w_input, w_forget, w_gate, w_out, below, above, inputs, bound, live, gain, copies,
    collective,
):
    parts = lax.axis_size("tensor")
    rows, width = normed.shape
    channels = width // 8
    own_rows = w_input.shape[1]
    somewhere = pl.BlockSpec(memory_space=pl.ANY)
    vmem = pl.BlockSpec(memory_space=pltpu.VMEM)
    wide = (8, rows, width)
    weights = (3, 8 * copies, parts, own_rows, channels)
    project = (copies, parts, own_rows, width)
    flat = (8 * rows, channels)
    lanes = min(128, channels)
    strips = (channels // lanes, 8 * rows, lanes)
    shaped = (8, rows, channels)
    half = rows // 2
    dma = pltpu.SemaphoreType.DMA
    return pl.pallas_call(
        functools.partial(mixer_forward_kernel, copies),
        out_shape=[
            jax.ShapeDtypeStruct(wide, bf16),
            jax.ShapeDtypeStruct(weights, bf16),
            jax.ShapeDtypeStruct(project, bf16),
            jax.ShapeDtypeStruct((2,) + flat, f32),
            jax.ShapeDtypeStruct(strips, f32),
            jax.ShapeDtypeStruct(strips, f32),
            jax.ShapeDtypeStruct((8, 1, channels), f32),
            jax.ShapeDtypeStruct(shaped, bf16),
            jax.ShapeDtypeStruct((parts, rows, width), bf16),
            jax.ShapeDtypeStruct((rows, width), f32),
            jax.ShapeDtypeStruct((rows, width), bf16),
        ],
        in_specs=[somewhere] * 8 + [vmem] * 3,
        out_specs=[somewhere] * 9 + [vmem] * 2,
        scratch_shapes=[
            pltpu.VMEM(wide, bf16),
            pltpu.VMEM(weights, bf16),
            pltpu.VMEM(project, bf16),
            pltpu.VMEM((2,) + flat, f32),
            pltpu.VMEM(strips, f32),
            pltpu.VMEM(strips, f32),
            pltpu.VMEM(strips, f32),
            pltpu.VMEM(strips, f32),
            pltpu.VMEM((parts, 2, 8, channels), f32),
            pltpu.VMEM((8, 1, channels), f32),
            pltpu.VMEM(shaped, bf16),
            pltpu.VMEM((4, rows, width), bf16),
            pltpu.VMEM((3, half, width), bf16),
            pltpu.VMEM((3, half, width), bf16),
            pltpu.VMEM((4, rows, width), bf16),
            pltpu.VMEM((rows, width), f32),
            dma,
            dma((14,)),
            dma((14,)),
            dma((3, 7)),
            dma((3, 7)),
            dma((4,)),
            dma((4, parts - 1)),
            dma((4, parts - 1)),
            dma((4, parts)),
            dma((parts - 1,)),
            dma((parts - 1,)),
            dma((10,)),
            dma((10,)),
            dma((parts - 1,)),
            dma((parts - 1,)),
            dma((parts,)),
            dma((8,)),
            dma,
        ],
        compiler_params=pltpu.CompilerParams(
            collective_id=collective, has_side_effects=True, vmem_limit_bytes=56 * 1024 * 1024
        ),
        cost_estimate=pl.CostEstimate(
            flops=8 * rows * width * width,
            bytes_accessed=900 * rows * width,
            transcendentals=0,
        ),
    )(normed, w_input, w_forget, w_gate, w_out, below, above, inputs, bound, live, gain)


def mixer_backward_kernel(
    copies, masks,
    norm_hbm, normed_hbm, weights_hbm, project_hbm, pre_hbm, squash_hbm, state_hbm, mixed_hbm,
    unit_hbm, stream_hbm, cotangent_hbm, entering_ref, bound_ref, live_ref, gain_ref, scale_ref, gain_two_ref,
    rows_hbm, moved_hbm,
    result_ref, input_sum, forget_sum, gate_sum, project_sum, small_sums, moved_out,
    rows_buf, weights, project, pre, squashed, state, mixed, unit, stream, drive, decay, ends,
    entered, grad_pre, grad_w, grad_project, line_w, line_project, bound_sum, whole_w, spread_w,
    small_recv, small_ring, gain_sum, gain_two_sum, near_buf, one_buf, two_buf, part_buf,
    load_sem, gather_send, gather_recv, carry_send, carry_recv, up_send, down_send, line_recv,
    scatter_send, scatter_recv, spread_send, spread_recv, spread_own, small_send, small_got,
    moved_sem, moved_send, moved_recv, first_sem,
):
    parts = lax.axis_size("tensor")
    here = lax.axis_index("tensor")
    seqs, rows, width = rows_buf.shape
    strips, _, lanes = drive.shape
    channels = strips * lanes
    own_rows = weights.shape[3]
    weight_sums = (input_sum, forget_sum, gate_sum)
    near, one, two = copies, 2 * copies, 4 * copies
    mine = slot_of(copies, ())
    greet_all(copies, masks)
    firsts = [
        pltpu.make_async_copy(source, target, first_sem.at[n])
        for n, (source, target) in enumerate(
            ((norm_hbm, result_ref), (stream_hbm, unit), (cotangent_hbm, stream))
        )
    ]
    for load in firsts:
        load.start()
    begin, pass_first, pass_second, pass_last, arrive, finish = plane_gather_steps(
        copies, rows_buf.at[mine], rows_buf, None, gather_send, gather_recv
    )

    at_start, at_end = here == 0, here == parts - 1
    inside = jnp.logical_not(jnp.logical_or(at_start, at_end))
    low_half = here == 1

    def fetch(block, came, first, second):
        loads = (
            pltpu.make_async_copy(rows_hbm.at[block], part_buf.at[first], moved_sem.at[0]),
            pltpu.make_async_copy(came, part_buf.at[second], moved_sem.at[1]),
        )
        for load in loads:
            load.start()
        for load in loads:
            load.wait()
        part_buf[first] = (
            part_buf[first].astype(f32) + part_buf[second].astype(f32)
        ).astype(bf16)

    def moved_copy(n, step, source):
        return along(step, source, moved_out.at[n], moved_send.at[n], moved_recv.at[n])

    def moved_second():
        @pl.when(at_start)
        def _():
            moved_copy(0, 1, rows_hbm.at[2]).start()

        @pl.when(at_end)
        def _():
            moved_copy(1, -1, rows_hbm.at[1]).start()

        @pl.when(inside)
        def _():
            fetch(3 - 3 * (here - 1), moved_hbm, 0, 1)

        @pl.when(low_half)
        def _():
            moved_copy(0, 1, part_buf.at[0]).start()

        @pl.when(here == 2)
        def _():
            moved_copy(1, -1, part_buf.at[0]).start()

    def moved_last():
        @pl.when(at_start)
        def _():
            moved_copy(0, 1, rows_hbm.at[2]).wait_send()
            moved_copy(2, 1, rows_hbm.at[1]).start()

        @pl.when(at_end)
        def _():
            moved_copy(1, -1, rows_hbm.at[1]).wait_send()
            moved_copy(3, -1, rows_hbm.at[2]).start()

        @pl.when(inside)
        def _():
            moved_copy(0, 1, part_buf.at[0]).wait_recv()
            fetch(here + 1, moved_out.at[0], 1, 2)
            moved_copy(2, 1, part_buf.at[1]).start()

        @pl.when(low_half)
        def _():
            moved_copy(0, 1, part_buf.at[0]).wait_send()

        @pl.when(here == 2)
        def _():
            moved_copy(1, -1, part_buf.at[0]).wait_send()

        @pl.when(inside)
        def _():
            moved_copy(1, -1, part_buf.at[0]).wait_recv()
            fetch(here - 1, moved_out.at[1], 2, 3)
            moved_copy(3, -1, part_buf.at[2]).start()

    def moved_end():
        @pl.when(here < parts - 1)
        def _():
            moved_copy(2, 1, part_buf.at[1]).wait_send()
            moved_copy(3, -1, part_buf.at[2]).wait_recv()

        @pl.when(here > 0)
        def _():
            moved_copy(3, -1, part_buf.at[2]).wait_send()
            moved_copy(2, 1, part_buf.at[1]).wait_recv()

    loads = [
        pltpu.make_async_copy(source, target, load_sem.at[n + 1])
        for n, (source, target) in enumerate(
            (
                (project_hbm, project),
                (pre_hbm, pre),
                (state_hbm, state),
                (mixed_hbm, mixed),
                (squash_hbm, squashed),
                (weights_hbm, weights),
                (unit_hbm, unit),
            )
        )
    ]
    for load in loads[:-1]:
        load.start()

    for load in firsts:
        load.wait()
    gain_two_sum[...] = jnp.zeros_like(gain_two_sum)
    some_rows = min(64, rows)

    @pl.loop(0, rows // some_rows)
    def _(k):
        some = pl.ds(pl.multiple_of(k * some_rows, some_rows), some_rows)
        at = pl.ds(pl.multiple_of(mine * rows + k * some_rows, some_rows), some_rows)
        scale, units = norm_rows(unit[some, :])
        grad_norm = result_ref[some, :]
        gain_two_sum[...] += jnp.sum(grad_norm * units, axis=0, keepdims=True)
        total = live_ref[at, :] * stream[some, :] + norm_back(
            grad_norm, units, scale, gain_two_ref[...]
        )
        stream[some, :] = total
        rows_buf[mine, some, :] = total.astype(bf16)

    begin()
    loads[-1].start()
    moved_second()
    for load in loads[:3]:
        load.wait()

    def slot_rows(slot):
        return pl.ds(pl.multiple_of(slot * rows, rows), rows)

    def take(slot):
        some = slot_rows(slot)
        grad_mixed = matmul_rt(rows_buf[slot], project[...].reshape(channels, width))
        gate = pre[1, some, :]
        squash = jax.nn.sigmoid(gate)
        act = gate * squash
        slope = squash * (1.0 + gate * (1.0 - squash))
        for n in range(strips):
            columns = slice(n * lanes, (n + 1) * lanes)
            part = grad_mixed[:, columns]
            drive[n, some, :] = part * act[:, columns]
            at = 2 * channels + n * lanes
            grad_pre[slot, :, at : at + lanes] = (
                part * state[n, some, :] * slope[:, columns]
            ).astype(bf16)

    pass_first()
    pass_second()
    arrive(slice(0, 6))
    for flips in ((), (near,), (one,), (two,), (near, one), (near, two)):
        take(slot_of(copies, flips))
    moved_last()
    pass_last()
    take(slot_of(copies, (one, two)))
    arrive(slice(6, 8))
    take(slot_of(copies, (near, one, two)))

    tile = min(512, width)
    loads[3].wait()

    @pl.loop(0, width // tile)
    def _(k):
        columns = pl.ds(pl.multiple_of(k * tile, tile), tile)
        value = matmul_lt(
            mixed[...].reshape(seqs * rows, channels),
            rows_buf[:, :, columns].reshape(seqs * rows, tile),
        )
        grad_project[:, :, :, columns] = value.astype(bf16).reshape(
            copies, parts, own_rows, tile
        )

    def part_of(kind, block):
        return grad_project.at[:, block] if kind == 3 else grad_w.at[kind, :, block]

    def room_of(kind, index):
        return line_project.at[index] if kind == 3 else line_w.at[kind, index]

    def line_up(kind, k):
        block = parts - 1 - k + here
        return along(
            1, part_of(kind, block), room_of(kind, block), up_send.at[kind, k],
            line_recv.at[kind, block],
        )

    def line_down(kind, k):
        block = k - parts + 1 + here
        index = parts if k == parts - 2 else block
        return along(
            -1, part_of(kind, block), room_of(kind, index), down_send.at[kind, k],
            line_recv.at[kind, index],
        )

    def came(kind, index):
        return along(1, part_of(kind, 0), room_of(kind, index), up_send.at[kind, 0],
                     line_recv.at[kind, index])

    def add_came(kind, block):
        came(kind, block).wait_recv()
        if kind == 3:
            total = grad_project[:, block].astype(f32) + line_project[block].astype(f32)
            grad_project[:, block] = total.astype(bf16)
        else:
            total = grad_w[kind, :, block].astype(f32) + line_w[kind, block].astype(f32)
            grad_w[kind, :, block] = total.astype(bf16)

    def goes_up(k):
        return jnp.logical_and(here <= k, here < parts - 1)

    def goes_down(k):
        return jnp.logical_and(parts - 1 - here <= k, here > 0)

    def line_step(kind, k):
        @pl.when(jnp.logical_and(goes_up(k), here > 0))
        def _():
            add_came(kind, parts - 1 - k + here)

        @pl.when(goes_up(k))
        def _():
            line_up(kind, k).start()

        @pl.when(jnp.logical_and(goes_down(k), here < parts - 1))
        def _():
            add_came(kind, k - parts + 1 + here)

        @pl.when(goes_down(k))
        def _():
            line_down(kind, k).start()

    def advance(kind, k):
        if k + 1 < parts - 1:
            line_step(kind, k + 1)
            return

        @pl.when(here > 0)
        def _():
            came(kind, here).wait_recv()

        @pl.when(here < parts - 1)
        def _():
            came(kind, parts).wait_recv()

        if kind == 3:
            project_sum[...] = (
                grad_project[:, here].astype(f32)
                + line_project[here].astype(f32)
                + line_project[parts].astype(f32)
            )
        else:
            total = (
                grad_w[kind, :, here].astype(f32)
                + line_w[kind, here].astype(f32)
                + line_w[kind, parts].astype(f32)
            )
            whole_w[kind] = total.astype(bf16)
            for copy in spread_copies(kind):
                copy.start()

    @pl.when(at_start)
    def _():
        line_w[:, 0] = jnp.zeros_like(line_w[:, 0])
        line_project[0] = jnp.zeros_like(line_project[0])

    @pl.when(at_end)
    def _():
        line_w[:, parts] = jnp.zeros_like(line_w[:, parts])
        line_project[parts] = jnp.zeros_like(line_project[parts])

    def spread_copies(kind, own=True):
        found = []
        for k in range(1, 8):
            there = group_member(copies, k)
            source = pl.ds(pl.multiple_of(lax.div(there, copies) * copies, copies), copies)
            found.append(
                pltpu.make_async_remote_copy(
                    src_ref=whole_w.at[kind, source],
                    dst_ref=spread_w.at[kind, mine],
                    send_sem=spread_send.at[kind, k - 1],
                    recv_sem=spread_recv.at[kind, k - 1],
                    device_id={"dp": there},
                    device_id_type=pl.DeviceIdType.MESH,
                )
            )
        if own:
            source = pl.ds(pl.multiple_of(mine * copies, copies), copies)
            found.append(
                pltpu.make_async_copy(
                    whole_w.at[kind, source], spread_w.at[kind, mine], spread_own.at[kind]
                )
            )
        return found

    line_step(3, 0)
    finish()
    normed_load = pltpu.make_async_copy(normed_hbm, rows_buf, load_sem.at[0])
    normed_load.start()
    loads[4].wait()

    def step(k, carry):
        some = pl.ds(rows - 1 - k, seqs, stride=rows)
        following = []
        for n, (coming, product) in enumerate(carry):
            bound = bound_ref[:, n * lanes : (n + 1) * lanes]
            keep = bound + (1.0 - bound) * squashed[n, some, :]
            carried = drive[n, some, :] + coming
            drive[n, some, :] = carried
            decay[n, some, :] = product
            following.append((keep * carried, product * keep))
        return tuple(following)

    start = (jnp.zeros((seqs, lanes), f32), jnp.ones((seqs, lanes), f32))
    carry = lax.fori_loop(0, rows, step, (start,) * strips, unroll=8)
    for n, (coming, product) in enumerate(carry):
        ends[here, 0, :, n * lanes : (n + 1) * lanes] = coming
        ends[here, 1, :, n * lanes : (n + 1) * lanes] = product
    carries = []
    for k in range(1, parts):
        copy = pltpu.make_async_remote_copy(
            src_ref=ends.at[here],
            dst_ref=ends.at[here],
            send_sem=carry_send.at[k - 1],
            recv_sem=carry_recv.at[k - 1],
            device_id={"tensor": beside(k)},
            device_id_type=pl.DeviceIdType.MESH,
        )
        copy.start()
        carries.append(copy)
    normed_load.wait()

    def weight_grad(kind):
        @pl.loop(0, width // tile)
        def _(k):
            columns = pl.ds(pl.multiple_of(k * tile, tile), tile)
            value = matmul_lt(
                grad_pre[:, :, kind * channels : (kind + 1) * channels].reshape(
                    seqs * rows, channels
                ),
                rows_buf[:, :, columns].reshape(seqs * rows, tile),
            )
            count = tile // (parts * own_rows)
            grad_w[kind, pl.ds(k * count, count)] = value.T.astype(bf16).reshape(
                count, parts, own_rows, channels
            )

        line_step(kind, 0)

    advance(3, 0)
    weight_grad(2)
    for copy in carries:
        copy.wait_recv()
    coming = jnp.zeros((seqs, channels), f32)
    arrived = coming
    for k in range(parts - 1, 0, -1):
        coming = ends[k, 1] * coming + ends[k, 0]
        arrived = jnp.where(here == k - 1, coming, arrived)
    for n in range(seqs):
        entered[n] = arrived[n : n + 1]
    bound_sum[...] = jnp.zeros_like(bound_sum)
    first_row = lax.broadcasted_iota(jnp.int32, (rows, lanes), 0) == 0

    @pl.loop(0, seqs)
    def _(slot):
        some = slot_rows(slot)
        alive = live_ref[some, :]
        for n in range(strips):
            columns = slice(n * lanes, (n + 1) * lanes)
            bound = bound_ref[:, columns]
            squash = squashed[n, some, :]
            keep = bound + (1.0 - bound) * squash
            carried = drive[n, some, :] + decay[n, some, :] * entered[slot, :, columns]
            prior = jnp.where(
                first_row, entering_ref[slot, :, columns], pltpu.roll(state[n, some, :], 1, 0)
            )
            value = pre[0, some, columns]
            gate = jax.nn.sigmoid(value)
            slope = gate * (1.0 + value * (1.0 - gate))
            grad_forget = carried * prior - carried * alive * value * gate
            at = n * lanes
            grad_pre[slot, :, at : at + lanes] = (
                carried * alive * (1.0 - keep) * slope
            ).astype(bf16)
            at = channels + n * lanes
            grad_pre[slot, :, at : at + lanes] = (
                grad_forget * (1.0 - bound) * squash * (1.0 - squash)
            ).astype(bf16)
            bound_sum[:, columns] += jnp.sum(
                grad_forget * (1.0 - squash), axis=0, keepdims=True
            )

    advance(3, 1)
    loads[5].wait()
    moved_end()

    def normed_product(slot, columns):
        at = lax.div(columns.start, parts * own_rows)
        count = tile // (parts * own_rows)
        total = None
        for kind in range(3):
            part = matmul_rt(
                grad_pre[slot, :, kind * channels : (kind + 1) * channels],
                weights[kind, pl.ds(at, count)].reshape(tile, channels),
            )
            total = part if total is None else total + part
        return total

    def between(point):
        if point == "sent":
            weight_grad(0)
            advance(2, 0)
            weight_grad(1)
            advance(3, 2)
        elif point == "added":
            advance(2, 1)
            advance(0, 0)
        elif point == "top":
            advance(1, 0)
            advance(2, 2)
        elif point == "low":
            advance(0, 1)
            advance(1, 1)

    plane_scatter_steps(
        copies, result_ref, near_buf, one_buf, two_buf, part_buf, scatter_send, scatter_recv,
        normed_product, between,
    )

    loads[6].wait()
    gain_sum[...] = jnp.zeros_like(gain_sum)

    @pl.loop(0, rows // some_rows)
    def _(k):
        some = pl.ds(pl.multiple_of(k * some_rows, some_rows), some_rows)
        grad_norm = result_ref[some, :]
        units = unit[some, :]
        gain_sum[...] += jnp.sum(grad_norm * units, axis=0, keepdims=True)
        scaled = grad_norm * gain_ref[...]
        mean = jnp.mean(scaled * units, axis=-1, keepdims=True)
        result_ref[some, :] = stream[some, :] + scale_ref[some, :] * (scaled - units * mean)

    for n in range(8):
        columns = slice(n * channels, (n + 1) * channels)
        small_sums[n : n + 1, :] = gain_sum[:, columns]
        small_sums[8 + n : 9 + n, :] = gain_two_sum[:, columns]
        small_sums[16 + n : 17 + n, :] = jnp.where(mine == n, bound_sum[...], 0.0)

    plane_small = []
    for k in range(1, 8):
        copy = pltpu.make_async_remote_copy(
            src_ref=small_sums,
            dst_ref=small_recv.at[k - 1],
            send_sem=small_send.at[k - 1],
            recv_sem=small_got.at[k - 1],
            device_id={"dp": group_member(copies, k)},
            device_id_type=pl.DeviceIdType.MESH,
        )
        copy.start()
        plane_small.append(copy)

    def small_copy(n):
        return pltpu.make_async_remote_copy(
            src_ref=small_sums,
            dst_ref=small_recv.at[7 + n],
            send_sem=small_send.at[7 + n],
            recv_sem=small_got.at[7 + n],
            device_id={"dp": partner(masks[n])},
            device_id_type=pl.DeviceIdType.MESH,
        )

    advance(0, 2)
    advance(1, 2)
    for copy in plane_small:
        copy.wait()
    for k in range(7):
        small_sums[...] += small_recv[k]
    for n in range(len(masks)):
        small_copy(n).start()
        small_copy(n).wait()
        small_sums[...] += small_recv[7 + n]
    ring_small = []
    for k in range(1, parts):
        copy = pltpu.make_async_remote_copy(
            src_ref=small_sums,
            dst_ref=small_ring.at[k - 1],
            send_sem=small_send.at[7 + len(masks) + k - 1],
            recv_sem=small_got.at[7 + len(masks) + k - 1],
            device_id={"tensor": beside(k)},
            device_id_type=pl.DeviceIdType.MESH,
        )
        copy.start()
        ring_small.append(copy)
    for kind in (2, 0, 1):
        spread = spread_copies(kind)
        for copy in spread[:-1]:
            copy.wait_recv()
        spread[-1].wait()
        for slot in range(8):
            weight_sums[kind][:, :, slot * channels : (slot + 1) * channels] = spread_w[
                kind, slot
            ].astype(f32)
    for copy in ring_small:
        copy.wait()
    for k in range(parts - 1):
        small_sums[...] += small_ring[k]
    for kind in range(4):
        for k in range(parts - 1):

            @pl.when(goes_up(k))
            def _():
                line_up(kind, k).wait_send()

            @pl.when(goes_down(k))
            def _():
                line_down(kind, k).wait_send()

    for kind in range(3):
        for copy in spread_copies(kind, False):
            copy.wait_send()
    for copy in carries:
        copy.wait_send()


def mixer_backward(
    grad_norm, normed, weights, project, pre, squashed, state, mixed, unit, stream, cotangent,
    entering, bound, live, gain, scale, gain_two, out_rows, out_moved, copies, masks, collective,
):
    parts = lax.axis_size("tensor")
    _, rows, width = normed.shape
    channels = width // 8
    own_rows = project.shape[2]
    somewhere = pl.BlockSpec(memory_space=pl.ANY)
    vmem = pl.BlockSpec(memory_space=pltpu.VMEM)
    half = rows // 2
    dma = pltpu.SemaphoreType.DMA
    blocks = (8 * copies, own_rows, channels)
    small = (24, channels)
    return pl.pallas_call(
        functools.partial(mixer_backward_kernel, copies, masks),
        out_shape=[
            jax.ShapeDtypeStruct((rows, width), f32),
        ]
        + [jax.ShapeDtypeStruct((copies, own_rows, width), f32)] * 4
        + [
            jax.ShapeDtypeStruct(small, f32),
            jax.ShapeDtypeStruct((4, rows, width), bf16),
        ],
        in_specs=[somewhere] * 11 + [vmem] * 6 + [somewhere] * 2,
        out_specs=[vmem] * 6 + [somewhere],
        scratch_shapes=[
            pltpu.VMEM(normed.shape, bf16),
            pltpu.VMEM(weights.shape, bf16),
            pltpu.VMEM(project.shape, bf16),
            pltpu.VMEM(pre.shape, f32),
            pltpu.VMEM(squashed.shape, f32),
            pltpu.VMEM(state.shape, f32),
            pltpu.VMEM(mixed.shape, bf16),
            pltpu.VMEM((rows, width), f32),
            pltpu.VMEM((rows, width), f32),
            pltpu.VMEM(state.shape, f32),
            pltpu.VMEM(state.shape, f32),
            pltpu.VMEM((parts, 2, 8, channels), f32),
            pltpu.VMEM((8, 1, channels), f32),
            pltpu.VMEM((8, rows, 3 * channels), bf16),
            pltpu.VMEM(weights.shape, bf16),
            pltpu.VMEM(project.shape, bf16),
            pltpu.VMEM((3, parts + 1) + blocks, bf16),
            pltpu.VMEM((parts + 1, copies, own_rows, width), bf16),
            pltpu.VMEM((1, channels), f32),
            pltpu.VMEM((3,) + blocks, bf16),
            pltpu.VMEM((3, 8, copies, own_rows, channels), bf16),
            pltpu.VMEM((7 + len(masks),) + small, f32),
            pltpu.VMEM((parts - 1,) + small, f32),
            pltpu.VMEM((1, width), f32),
            pltpu.VMEM((1, width), f32),
            pltpu.VMEM((4, rows, width), bf16),
            pltpu.VMEM((3, half, width), bf16),
            pltpu.VMEM((3, half, width), bf16),
            pltpu.VMEM((4, rows, width), bf16),
            dma((9,)),
            dma((14,)),
            dma((14,)),
            dma((parts - 1,)),
            dma((parts - 1,)),
            dma((4, parts - 1)),
            dma((4, parts - 1)),
            dma((4, parts + 1)),
            dma((10,)),
            dma((10,)),
            dma((3, 7)),
            dma((3, 7)),
            dma((3,)),
            dma((7 + len(masks) + parts - 1,)),
            dma((7 + len(masks) + parts - 1,)),
            dma((2,)),
            dma((4,)),
            dma((4,)),
            dma((3,)),
        ],
        compiler_params=pltpu.CompilerParams(
            collective_id=collective, has_side_effects=True, vmem_limit_bytes=62 * 1024 * 1024
        ),
        cost_estimate=pl.CostEstimate(
            flops=16 * rows * width * width,
            bytes_accessed=900 * rows * width,
            transcendentals=0,
        ),
    )(
        grad_norm, normed, weights, project, pre, squashed, state, mixed, unit, stream, cotangent,
        entering, bound, live, gain, scale, gain_two, out_rows, out_moved,
    )


def on_device(
    inputs,
    lengths,
    gain_mix,
    gain_glu,
    lower_bound,
    w_input,
    w_forget,
    w_gate_mix,
    w_out,
    w_gate,
    w_up,
    w_down,
    cotangent,
):
    tensor_parts = lax.axis_size("tensor")
    data_parts = lax.axis_size("dp")
    tensor_index = lax.axis_index("tensor")
    data_index = lax.axis_index("dp")
    rows_here, width = inputs.shape
    group = min(8, data_parts)
    copies = data_parts // group
    group_index = lax.div(data_index, copies)
    copy_index = lax.rem(data_index, copies)
    group_masks = [copies << k for k in range(group.bit_length() - 1)]
    copy_masks = [1 << k for k in range(copies.bit_length() - 1)]
    all_masks = [1 << k for k in range(data_parts.bit_length() - 1)]
    group_lists = [[g * copies + o for g in range(group)] for o in range(copies)]
    channels = width // group
    own_rows = w_input.shape[0]

    high = lax.div(lengths, 32).astype(bf16)
    low = lax.rem(lengths, 32).astype(bf16)
    length_row = jnp.concatenate([high, low, jnp.zeros((own_rows - 2,), bf16)])
    small = jnp.stack([gain_mix, gain_glu, lower_bound, length_row])
    small = in_order(shifted_blocks(small))
    small = gather_bits(small, sorted(all_masks, reverse=True)).astype(f32)
    small = small.reshape((data_parts * tensor_parts,) + small.shape[2:])
    gain_one = small[:, 0].reshape(width)
    gain_two = small[:, 1].reshape(width)
    bound = lax.dynamic_slice_in_dim(small[:, 2].reshape(width), group_index * channels, channels)
    every_length = small[:, 3].reshape(data_parts, tensor_parts, own_rows)[:, 0, :2]
    every_length = (every_length[:, 0] * 32.0 + every_length[:, 1]).astype(jnp.int32)
    group_lengths = lax.dynamic_index_in_dim(
        every_length.reshape(group, copies), copy_index, axis=1, keepdims=False
    )
    position = tensor_index * rows_here + jnp.arange(rows_here, dtype=jnp.int32)
    live_own = (position < lengths[0]).astype(f32)[:, None]
    live = (position[None, :] < group_lengths[:, None]).astype(f32)
    live = live.reshape(group * rows_here, 1)

    mixer_weights = [w_input, w_forget, w_gate_mix, w_out]
    if copies > 1:
        mixer_weights = [gather_bits(weight, copy_masks[::-1]) for weight in mixer_weights]
    mixer_weights = [weight.reshape(copies, own_rows, width) for weight in mixer_weights]

    masked_own = (live_own * cotangent).astype(bf16)
    masked_below, masked_above = (
        lax.ppermute(
            masked_own,
            "tensor",
            [(i, i + step) for i in range(tensor_parts) if 0 <= i + step < tensor_parts],
        )
        for step in (1, -1)
    )

    scale_one, unit_one = norm_rows(inputs)
    rows_all = group * rows_here
    *mixer_kept, mixed, masked_others, stream, normed_two = (
        mixer_forward(
            (unit_one * gain_one).astype(bf16),
            *mixer_weights,
            masked_below,
            masked_above,
            inputs,
            bound[None, :],
            live,
            gain_two[None, :],
            copies,
            1,
        )
    )

    hidden_here = w_gate.shape[1]
    gate_w, up_w = (
        lax.all_gather(weight, "dp", axis=0, tiled=True).reshape(group, channels, hidden_here)
        for weight in (w_gate, w_up)
    )
    down_part = w_down.T
    if copies > 1:
        down_part = gather_bits(down_part, copy_masks[::-1]).reshape(channels, hidden_here)

    out_rows, out_moved, grad_norm_two, *weight_sums = swiglu(
        normed_two,
        masked_own,
        masked_below,
        masked_above,
        masked_others,
        gate_w,
        up_w,
        down_part,
        copies,
        4,
    )
    if copies > 1:
        weight_sums = [
            scatter_bits(total.reshape(copies, width // data_parts, hidden_here), copy_masks, f32)
            for total in weight_sums
        ]
    grad_gate_mine, grad_up_mine, grad_down_mine = weight_sums
    grad_down_mine = grad_down_mine.T

    normed_one, mixer_w, out_w, pre, squashed, state, entering = mixer_kept
    grad_inputs, *grad_weights, small_sums, out_others = mixer_backward(
        grad_norm_two,
        normed_one,
        mixer_w,
        out_w,
        pre,
        squashed,
        state,
        mixed,
        unit_one,
        stream,
        cotangent,
        entering,
        bound[None, :],
        live,
        gain_one[None, :],
        scale_one,
        gain_two[None, :],
        out_rows,
        out_moved,
        copies,
        copy_masks,
        3,
    )
    out_sum = lax.dynamic_index_in_dim(out_rows, tensor_index, 0, keepdims=False).astype(f32)
    out_sum += jnp.where(tensor_index > 0, out_others[2].astype(f32), 0.0)
    out_sum += jnp.where(tensor_index < tensor_parts - 1, out_others[3].astype(f32), 0.0)
    output = live_own * (stream + out_sum)
    if copies > 1:
        grad_weights = [scatter_bits(total, copy_masks, f32) for total in grad_weights]
    grad_weights = [total.reshape(own_rows, width) for total in grad_weights]
    place = (data_index * tensor_parts + tensor_index) * own_rows
    small_own = lax.dynamic_slice(small_sums.reshape(3, width), (0, place), (3, own_rows))
    return (
        output,
        grad_inputs,
        small_own[0],
        small_own[1],
        small_own[2],
        *grad_weights,
        grad_gate_mine,
        grad_up_mine,
        grad_down_mine,
    )


def solution(mesh):
    both = ("dp", "tensor")
    placed = (
        P(both, None),
        P("dp"),
        P(both),
        P(both),
        P(both),
        P(both, None),
        P(both, None),
        P(both, None),
        P(both, None),
        P("dp", "tensor"),
        P("dp", "tensor"),
        P("tensor", "dp"),
        P(both, None),
    )
    return jax.shard_map(
        on_device,
        mesh=mesh,
        in_specs=placed,
        out_specs=(
            P(both, None),
            P(both, None),
            P(both),
            P(both),
            P(both),
            P(both, None),
            P(both, None),
            P(both, None),
            P(both, None),
            P("dp", "tensor"),
            P("dp", "tensor"),
            P("tensor", "dp"),
        ),
        check_vma=False,
    )
```

```python
import functools

import jax
import jax.numpy as jnp
from jax import lax
from jax.experimental import pallas as pl
from jax.experimental.pallas import tpu as pltpu
from jax.sharding import PartitionSpec as P

epsilon = 1e-06
bf16 = jnp.bfloat16
f32 = jnp.float32


def matmul(left, right):
    return jnp.dot(left, right, preferred_element_type=f32)


def matmul_rt(left, right):
    return lax.dot_general(left, right, (((1,), (1,)), ((), ())), preferred_element_type=f32)


def matmul_lt(left, right):
    return lax.dot_general(left, right, (((0,), (0,)), ((), ())), preferred_element_type=f32)


def silu_of(value):
    return value * jax.nn.sigmoid(value)


def silu_slope(value):
    squash = jax.nn.sigmoid(value)
    return squash * (1.0 + value * (1.0 - squash))


def norm_rows(value):
    scale = lax.rsqrt(jnp.mean(value * value, axis=-1, keepdims=True) + epsilon)
    return (scale, value * scale)


def norm_back(grad_norm, unit, scale, gain):
    scaled = grad_norm * gain
    return scale * (scaled - unit * jnp.mean(scaled * unit, axis=-1, keepdims=True))


def untouched_kernel(*refs):
    pass


def after(value, *others):
    somewhere = pl.BlockSpec(memory_space=pl.ANY)
    return pl.pallas_call(
        untouched_kernel,
        out_shape=jax.ShapeDtypeStruct(value.shape, value.dtype),
        in_specs=[somewhere] * (1 + len(others)),
        out_specs=somewhere,
        input_output_aliases={0: 0},
        cost_estimate=pl.CostEstimate(flops=0, bytes_accessed=0, transcendentals=0),
    )(value, *others)


def swap(value, mask):
    return lax.ppermute(value, "dp", [(i, i ^ mask) for i in range(lax.axis_size("dp"))])


def own_bit(mask):
    return lax.rem(lax.div(lax.axis_index("dp"), mask), 2)


def gather_bits(value, order):
    base = value.shape
    done = []
    for mask in order:
        other = swap(value, mask)
        at = sum(1 for seen in done if seen > mask)
        low = jnp.stack([value, other], axis=at)
        high = jnp.stack([other, value], axis=at)
        value = jnp.where(own_bit(mask) == 0, low, high)
        done.append(mask)
    return value.reshape((1 << len(order),) + base)


def scatter_bits(value, order, sent=bf16, hold=(None, None)):
    count = len(order)
    value = value.reshape((2,) * count + value.shape[1:])
    left = sorted(order, reverse=True)
    for mask in order:
        at = left.index(mask)
        left.remove(mask)
        bit = own_bit(mask)
        send = lax.dynamic_index_in_dim(value, 1 - bit, at, keepdims=False).astype(sent)
        keep = lax.dynamic_index_in_dim(value, bit, at, keepdims=False)
        if hold[0] == count - len(left) - 1:
            send = after(send, hold[1])
        total = keep.astype(f32) + swap(send, mask).astype(f32)
        value = total.astype(sent) if left else total
    return value


def orders(masks):
    down = sorted(masks, reverse=True)
    if len(down) < 3:
        return down, down
    return down, [down[1], down[0]] + down[2:]


def gather_halves(value, masks):
    first, second = orders(masks)
    half = value.shape[-1] // 2
    return gather_bits(value[..., :half], first), gather_bits(value[..., half:], second)


def scatter_halves(left, right, masks):
    first, second = orders(masks)
    return jnp.concatenate(
        [scatter_bits(left, first[::-1]), scatter_bits(right, second[::-1])], axis=-1
    )


def ring(value):
    parts = lax.axis_size("tensor")
    return lax.ppermute(value, "tensor", [(i, (i + 1) % parts) for i in range(parts)])


def ring_blocks(value):
    blocks = [value]
    for _ in range(lax.axis_size("tensor") - 1):
        blocks.append(ring(blocks[-1]))
    return blocks


def ring_scatter(blocks):
    total = blocks[1 % len(blocks)]
    totals = [total]
    for k in range(2, len(blocks) + 1):
        moved = ring(total).astype(f32)
        total = moved + blocks[k % len(blocks)].astype(f32)
        if k < len(blocks):
            total = total.astype(bf16)
            totals.append(total)
    return total, totals


def shifted_blocks(value):
    parts = lax.axis_size("tensor")
    blocks = [value]
    for k in range(1, parts):
        blocks.append(lax.ppermute(value, "tensor", [(i, (i + k) % parts) for i in range(parts)]))
    return blocks


def scatter_straight(value):
    here = lax.axis_index("tensor")
    parts = lax.axis_size("tensor")
    total = lax.dynamic_index_in_dim(value, here, 0, keepdims=False)
    for k in range(1, parts):
        send = lax.dynamic_index_in_dim(value, lax.rem(here + k, parts), 0, keepdims=False)
        total += lax.ppermute(send, "tensor", [(i, (i + k) % parts) for i in range(parts)])
    return total


def in_order(blocks):
    here = lax.axis_index("tensor")
    parts = len(blocks)
    stacked = jnp.stack(blocks[::-1] + blocks[::-1])
    return lax.dynamic_slice_in_dim(stacked, parts - 1 - here, parts, 0)


def partner(mask):
    me = lax.axis_index("dp")
    return me + mask * (1 - 2 * lax.rem(lax.div(me, mask), 2))


def greet(masks, ring_too=False):
    barrier = pltpu.get_barrier_semaphore()
    others = [{"dp": partner(mask)} for mask in masks]
    if ring_too:
        others += [{"tensor": beside(1)}, {"tensor": beside(-1)}]
    for other in others:
        pl.semaphore_signal(
            barrier, inc=1, device_id=other, device_id_type=pl.DeviceIdType.MESH
        )
    pl.semaphore_wait(barrier, len(others))


def beside(step):
    parts = lax.axis_size("tensor")
    return lax.rem(lax.axis_index("tensor") + step + parts, parts)


def slot_of(copies, masks):
    me = lax.axis_index("dp")
    for mask in masks:
        me = me + mask * (1 - 2 * lax.rem(lax.div(me, mask), 2))
    return lax.div(me, copies)


def to_right(source, target, send_sem, recv_sem):
    return pltpu.make_async_remote_copy(
        src_ref=source,
        dst_ref=target,
        send_sem=send_sem,
        recv_sem=recv_sem,
        device_id={"tensor": beside(1)},
        device_id_type=pl.DeviceIdType.MESH,
    )


def along(step, source, target, send_sem, recv_sem):
    return pltpu.make_async_remote_copy(
        src_ref=source,
        dst_ref=target,
        send_sem=send_sem,
        recv_sem=recv_sem,
        device_id={"tensor": beside(step)},
        device_id_type=pl.DeviceIdType.MESH,
    )


def plane_gather_steps(copies, value_ref, all_ref, own_sem, send_sem, recv_sem):
    near, one, two = copies, 2 * copies, 4 * copies
    half = value_ref.shape[0] // 2
    top, low = pl.ds(0, half), pl.ds(half, half)
    mine = slot_of(copies, ())
    at_one, at_two = slot_of(copies, (one,)), slot_of(copies, (two,))
    at_both = slot_of(copies, (one, two))
    local = None
    if own_sem is not None:
        local = pltpu.make_async_copy(value_ref, all_ref.at[mine], own_sem)
    sent = []
    last = []

    def send(source, slot, rows, mask):
        index = len(sent)
        copy = pltpu.make_async_remote_copy(
            src_ref=source,
            dst_ref=all_ref.at[slot, rows],
            send_sem=send_sem.at[index],
            recv_sem=recv_sem.at[index],
            device_id={"dp": partner(mask)},
            device_id_type=pl.DeviceIdType.MESH,
        )
        copy.start()
        sent.append(copy)
        if mask == near:
            last.append(copy)
        return copy

    def forward(slot, rows, mask):
        return send(all_ref.at[slot, rows], slot, rows, mask)

    first = []
    second = []

    def begin():
        if local is not None:
            local.start()
        first.append(send(value_ref.at[top], mine, top, two))
        first.append(send(value_ref.at[low], mine, low, one))
        first.append(send(value_ref.at[low], mine, low, two))
        first.append(send(value_ref.at[top], mine, top, one))
        send(value_ref.at[top], mine, top, near)
        send(value_ref.at[low], mine, low, near)

    def pass_first():
        first[0].wait_recv()
        second.append(forward(at_two, top, one))
        forward(at_two, top, near)
        first[1].wait_recv()
        second.append(forward(at_one, low, two))
        forward(at_one, low, near)

    def pass_second():
        first[2].wait_recv()
        forward(at_two, low, near)
        first[3].wait_recv()
        forward(at_one, top, near)

    def pass_last():
        second[0].wait_recv()
        forward(at_both, top, near)
        second[1].wait_recv()
        forward(at_both, low, near)

    def arrive(some=slice(None)):
        for copy in last[some]:
            copy.wait_recv()
        if some == slice(None) and local is not None:
            local.wait()

    def finish():
        for copy in sent:
            copy.wait_send()

    return begin, pass_first, pass_second, pass_last, arrive, finish


def plane_scatter_steps(
    copies, sum_ref, near_ref, one_ref, two_ref, part_ref,
    send_sem, recv_sem, product, between,
):
    near, one, two = copies, 2 * copies, 4 * copies
    rows, width = sum_ref.shape
    half = rows // 2
    top, low = pl.ds(0, half), pl.ds(half, half)
    tile = min(512, width)
    flips = [(), (one,), (two,), (one, two)]
    copies_out = []

    def send(source, target, mask):
        index = len(copies_out)
        copy = pltpu.make_async_remote_copy(
            src_ref=source,
            dst_ref=target,
            send_sem=send_sem.at[index],
            recv_sem=recv_sem.at[index],
            device_id={"dp": partner(mask)},
            device_id_type=pl.DeviceIdType.MESH,
        )
        copy.start()
        copies_out.append(copy)
        return copy

    def each_tile(body):
        @pl.loop(0, width // tile)
        def _(k):
            body(pl.ds(pl.multiple_of(k * tile, tile), tile))

    arriving = {}
    for k in (3, 1, 2, 0):
        slot = slot_of(copies, flips[k] + (near,))

        def theirs(columns, k=k, slot=slot):
            part_ref[k, :, columns] = product(slot, columns).astype(bf16)

        each_tile(theirs)
        arriving[k] = send(part_ref.at[k], near_ref.at[k], near)

    between("sent")

    def added(k):
        slot = slot_of(copies, flips[k])
        arriving[k].wait_recv()

        def mine(columns):
            total = product(slot, columns) + near_ref[k, :, columns].astype(f32)
            if k == 0:
                sum_ref[:, columns] = total
            else:
                near_ref[k, :, columns] = total.astype(bf16)

        each_tile(mine)

    added(3)
    one_first = send(near_ref.at[3, top], one_ref.at[0], one)
    two_first = send(near_ref.at[3, low], two_ref.at[0], two)
    added(1)
    one_second = send(near_ref.at[1, top], one_ref.at[1], one)
    added(2)
    two_second = send(near_ref.at[2, low], two_ref.at[1], two)
    added(0)
    between("added")

    one_first.wait_recv()

    def pass_top(columns):
        total = near_ref[2, top, columns].astype(f32) + one_ref[0, :, columns].astype(f32)
        near_ref[2, top, columns] = total.astype(bf16)

    each_tile(pass_top)
    two_last = send(near_ref.at[2, top], two_ref.at[2], two)
    between("top")
    two_first.wait_recv()

    def pass_low(columns):
        total = near_ref[1, low, columns].astype(f32) + two_ref[0, :, columns].astype(f32)
        near_ref[1, low, columns] = total.astype(bf16)

    each_tile(pass_low)
    one_last = send(near_ref.at[1, low], one_ref.at[2], one)
    between("low")

    def finish(rows_at, first, at_first, second, at_second):
        def body(columns):
            sum_ref[rows_at, columns] += (
                first[at_first, :, columns].astype(f32) + second[at_second, :, columns].astype(f32)
            )

        each_tile(body)

    one_second.wait_recv()
    two_last.wait_recv()
    finish(top, one_ref, 1, two_ref, 2)
    two_second.wait_recv()
    one_last.wait_recv()
    finish(low, two_ref, 1, one_ref, 2)
    for copy in copies_out:
        copy.wait_send()


def column_tiles(width, most=512):
    return [(at, min(most, width - at)) for at in range(0, width, most)]


def swiglu_kernel(
    copies,
    normed_ref, own_ref, below_ref, others_ref, gate_hbm, up_hbm, down_ref,
    rows_out, moved_out, norm_sum, gate_sum, up_sum, down_sum,
    normed, masked, gate_w, up_w, down_w, hidden, gate_low, up_low, back, rows, ring_buf,
    one_buf, two_buf, lead, lead_near, in_sem, out_sem, gather_send, gather_recv, send_sem,
    recv_sem, sum_send, sum_recv, near_send, near_recv, one_send, one_recv, two_send, two_recv,
    ready_sem, moved_send, moved_recv,
):
    parts = lax.axis_size("tensor")
    near, one, two = copies, 2 * copies, 4 * copies
    greet((near, one, two), True)
    own = pltpu.make_async_copy(normed_ref, normed.at[0], in_sem.at[0])
    own.start()
    gather = plane_gather_steps(
        copies, down_ref, down_w, in_sem.at[4], gather_send, gather_recv
    )
    gather[0]()
    loads = [
        pltpu.make_async_copy(gate_hbm, gate_w, in_sem.at[1]),
        pltpu.make_async_copy(up_hbm, up_w, in_sem.at[2]),
        pltpu.make_async_copy(own_ref, masked.at[0], in_sem.at[3]),
    ]
    own.wait()
    for load in loads:
        load.start()
    here = lax.axis_index("tensor")
    at_start, at_end = here == 0, here == parts - 1

    for k in range(1, parts):
        source = below_ref if k == 1 else others_ref.at[beside(-k)]
        loads.append(pltpu.make_async_copy(source, masked.at[k], in_sem.at[4 + k]))
        loads[-1].start()

    _, block_rows, width = normed.shape
    hidden_width = hidden.shape[2]
    share = width // 8
    half = share // 2
    many = 2
    tile = many * share
    both = [pl.ds(n * (block_rows // 2), block_rows // 2) for n in range(2)]

    def hop(k, n):
        return to_right(
            normed.at[k, both[n]], normed.at[k + 1, both[n]], send_sem.at[k, n], recv_sem.at[k, n]
        )

    def sum_hop(k, n):
        return to_right(
            back.at[k + 1, both[n]], ring_buf.at[k, both[n]], sum_send.at[k, n], sum_recv.at[k, n]
        )

    for n in range(2):
        hop(0, n).start()
    for load in loads:
        load.wait()
    gather[1]()
    gather[2]()
    for n in range(2):
        hop(0, n).wait_recv()
        hop(1, n).start()
    gather[3]()
    gather[4]()

    def store(k):
        home = lax.rem(lax.axis_index("tensor") + parts - k, parts)
        slot = lax.rem(k, 2)
        return pltpu.make_async_copy(rows.at[slot], rows_out.at[home], out_sem.at[slot])

    def front(k):
        for at, size in column_tiles(hidden_width):
            columns = pl.ds(at, size)

            def weight(ref):
                return ref[:, :, columns].reshape(width, size)

            glu_gate = matmul(normed[k], weight(gate_w))
            glu_up = matmul(normed[k], weight(up_w))
            grad_hidden = matmul(masked[k], weight(down_w))
            squash = jax.nn.sigmoid(glu_gate)
            act = glu_gate * squash
            slope = squash * (1.0 + glu_gate * (1.0 - squash))
            hidden[k, :, columns] = (act * glu_up).astype(bf16)
            gate_low[k, :, columns] = (grad_hidden * glu_up * slope).astype(bf16)
            up_low[k, :, columns] = (grad_hidden * act).astype(bf16)

    def rear(k):
        slot = lax.rem(k, 2)

        @pl.loop(0, 8 // many)
        def _(n):
            some = pl.ds(pl.multiple_of(n * tile, tile), tile)

            def weight(ref):
                return ref[pl.ds(n * many, many)].reshape(tile, hidden_width)

            back[k, :, some] = (
                matmul_rt(gate_low[k], weight(gate_w)) + matmul_rt(up_low[k], weight(up_w))
            ).astype(bf16)
            rows[slot, :, some] = matmul_rt(hidden[k], weight(down_w)).astype(bf16)

        store(k).start()

    def block(k, nothing):
        for n in range(2):

            @pl.when(jnp.logical_and(k > 0, k < parts - 2))
            def _():
                hop(k, n).wait_recv()
                hop(k + 1, n).start()

            @pl.when(k == parts - 1)
            def _():
                hop(parts - 2, n).wait_recv()
                sum_hop(0, n).start()

        front(k)

        @pl.when(k > 1)
        def _():
            store(k - 2).wait()

        @pl.when(k < parts - 1)
        def _():
            rear(k)

        return nothing

    lax.fori_loop(0, parts, block, 0)

    tall = parts * block_rows
    kinds = (
        (normed, gate_low, gate_w, gate_sum),
        (normed, up_low, up_w, up_sum),
        (masked, hidden, down_w, down_sum),
    )

    def product(kind, slot, store):
        left, right, _, _ = kinds[kind]
        some = pl.ds(pl.multiple_of(slot * share, share), share)
        for at, size in column_tiles(hidden_width):
            columns = pl.ds(at, size)
            store(
                columns,
                matmul_lt(
                    left[:, :, some].reshape(tall, share), right[:, :, columns].reshape(tall, size)
                ),
            )

    def across(source, target, send, recv, mask):
        return pltpu.make_async_remote_copy(
            src_ref=source,
            dst_ref=target,
            send_sem=send,
            recv_sem=recv,
            device_id={"dp": partner(mask)},
            device_id_type=pl.DeviceIdType.MESH,
        )

    top, low = pl.ds(0, half), pl.ds(half, half)

    def near_copy(kind, k):
        room = kinds[kind][2]
        return across(
            room.at[k], room.at[4 + k], near_send.at[kind, k], near_recv.at[kind, k], near
        )

    def lead_copy(kind):
        return across(
            lead.at[kind], lead_near.at[kind], near_send.at[kind, 3], near_recv.at[kind, 3], near
        )

    def one_copy(kind, n):
        room = kinds[kind][2]
        source = (lead_near.at[kind, top], room.at[5, top], room.at[5, low])[n]
        return across(
            source, one_buf.at[kind, n], one_send.at[kind, n], one_recv.at[kind, n], one
        )

    def two_copy(kind, n):
        room = kinds[kind][2]
        source = (lead_near.at[kind, low], room.at[6, low], room.at[6, top])[n]
        return across(
            source, two_buf.at[kind, n], two_send.at[kind, n], two_recv.at[kind, n], two
        )

    def flipped(k, near_too):
        me = lax.axis_index("dp")

        def turn(mask, on):
            return on * mask * (1 - 2 * lax.rem(lax.div(me, mask), 2))

        there = me + turn(one, lax.rem(k, 2)) + turn(two, lax.div(k, 2)) + turn(near, near_too)
        return lax.div(there, copies)

    def sum_step(k):
        for n in range(2):
            sum_hop(k, n).wait_recv()

            @pl.loop(0, 8 // many)
            def _(at):
                some = pl.ds(pl.multiple_of(at * tile, tile), tile)
                moved = ring_buf[k, both[n], some].astype(f32)
                if k + 1 < parts - 1:
                    total = back[k + 2, both[n], some].astype(f32) + moved
                    back[k + 2, both[n], some] = total.astype(bf16)
                else:
                    norm_sum[both[n], some] = back[0, both[n], some].astype(f32) + moved

            if k + 1 < parts - 1:
                sum_hop(k + 1, n).start()

    def keep(ref, at):
        def store(columns, value):
            ref[at, :, columns] = value.astype(bf16)

        return store

    def add(ref, at):
        def store(columns, value):
            ref[at, :, columns] = (value + ref[at, :, columns].astype(f32)).astype(bf16)

        return store

    def add_wide(total_ref, ref, at):
        def store(columns, value):
            total_ref[:, columns] = value + ref[at, :, columns].astype(f32)

        return store

    for kind in range(3):
        product(kind, flipped(3, 1), keep(lead, kind))
        lead_copy(kind).start()
    for kind in range(3):
        lead_copy(kind).wait_recv()
        product(kind, flipped(3, 0), add(lead_near, kind))
        one_copy(kind, 0).start()
        two_copy(kind, 0).start()
    rear(parts - 1)

    gather[5]()
    pl.semaphore_signal(
        ready_sem,
        inc=1,
        device_id={"dp": partner(near)},
        device_id_type=pl.DeviceIdType.MESH,
    )
    pl.semaphore_wait(ready_sem, 1)

    def theirs(k):
        for kind in range(3):
            product(kind, flipped(k, 1), keep(kinds[kind][2], k))
            near_copy(kind, k).start()

    def mine(k):
        for kind in range(3):
            near_copy(kind, k).wait_recv()
            product(kind, flipped(k, 0), add(kinds[kind][2], 4 + k))
            if k == 1:
                one_copy(kind, 1).start()
            else:
                two_copy(kind, 1).start()

    sum_step(0)
    theirs(1)
    theirs(2)
    mine(1)
    mine(2)
    theirs(0)
    for kind in range(3):
        one_copy(kind, 0).wait_recv()
        room = kinds[kind][2]
        room[6, top] = (room[6, top].astype(f32) + one_buf[kind, 0].astype(f32)).astype(bf16)
        two_copy(kind, 2).start()
        two_copy(kind, 0).wait_recv()
        room[5, low] = (room[5, low].astype(f32) + two_buf[kind, 0].astype(f32)).astype(bf16)
        one_copy(kind, 2).start()
    for k in range(1, parts - 2):
        sum_step(k)
    for kind in range(3):
        near_copy(kind, 0).wait_recv()
        room, total_ref = kinds[kind][2:]
        product(kind, flipped(0, 0), add_wide(total_ref, room, 4))
    sum_step(parts - 2)
    for k in (parts - 2, parts - 1):
        store(k).wait()
    moved_up = along(1, rows_out.at[parts - 1], moved_out, moved_send, moved_recv)
    moved_down = along(-1, rows_out.at[0], moved_out, moved_send, moved_recv)

    @pl.when(at_start)
    def _():
        moved_up.start()

    @pl.when(at_end)
    def _():
        moved_down.start()

    for kind in range(3):
        total_ref = kinds[kind][3]
        one_copy(kind, 1).wait_recv()
        two_copy(kind, 2).wait_recv()
        total_ref[:half, :] += one_buf[kind, 1].astype(f32) + two_buf[kind, 2].astype(f32)
        two_copy(kind, 1).wait_recv()
        one_copy(kind, 2).wait_recv()
        total_ref[half:, :] += two_buf[kind, 1].astype(f32) + one_buf[kind, 2].astype(f32)
    for kind in range(3):
        lead_copy(kind).wait_send()
        for k in range(3):
            near_copy(kind, k).wait_send()
        for n in range(3):
            one_copy(kind, n).wait_send()
            two_copy(kind, n).wait_send()
    for k in range(parts - 1):
        for n in range(2):
            hop(k, n).wait_send()
            sum_hop(k, n).wait_send()

    @pl.when(at_start)
    def _():
        moved_up.wait_send()

    @pl.when(at_end)
    def _():
        moved_down.wait_send()

    @pl.when(jnp.logical_not(jnp.logical_or(at_start, at_end)))
    def _():
        moved_up.wait_recv()


def swiglu(normed, own, below, others, gate_w, up_w, down_w, copies, collective):
    parts = lax.axis_size("tensor")
    rows, width = normed.shape
    hidden = gate_w.shape[2]
    share = width // 8
    somewhere = pl.BlockSpec(memory_space=pl.ANY)
    vmem = pl.BlockSpec(memory_space=pltpu.VMEM)
    wide, narrow = (parts, rows, width), (parts, rows, hidden)
    return pl.pallas_call(
        functools.partial(swiglu_kernel, copies),
        out_shape=[
            jax.ShapeDtypeStruct(wide, bf16),
            jax.ShapeDtypeStruct((rows, width), bf16),
            jax.ShapeDtypeStruct((rows, width), f32),
        ]
        + [jax.ShapeDtypeStruct((share, hidden), f32)] * 3,
        in_specs=[somewhere] * 7,
        out_specs=[somewhere] * 2 + [vmem] * 4,
        scratch_shapes=[pltpu.VMEM(wide, bf16)] * 2
        + [pltpu.VMEM((8, share, hidden), bf16)] * 3
        + [pltpu.VMEM(narrow, bf16)] * 3
        + [
            pltpu.VMEM(wide, bf16),
            pltpu.VMEM((2, rows, width), bf16),
            pltpu.VMEM((parts - 1, rows, width), bf16),
        ]
        + [pltpu.VMEM((3, 3, share // 2, hidden), bf16)] * 2
        + [pltpu.VMEM((3, share, hidden), bf16)] * 2
        + [pltpu.SemaphoreType.DMA((8,)), pltpu.SemaphoreType.DMA((2,))]
        + [pltpu.SemaphoreType.DMA((14,))] * 2
        + [pltpu.SemaphoreType.DMA((parts - 1, 2))] * 4
        + [pltpu.SemaphoreType.DMA((3, 4))] * 2
        + [pltpu.SemaphoreType.DMA((3, 3))] * 4
        + [pltpu.SemaphoreType.REGULAR]
        + [pltpu.SemaphoreType.DMA] * 2,
        compiler_params=pltpu.CompilerParams(
            collective_id=collective, has_side_effects=True, vmem_limit_bytes=62 * 1024 * 1024
        ),
        cost_estimate=pl.CostEstimate(
            flops=18 * parts * rows * width * hidden,
            bytes_accessed=1100 * rows * width,
            transcendentals=parts * rows * hidden,
        ),
    )(normed, own, below, others, gate_w, up_w, down_w)


def greet_all(copies, masks):
    barrier = pltpu.get_barrier_semaphore()
    others = [{"dp": group_member(copies, k)} for k in range(1, 8)]
    others += [{"tensor": beside(k)} for k in range(1, lax.axis_size("tensor"))]
    others += [{"dp": partner(mask)} for mask in masks]
    for other in others:
        pl.semaphore_signal(
            barrier, inc=1, device_id=other, device_id_type=pl.DeviceIdType.MESH
        )
    pl.semaphore_wait(barrier, len(others))


def group_member(copies, step):
    me = lax.axis_index("dp")
    return lax.rem(lax.div(me, copies) + step, 8) * copies + lax.rem(me, copies)


def mixer_forward_kernel(
    copies,
    own_ref, input_hbm, forget_hbm, gate_hbm, out_hbm, masked_hbm, below_hbm, inputs_hbm, bound_ref,
    live_ref, gain_ref,
    normed_out, weights_out, project_out, pre_out, squash_out, state_out, entering_out, mixed_out,
    masked_out, stream_ref, following_ref,
    normed, weights, project, pre, squashed, forget, state, decay, ends, entering, mixed,
    near_buf, one_buf, two_buf, part_buf, inputs,
    own_sem, gather_send, gather_recv, spread_send, spread_recv, spread_own, up_send, down_send, line_recv,
    carry_send, carry_recv, scatter_send, scatter_recv, masked_up, masked_down, masked_recv, out_sem, inputs_sem,
):
    parts = lax.axis_size("tensor")
    here = lax.axis_index("tensor")
    seqs, rows, width = normed.shape
    strips, _, lanes = forget.shape
    channels = strips * lanes
    mine = slot_of(copies, ())
    greet_all(copies, ())

    def own_rows_of(index):
        return pl.ds(pl.multiple_of(index * copies, copies), copies)

    def columns_of(index):
        return pl.ds(pl.multiple_of(index * channels, channels), channels)

    spread = []
    for kind, source in enumerate((input_hbm, forget_hbm, gate_hbm)):
        target = weights.at[kind, own_rows_of(mine), here]
        kept = pltpu.make_async_copy(
            source.at[:, :, columns_of(mine)], target, spread_own.at[kind]
        )
        sent = []
        for k in range(1, 8):
            there = group_member(copies, k)
            sent.append(
                pltpu.make_async_remote_copy(
                    src_ref=source.at[:, :, columns_of(lax.div(there, copies))],
                    dst_ref=target,
                    send_sem=spread_send.at[kind, k - 1],
                    recv_sem=spread_recv.at[kind, k - 1],
                    device_id={"dp": there},
                    device_id_type=pl.DeviceIdType.MESH,
                )
            )
        spread.append((kept, sent))

    def block_of(kind, block):
        return project.at[:, block] if kind == 3 else weights.at[kind, :, block]

    def line_copy(kind, k, step):
        block = here - step * k
        target = block_of(kind, block)
        source = out_hbm if kind == 3 and k == 0 else target
        sems = up_send if step == 1 else down_send
        return along(step, source, target, sems.at[kind, k], line_recv.at[kind, block])

    def goes(k, step):
        if step == 1:
            return jnp.logical_and(here >= k, here < parts - 1)
        return jnp.logical_and(here + k < parts, here > 0)

    def comes(k, step):
        return here >= k if step == 1 else here + k < parts

    def line_step(kind, k):
        for step in (1, -1):
            if k > 0:

                @pl.when(comes(k, step))
                def _():
                    line_copy(kind, k, step).wait_recv()

            if k < parts - 1:

                @pl.when(goes(k, step))
                def _():
                    line_copy(kind, k, step).start()

    def spread_arrive(kind):
        kept, sent = spread[kind]
        kept.wait()
        for copy in sent:
            copy.wait_recv()

    inputs_load = pltpu.make_async_copy(inputs_hbm, inputs, inputs_sem)
    inputs_load.start()
    out_kept = pltpu.make_async_copy(out_hbm, project.at[:, here], spread_own.at[3])
    out_kept.start()
    for kept, sent in spread:
        kept.start()
        for copy in sent:
            copy.start()
    line_step(3, 0)
    begin, pass_first, pass_second, pass_last, arrive, finish = plane_gather_steps(
        copies, own_ref, normed, own_sem, gather_send, gather_recv
    )
    begin()
    spread_arrive(0)
    line_step(0, 0)
    spread_arrive(1)
    line_step(1, 0)
    spread_arrive(2)
    pass_first()
    line_step(0, 1)
    pass_second()
    line_step(1, 1)
    line_step(0, 2)
    line_step(1, 2)
    line_step(0, 3)
    line_step(2, 0)
    pass_last()
    line_step(1, 3)
    line_step(3, 1)
    arrive()

    many = 2

    def project_rows(kind, at):
        left = normed[pl.ds(at * many, many)].reshape(many * rows, width)
        return matmul(left, weights[kind].reshape(width, channels))

    def rows_at(at):
        return pl.ds(pl.multiple_of(at * many * rows, many * rows), many * rows)

    def strip_of(value, n):
        return value[:, n * lanes : (n + 1) * lanes]

    @pl.loop(0, seqs // many)
    def _(at):
        some = rows_at(at)
        value = project_rows(0, at)
        pre[0, some, :] = value
        inflow = live_ref[some, :] * silu_of(value)
        for n in range(strips):
            state[n, some, :] = strip_of(inflow, n)

    line_step(2, 1)

    @pl.loop(0, seqs // many)
    def _(at):
        some = rows_at(at)
        squash = jax.nn.sigmoid(project_rows(1, at))
        bound = bound_ref[...]
        value = bound + (1.0 - bound) * squash
        for n in range(strips):
            squashed[n, some, :] = strip_of(squash, n)
            forget[n, some, :] = strip_of(value, n)
            state[n, some, :] = (1.0 - strip_of(value, n)) * state[n, some, :]

    line_step(3, 2)

    def step(at, carry):
        some = pl.ds(at, seqs, stride=rows)
        following = []
        for n, (total, product) in enumerate(carry):
            keep = forget[n, some, :]
            total = keep * total + state[n, some, :]
            product = product * keep
            state[n, some, :] = total
            decay[n, some, :] = product
            following.append((total, product))
        return tuple(following)

    start = (jnp.zeros((seqs, lanes), f32), jnp.ones((seqs, lanes), f32))
    carry = lax.fori_loop(0, rows, step, (start,) * strips, unroll=8)
    for n, (total, product) in enumerate(carry):
        ends[here, 0, :, n * lanes : (n + 1) * lanes] = total
        ends[here, 1, :, n * lanes : (n + 1) * lanes] = product
    carries = []
    for k in range(1, parts):
        copy = pltpu.make_async_remote_copy(
            src_ref=ends.at[here],
            dst_ref=ends.at[here],
            send_sem=carry_send.at[k - 1],
            recv_sem=carry_recv.at[k - 1],
            device_id={"tensor": beside(k)},
            device_id_type=pl.DeviceIdType.MESH,
        )
        copy.start()
        carries.append(copy)
    line_step(2, 2)

    inner = jnp.logical_and(here > 0, here < parts - 1)

    def masked_down_copy(k):
        block = here + k
        source = masked_hbm if k == 0 else masked_out.at[block]
        return along(-1, source, masked_out.at[block], masked_down.at[k], masked_recv.at[block])

    def masked_up_copy(k):
        block = here - 1 - k
        source = below_hbm if k == 0 else masked_out.at[block]
        return along(1, source, masked_out.at[block], masked_up.at[k], masked_recv.at[block])

    def masked_came(block):
        along(1, below_hbm, masked_out.at[block], masked_up.at[0], masked_recv.at[block]).wait_recv()

    def masked_step(k):
        if k == 1:

            @pl.when(here > 0)
            def _():
                masked_down_copy(0).start()

            @pl.when(inner)
            def _():
                masked_up_copy(0).start()

        elif k == 2:

            @pl.when(here < parts - 1)
            def _():
                masked_came(here + 1)

            @pl.when(inner)
            def _():
                masked_down_copy(1).start()

            @pl.when(here > 1)
            def _():
                masked_came(here - 2)

            @pl.when(here == 2)
            def _():
                masked_up_copy(1).start()

        else:

            @pl.when(here < 2)
            def _():
                masked_came(here + 2)

            @pl.when(here == parts - 1)
            def _():
                masked_came(0)

    for copy in carries:
        copy.wait_recv()
    coming = jnp.zeros((seqs, channels), f32)
    entered = coming
    for k in range(parts - 1):
        coming = ends[k, 1] * coming + ends[k, 0]
        entered = jnp.where(here == k + 1, coming, entered)
    for n in range(seqs):
        entering[n] = entered[n : n + 1]
    line_step(3, 3)
    line_step(2, 3)

    @pl.loop(0, seqs // many)
    def _(at):
        some = rows_at(at)
        value = project_rows(2, at)
        pre[1, some, :] = value
        act = silu_of(value)
        for n in range(many):
            slot = at * many + n
            one = pl.ds(pl.multiple_of(slot * rows, rows), rows)
            for strip in range(strips):
                columns = slice(strip * lanes, (strip + 1) * lanes)
                whole = state[strip, one, :] + (
                    decay[strip, one, :] * entering[slot, :, columns]
                )
                state[strip, one, :] = whole
                mixed[slot, :, columns] = (
                    whole * act[n * rows : (n + 1) * rows, columns]
                ).astype(bf16)

    out_kept.wait()
    stores = [
        pltpu.make_async_copy(source, target, out_sem.at[n])
        for n, (source, target) in enumerate(
            (
                (normed, normed_out),
                (weights, weights_out),
                (project, project_out),
                (pre, pre_out),
                (squashed, squash_out),
                (state, state_out),
                (entering, entering_out),
                (mixed, mixed_out),
            )
        )
    ]
    for store in stores:
        store.start()

    def out_product(slot, columns):
        right = project[:, :, :, columns]
        return matmul(mixed[slot], right.reshape(channels, right.shape[-1]))

    masked_step(1)

    def between(point):
        if point == "low":
            masked_step(2)

    plane_scatter_steps(
        copies, stream_ref, near_buf, one_buf, two_buf, part_buf, scatter_send, scatter_recv,
        out_product, between,
    )

    inputs_load.wait()
    some_rows = min(64, rows)

    @pl.loop(0, rows // some_rows)
    def _(k):
        some = pl.ds(pl.multiple_of(k * some_rows, some_rows), some_rows)
        stream = inputs[some, :] + stream_ref[some, :]
        stream_ref[some, :] = stream
        following_ref[some, :] = (norm_rows(stream)[1] * gain_ref[...]).astype(bf16)

    masked_step(3)

    @pl.when(here > 0)
    def _():
        masked_down_copy(0).wait_send()

    @pl.when(inner)
    def _():
        masked_up_copy(0).wait_send()
        masked_down_copy(1).wait_send()

    @pl.when(here == 2)
    def _():
        masked_up_copy(1).wait_send()

    finish()
    for kept, sent in spread:
        for copy in sent:
            copy.wait_send()
    for kind in range(4):
        for k in range(parts - 1):
            for step in (1, -1):

                @pl.when(goes(k, step))
                def _():
                    line_copy(kind, k, step).wait_send()

    for copy in carries:
        copy.wait_send()
    for store in stores:
        store.wait()


def mixer_forward(
    normed, w_input, w_forget, w_gate, w_out, masked, below, inputs, bound, live, gain, copies,
    collective,
):
    parts = lax.axis_size("tensor")
    rows, width = normed.shape
    channels = width // 8
    own_rows = w_input.shape[1]
    somewhere = pl.BlockSpec(memory_space=pl.ANY)
    vmem = pl.BlockSpec(memory_space=pltpu.VMEM)
    wide = (8, rows, width)
    weights = (3, 8 * copies, parts, own_rows, channels)
    project = (copies, parts, own_rows, width)
    flat = (8 * rows, channels)
    lanes = min(128, channels)
    strips = (channels // lanes, 8 * rows, lanes)
    shaped = (8, rows, channels)
    half = rows // 2
    dma = pltpu.SemaphoreType.DMA
    return pl.pallas_call(
        functools.partial(mixer_forward_kernel, copies),
        out_shape=[
            jax.ShapeDtypeStruct(wide, bf16),
            jax.ShapeDtypeStruct(weights, bf16),
            jax.ShapeDtypeStruct(project, bf16),
            jax.ShapeDtypeStruct((2,) + flat, f32),
            jax.ShapeDtypeStruct(strips, f32),
            jax.ShapeDtypeStruct(strips, f32),
            jax.ShapeDtypeStruct((8, 1, channels), f32),
            jax.ShapeDtypeStruct(shaped, bf16),
            jax.ShapeDtypeStruct((parts, rows, width), bf16),
            jax.ShapeDtypeStruct((rows, width), f32),
            jax.ShapeDtypeStruct((rows, width), bf16),
        ],
        in_specs=[somewhere] * 8 + [vmem] * 3,
        out_specs=[somewhere] * 9 + [vmem] * 2,
        scratch_shapes=[
            pltpu.VMEM(wide, bf16),
            pltpu.VMEM(weights, bf16),
            pltpu.VMEM(project, bf16),
            pltpu.VMEM((2,) + flat, f32),
            pltpu.VMEM(strips, f32),
            pltpu.VMEM(strips, f32),
            pltpu.VMEM(strips, f32),
            pltpu.VMEM(strips, f32),
            pltpu.VMEM((parts, 2, 8, channels), f32),
            pltpu.VMEM((8, 1, channels), f32),
            pltpu.VMEM(shaped, bf16),
            pltpu.VMEM((4, rows, width), bf16),
            pltpu.VMEM((3, half, width), bf16),
            pltpu.VMEM((3, half, width), bf16),
            pltpu.VMEM((4, rows, width), bf16),
            pltpu.VMEM((rows, width), f32),
            dma,
            dma((14,)),
            dma((14,)),
            dma((3, 7)),
            dma((3, 7)),
            dma((4,)),
            dma((4, parts - 1)),
            dma((4, parts - 1)),
            dma((4, parts)),
            dma((parts - 1,)),
            dma((parts - 1,)),
            dma((10,)),
            dma((10,)),
            dma((parts - 1,)),
            dma((parts - 1,)),
            dma((parts,)),
            dma((8,)),
            dma,
        ],
        compiler_params=pltpu.CompilerParams(
            collective_id=collective, has_side_effects=True, vmem_limit_bytes=56 * 1024 * 1024
        ),
        cost_estimate=pl.CostEstimate(
            flops=8 * rows * width * width,
            bytes_accessed=900 * rows * width,
            transcendentals=0,
        ),
    )(normed, w_input, w_forget, w_gate, w_out, masked, below, inputs, bound, live, gain)


def mixer_backward_kernel(
    copies, masks,
    norm_hbm, normed_hbm, weights_hbm, project_hbm, pre_hbm, squash_hbm, state_hbm, mixed_hbm,
    unit_hbm, stream_hbm, cotangent_hbm, entering_ref, bound_ref, live_ref, gain_ref, scale_ref, gain_two_ref,
    rows_hbm, moved_hbm,
    result_ref, input_sum, forget_sum, gate_sum, project_sum, small_sums, moved_out,
    rows_buf, weights, project, pre, squashed, state, mixed, unit, stream, drive, decay, ends,
    entered, grad_pre, grad_w, grad_project, line_w, line_project, bound_sum, whole_w, spread_w,
    small_recv, small_ring, gain_sum, gain_two_sum, near_buf, one_buf, two_buf, part_buf,
    load_sem, gather_send, gather_recv, carry_send, carry_recv, up_send, down_send, line_recv,
    scatter_send, scatter_recv, spread_send, spread_recv, spread_own, small_send, small_got,
    moved_sem, moved_send, moved_recv, first_sem,
):
    parts = lax.axis_size("tensor")
    here = lax.axis_index("tensor")
    seqs, rows, width = rows_buf.shape
    strips, _, lanes = drive.shape
    channels = strips * lanes
    own_rows = weights.shape[3]
    weight_sums = (input_sum, forget_sum, gate_sum)
    near, one, two = copies, 2 * copies, 4 * copies
    mine = slot_of(copies, ())
    greet_all(copies, masks)
    firsts = [
        pltpu.make_async_copy(source, target, first_sem.at[n])
        for n, (source, target) in enumerate(
            ((norm_hbm, result_ref), (stream_hbm, unit), (cotangent_hbm, stream))
        )
    ]
    for load in firsts:
        load.start()
    begin, pass_first, pass_second, pass_last, arrive, finish = plane_gather_steps(
        copies, rows_buf.at[mine], rows_buf, None, gather_send, gather_recv
    )

    at_start, at_end = here == 0, here == parts - 1
    inside = jnp.logical_not(jnp.logical_or(at_start, at_end))
    low_half = here == 1

    def fetch(block, came, first, second):
        loads = (
            pltpu.make_async_copy(rows_hbm.at[block], part_buf.at[first], moved_sem.at[0]),
            pltpu.make_async_copy(came, part_buf.at[second], moved_sem.at[1]),
        )
        for load in loads:
            load.start()
        for load in loads:
            load.wait()
        part_buf[first] = (
            part_buf[first].astype(f32) + part_buf[second].astype(f32)
        ).astype(bf16)

    def moved_copy(n, step, source):
        return along(step, source, moved_out.at[n], moved_send.at[n], moved_recv.at[n])

    def moved_second():
        @pl.when(at_start)
        def _():
            moved_copy(0, 1, rows_hbm.at[2]).start()

        @pl.when(at_end)
        def _():
            moved_copy(1, -1, rows_hbm.at[1]).start()

        @pl.when(inside)
        def _():
            fetch(3 - 3 * (here - 1), moved_hbm, 0, 1)

        @pl.when(low_half)
        def _():
            moved_copy(0, 1, part_buf.at[0]).start()

        @pl.when(here == 2)
        def _():
            moved_copy(1, -1, part_buf.at[0]).start()

    def moved_last():
        @pl.when(at_start)
        def _():
            moved_copy(0, 1, rows_hbm.at[2]).wait_send()
            moved_copy(2, 1, rows_hbm.at[1]).start()

        @pl.when(at_end)
        def _():
            moved_copy(1, -1, rows_hbm.at[1]).wait_send()
            moved_copy(3, -1, rows_hbm.at[2]).start()

        @pl.when(inside)
        def _():
            moved_copy(0, 1, part_buf.at[0]).wait_recv()
            fetch(here + 1, moved_out.at[0], 1, 2)
            moved_copy(2, 1, part_buf.at[1]).start()

        @pl.when(low_half)
        def _():
            moved_copy(0, 1, part_buf.at[0]).wait_send()

        @pl.when(here == 2)
        def _():
            moved_copy(1, -1, part_buf.at[0]).wait_send()

        @pl.when(inside)
        def _():
            moved_copy(1, -1, part_buf.at[0]).wait_recv()
            fetch(here - 1, moved_out.at[1], 2, 3)
            moved_copy(3, -1, part_buf.at[2]).start()

    def moved_end():
        @pl.when(here < parts - 1)
        def _():
            moved_copy(2, 1, part_buf.at[1]).wait_send()
            moved_copy(3, -1, part_buf.at[2]).wait_recv()

        @pl.when(here > 0)
        def _():
            moved_copy(3, -1, part_buf.at[2]).wait_send()
            moved_copy(2, 1, part_buf.at[1]).wait_recv()

    loads = [
        pltpu.make_async_copy(source, target, load_sem.at[n + 1])
        for n, (source, target) in enumerate(
            (
                (project_hbm, project),
                (pre_hbm, pre),
                (state_hbm, state),
                (mixed_hbm, mixed),
                (squash_hbm, squashed),
                (weights_hbm, weights),
                (unit_hbm, unit),
            )
        )
    ]
    for load in loads[:-1]:
        load.start()

    for load in firsts:
        load.wait()
    gain_two_sum[...] = jnp.zeros_like(gain_two_sum)
    some_rows = min(64, rows)

    @pl.loop(0, rows // some_rows)
    def _(k):
        some = pl.ds(pl.multiple_of(k * some_rows, some_rows), some_rows)
        at = pl.ds(pl.multiple_of(mine * rows + k * some_rows, some_rows), some_rows)
        scale, units = norm_rows(unit[some, :])
        grad_norm = result_ref[some, :]
        gain_two_sum[...] += jnp.sum(grad_norm * units, axis=0, keepdims=True)
        total = live_ref[at, :] * stream[some, :] + norm_back(
            grad_norm, units, scale, gain_two_ref[...]
        )
        stream[some, :] = total
        rows_buf[mine, some, :] = total.astype(bf16)

    begin()
    loads[-1].start()
    moved_second()
    for load in loads[:3]:
        load.wait()

    def slot_rows(slot):
        return pl.ds(pl.multiple_of(slot * rows, rows), rows)

    def take(slot):
        some = slot_rows(slot)
        grad_mixed = matmul_rt(rows_buf[slot], project[...].reshape(channels, width))
        gate = pre[1, some, :]
        squash = jax.nn.sigmoid(gate)
        act = gate * squash
        slope = squash * (1.0 + gate * (1.0 - squash))
        for n in range(strips):
            columns = slice(n * lanes, (n + 1) * lanes)
            part = grad_mixed[:, columns]
            drive[n, some, :] = part * act[:, columns]
            at = 2 * channels + n * lanes
            grad_pre[slot, :, at : at + lanes] = (
                part * state[n, some, :] * slope[:, columns]
            ).astype(bf16)

    pass_first()
    pass_second()
    arrive(slice(0, 6))
    for flips in ((), (near,), (one,), (two,), (near, one), (near, two)):
        take(slot_of(copies, flips))
    moved_last()
    pass_last()
    take(slot_of(copies, (one, two)))
    arrive(slice(6, 8))
    take(slot_of(copies, (near, one, two)))

    tile = min(512, width)
    loads[3].wait()

    @pl.loop(0, width // tile)
    def _(k):
        columns = pl.ds(pl.multiple_of(k * tile, tile), tile)
        value = matmul_lt(
            mixed[...].reshape(seqs * rows, channels),
            rows_buf[:, :, columns].reshape(seqs * rows, tile),
        )
        grad_project[:, :, :, columns] = value.astype(bf16).reshape(
            copies, parts, own_rows, tile
        )

    def part_of(kind, block):
        return grad_project.at[:, block] if kind == 3 else grad_w.at[kind, :, block]

    def room_of(kind, index):
        return line_project.at[index] if kind == 3 else line_w.at[kind, index]

    def line_up(kind, k):
        block = parts - 1 - k + here
        return along(
            1, part_of(kind, block), room_of(kind, block), up_send.at[kind, k],
            line_recv.at[kind, block],
        )

    def line_down(kind, k):
        block = k - parts + 1 + here
        index = parts if k == parts - 2 else block
        return along(
            -1, part_of(kind, block), room_of(kind, index), down_send.at[kind, k],
            line_recv.at[kind, index],
        )

    def came(kind, index):
        return along(1, part_of(kind, 0), room_of(kind, index), up_send.at[kind, 0],
                     line_recv.at[kind, index])

    def add_came(kind, block):
        came(kind, block).wait_recv()
        if kind == 3:
            total = grad_project[:, block].astype(f32) + line_project[block].astype(f32)
            grad_project[:, block] = total.astype(bf16)
        else:
            total = grad_w[kind, :, block].astype(f32) + line_w[kind, block].astype(f32)
            grad_w[kind, :, block] = total.astype(bf16)

    def goes_up(k):
        return jnp.logical_and(here <= k, here < parts - 1)

    def goes_down(k):
        return jnp.logical_and(parts - 1 - here <= k, here > 0)

    def line_step(kind, k):
        @pl.when(jnp.logical_and(goes_up(k), here > 0))
        def _():
            add_came(kind, parts - 1 - k + here)

        @pl.when(goes_up(k))
        def _():
            line_up(kind, k).start()

        @pl.when(jnp.logical_and(goes_down(k), here < parts - 1))
        def _():
            add_came(kind, k - parts + 1 + here)

        @pl.when(goes_down(k))
        def _():
            line_down(kind, k).start()

    def advance(kind, k):
        if k + 1 < parts - 1:
            line_step(kind, k + 1)
            return

        @pl.when(here > 0)
        def _():
            came(kind, here).wait_recv()

        @pl.when(here < parts - 1)
        def _():
            came(kind, parts).wait_recv()

        if kind == 3:
            project_sum[...] = (
                grad_project[:, here].astype(f32)
                + line_project[here].astype(f32)
                + line_project[parts].astype(f32)
            )
        else:
            total = (
                grad_w[kind, :, here].astype(f32)
                + line_w[kind, here].astype(f32)
                + line_w[kind, parts].astype(f32)
            )
            whole_w[kind] = total.astype(bf16)
            for copy in spread_copies(kind):
                copy.start()

    @pl.when(at_start)
    def _():
        line_w[:, 0] = jnp.zeros_like(line_w[:, 0])
        line_project[0] = jnp.zeros_like(line_project[0])

    @pl.when(at_end)
    def _():
        line_w[:, parts] = jnp.zeros_like(line_w[:, parts])
        line_project[parts] = jnp.zeros_like(line_project[parts])

    def spread_copies(kind, own=True):
        found = []
        for k in range(1, 8):
            there = group_member(copies, k)
            source = pl.ds(pl.multiple_of(lax.div(there, copies) * copies, copies), copies)
            found.append(
                pltpu.make_async_remote_copy(
                    src_ref=whole_w.at[kind, source],
                    dst_ref=spread_w.at[kind, mine],
                    send_sem=spread_send.at[kind, k - 1],
                    recv_sem=spread_recv.at[kind, k - 1],
                    device_id={"dp": there},
                    device_id_type=pl.DeviceIdType.MESH,
                )
            )
        if own:
            source = pl.ds(pl.multiple_of(mine * copies, copies), copies)
            found.append(
                pltpu.make_async_copy(
                    whole_w.at[kind, source], spread_w.at[kind, mine], spread_own.at[kind]
                )
            )
        return found

    line_step(3, 0)
    finish()
    normed_load = pltpu.make_async_copy(normed_hbm, rows_buf, load_sem.at[0])
    normed_load.start()
    loads[4].wait()

    def step(k, carry):
        some = pl.ds(rows - 1 - k, seqs, stride=rows)
        following = []
        for n, (coming, product) in enumerate(carry):
            bound = bound_ref[:, n * lanes : (n + 1) * lanes]
            keep = bound + (1.0 - bound) * squashed[n, some, :]
            carried = drive[n, some, :] + coming
            drive[n, some, :] = carried
            decay[n, some, :] = product
            following.append((keep * carried, product * keep))
        return tuple(following)

    start = (jnp.zeros((seqs, lanes), f32), jnp.ones((seqs, lanes), f32))
    carry = lax.fori_loop(0, rows, step, (start,) * strips, unroll=8)
    for n, (coming, product) in enumerate(carry):
        ends[here, 0, :, n * lanes : (n + 1) * lanes] = coming
        ends[here, 1, :, n * lanes : (n + 1) * lanes] = product
    carries = []
    for k in range(1, parts):
        copy = pltpu.make_async_remote_copy(
            src_ref=ends.at[here],
            dst_ref=ends.at[here],
            send_sem=carry_send.at[k - 1],
            recv_sem=carry_recv.at[k - 1],
            device_id={"tensor": beside(k)},
            device_id_type=pl.DeviceIdType.MESH,
        )
        copy.start()
        carries.append(copy)
    normed_load.wait()

    def weight_grad(kind):
        @pl.loop(0, width // tile)
        def _(k):
            columns = pl.ds(pl.multiple_of(k * tile, tile), tile)
            value = matmul_lt(
                grad_pre[:, :, kind * channels : (kind + 1) * channels].reshape(
                    seqs * rows, channels
                ),
                rows_buf[:, :, columns].reshape(seqs * rows, tile),
            )
            count = tile // (parts * own_rows)
            grad_w[kind, pl.ds(k * count, count)] = value.T.astype(bf16).reshape(
                count, parts, own_rows, channels
            )

        line_step(kind, 0)

    advance(3, 0)
    weight_grad(2)
    for copy in carries:
        copy.wait_recv()
    coming = jnp.zeros((seqs, channels), f32)
    arrived = coming
    for k in range(parts - 1, 0, -1):
        coming = ends[k, 1] * coming + ends[k, 0]
        arrived = jnp.where(here == k - 1, coming, arrived)
    for n in range(seqs):
        entered[n] = arrived[n : n + 1]
    bound_sum[...] = jnp.zeros_like(bound_sum)
    first_row = lax.broadcasted_iota(jnp.int32, (rows, lanes), 0) == 0

    @pl.loop(0, seqs)
    def _(slot):
        some = slot_rows(slot)
        alive = live_ref[some, :]
        for n in range(strips):
            columns = slice(n * lanes, (n + 1) * lanes)
            bound = bound_ref[:, columns]
            squash = squashed[n, some, :]
            keep = bound + (1.0 - bound) * squash
            carried = drive[n, some, :] + decay[n, some, :] * entered[slot, :, columns]
            prior = jnp.where(
                first_row, entering_ref[slot, :, columns], pltpu.roll(state[n, some, :], 1, 0)
            )
            value = pre[0, some, columns]
            gate = jax.nn.sigmoid(value)
            slope = gate * (1.0 + value * (1.0 - gate))
            grad_forget = carried * prior - carried * alive * value * gate
            at = n * lanes
            grad_pre[slot, :, at : at + lanes] = (
                carried * alive * (1.0 - keep) * slope
            ).astype(bf16)
            at = channels + n * lanes
            grad_pre[slot, :, at : at + lanes] = (
                grad_forget * (1.0 - bound) * squash * (1.0 - squash)
            ).astype(bf16)
            bound_sum[:, columns] += jnp.sum(
                grad_forget * (1.0 - squash), axis=0, keepdims=True
            )

    advance(3, 1)
    loads[5].wait()
    moved_end()

    def normed_product(slot, columns):
        at = lax.div(columns.start, parts * own_rows)
        count = tile // (parts * own_rows)
        total = None
        for kind in range(3):
            part = matmul_rt(
                grad_pre[slot, :, kind * channels : (kind + 1) * channels],
                weights[kind, pl.ds(at, count)].reshape(tile, channels),
            )
            total = part if total is None else total + part
        return total

    def between(point):
        if point == "sent":
            weight_grad(0)
            advance(2, 0)
            weight_grad(1)
            advance(3, 2)
        elif point == "added":
            advance(2, 1)
            advance(0, 0)
        elif point == "top":
            advance(1, 0)
            advance(2, 2)
        elif point == "low":
            advance(0, 1)
            advance(1, 1)

    plane_scatter_steps(
        copies, result_ref, near_buf, one_buf, two_buf, part_buf, scatter_send, scatter_recv,
        normed_product, between,
    )

    loads[6].wait()
    gain_sum[...] = jnp.zeros_like(gain_sum)

    @pl.loop(0, rows // some_rows)
    def _(k):
        some = pl.ds(pl.multiple_of(k * some_rows, some_rows), some_rows)
        grad_norm = result_ref[some, :]
        units = unit[some, :]
        gain_sum[...] += jnp.sum(grad_norm * units, axis=0, keepdims=True)
        scaled = grad_norm * gain_ref[...]
        mean = jnp.mean(scaled * units, axis=-1, keepdims=True)
        result_ref[some, :] = stream[some, :] + scale_ref[some, :] * (scaled - units * mean)

    for n in range(8):
        columns = slice(n * channels, (n + 1) * channels)
        small_sums[n : n + 1, :] = gain_sum[:, columns]
        small_sums[8 + n : 9 + n, :] = gain_two_sum[:, columns]
        small_sums[16 + n : 17 + n, :] = jnp.where(mine == n, bound_sum[...], 0.0)

    plane_small = []
    for k in range(1, 8):
        copy = pltpu.make_async_remote_copy(
            src_ref=small_sums,
            dst_ref=small_recv.at[k - 1],
            send_sem=small_send.at[k - 1],
            recv_sem=small_got.at[k - 1],
            device_id={"dp": group_member(copies, k)},
            device_id_type=pl.DeviceIdType.MESH,
        )
        copy.start()
        plane_small.append(copy)

    def small_copy(n):
        return pltpu.make_async_remote_copy(
            src_ref=small_sums,
            dst_ref=small_recv.at[7 + n],
            send_sem=small_send.at[7 + n],
            recv_sem=small_got.at[7 + n],
            device_id={"dp": partner(masks[n])},
            device_id_type=pl.DeviceIdType.MESH,
        )

    advance(0, 2)
    advance(1, 2)
    for copy in plane_small:
        copy.wait()
    for k in range(7):
        small_sums[...] += small_recv[k]
    for n in range(len(masks)):
        small_copy(n).start()
        small_copy(n).wait()
        small_sums[...] += small_recv[7 + n]
    ring_small = []
    for k in range(1, parts):
        copy = pltpu.make_async_remote_copy(
            src_ref=small_sums,
            dst_ref=small_ring.at[k - 1],
            send_sem=small_send.at[7 + len(masks) + k - 1],
            recv_sem=small_got.at[7 + len(masks) + k - 1],
            device_id={"tensor": beside(k)},
            device_id_type=pl.DeviceIdType.MESH,
        )
        copy.start()
        ring_small.append(copy)
    for kind in (2, 0, 1):
        spread = spread_copies(kind)
        for copy in spread[:-1]:
            copy.wait_recv()
        spread[-1].wait()
        for slot in range(8):
            weight_sums[kind][:, :, slot * channels : (slot + 1) * channels] = spread_w[
                kind, slot
            ].astype(f32)
    for copy in ring_small:
        copy.wait()
    for k in range(parts - 1):
        small_sums[...] += small_ring[k]
    for kind in range(4):
        for k in range(parts - 1):

            @pl.when(goes_up(k))
            def _():
                line_up(kind, k).wait_send()

            @pl.when(goes_down(k))
            def _():
                line_down(kind, k).wait_send()

    for kind in range(3):
        for copy in spread_copies(kind, False):
            copy.wait_send()
    for copy in carries:
        copy.wait_send()


def mixer_backward(
    grad_norm, normed, weights, project, pre, squashed, state, mixed, unit, stream, cotangent,
    entering, bound, live, gain, scale, gain_two, out_rows, out_moved, copies, masks, collective,
):
    parts = lax.axis_size("tensor")
    _, rows, width = normed.shape
    channels = width // 8
    own_rows = project.shape[2]
    somewhere = pl.BlockSpec(memory_space=pl.ANY)
    vmem = pl.BlockSpec(memory_space=pltpu.VMEM)
    half = rows // 2
    dma = pltpu.SemaphoreType.DMA
    blocks = (8 * copies, own_rows, channels)
    small = (24, channels)
    return pl.pallas_call(
        functools.partial(mixer_backward_kernel, copies, masks),
        out_shape=[
            jax.ShapeDtypeStruct((rows, width), f32),
        ]
        + [jax.ShapeDtypeStruct((copies, own_rows, width), f32)] * 4
        + [
            jax.ShapeDtypeStruct(small, f32),
            jax.ShapeDtypeStruct((4, rows, width), bf16),
        ],
        in_specs=[somewhere] * 11 + [vmem] * 6 + [somewhere] * 2,
        out_specs=[vmem] * 6 + [somewhere],
        scratch_shapes=[
            pltpu.VMEM(normed.shape, bf16),
            pltpu.VMEM(weights.shape, bf16),
            pltpu.VMEM(project.shape, bf16),
            pltpu.VMEM(pre.shape, f32),
            pltpu.VMEM(squashed.shape, f32),
            pltpu.VMEM(state.shape, f32),
            pltpu.VMEM(mixed.shape, bf16),
            pltpu.VMEM((rows, width), f32),
            pltpu.VMEM((rows, width), f32),
            pltpu.VMEM(state.shape, f32),
            pltpu.VMEM(state.shape, f32),
            pltpu.VMEM((parts, 2, 8, channels), f32),
            pltpu.VMEM((8, 1, channels), f32),
            pltpu.VMEM((8, rows, 3 * channels), bf16),
            pltpu.VMEM(weights.shape, bf16),
            pltpu.VMEM(project.shape, bf16),
            pltpu.VMEM((3, parts + 1) + blocks, bf16),
            pltpu.VMEM((parts + 1, copies, own_rows, width), bf16),
            pltpu.VMEM((1, channels), f32),
            pltpu.VMEM((3,) + blocks, bf16),
            pltpu.VMEM((3, 8, copies, own_rows, channels), bf16),
            pltpu.VMEM((7 + len(masks),) + small, f32),
            pltpu.VMEM((parts - 1,) + small, f32),
            pltpu.VMEM((1, width), f32),
            pltpu.VMEM((1, width), f32),
            pltpu.VMEM((4, rows, width), bf16),
            pltpu.VMEM((3, half, width), bf16),
            pltpu.VMEM((3, half, width), bf16),
            pltpu.VMEM((4, rows, width), bf16),
            dma((9,)),
            dma((14,)),
            dma((14,)),
            dma((parts - 1,)),
            dma((parts - 1,)),
            dma((4, parts - 1)),
            dma((4, parts - 1)),
            dma((4, parts + 1)),
            dma((10,)),
            dma((10,)),
            dma((3, 7)),
            dma((3, 7)),
            dma((3,)),
            dma((7 + len(masks) + parts - 1,)),
            dma((7 + len(masks) + parts - 1,)),
            dma((2,)),
            dma((4,)),
            dma((4,)),
            dma((3,)),
        ],
        compiler_params=pltpu.CompilerParams(
            collective_id=collective, has_side_effects=True, vmem_limit_bytes=62 * 1024 * 1024
        ),
        cost_estimate=pl.CostEstimate(
            flops=16 * rows * width * width,
            bytes_accessed=900 * rows * width,
            transcendentals=0,
        ),
    )(
        grad_norm, normed, weights, project, pre, squashed, state, mixed, unit, stream, cotangent,
        entering, bound, live, gain, scale, gain_two, out_rows, out_moved,
    )


def on_device(
    inputs,
    lengths,
    gain_mix,
    gain_glu,
    lower_bound,
    w_input,
    w_forget,
    w_gate_mix,
    w_out,
    w_gate,
    w_up,
    w_down,
    cotangent,
):
    tensor_parts = lax.axis_size("tensor")
    data_parts = lax.axis_size("dp")
    tensor_index = lax.axis_index("tensor")
    data_index = lax.axis_index("dp")
    rows_here, width = inputs.shape
    group = min(8, data_parts)
    copies = data_parts // group
    group_index = lax.div(data_index, copies)
    copy_index = lax.rem(data_index, copies)
    group_masks = [copies << k for k in range(group.bit_length() - 1)]
    copy_masks = [1 << k for k in range(copies.bit_length() - 1)]
    all_masks = [1 << k for k in range(data_parts.bit_length() - 1)]
    group_lists = [[g * copies + o for g in range(group)] for o in range(copies)]
    channels = width // group
    own_rows = w_input.shape[0]

    high = lax.div(lengths, 32).astype(bf16)
    low = lax.rem(lengths, 32).astype(bf16)
    length_row = jnp.concatenate([high, low, jnp.zeros((own_rows - 2,), bf16)])
    small = jnp.stack([gain_mix, gain_glu, lower_bound, length_row])
    small = in_order(shifted_blocks(small))
    small = gather_bits(small, sorted(all_masks, reverse=True)).astype(f32)
    small = small.reshape((data_parts * tensor_parts,) + small.shape[2:])
    gain_one = small[:, 0].reshape(width)
    gain_two = small[:, 1].reshape(width)
    bound = lax.dynamic_slice_in_dim(small[:, 2].reshape(width), group_index * channels, channels)
    every_length = small[:, 3].reshape(data_parts, tensor_parts, own_rows)[:, 0, :2]
    every_length = (every_length[:, 0] * 32.0 + every_length[:, 1]).astype(jnp.int32)
    group_lengths = lax.dynamic_index_in_dim(
        every_length.reshape(group, copies), copy_index, axis=1, keepdims=False
    )
    position = tensor_index * rows_here + jnp.arange(rows_here, dtype=jnp.int32)
    live_own = (position < lengths[0]).astype(f32)[:, None]
    live = (position[None, :] < group_lengths[:, None]).astype(f32)
    live = live.reshape(group * rows_here, 1)

    mixer_weights = [w_input, w_forget, w_gate_mix, w_out]
    if copies > 1:
        mixer_weights = [gather_bits(weight, copy_masks[::-1]) for weight in mixer_weights]
    mixer_weights = [weight.reshape(copies, own_rows, width) for weight in mixer_weights]

    masked_own = (live_own * cotangent).astype(bf16)
    masked_below = ring(masked_own)

    scale_one, unit_one = norm_rows(inputs)
    rows_all = group * rows_here
    *mixer_kept, mixed, masked_others, stream, normed_two = (
        mixer_forward(
            (unit_one * gain_one).astype(bf16),
            *mixer_weights,
            masked_own,
            masked_below,
            inputs,
            bound[None, :],
            live,
            gain_two[None, :],
            copies,
            1,
        )
    )

    hidden_here = w_gate.shape[1]
    gate_w, up_w = (
        lax.all_gather(weight, "dp", axis=0, tiled=True).reshape(group, channels, hidden_here)
        for weight in (w_gate, w_up)
    )
    down_part = w_down.T
    if copies > 1:
        down_part = gather_bits(down_part, copy_masks[::-1]).reshape(channels, hidden_here)

    out_rows, out_moved, grad_norm_two, *weight_sums = swiglu(
        normed_two,
        masked_own,
        masked_below,
        masked_others,
        gate_w,
        up_w,
        down_part,
        copies,
        4,
    )
    if copies > 1:
        weight_sums = [
            scatter_bits(total.reshape(copies, width // data_parts, hidden_here), copy_masks, f32)
            for total in weight_sums
        ]
    grad_gate_mine, grad_up_mine, grad_down_mine = weight_sums
    grad_down_mine = grad_down_mine.T

    normed_one, mixer_w, out_w, pre, squashed, state, entering = mixer_kept
    grad_inputs, *grad_weights, small_sums, out_others = mixer_backward(
        grad_norm_two,
        normed_one,
        mixer_w,
        out_w,
        pre,
        squashed,
        state,
        mixed,
        unit_one,
        stream,
        cotangent,
        entering,
        bound[None, :],
        live,
        gain_one[None, :],
        scale_one,
        gain_two[None, :],
        out_rows,
        out_moved,
        copies,
        copy_masks,
        3,
    )
    out_sum = lax.dynamic_index_in_dim(out_rows, tensor_index, 0, keepdims=False).astype(f32)
    out_sum += jnp.where(tensor_index > 0, out_others[2].astype(f32), 0.0)
    out_sum += jnp.where(tensor_index < tensor_parts - 1, out_others[3].astype(f32), 0.0)
    output = live_own * (stream + out_sum)
    if copies > 1:
        grad_weights = [scatter_bits(total, copy_masks, f32) for total in grad_weights]
    grad_weights = [total.reshape(own_rows, width) for total in grad_weights]
    place = (data_index * tensor_parts + tensor_index) * own_rows
    small_own = lax.dynamic_slice(
        small_sums.reshape(3, 8, channels),
        (0, lax.div(place, channels), lax.rem(place, channels)),
        (3, 1, own_rows),
    )[:, 0]
    return (
        output,
        grad_inputs,
        small_own[0],
        small_own[1],
        small_own[2],
        *grad_weights,
        grad_gate_mine,
        grad_up_mine,
        grad_down_mine,
    )


def solution(mesh):
    both = ("dp", "tensor")
    placed = (
        P(both, None),
        P("dp"),
        P(both),
        P(both),
        P(both),
        P(both, None),
        P(both, None),
        P(both, None),
        P(both, None),
        P("dp", "tensor"),
        P("dp", "tensor"),
        P("tensor", "dp"),
        P(both, None),
    )
    return jax.shard_map(
        on_device,
        mesh=mesh,
        in_specs=placed,
        out_specs=(
            P(both, None),
            P(both, None),
            P(both),
            P(both),
            P(both),
            P(both, None),
            P(both, None),
            P(both, None),
            P(both, None),
            P("dp", "tensor"),
            P("dp", "tensor"),
            P("tensor", "dp"),
        ),
        check_vma=False,
    )
```

```python
import functools

import jax
import jax.numpy as jnp
from jax import lax
from jax.experimental import pallas as pl
from jax.experimental.pallas import tpu as pltpu
from jax.sharding import PartitionSpec as P

epsilon = 1e-06
bf16 = jnp.bfloat16
f32 = jnp.float32


def matmul(left, right):
    return jnp.dot(left, right, preferred_element_type=f32)


def matmul_rt(left, right):
    return lax.dot_general(left, right, (((1,), (1,)), ((), ())), preferred_element_type=f32)


def matmul_lt(left, right):
    return lax.dot_general(left, right, (((0,), (0,)), ((), ())), preferred_element_type=f32)


def silu_of(value):
    return value * jax.nn.sigmoid(value)


def silu_slope(value):
    squash = jax.nn.sigmoid(value)
    return squash * (1.0 + value * (1.0 - squash))


def norm_rows(value):
    scale = lax.rsqrt(jnp.mean(value * value, axis=-1, keepdims=True) + epsilon)
    return (scale, value * scale)


def norm_back(grad_norm, unit, scale, gain):
    scaled = grad_norm * gain
    return scale * (scaled - unit * jnp.mean(scaled * unit, axis=-1, keepdims=True))


def untouched_kernel(*refs):
    pass


def after(value, *others):
    somewhere = pl.BlockSpec(memory_space=pl.ANY)
    return pl.pallas_call(
        untouched_kernel,
        out_shape=jax.ShapeDtypeStruct(value.shape, value.dtype),
        in_specs=[somewhere] * (1 + len(others)),
        out_specs=somewhere,
        input_output_aliases={0: 0},
        cost_estimate=pl.CostEstimate(flops=0, bytes_accessed=0, transcendentals=0),
    )(value, *others)


def swap(value, mask):
    return lax.ppermute(value, "dp", [(i, i ^ mask) for i in range(lax.axis_size("dp"))])


def own_bit(mask):
    return lax.rem(lax.div(lax.axis_index("dp"), mask), 2)


def gather_bits(value, order):
    base = value.shape
    done = []
    for mask in order:
        other = swap(value, mask)
        at = sum(1 for seen in done if seen > mask)
        low = jnp.stack([value, other], axis=at)
        high = jnp.stack([other, value], axis=at)
        value = jnp.where(own_bit(mask) == 0, low, high)
        done.append(mask)
    return value.reshape((1 << len(order),) + base)


def scatter_bits(value, order, sent=bf16, hold=(None, None)):
    count = len(order)
    value = value.reshape((2,) * count + value.shape[1:])
    left = sorted(order, reverse=True)
    for mask in order:
        at = left.index(mask)
        left.remove(mask)
        bit = own_bit(mask)
        send = lax.dynamic_index_in_dim(value, 1 - bit, at, keepdims=False).astype(sent)
        keep = lax.dynamic_index_in_dim(value, bit, at, keepdims=False)
        if hold[0] == count - len(left) - 1:
            send = after(send, hold[1])
        total = keep.astype(f32) + swap(send, mask).astype(f32)
        value = total.astype(sent) if left else total
    return value


def orders(masks):
    down = sorted(masks, reverse=True)
    if len(down) < 3:
        return down, down
    return down, [down[1], down[0]] + down[2:]


def gather_halves(value, masks):
    first, second = orders(masks)
    half = value.shape[-1] // 2
    return gather_bits(value[..., :half], first), gather_bits(value[..., half:], second)


def scatter_halves(left, right, masks):
    first, second = orders(masks)
    return jnp.concatenate(
        [scatter_bits(left, first[::-1]), scatter_bits(right, second[::-1])], axis=-1
    )


def ring(value):
    parts = lax.axis_size("tensor")
    return lax.ppermute(value, "tensor", [(i, (i + 1) % parts) for i in range(parts)])


def ring_blocks(value):
    blocks = [value]
    for _ in range(lax.axis_size("tensor") - 1):
        blocks.append(ring(blocks[-1]))
    return blocks


def ring_scatter(blocks):
    total = blocks[1 % len(blocks)]
    totals = [total]
    for k in range(2, len(blocks) + 1):
        moved = ring(total).astype(f32)
        total = moved + blocks[k % len(blocks)].astype(f32)
        if k < len(blocks):
            total = total.astype(bf16)
            totals.append(total)
    return total, totals


def shifted_blocks(value):
    parts = lax.axis_size("tensor")
    blocks = [value]
    for k in range(1, parts):
        blocks.append(lax.ppermute(value, "tensor", [(i, (i + k) % parts) for i in range(parts)]))
    return blocks


def scatter_straight(value):
    here = lax.axis_index("tensor")
    parts = lax.axis_size("tensor")
    total = lax.dynamic_index_in_dim(value, here, 0, keepdims=False)
    for k in range(1, parts):
        send = lax.dynamic_index_in_dim(value, lax.rem(here + k, parts), 0, keepdims=False)
        total += lax.ppermute(send, "tensor", [(i, (i + k) % parts) for i in range(parts)])
    return total


def in_order(blocks):
    here = lax.axis_index("tensor")
    parts = len(blocks)
    stacked = jnp.stack(blocks[::-1] + blocks[::-1])
    return lax.dynamic_slice_in_dim(stacked, parts - 1 - here, parts, 0)


def partner(mask):
    me = lax.axis_index("dp")
    return me + mask * (1 - 2 * lax.rem(lax.div(me, mask), 2))


def greet(masks, ring_too=False):
    barrier = pltpu.get_barrier_semaphore()
    others = [{"dp": partner(mask)} for mask in masks]
    if ring_too:
        others += [{"tensor": beside(1)}, {"tensor": beside(-1)}]
    for other in others:
        pl.semaphore_signal(
            barrier, inc=1, device_id=other, device_id_type=pl.DeviceIdType.MESH
        )
    pl.semaphore_wait(barrier, len(others))


def beside(step):
    parts = lax.axis_size("tensor")
    return lax.rem(lax.axis_index("tensor") + step + parts, parts)


def slot_of(copies, masks):
    me = lax.axis_index("dp")
    for mask in masks:
        me = me + mask * (1 - 2 * lax.rem(lax.div(me, mask), 2))
    return lax.div(me, copies)


def to_right(source, target, send_sem, recv_sem):
    return pltpu.make_async_remote_copy(
        src_ref=source,
        dst_ref=target,
        send_sem=send_sem,
        recv_sem=recv_sem,
        device_id={"tensor": beside(1)},
        device_id_type=pl.DeviceIdType.MESH,
    )


def along(step, source, target, send_sem, recv_sem):
    return pltpu.make_async_remote_copy(
        src_ref=source,
        dst_ref=target,
        send_sem=send_sem,
        recv_sem=recv_sem,
        device_id={"tensor": beside(step)},
        device_id_type=pl.DeviceIdType.MESH,
    )


def plane_gather_steps(copies, value_ref, all_ref, own_sem, send_sem, recv_sem):
    near, one, two = copies, 2 * copies, 4 * copies
    half = value_ref.shape[0] // 2
    top, low = pl.ds(0, half), pl.ds(half, half)
    mine = slot_of(copies, ())
    at_one, at_two = slot_of(copies, (one,)), slot_of(copies, (two,))
    at_both = slot_of(copies, (one, two))
    local = None
    if own_sem is not None:
        local = pltpu.make_async_copy(value_ref, all_ref.at[mine], own_sem)
    sent = []
    last = []

    def send(source, slot, rows, mask):
        index = len(sent)
        copy = pltpu.make_async_remote_copy(
            src_ref=source,
            dst_ref=all_ref.at[slot, rows],
            send_sem=send_sem.at[index],
            recv_sem=recv_sem.at[index],
            device_id={"dp": partner(mask)},
            device_id_type=pl.DeviceIdType.MESH,
        )
        copy.start()
        sent.append(copy)
        if mask == near:
            last.append(copy)
        return copy

    def forward(slot, rows, mask):
        return send(all_ref.at[slot, rows], slot, rows, mask)

    first = []
    second = []

    def begin():
        if local is not None:
            local.start()
        first.append(send(value_ref.at[top], mine, top, two))
        first.append(send(value_ref.at[low], mine, low, one))
        first.append(send(value_ref.at[low], mine, low, two))
        first.append(send(value_ref.at[top], mine, top, one))
        send(value_ref.at[top], mine, top, near)
        send(value_ref.at[low], mine, low, near)

    def pass_first():
        first[0].wait_recv()
        second.append(forward(at_two, top, one))
        forward(at_two, top, near)
        first[1].wait_recv()
        second.append(forward(at_one, low, two))
        forward(at_one, low, near)

    def pass_second():
        first[2].wait_recv()
        forward(at_two, low, near)
        first[3].wait_recv()
        forward(at_one, top, near)

    def pass_last():
        second[0].wait_recv()
        forward(at_both, top, near)
        second[1].wait_recv()
        forward(at_both, low, near)

    def arrive(some=slice(None)):
        for copy in last[some]:
            copy.wait_recv()
        if some == slice(None) and local is not None:
            local.wait()

    def finish():
        for copy in sent:
            copy.wait_send()

    return begin, pass_first, pass_second, pass_last, arrive, finish


def plane_scatter_steps(
    copies, sum_ref, near_ref, one_ref, two_ref, part_ref,
    send_sem, recv_sem, product, between,
):
    near, one, two = copies, 2 * copies, 4 * copies
    rows, width = sum_ref.shape
    half = rows // 2
    top, low = pl.ds(0, half), pl.ds(half, half)
    tile = min(512, width)
    flips = [(), (one,), (two,), (one, two)]
    copies_out = []

    def send(source, target, mask):
        index = len(copies_out)
        copy = pltpu.make_async_remote_copy(
            src_ref=source,
            dst_ref=target,
            send_sem=send_sem.at[index],
            recv_sem=recv_sem.at[index],
            device_id={"dp": partner(mask)},
            device_id_type=pl.DeviceIdType.MESH,
        )
        copy.start()
        copies_out.append(copy)
        return copy

    def each_tile(body):
        @pl.loop(0, width // tile)
        def _(k):
            body(pl.ds(pl.multiple_of(k * tile, tile), tile))

    arriving = {}
    for k in (3, 1, 2, 0):
        slot = slot_of(copies, flips[k] + (near,))

        def theirs(columns, k=k, slot=slot):
            part_ref[k, :, columns] = product(slot, columns).astype(bf16)

        each_tile(theirs)
        arriving[k] = send(part_ref.at[k], near_ref.at[k], near)

    between("sent")

    def added(k):
        slot = slot_of(copies, flips[k])
        arriving[k].wait_recv()

        def mine(columns):
            total = product(slot, columns) + near_ref[k, :, columns].astype(f32)
            if k == 0:
                sum_ref[:, columns] = total
            else:
                near_ref[k, :, columns] = total.astype(bf16)

        each_tile(mine)

    added(3)
    one_first = send(near_ref.at[3, top], one_ref.at[0], one)
    two_first = send(near_ref.at[3, low], two_ref.at[0], two)
    added(1)
    one_second = send(near_ref.at[1, top], one_ref.at[1], one)
    added(2)
    two_second = send(near_ref.at[2, low], two_ref.at[1], two)
    added(0)
    between("added")

    one_first.wait_recv()

    def pass_top(columns):
        total = near_ref[2, top, columns].astype(f32) + one_ref[0, :, columns].astype(f32)
        near_ref[2, top, columns] = total.astype(bf16)

    each_tile(pass_top)
    two_last = send(near_ref.at[2, top], two_ref.at[2], two)
    between("top")
    two_first.wait_recv()

    def pass_low(columns):
        total = near_ref[1, low, columns].astype(f32) + two_ref[0, :, columns].astype(f32)
        near_ref[1, low, columns] = total.astype(bf16)

    each_tile(pass_low)
    one_last = send(near_ref.at[1, low], one_ref.at[2], one)
    between("low")

    def finish(rows_at, first, at_first, second, at_second):
        def body(columns):
            sum_ref[rows_at, columns] += (
                first[at_first, :, columns].astype(f32) + second[at_second, :, columns].astype(f32)
            )

        each_tile(body)

    one_second.wait_recv()
    two_last.wait_recv()
    finish(top, one_ref, 1, two_ref, 2)
    two_second.wait_recv()
    one_last.wait_recv()
    finish(low, two_ref, 1, one_ref, 2)
    for copy in copies_out:
        copy.wait_send()


def column_tiles(width, most=512):
    return [(at, min(most, width - at)) for at in range(0, width, most)]


def swiglu_kernel(
    copies,
    normed_ref, own_ref, below_ref, others_ref, gate_hbm, up_hbm, down_ref,
    rows_out, moved_out, norm_sum, gate_sum, up_sum, down_sum,
    normed, masked, gate_w, up_w, down_w, hidden, gate_low, up_low, back, rows, ring_buf,
    one_buf, two_buf, lead, lead_near, in_sem, out_sem, gather_send, gather_recv, send_sem,
    recv_sem, sum_send, sum_recv, near_send, near_recv, one_send, one_recv, two_send, two_recv,
    ready_sem, moved_send, moved_recv,
):
    parts = lax.axis_size("tensor")
    near, one, two = copies, 2 * copies, 4 * copies
    greet((near, one, two), True)
    own = pltpu.make_async_copy(normed_ref, normed.at[0], in_sem.at[0])
    own.start()
    gather = plane_gather_steps(
        copies, down_ref, down_w, in_sem.at[4], gather_send, gather_recv
    )
    gather[0]()
    loads = [
        pltpu.make_async_copy(gate_hbm, gate_w, in_sem.at[1]),
        pltpu.make_async_copy(up_hbm, up_w, in_sem.at[2]),
        pltpu.make_async_copy(own_ref, masked.at[0], in_sem.at[3]),
    ]
    own.wait()
    for load in loads:
        load.start()
    here = lax.axis_index("tensor")
    at_start, at_end = here == 0, here == parts - 1

    for k in range(1, parts):
        source = below_ref if k == 1 else others_ref.at[beside(-k)]
        loads.append(pltpu.make_async_copy(source, masked.at[k], in_sem.at[4 + k]))
        loads[-1].start()

    _, block_rows, width = normed.shape
    hidden_width = hidden.shape[2]
    share = width // 8
    half = share // 2
    many = 2
    tile = many * share
    both = [pl.ds(n * (block_rows // 2), block_rows // 2) for n in range(2)]

    def hop(k, n):
        return to_right(
            normed.at[k, both[n]], normed.at[k + 1, both[n]], send_sem.at[k, n], recv_sem.at[k, n]
        )

    def sum_hop(k, n):
        return to_right(
            back.at[k + 1, both[n]], ring_buf.at[k, both[n]], sum_send.at[k, n], sum_recv.at[k, n]
        )

    for n in range(2):
        hop(0, n).start()
    for load in loads:
        load.wait()
    gather[1]()
    gather[2]()
    for n in range(2):
        hop(0, n).wait_recv()
        hop(1, n).start()
    gather[3]()
    gather[4]()

    def store(k):
        home = lax.rem(lax.axis_index("tensor") + parts - k, parts)
        slot = lax.rem(k, 2)
        return pltpu.make_async_copy(rows.at[slot], rows_out.at[home], out_sem.at[slot])

    def front(k):
        for at, size in column_tiles(hidden_width):
            columns = pl.ds(at, size)

            def weight(ref):
                return ref[:, :, columns].reshape(width, size)

            glu_gate = matmul(normed[k], weight(gate_w))
            glu_up = matmul(normed[k], weight(up_w))
            grad_hidden = matmul(masked[k], weight(down_w))
            squash = jax.nn.sigmoid(glu_gate)
            act = glu_gate * squash
            slope = squash * (1.0 + glu_gate * (1.0 - squash))
            hidden[k, :, columns] = (act * glu_up).astype(bf16)
            gate_low[k, :, columns] = (grad_hidden * glu_up * slope).astype(bf16)
            up_low[k, :, columns] = (grad_hidden * act).astype(bf16)

    def rear(k):
        slot = lax.rem(k, 2)

        @pl.loop(0, 8 // many)
        def _(n):
            some = pl.ds(pl.multiple_of(n * tile, tile), tile)

            def weight(ref):
                return ref[pl.ds(n * many, many)].reshape(tile, hidden_width)

            back[k, :, some] = (
                matmul_rt(gate_low[k], weight(gate_w)) + matmul_rt(up_low[k], weight(up_w))
            ).astype(bf16)
            rows[slot, :, some] = matmul_rt(hidden[k], weight(down_w)).astype(bf16)

        store(k).start()

    def block(k, nothing):
        for n in range(2):

            @pl.when(jnp.logical_and(k > 0, k < parts - 2))
            def _():
                hop(k, n).wait_recv()
                hop(k + 1, n).start()

            @pl.when(k == parts - 1)
            def _():
                hop(parts - 2, n).wait_recv()
                sum_hop(0, n).start()

        front(k)

        @pl.when(k > 1)
        def _():
            store(k - 2).wait()

        @pl.when(k < parts - 1)
        def _():
            rear(k)

        return nothing

    lax.fori_loop(0, parts, block, 0)

    tall = parts * block_rows
    kinds = (
        (normed, gate_low, gate_w, gate_sum),
        (normed, up_low, up_w, up_sum),
        (masked, hidden, down_w, down_sum),
    )

    def product(kind, slot, store):
        left, right, _, _ = kinds[kind]
        some = pl.ds(pl.multiple_of(slot * share, share), share)
        for at, size in column_tiles(hidden_width):
            columns = pl.ds(at, size)
            store(
                columns,
                matmul_lt(
                    left[:, :, some].reshape(tall, share), right[:, :, columns].reshape(tall, size)
                ),
            )

    def across(source, target, send, recv, mask):
        return pltpu.make_async_remote_copy(
            src_ref=source,
            dst_ref=target,
            send_sem=send,
            recv_sem=recv,
            device_id={"dp": partner(mask)},
            device_id_type=pl.DeviceIdType.MESH,
        )

    top, low = pl.ds(0, half), pl.ds(half, half)

    def near_copy(kind, k):
        room = kinds[kind][2]
        return across(
            room.at[k], room.at[4 + k], near_send.at[kind, k], near_recv.at[kind, k], near
        )

    def lead_copy(kind):
        return across(
            lead.at[kind], lead_near.at[kind], near_send.at[kind, 3], near_recv.at[kind, 3], near
        )

    def one_copy(kind, n):
        room = kinds[kind][2]
        source = (lead_near.at[kind, top], room.at[5, top], room.at[5, low])[n]
        return across(
            source, one_buf.at[kind, n], one_send.at[kind, n], one_recv.at[kind, n], one
        )

    def two_copy(kind, n):
        room = kinds[kind][2]
        source = (lead_near.at[kind, low], room.at[6, low], room.at[6, top])[n]
        return across(
            source, two_buf.at[kind, n], two_send.at[kind, n], two_recv.at[kind, n], two
        )

    def flipped(k, near_too):
        me = lax.axis_index("dp")

        def turn(mask, on):
            return on * mask * (1 - 2 * lax.rem(lax.div(me, mask), 2))

        there = me + turn(one, lax.rem(k, 2)) + turn(two, lax.div(k, 2)) + turn(near, near_too)
        return lax.div(there, copies)

    def sum_step(k):
        for n in range(2):
            sum_hop(k, n).wait_recv()

            @pl.loop(0, 8 // many)
            def _(at):
                some = pl.ds(pl.multiple_of(at * tile, tile), tile)
                moved = ring_buf[k, both[n], some].astype(f32)
                if k + 1 < parts - 1:
                    total = back[k + 2, both[n], some].astype(f32) + moved
                    back[k + 2, both[n], some] = total.astype(bf16)
                else:
                    norm_sum[both[n], some] = back[0, both[n], some].astype(f32) + moved

            if k + 1 < parts - 1:
                sum_hop(k + 1, n).start()

    def keep(ref, at):
        def store(columns, value):
            ref[at, :, columns] = value.astype(bf16)

        return store

    def add(ref, at):
        def store(columns, value):
            ref[at, :, columns] = (value + ref[at, :, columns].astype(f32)).astype(bf16)

        return store

    def add_wide(total_ref, ref, at):
        def store(columns, value):
            total_ref[:, columns] = value + ref[at, :, columns].astype(f32)

        return store

    for kind in range(3):
        product(kind, flipped(3, 1), keep(lead, kind))
        lead_copy(kind).start()
    for kind in range(3):
        lead_copy(kind).wait_recv()
        product(kind, flipped(3, 0), add(lead_near, kind))
        one_copy(kind, 0).start()
        two_copy(kind, 0).start()
    rear(parts - 1)

    gather[5]()
    pl.semaphore_signal(
        ready_sem,
        inc=1,
        device_id={"dp": partner(near)},
        device_id_type=pl.DeviceIdType.MESH,
    )
    pl.semaphore_wait(ready_sem, 1)

    def theirs(k):
        for kind in range(3):
            product(kind, flipped(k, 1), keep(kinds[kind][2], k))
            near_copy(kind, k).start()

    def mine(k):
        for kind in range(3):
            near_copy(kind, k).wait_recv()
            product(kind, flipped(k, 0), add(kinds[kind][2], 4 + k))
            if k == 1:
                one_copy(kind, 1).start()
            else:
                two_copy(kind, 1).start()

    sum_step(0)
    theirs(1)
    theirs(2)
    mine(1)
    mine(2)
    theirs(0)
    for kind in range(3):
        one_copy(kind, 0).wait_recv()
        room = kinds[kind][2]
        room[6, top] = (room[6, top].astype(f32) + one_buf[kind, 0].astype(f32)).astype(bf16)
        two_copy(kind, 2).start()
        two_copy(kind, 0).wait_recv()
        room[5, low] = (room[5, low].astype(f32) + two_buf[kind, 0].astype(f32)).astype(bf16)
        one_copy(kind, 2).start()
    for k in range(1, parts - 2):
        sum_step(k)
    for kind in range(3):
        near_copy(kind, 0).wait_recv()
        room, total_ref = kinds[kind][2:]
        product(kind, flipped(0, 0), add_wide(total_ref, room, 4))
    sum_step(parts - 2)
    for k in (parts - 2, parts - 1):
        store(k).wait()
    moved_up = along(1, rows_out.at[parts - 1], moved_out, moved_send, moved_recv)
    moved_down = along(-1, rows_out.at[0], moved_out, moved_send, moved_recv)

    @pl.when(at_start)
    def _():
        moved_up.start()

    @pl.when(at_end)
    def _():
        moved_down.start()

    for kind in range(3):
        total_ref = kinds[kind][3]
        one_copy(kind, 1).wait_recv()
        two_copy(kind, 2).wait_recv()
        total_ref[:half, :] += one_buf[kind, 1].astype(f32) + two_buf[kind, 2].astype(f32)
        two_copy(kind, 1).wait_recv()
        one_copy(kind, 2).wait_recv()
        total_ref[half:, :] += two_buf[kind, 1].astype(f32) + one_buf[kind, 2].astype(f32)
    for kind in range(3):
        lead_copy(kind).wait_send()
        for k in range(3):
            near_copy(kind, k).wait_send()
        for n in range(3):
            one_copy(kind, n).wait_send()
            two_copy(kind, n).wait_send()
    for k in range(parts - 1):
        for n in range(2):
            hop(k, n).wait_send()
            sum_hop(k, n).wait_send()

    @pl.when(at_start)
    def _():
        moved_up.wait_send()

    @pl.when(at_end)
    def _():
        moved_down.wait_send()

    @pl.when(jnp.logical_not(jnp.logical_or(at_start, at_end)))
    def _():
        moved_up.wait_recv()


def swiglu(normed, own, below, others, gate_w, up_w, down_w, copies, collective):
    parts = lax.axis_size("tensor")
    rows, width = normed.shape
    hidden = gate_w.shape[2]
    share = width // 8
    somewhere = pl.BlockSpec(memory_space=pl.ANY)
    vmem = pl.BlockSpec(memory_space=pltpu.VMEM)
    wide, narrow = (parts, rows, width), (parts, rows, hidden)
    return pl.pallas_call(
        functools.partial(swiglu_kernel, copies),
        out_shape=[
            jax.ShapeDtypeStruct(wide, bf16),
            jax.ShapeDtypeStruct((rows, width), bf16),
            jax.ShapeDtypeStruct((rows, width), f32),
        ]
        + [jax.ShapeDtypeStruct((share, hidden), f32)] * 3,
        in_specs=[somewhere] * 7,
        out_specs=[somewhere] * 2 + [vmem] * 4,
        scratch_shapes=[pltpu.VMEM(wide, bf16)] * 2
        + [pltpu.VMEM((8, share, hidden), bf16)] * 3
        + [pltpu.VMEM(narrow, bf16)] * 3
        + [
            pltpu.VMEM(wide, bf16),
            pltpu.VMEM((2, rows, width), bf16),
            pltpu.VMEM((parts - 1, rows, width), bf16),
        ]
        + [pltpu.VMEM((3, 3, share // 2, hidden), bf16)] * 2
        + [pltpu.VMEM((3, share, hidden), bf16)] * 2
        + [pltpu.SemaphoreType.DMA((8,)), pltpu.SemaphoreType.DMA((2,))]
        + [pltpu.SemaphoreType.DMA((14,))] * 2
        + [pltpu.SemaphoreType.DMA((parts - 1, 2))] * 4
        + [pltpu.SemaphoreType.DMA((3, 4))] * 2
        + [pltpu.SemaphoreType.DMA((3, 3))] * 4
        + [pltpu.SemaphoreType.REGULAR]
        + [pltpu.SemaphoreType.DMA] * 2,
        compiler_params=pltpu.CompilerParams(
            collective_id=collective, has_side_effects=True, vmem_limit_bytes=62 * 1024 * 1024
        ),
        cost_estimate=pl.CostEstimate(
            flops=18 * parts * rows * width * hidden,
            bytes_accessed=1100 * rows * width,
            transcendentals=parts * rows * hidden,
        ),
    )(normed, own, below, others, gate_w, up_w, down_w)


def greet_all(copies, masks):
    barrier = pltpu.get_barrier_semaphore()
    others = [{"dp": group_member(copies, k)} for k in range(1, 8)]
    others += [{"tensor": beside(k)} for k in range(1, lax.axis_size("tensor"))]
    others += [{"dp": partner(mask)} for mask in masks]
    for other in others:
        pl.semaphore_signal(
            barrier, inc=1, device_id=other, device_id_type=pl.DeviceIdType.MESH
        )
    pl.semaphore_wait(barrier, len(others))


def group_member(copies, step):
    me = lax.axis_index("dp")
    return lax.rem(lax.div(me, copies) + step, 8) * copies + lax.rem(me, copies)


def mixer_forward_kernel(
    copies,
    own_ref, input_hbm, forget_hbm, gate_hbm, out_hbm, masked_hbm, below_hbm, inputs_hbm, bound_ref,
    live_ref, gain_ref,
    normed_out, weights_out, project_out, pre_out, squash_out, state_out, entering_out, mixed_out,
    masked_out, stream_ref, following_ref,
    normed, weights, project, pre, squashed, forget, state, decay, ends, entering, mixed,
    near_buf, one_buf, two_buf, part_buf, inputs,
    own_sem, gather_send, gather_recv, spread_send, spread_recv, spread_own, up_send, down_send, line_recv,
    carry_send, carry_recv, scatter_send, scatter_recv, masked_up, masked_down, masked_recv, out_sem, inputs_sem,
):
    parts = lax.axis_size("tensor")
    here = lax.axis_index("tensor")
    seqs, rows, width = normed.shape
    strips, _, lanes = forget.shape
    channels = strips * lanes
    mine = slot_of(copies, ())
    greet_all(copies, ())

    def own_rows_of(index):
        return pl.ds(pl.multiple_of(index * copies, copies), copies)

    def columns_of(index):
        return pl.ds(pl.multiple_of(index * channels, channels), channels)

    spread = []
    for kind, source in enumerate((input_hbm, forget_hbm, gate_hbm)):
        target = weights.at[kind, own_rows_of(mine), here]
        kept = pltpu.make_async_copy(
            source.at[:, :, columns_of(mine)], target, spread_own.at[kind]
        )
        sent = []
        for k in range(1, 8):
            there = group_member(copies, k)
            sent.append(
                pltpu.make_async_remote_copy(
                    src_ref=source.at[:, :, columns_of(lax.div(there, copies))],
                    dst_ref=target,
                    send_sem=spread_send.at[kind, k - 1],
                    recv_sem=spread_recv.at[kind, k - 1],
                    device_id={"dp": there},
                    device_id_type=pl.DeviceIdType.MESH,
                )
            )
        spread.append((kept, sent))

    def block_of(kind, block):
        return project.at[:, block] if kind == 3 else weights.at[kind, :, block]

    def line_copy(kind, k, step):
        block = here - step * k
        target = block_of(kind, block)
        source = out_hbm if kind == 3 and k == 0 else target
        sems = up_send if step == 1 else down_send
        return along(step, source, target, sems.at[kind, k], line_recv.at[kind, block])

    def goes(k, step):
        if step == 1:
            return jnp.logical_and(here >= k, here < parts - 1)
        return jnp.logical_and(here + k < parts, here > 0)

    def comes(k, step):
        return here >= k if step == 1 else here + k < parts

    def line_step(kind, k):
        for step in (1, -1):
            if k > 0:

                @pl.when(comes(k, step))
                def _():
                    line_copy(kind, k, step).wait_recv()

            if k < parts - 1:

                @pl.when(goes(k, step))
                def _():
                    line_copy(kind, k, step).start()

    def spread_arrive(kind):
        kept, sent = spread[kind]
        kept.wait()
        for copy in sent:
            copy.wait_recv()

    inputs_load = pltpu.make_async_copy(inputs_hbm, inputs, inputs_sem)
    inputs_load.start()
    out_kept = pltpu.make_async_copy(out_hbm, project.at[:, here], spread_own.at[3])
    out_kept.start()
    for kept, sent in spread:
        kept.start()
        for copy in sent:
            copy.start()
    line_step(3, 0)
    begin, pass_first, pass_second, pass_last, arrive, finish = plane_gather_steps(
        copies, own_ref, normed, own_sem, gather_send, gather_recv
    )
    begin()
    spread_arrive(0)
    line_step(0, 0)
    spread_arrive(1)
    line_step(1, 0)
    spread_arrive(2)
    pass_first()
    line_step(0, 1)
    pass_second()
    line_step(1, 1)
    line_step(0, 2)
    line_step(1, 2)
    line_step(0, 3)
    line_step(2, 0)
    pass_last()
    line_step(1, 3)
    line_step(3, 1)
    arrive()

    many = 2

    def project_rows(kind, at):
        left = normed[pl.ds(at * many, many)].reshape(many * rows, width)
        return matmul(left, weights[kind].reshape(width, channels))

    def rows_at(at):
        return pl.ds(pl.multiple_of(at * many * rows, many * rows), many * rows)

    def strip_of(value, n):
        return value[:, n * lanes : (n + 1) * lanes]

    @pl.loop(0, seqs // many)
    def _(at):
        some = rows_at(at)
        value = project_rows(0, at)
        pre[0, some, :] = value
        inflow = live_ref[some, :] * silu_of(value)
        for n in range(strips):
            state[n, some, :] = strip_of(inflow, n)

    line_step(2, 1)

    @pl.loop(0, seqs // many)
    def _(at):
        some = rows_at(at)
        squash = jax.nn.sigmoid(project_rows(1, at))
        bound = bound_ref[...]
        value = bound + (1.0 - bound) * squash
        for n in range(strips):
            squashed[n, some, :] = strip_of(squash, n)
            forget[n, some, :] = strip_of(value, n)
            state[n, some, :] = (1.0 - strip_of(value, n)) * state[n, some, :]

    line_step(3, 2)

    ahead = 8

    def step(at, carry):
        places = [pl.ds(at * ahead + u, seqs, stride=rows) for u in range(ahead)]
        read = [
            [(forget[n, some, :], state[n, some, :]) for some in places] for n in range(strips)
        ]
        following = []
        for n, (total, product) in enumerate(carry):
            for some, (keep, drive) in zip(places, read[n]):
                total = keep * total + drive
                product = product * keep
                state[n, some, :] = total
                decay[n, some, :] = product
            following.append((total, product))
        return tuple(following)

    start = (jnp.zeros((seqs, lanes), f32), jnp.ones((seqs, lanes), f32))
    carry = lax.fori_loop(0, rows // ahead, step, (start,) * strips)
    for n, (total, product) in enumerate(carry):
        ends[here, 0, :, n * lanes : (n + 1) * lanes] = total
        ends[here, 1, :, n * lanes : (n + 1) * lanes] = product
    carries = []
    for k in range(1, parts):
        copy = pltpu.make_async_remote_copy(
            src_ref=ends.at[here],
            dst_ref=ends.at[here],
            send_sem=carry_send.at[k - 1],
            recv_sem=carry_recv.at[k - 1],
            device_id={"tensor": beside(k)},
            device_id_type=pl.DeviceIdType.MESH,
        )
        copy.start()
        carries.append(copy)
    line_step(2, 2)

    inner = jnp.logical_and(here > 0, here < parts - 1)

    def masked_down_copy(k):
        block = here + k
        source = masked_hbm if k == 0 else masked_out.at[block]
        return along(-1, source, masked_out.at[block], masked_down.at[k], masked_recv.at[block])

    def masked_up_copy(k):
        block = here - 1 - k
        source = below_hbm if k == 0 else masked_out.at[block]
        return along(1, source, masked_out.at[block], masked_up.at[k], masked_recv.at[block])

    def masked_came(block):
        along(1, below_hbm, masked_out.at[block], masked_up.at[0], masked_recv.at[block]).wait_recv()

    def masked_step(k):
        if k == 1:

            @pl.when(here > 0)
            def _():
                masked_down_copy(0).start()

            @pl.when(inner)
            def _():
                masked_up_copy(0).start()

        elif k == 2:

            @pl.when(here < parts - 1)
            def _():
                masked_came(here + 1)

            @pl.when(inner)
            def _():
                masked_down_copy(1).start()

            @pl.when(here > 1)
            def _():
                masked_came(here - 2)

            @pl.when(here == 2)
            def _():
                masked_up_copy(1).start()

        else:

            @pl.when(here < 2)
            def _():
                masked_came(here + 2)

            @pl.when(here == parts - 1)
            def _():
                masked_came(0)

    for copy in carries:
        copy.wait_recv()
    coming = jnp.zeros((seqs, channels), f32)
    entered = coming
    for k in range(parts - 1):
        coming = ends[k, 1] * coming + ends[k, 0]
        entered = jnp.where(here == k + 1, coming, entered)
    for n in range(seqs):
        entering[n] = entered[n : n + 1]
    line_step(3, 3)
    line_step(2, 3)

    @pl.loop(0, seqs // many)
    def _(at):
        some = rows_at(at)
        value = project_rows(2, at)
        pre[1, some, :] = value
        act = silu_of(value)
        for n in range(many):
            slot = at * many + n
            one = pl.ds(pl.multiple_of(slot * rows, rows), rows)
            for strip in range(strips):
                columns = slice(strip * lanes, (strip + 1) * lanes)
                whole = state[strip, one, :] + (
                    decay[strip, one, :] * entering[slot, :, columns]
                )
                state[strip, one, :] = whole
                mixed[slot, :, columns] = (
                    whole * act[n * rows : (n + 1) * rows, columns]
                ).astype(bf16)

    out_kept.wait()
    stores = [
        pltpu.make_async_copy(source, target, out_sem.at[n])
        for n, (source, target) in enumerate(
            (
                (normed, normed_out),
                (weights, weights_out),
                (project, project_out),
                (pre, pre_out),
                (squashed, squash_out),
                (state, state_out),
                (entering, entering_out),
                (mixed, mixed_out),
            )
        )
    ]
    for store in stores:
        store.start()

    def out_product(slot, columns):
        right = project[:, :, :, columns]
        return matmul(mixed[slot], right.reshape(channels, right.shape[-1]))

    masked_step(1)

    def between(point):
        if point == "low":
            masked_step(2)

    plane_scatter_steps(
        copies, stream_ref, near_buf, one_buf, two_buf, part_buf, scatter_send, scatter_recv,
        out_product, between,
    )

    inputs_load.wait()
    some_rows = min(64, rows)

    @pl.loop(0, rows // some_rows)
    def _(k):
        some = pl.ds(pl.multiple_of(k * some_rows, some_rows), some_rows)
        stream = inputs[some, :] + stream_ref[some, :]
        stream_ref[some, :] = stream
        following_ref[some, :] = (norm_rows(stream)[1] * gain_ref[...]).astype(bf16)

    masked_step(3)

    @pl.when(here > 0)
    def _():
        masked_down_copy(0).wait_send()

    @pl.when(inner)
    def _():
        masked_up_copy(0).wait_send()
        masked_down_copy(1).wait_send()

    @pl.when(here == 2)
    def _():
        masked_up_copy(1).wait_send()

    finish()
    for kept, sent in spread:
        for copy in sent:
            copy.wait_send()
    for kind in range(4):
        for k in range(parts - 1):
            for step in (1, -1):

                @pl.when(goes(k, step))
                def _():
                    line_copy(kind, k, step).wait_send()

    for copy in carries:
        copy.wait_send()
    for store in stores:
        store.wait()


def mixer_forward(
    normed, w_input, w_forget, w_gate, w_out, masked, below, inputs, bound, live, gain, copies,
    collective,
):
    parts = lax.axis_size("tensor")
    rows, width = normed.shape
    channels = width // 8
    own_rows = w_input.shape[1]
    somewhere = pl.BlockSpec(memory_space=pl.ANY)
    vmem = pl.BlockSpec(memory_space=pltpu.VMEM)
    wide = (8, rows, width)
    weights = (3, 8 * copies, parts, own_rows, channels)
    project = (copies, parts, own_rows, width)
    flat = (8 * rows, channels)
    lanes = min(128, channels)
    strips = (channels // lanes, 8 * rows, lanes)
    shaped = (8, rows, channels)
    half = rows // 2
    dma = pltpu.SemaphoreType.DMA
    return pl.pallas_call(
        functools.partial(mixer_forward_kernel, copies),
        out_shape=[
            jax.ShapeDtypeStruct(wide, bf16),
            jax.ShapeDtypeStruct(weights, bf16),
            jax.ShapeDtypeStruct(project, bf16),
            jax.ShapeDtypeStruct((2,) + flat, f32),
            jax.ShapeDtypeStruct(strips, f32),
            jax.ShapeDtypeStruct(strips, f32),
            jax.ShapeDtypeStruct((8, 1, channels), f32),
            jax.ShapeDtypeStruct(shaped, bf16),
            jax.ShapeDtypeStruct((parts, rows, width), bf16),
            jax.ShapeDtypeStruct((rows, width), f32),
            jax.ShapeDtypeStruct((rows, width), bf16),
        ],
        in_specs=[somewhere] * 8 + [vmem] * 3,
        out_specs=[somewhere] * 9 + [vmem] * 2,
        scratch_shapes=[
            pltpu.VMEM(wide, bf16),
            pltpu.VMEM(weights, bf16),
            pltpu.VMEM(project, bf16),
            pltpu.VMEM((2,) + flat, f32),
            pltpu.VMEM(strips, f32),
            pltpu.VMEM(strips, f32),
            pltpu.VMEM(strips, f32),
            pltpu.VMEM(strips, f32),
            pltpu.VMEM((parts, 2, 8, channels), f32),
            pltpu.VMEM((8, 1, channels), f32),
            pltpu.VMEM(shaped, bf16),
            pltpu.VMEM((4, rows, width), bf16),
            pltpu.VMEM((3, half, width), bf16),
            pltpu.VMEM((3, half, width), bf16),
            pltpu.VMEM((4, rows, width), bf16),
            pltpu.VMEM((rows, width), f32),
            dma,
            dma((14,)),
            dma((14,)),
            dma((3, 7)),
            dma((3, 7)),
            dma((4,)),
            dma((4, parts - 1)),
            dma((4, parts - 1)),
            dma((4, parts)),
            dma((parts - 1,)),
            dma((parts - 1,)),
            dma((10,)),
            dma((10,)),
            dma((parts - 1,)),
            dma((parts - 1,)),
            dma((parts,)),
            dma((8,)),
            dma,
        ],
        compiler_params=pltpu.CompilerParams(
            collective_id=collective, has_side_effects=True, vmem_limit_bytes=56 * 1024 * 1024
        ),
        cost_estimate=pl.CostEstimate(
            flops=8 * rows * width * width,
            bytes_accessed=900 * rows * width,
            transcendentals=0,
        ),
    )(normed, w_input, w_forget, w_gate, w_out, masked, below, inputs, bound, live, gain)


def mixer_backward_kernel(
    copies, masks,
    norm_hbm, normed_hbm, weights_hbm, project_hbm, pre_hbm, squash_hbm, state_hbm, mixed_hbm,
    unit_hbm, stream_hbm, cotangent_hbm, entering_ref, bound_ref, live_ref, gain_ref, scale_ref, gain_two_ref,
    rows_hbm, moved_hbm,
    result_ref, input_sum, forget_sum, gate_sum, project_sum, small_sums, moved_out,
    rows_buf, weights, project, pre, squashed, state, mixed, unit, stream, drive, decay, ends,
    entered, grad_pre, grad_w, grad_project, line_w, line_project, bound_sum, whole_w, spread_w,
    small_recv, small_ring, gain_sum, gain_two_sum, near_buf, one_buf, two_buf, part_buf,
    load_sem, gather_send, gather_recv, carry_send, carry_recv, up_send, down_send, line_recv,
    scatter_send, scatter_recv, spread_send, spread_recv, spread_own, small_send, small_got,
    moved_sem, moved_send, moved_recv, first_sem,
):
    parts = lax.axis_size("tensor")
    here = lax.axis_index("tensor")
    seqs, rows, width = rows_buf.shape
    strips, _, lanes = drive.shape
    channels = strips * lanes
    own_rows = weights.shape[3]
    weight_sums = (input_sum, forget_sum, gate_sum)
    near, one, two = copies, 2 * copies, 4 * copies
    mine = slot_of(copies, ())
    greet_all(copies, masks)
    firsts = [
        pltpu.make_async_copy(source, target, first_sem.at[n])
        for n, (source, target) in enumerate(
            ((norm_hbm, result_ref), (stream_hbm, unit), (cotangent_hbm, stream))
        )
    ]
    for load in firsts:
        load.start()
    begin, pass_first, pass_second, pass_last, arrive, finish = plane_gather_steps(
        copies, rows_buf.at[mine], rows_buf, None, gather_send, gather_recv
    )

    at_start, at_end = here == 0, here == parts - 1
    inside = jnp.logical_not(jnp.logical_or(at_start, at_end))
    low_half = here == 1

    def fetch(block, came, first, second):
        loads = (
            pltpu.make_async_copy(rows_hbm.at[block], part_buf.at[first], moved_sem.at[0]),
            pltpu.make_async_copy(came, part_buf.at[second], moved_sem.at[1]),
        )
        for load in loads:
            load.start()
        for load in loads:
            load.wait()
        part_buf[first] = (
            part_buf[first].astype(f32) + part_buf[second].astype(f32)
        ).astype(bf16)

    def moved_copy(n, step, source):
        return along(step, source, moved_out.at[n], moved_send.at[n], moved_recv.at[n])

    def moved_second():
        @pl.when(at_start)
        def _():
            moved_copy(0, 1, rows_hbm.at[2]).start()

        @pl.when(at_end)
        def _():
            moved_copy(1, -1, rows_hbm.at[1]).start()

        @pl.when(inside)
        def _():
            fetch(3 - 3 * (here - 1), moved_hbm, 0, 1)

        @pl.when(low_half)
        def _():
            moved_copy(0, 1, part_buf.at[0]).start()

        @pl.when(here == 2)
        def _():
            moved_copy(1, -1, part_buf.at[0]).start()

    def moved_last():
        @pl.when(at_start)
        def _():
            moved_copy(0, 1, rows_hbm.at[2]).wait_send()
            moved_copy(2, 1, rows_hbm.at[1]).start()

        @pl.when(at_end)
        def _():
            moved_copy(1, -1, rows_hbm.at[1]).wait_send()
            moved_copy(3, -1, rows_hbm.at[2]).start()

        @pl.when(inside)
        def _():
            moved_copy(0, 1, part_buf.at[0]).wait_recv()
            fetch(here + 1, moved_out.at[0], 1, 2)
            moved_copy(2, 1, part_buf.at[1]).start()

        @pl.when(low_half)
        def _():
            moved_copy(0, 1, part_buf.at[0]).wait_send()

        @pl.when(here == 2)
        def _():
            moved_copy(1, -1, part_buf.at[0]).wait_send()

        @pl.when(inside)
        def _():
            moved_copy(1, -1, part_buf.at[0]).wait_recv()
            fetch(here - 1, moved_out.at[1], 2, 3)
            moved_copy(3, -1, part_buf.at[2]).start()

    def moved_end():
        @pl.when(here < parts - 1)
        def _():
            moved_copy(2, 1, part_buf.at[1]).wait_send()
            moved_copy(3, -1, part_buf.at[2]).wait_recv()

        @pl.when(here > 0)
        def _():
            moved_copy(3, -1, part_buf.at[2]).wait_send()
            moved_copy(2, 1, part_buf.at[1]).wait_recv()

    loads = [
        pltpu.make_async_copy(source, target, load_sem.at[n + 1])
        for n, (source, target) in enumerate(
            (
                (project_hbm, project),
                (pre_hbm, pre),
                (state_hbm, state),
                (mixed_hbm, mixed),
                (squash_hbm, squashed),
                (weights_hbm, weights),
                (unit_hbm, unit),
            )
        )
    ]
    for load in loads[:-1]:
        load.start()

    for load in firsts:
        load.wait()
    gain_two_sum[...] = jnp.zeros_like(gain_two_sum)
    some_rows = min(64, rows)

    @pl.loop(0, rows // some_rows)
    def _(k):
        some = pl.ds(pl.multiple_of(k * some_rows, some_rows), some_rows)
        at = pl.ds(pl.multiple_of(mine * rows + k * some_rows, some_rows), some_rows)
        scale, units = norm_rows(unit[some, :])
        grad_norm = result_ref[some, :]
        gain_two_sum[...] += jnp.sum(grad_norm * units, axis=0, keepdims=True)
        total = live_ref[at, :] * stream[some, :] + norm_back(
            grad_norm, units, scale, gain_two_ref[...]
        )
        stream[some, :] = total
        rows_buf[mine, some, :] = total.astype(bf16)

    begin()
    loads[-1].start()
    moved_second()
    for load in loads[:3]:
        load.wait()

    def slot_rows(slot):
        return pl.ds(pl.multiple_of(slot * rows, rows), rows)

    def take(slot):
        some = slot_rows(slot)
        grad_mixed = matmul_rt(rows_buf[slot], project[...].reshape(channels, width))
        gate = pre[1, some, :]
        squash = jax.nn.sigmoid(gate)
        act = gate * squash
        slope = squash * (1.0 + gate * (1.0 - squash))
        for n in range(strips):
            columns = slice(n * lanes, (n + 1) * lanes)
            part = grad_mixed[:, columns]
            drive[n, some, :] = part * act[:, columns]
            at = 2 * channels + n * lanes
            grad_pre[slot, :, at : at + lanes] = (
                part * state[n, some, :] * slope[:, columns]
            ).astype(bf16)

    pass_first()
    pass_second()
    arrive(slice(0, 6))
    for flips in ((), (near,), (one,), (two,), (near, one), (near, two)):
        take(slot_of(copies, flips))
    moved_last()
    pass_last()
    take(slot_of(copies, (one, two)))
    arrive(slice(6, 8))
    take(slot_of(copies, (near, one, two)))

    tile = min(512, width)
    loads[3].wait()

    @pl.loop(0, width // tile)
    def _(k):
        columns = pl.ds(pl.multiple_of(k * tile, tile), tile)
        value = matmul_lt(
            mixed[...].reshape(seqs * rows, channels),
            rows_buf[:, :, columns].reshape(seqs * rows, tile),
        )
        grad_project[:, :, :, columns] = value.astype(bf16).reshape(
            copies, parts, own_rows, tile
        )

    def part_of(kind, block):
        return grad_project.at[:, block] if kind == 3 else grad_w.at[kind, :, block]

    def room_of(kind, index):
        return line_project.at[index] if kind == 3 else line_w.at[kind, index]

    def line_up(kind, k):
        block = parts - 1 - k + here
        return along(
            1, part_of(kind, block), room_of(kind, block), up_send.at[kind, k],
            line_recv.at[kind, block],
        )

    def line_down(kind, k):
        block = k - parts + 1 + here
        index = parts if k == parts - 2 else block
        return along(
            -1, part_of(kind, block), room_of(kind, index), down_send.at[kind, k],
            line_recv.at[kind, index],
        )

    def came(kind, index):
        return along(1, part_of(kind, 0), room_of(kind, index), up_send.at[kind, 0],
                     line_recv.at[kind, index])

    def add_came(kind, block):
        came(kind, block).wait_recv()
        if kind == 3:
            total = grad_project[:, block].astype(f32) + line_project[block].astype(f32)
            grad_project[:, block] = total.astype(bf16)
        else:
            total = grad_w[kind, :, block].astype(f32) + line_w[kind, block].astype(f32)
            grad_w[kind, :, block] = total.astype(bf16)

    def goes_up(k):
        return jnp.logical_and(here <= k, here < parts - 1)

    def goes_down(k):
        return jnp.logical_and(parts - 1 - here <= k, here > 0)

    def line_step(kind, k):
        @pl.when(jnp.logical_and(goes_up(k), here > 0))
        def _():
            add_came(kind, parts - 1 - k + here)

        @pl.when(goes_up(k))
        def _():
            line_up(kind, k).start()

        @pl.when(jnp.logical_and(goes_down(k), here < parts - 1))
        def _():
            add_came(kind, k - parts + 1 + here)

        @pl.when(goes_down(k))
        def _():
            line_down(kind, k).start()

    def advance(kind, k):
        if k + 1 < parts - 1:
            line_step(kind, k + 1)
            return

        @pl.when(here > 0)
        def _():
            came(kind, here).wait_recv()

        @pl.when(here < parts - 1)
        def _():
            came(kind, parts).wait_recv()

        if kind == 3:
            project_sum[...] = (
                grad_project[:, here].astype(f32)
                + line_project[here].astype(f32)
                + line_project[parts].astype(f32)
            )
        else:
            total = (
                grad_w[kind, :, here].astype(f32)
                + line_w[kind, here].astype(f32)
                + line_w[kind, parts].astype(f32)
            )
            whole_w[kind] = total.astype(bf16)
            for copy in spread_copies(kind):
                copy.start()

    @pl.when(at_start)
    def _():
        line_w[:, 0] = jnp.zeros_like(line_w[:, 0])
        line_project[0] = jnp.zeros_like(line_project[0])

    @pl.when(at_end)
    def _():
        line_w[:, parts] = jnp.zeros_like(line_w[:, parts])
        line_project[parts] = jnp.zeros_like(line_project[parts])

    def spread_copies(kind, own=True):
        found = []
        for k in range(1, 8):
            there = group_member(copies, k)
            source = pl.ds(pl.multiple_of(lax.div(there, copies) * copies, copies), copies)
            found.append(
                pltpu.make_async_remote_copy(
                    src_ref=whole_w.at[kind, source],
                    dst_ref=spread_w.at[kind, mine],
                    send_sem=spread_send.at[kind, k - 1],
                    recv_sem=spread_recv.at[kind, k - 1],
                    device_id={"dp": there},
                    device_id_type=pl.DeviceIdType.MESH,
                )
            )
        if own:
            source = pl.ds(pl.multiple_of(mine * copies, copies), copies)
            found.append(
                pltpu.make_async_copy(
                    whole_w.at[kind, source], spread_w.at[kind, mine], spread_own.at[kind]
                )
            )
        return found

    line_step(3, 0)
    finish()
    normed_load = pltpu.make_async_copy(normed_hbm, rows_buf, load_sem.at[0])
    normed_load.start()
    loads[4].wait()

    ahead = 8

    def step(k, carry):
        places = [pl.ds(rows - 1 - u - k * ahead, seqs, stride=rows) for u in range(ahead)]
        read = [
            [(squashed[n, some, :], drive[n, some, :]) for some in places] for n in range(strips)
        ]
        following = []
        for n, (coming, product) in enumerate(carry):
            bound = bound_ref[:, n * lanes : (n + 1) * lanes]
            for some, (squash, given) in zip(places, read[n]):
                keep = bound + (1.0 - bound) * squash
                carried = given + coming
                drive[n, some, :] = carried
                decay[n, some, :] = product
                coming = keep * carried
                product = product * keep
            following.append((coming, product))
        return tuple(following)

    start = (jnp.zeros((seqs, lanes), f32), jnp.ones((seqs, lanes), f32))
    carry = lax.fori_loop(0, rows // ahead, step, (start,) * strips)
    for n, (coming, product) in enumerate(carry):
        ends[here, 0, :, n * lanes : (n + 1) * lanes] = coming
        ends[here, 1, :, n * lanes : (n + 1) * lanes] = product
    carries = []
    for k in range(1, parts):
        copy = pltpu.make_async_remote_copy(
            src_ref=ends.at[here],
            dst_ref=ends.at[here],
            send_sem=carry_send.at[k - 1],
            recv_sem=carry_recv.at[k - 1],
            device_id={"tensor": beside(k)},
            device_id_type=pl.DeviceIdType.MESH,
        )
        copy.start()
        carries.append(copy)
    normed_load.wait()

    def weight_grad(kind):
        @pl.loop(0, width // tile)
        def _(k):
            columns = pl.ds(pl.multiple_of(k * tile, tile), tile)
            value = matmul_lt(
                grad_pre[:, :, kind * channels : (kind + 1) * channels].reshape(
                    seqs * rows, channels
                ),
                rows_buf[:, :, columns].reshape(seqs * rows, tile),
            )
            count = tile // (parts * own_rows)
            grad_w[kind, pl.ds(k * count, count)] = value.T.astype(bf16).reshape(
                count, parts, own_rows, channels
            )

        line_step(kind, 0)

    advance(3, 0)
    weight_grad(2)
    for copy in carries:
        copy.wait_recv()
    coming = jnp.zeros((seqs, channels), f32)
    arrived = coming
    for k in range(parts - 1, 0, -1):
        coming = ends[k, 1] * coming + ends[k, 0]
        arrived = jnp.where(here == k - 1, coming, arrived)
    for n in range(seqs):
        entered[n] = arrived[n : n + 1]
    bound_sum[...] = jnp.zeros_like(bound_sum)
    first_row = lax.broadcasted_iota(jnp.int32, (rows, lanes), 0) == 0

    @pl.loop(0, seqs)
    def _(slot):
        some = slot_rows(slot)
        alive = live_ref[some, :]
        for n in range(strips):
            columns = slice(n * lanes, (n + 1) * lanes)
            bound = bound_ref[:, columns]
            squash = squashed[n, some, :]
            keep = bound + (1.0 - bound) * squash
            carried = drive[n, some, :] + decay[n, some, :] * entered[slot, :, columns]
            prior = jnp.where(
                first_row, entering_ref[slot, :, columns], pltpu.roll(state[n, some, :], 1, 0)
            )
            value = pre[0, some, columns]
            gate = jax.nn.sigmoid(value)
            slope = gate * (1.0 + value * (1.0 - gate))
            grad_forget = carried * prior - carried * alive * value * gate
            at = n * lanes
            grad_pre[slot, :, at : at + lanes] = (
                carried * alive * (1.0 - keep) * slope
            ).astype(bf16)
            at = channels + n * lanes
            grad_pre[slot, :, at : at + lanes] = (
                grad_forget * (1.0 - bound) * squash * (1.0 - squash)
            ).astype(bf16)
            bound_sum[:, columns] += jnp.sum(
                grad_forget * (1.0 - squash), axis=0, keepdims=True
            )

    advance(3, 1)
    loads[5].wait()
    moved_end()

    def normed_product(slot, columns):
        at = lax.div(columns.start, parts * own_rows)
        count = tile // (parts * own_rows)
        total = None
        for kind in range(3):
            part = matmul_rt(
                grad_pre[slot, :, kind * channels : (kind + 1) * channels],
                weights[kind, pl.ds(at, count)].reshape(tile, channels),
            )
            total = part if total is None else total + part
        return total

    def between(point):
        if point == "sent":
            weight_grad(0)
            advance(2, 0)
            weight_grad(1)
            advance(3, 2)
        elif point == "added":
            advance(2, 1)
            advance(0, 0)
        elif point == "top":
            advance(1, 0)
            advance(2, 2)
        elif point == "low":
            advance(0, 1)
            advance(1, 1)

    plane_scatter_steps(
        copies, result_ref, near_buf, one_buf, two_buf, part_buf, scatter_send, scatter_recv,
        normed_product, between,
    )

    loads[6].wait()
    gain_sum[...] = jnp.zeros_like(gain_sum)

    @pl.loop(0, rows // some_rows)
    def _(k):
        some = pl.ds(pl.multiple_of(k * some_rows, some_rows), some_rows)
        grad_norm = result_ref[some, :]
        units = unit[some, :]
        gain_sum[...] += jnp.sum(grad_norm * units, axis=0, keepdims=True)
        scaled = grad_norm * gain_ref[...]
        mean = jnp.mean(scaled * units, axis=-1, keepdims=True)
        result_ref[some, :] = stream[some, :] + scale_ref[some, :] * (scaled - units * mean)

    for n in range(8):
        columns = slice(n * channels, (n + 1) * channels)
        small_sums[n : n + 1, :] = gain_sum[:, columns]
        small_sums[8 + n : 9 + n, :] = gain_two_sum[:, columns]
        small_sums[16 + n : 17 + n, :] = jnp.where(mine == n, bound_sum[...], 0.0)

    plane_small = []
    for k in range(1, 8):
        copy = pltpu.make_async_remote_copy(
            src_ref=small_sums,
            dst_ref=small_recv.at[k - 1],
            send_sem=small_send.at[k - 1],
            recv_sem=small_got.at[k - 1],
            device_id={"dp": group_member(copies, k)},
            device_id_type=pl.DeviceIdType.MESH,
        )
        copy.start()
        plane_small.append(copy)

    def small_copy(n):
        return pltpu.make_async_remote_copy(
            src_ref=small_sums,
            dst_ref=small_recv.at[7 + n],
            send_sem=small_send.at[7 + n],
            recv_sem=small_got.at[7 + n],
            device_id={"dp": partner(masks[n])},
            device_id_type=pl.DeviceIdType.MESH,
        )

    advance(0, 2)
    advance(1, 2)
    for copy in plane_small:
        copy.wait()
    for k in range(7):
        small_sums[...] += small_recv[k]
    for n in range(len(masks)):
        small_copy(n).start()
        small_copy(n).wait()
        small_sums[...] += small_recv[7 + n]
    ring_small = []
    for k in range(1, parts):
        copy = pltpu.make_async_remote_copy(
            src_ref=small_sums,
            dst_ref=small_ring.at[k - 1],
            send_sem=small_send.at[7 + len(masks) + k - 1],
            recv_sem=small_got.at[7 + len(masks) + k - 1],
            device_id={"tensor": beside(k)},
            device_id_type=pl.DeviceIdType.MESH,
        )
        copy.start()
        ring_small.append(copy)
    for kind in (2, 0, 1):
        spread = spread_copies(kind)
        for copy in spread[:-1]:
            copy.wait_recv()
        spread[-1].wait()
        for slot in range(8):
            weight_sums[kind][:, :, slot * channels : (slot + 1) * channels] = spread_w[
                kind, slot
            ].astype(f32)
    for copy in ring_small:
        copy.wait()
    for k in range(parts - 1):
        small_sums[...] += small_ring[k]
    for kind in range(4):
        for k in range(parts - 1):

            @pl.when(goes_up(k))
            def _():
                line_up(kind, k).wait_send()

            @pl.when(goes_down(k))
            def _():
                line_down(kind, k).wait_send()

    for kind in range(3):
        for copy in spread_copies(kind, False):
            copy.wait_send()
    for copy in carries:
        copy.wait_send()


def mixer_backward(
    grad_norm, normed, weights, project, pre, squashed, state, mixed, unit, stream, cotangent,
    entering, bound, live, gain, scale, gain_two, out_rows, out_moved, copies, masks, collective,
):
    parts = lax.axis_size("tensor")
    _, rows, width = normed.shape
    channels = width // 8
    own_rows = project.shape[2]
    somewhere = pl.BlockSpec(memory_space=pl.ANY)
    vmem = pl.BlockSpec(memory_space=pltpu.VMEM)
    half = rows // 2
    dma = pltpu.SemaphoreType.DMA
    blocks = (8 * copies, own_rows, channels)
    small = (24, channels)
    return pl.pallas_call(
        functools.partial(mixer_backward_kernel, copies, masks),
        out_shape=[
            jax.ShapeDtypeStruct((rows, width), f32),
        ]
        + [jax.ShapeDtypeStruct((copies, own_rows, width), f32)] * 4
        + [
            jax.ShapeDtypeStruct(small, f32),
            jax.ShapeDtypeStruct((4, rows, width), bf16),
        ],
        in_specs=[somewhere] * 11 + [vmem] * 6 + [somewhere] * 2,
        out_specs=[vmem] * 6 + [somewhere],
        scratch_shapes=[
            pltpu.VMEM(normed.shape, bf16),
            pltpu.VMEM(weights.shape, bf16),
            pltpu.VMEM(project.shape, bf16),
            pltpu.VMEM(pre.shape, f32),
            pltpu.VMEM(squashed.shape, f32),
            pltpu.VMEM(state.shape, f32),
            pltpu.VMEM(mixed.shape, bf16),
            pltpu.VMEM((rows, width), f32),
            pltpu.VMEM((rows, width), f32),
            pltpu.VMEM(state.shape, f32),
            pltpu.VMEM(state.shape, f32),
            pltpu.VMEM((parts, 2, 8, channels), f32),
            pltpu.VMEM((8, 1, channels), f32),
            pltpu.VMEM((8, rows, 3 * channels), bf16),
            pltpu.VMEM(weights.shape, bf16),
            pltpu.VMEM(project.shape, bf16),
            pltpu.VMEM((3, parts + 1) + blocks, bf16),
            pltpu.VMEM((parts + 1, copies, own_rows, width), bf16),
            pltpu.VMEM((1, channels), f32),
            pltpu.VMEM((3,) + blocks, bf16),
            pltpu.VMEM((3, 8, copies, own_rows, channels), bf16),
            pltpu.VMEM((7 + len(masks),) + small, f32),
            pltpu.VMEM((parts - 1,) + small, f32),
            pltpu.VMEM((1, width), f32),
            pltpu.VMEM((1, width), f32),
            pltpu.VMEM((4, rows, width), bf16),
            pltpu.VMEM((3, half, width), bf16),
            pltpu.VMEM((3, half, width), bf16),
            pltpu.VMEM((4, rows, width), bf16),
            dma((9,)),
            dma((14,)),
            dma((14,)),
            dma((parts - 1,)),
            dma((parts - 1,)),
            dma((4, parts - 1)),
            dma((4, parts - 1)),
            dma((4, parts + 1)),
            dma((10,)),
            dma((10,)),
            dma((3, 7)),
            dma((3, 7)),
            dma((3,)),
            dma((7 + len(masks) + parts - 1,)),
            dma((7 + len(masks) + parts - 1,)),
            dma((2,)),
            dma((4,)),
            dma((4,)),
            dma((3,)),
        ],
        compiler_params=pltpu.CompilerParams(
            collective_id=collective, has_side_effects=True, vmem_limit_bytes=62 * 1024 * 1024
        ),
        cost_estimate=pl.CostEstimate(
            flops=16 * rows * width * width,
            bytes_accessed=900 * rows * width,
            transcendentals=0,
        ),
    )(
        grad_norm, normed, weights, project, pre, squashed, state, mixed, unit, stream, cotangent,
        entering, bound, live, gain, scale, gain_two, out_rows, out_moved,
    )


def on_device(
    inputs,
    lengths,
    gain_mix,
    gain_glu,
    lower_bound,
    w_input,
    w_forget,
    w_gate_mix,
    w_out,
    w_gate,
    w_up,
    w_down,
    cotangent,
):
    tensor_parts = lax.axis_size("tensor")
    data_parts = lax.axis_size("dp")
    tensor_index = lax.axis_index("tensor")
    data_index = lax.axis_index("dp")
    rows_here, width = inputs.shape
    group = min(8, data_parts)
    copies = data_parts // group
    group_index = lax.div(data_index, copies)
    copy_index = lax.rem(data_index, copies)
    group_masks = [copies << k for k in range(group.bit_length() - 1)]
    copy_masks = [1 << k for k in range(copies.bit_length() - 1)]
    all_masks = [1 << k for k in range(data_parts.bit_length() - 1)]
    group_lists = [[g * copies + o for g in range(group)] for o in range(copies)]
    channels = width // group
    own_rows = w_input.shape[0]

    high = lax.div(lengths, 32).astype(bf16)
    low = lax.rem(lengths, 32).astype(bf16)
    length_row = jnp.concatenate([high, low, jnp.zeros((own_rows - 2,), bf16)])
    small = jnp.stack([gain_mix, gain_glu, lower_bound, length_row])
    small = in_order(shifted_blocks(small))
    small = gather_bits(small, sorted(all_masks, reverse=True)).astype(f32)
    small = small.reshape((data_parts * tensor_parts,) + small.shape[2:])
    gain_one = small[:, 0].reshape(width)
    gain_two = small[:, 1].reshape(width)
    bound = lax.dynamic_slice_in_dim(small[:, 2].reshape(width), group_index * channels, channels)
    every_length = small[:, 3].reshape(data_parts, tensor_parts, own_rows)[:, 0, :2]
    every_length = (every_length[:, 0] * 32.0 + every_length[:, 1]).astype(jnp.int32)
    group_lengths = lax.dynamic_index_in_dim(
        every_length.reshape(group, copies), copy_index, axis=1, keepdims=False
    )
    position = tensor_index * rows_here + jnp.arange(rows_here, dtype=jnp.int32)
    live_own = (position < lengths[0]).astype(f32)[:, None]
    live = (position[None, :] < group_lengths[:, None]).astype(f32)
    live = live.reshape(group * rows_here, 1)

    mixer_weights = [w_input, w_forget, w_gate_mix, w_out]
    if copies > 1:
        mixer_weights = [gather_bits(weight, copy_masks[::-1]) for weight in mixer_weights]
    mixer_weights = [weight.reshape(copies, own_rows, width) for weight in mixer_weights]

    masked_own = (live_own * cotangent).astype(bf16)
    masked_below = ring(masked_own)

    scale_one, unit_one = norm_rows(inputs)
    rows_all = group * rows_here
    *mixer_kept, mixed, masked_others, stream, normed_two = (
        mixer_forward(
            (unit_one * gain_one).astype(bf16),
            *mixer_weights,
            masked_own,
            masked_below,
            inputs,
            bound[None, :],
            live,
            gain_two[None, :],
            copies,
            1,
        )
    )

    hidden_here = w_gate.shape[1]
    gate_w, up_w = (
        lax.all_gather(weight, "dp", axis=0, tiled=True).reshape(group, channels, hidden_here)
        for weight in (w_gate, w_up)
    )
    down_part = w_down.T
    if copies > 1:
        down_part = gather_bits(down_part, copy_masks[::-1]).reshape(channels, hidden_here)

    out_rows, out_moved, grad_norm_two, *weight_sums = swiglu(
        normed_two,
        masked_own,
        masked_below,
        masked_others,
        gate_w,
        up_w,
        down_part,
        copies,
        4,
    )
    if copies > 1:
        weight_sums = [
            scatter_bits(total.reshape(copies, width // data_parts, hidden_here), copy_masks, f32)
            for total in weight_sums
        ]
    grad_gate_mine, grad_up_mine, grad_down_mine = weight_sums
    grad_down_mine = grad_down_mine.T

    normed_one, mixer_w, out_w, pre, squashed, state, entering = mixer_kept
    grad_inputs, *grad_weights, small_sums, out_others = mixer_backward(
        grad_norm_two,
        normed_one,
        mixer_w,
        out_w,
        pre,
        squashed,
        state,
        mixed,
        unit_one,
        stream,
        cotangent,
        entering,
        bound[None, :],
        live,
        gain_one[None, :],
        scale_one,
        gain_two[None, :],
        out_rows,
        out_moved,
        copies,
        copy_masks,
        3,
    )
    out_sum = lax.dynamic_index_in_dim(out_rows, tensor_index, 0, keepdims=False).astype(f32)
    out_sum += jnp.where(tensor_index > 0, out_others[2].astype(f32), 0.0)
    out_sum += jnp.where(tensor_index < tensor_parts - 1, out_others[3].astype(f32), 0.0)
    output = live_own * (stream + out_sum)
    if copies > 1:
        grad_weights = [scatter_bits(total, copy_masks, f32) for total in grad_weights]
    grad_weights = [total.reshape(own_rows, width) for total in grad_weights]
    place = (data_index * tensor_parts + tensor_index) * own_rows
    small_own = lax.dynamic_slice(
        small_sums.reshape(3, 8, channels),
        (0, lax.div(place, channels), lax.rem(place, channels)),
        (3, 1, own_rows),
    )[:, 0]
    return (
        output,
        grad_inputs,
        small_own[0],
        small_own[1],
        small_own[2],
        *grad_weights,
        grad_gate_mine,
        grad_up_mine,
        grad_down_mine,
    )


def solution(mesh):
    both = ("dp", "tensor")
    placed = (
        P(both, None),
        P("dp"),
        P(both),
        P(both),
        P(both),
        P(both, None),
        P(both, None),
        P(both, None),
        P(both, None),
        P("dp", "tensor"),
        P("dp", "tensor"),
        P("tensor", "dp"),
        P(both, None),
    )
    return jax.shard_map(
        on_device,
        mesh=mesh,
        in_specs=placed,
        out_specs=(
            P(both, None),
            P(both, None),
            P(both),
            P(both),
            P(both),
            P(both, None),
            P(both, None),
            P(both, None),
            P(both, None),
            P("dp", "tensor"),
            P("dp", "tensor"),
            P("tensor", "dp"),
        ),
        check_vma=False,
    )
```
